32 devices in a mesh: dp: 4 (over y, x), tensor: 8 (over z, core).
Axes of the slice: x: 2, y: 2, z: 4, core: 2. Of those that a mesh axis runs over, the one named last changes fastest.
Arguments:
- inputs: bfloat16 [512, 6144], P('dp'), may hold values from -6 to 6
- targets: bfloat16 [512, 6144], P('dp'), may hold values from -6 to 6
- lengths: int32 [4], P('dp'), may hold values from 1 to 128, 384 in all
- ln_gain: float32 [6144], replicated, may hold values from 0.5 to 1.5
- ln_bias: float32 [6144], replicated, may hold values from -0.8 to 0.8
- query_weight: bfloat16 [6144, 3072], P(None, 'tensor'), may hold values from -0.078125 to 0.078125
- w_key: bfloat16 [6144, 3072], P(None, 'tensor'), may hold values from -0.078125 to 0.078125
- value_weight: bfloat16 [6144, 3072], P(None, 'tensor'), may hold values from -0.078125 to 0.078125
- w_out: bfloat16 [3072, 6144], P('tensor'), may hold values from -0.109375 to 0.109375
- down_query: bfloat16 [6144, 16], replicated, may hold values from -0.078125 to 0.078125
- down_value: bfloat16 [6144, 16], replicated, may hold values from -0.078125 to 0.078125
- query_up_factor: float32 [16, 3072], P(None, 'tensor'), may hold values from -0.6 to 0.6
- value_up_factor: float32 [16, 3072], P(None, 'tensor'), may hold values from -0.6 to 0.6
Outputs:
- step_query: float32 [16, 3072], P(None, 'tensor')
- step_value: float32 [16, 3072], P(None, 'tensor')
- remain_query: float32 [16, 3072], P(None, 'tensor')
- remain_value: float32 [16, 3072], P(None, 'tensor')
The draws below stay inside these ranges and needn't reach their ends.
Inputs may be any that keep to these rules, and one draw needn't show every extreme that they name: `lengths`: live tokens of each sequence; one sequence has exactly 128.
All inputs are finite; a program needn't handle non-finite values. No bound on the sum of `lengths` on one device may be relied on, other than what follows from the above.
Results may differ from the reference program's by a relative error of at most 0.035.
Values sent between devices are 32-bit elements; how exact they have to be, the bound alone decides.
No kernel may reach another device: no remote copies, remote signals or barrier semaphores. Data moves between devices by JAX's collectives and lax.ppermute only.
A program may use at most 128 MiB of HBM per device.

```python
import math
import jax
import jax.numpy as jnp
import numpy as np
from jax import lax

D = 6144
HEAD_DIM = 128
R = 16
LENGTH = 128
CG_STEPS = 3
INNER = 3072
SEQS = 4
TOKENS = 512
N_DP = 4


def block_scale(own_key, extent, cuts, least, top_value):
    loudness = 1.0
    for dim, blocks in cuts:
        draws = jax.random.uniform(jax.random.fold_in(jax.random.fold_in(own_key, 6), dim), (blocks,), jnp.float32, least / len(cuts), top_value / len(cuts))
        loudness = loudness * jnp.repeat(jnp.exp(draws), extent[dim] // blocks).reshape((-1,) + (1,) * (len(extent) - 1 - dim))
    return loudness


def length_profile(number_of, total, reach, slope):
    weights = [(1 << 20) // math.isqrt(grade ** slope) + 1 for grade in range(2, number_of + 1)]
    rest, given = total - reach - (number_of - 1), [1] * (number_of - 1)
    while rest > 0:
        free = [i for i in range(number_of - 1) if given[i] < reach]
        pool, remaining = sum([weights[i] for i in free]), rest
        for i in free:
            more = min(reach - given[i], max(1, remaining * weights[i] // pool), rest)
            given[i] = given[i] + more
            rest = rest - more
    return np.array([reach] + given)


def ragged(rng, amount, total, bound, lean):
    if amount == 2:
        one = jax.random.randint(rng, (), max(1, total - bound), min(bound, total - 1) + 1)
        return jnp.stack([one, total - one])
    sizes = jnp.asarray(length_profile(amount, total, bound, lean), jnp.int32)
    pairs = (amount - 1) // 2
    source_of, receiver = sizes[1:1 + 2 * pairs:2], sizes[2:2 + 2 * pairs:2]
    room = jnp.minimum(source_of - 1, bound - receiver)
    shifted = jax.random.randint(jax.random.fold_in(rng, 1), (pairs,), 0, 1 << 20) % (room + 1)
    sizes = sizes.at[1:1 + 2 * pairs:2].set(source_of - shifted).at[2:2 + 2 * pairs:2].set(receiver + shifted)
    return sizes[jax.random.permutation(jax.random.fold_in(rng, 2), amount)]


def scatter_about(key, extent, width, most, pieces=(), kind=jnp.bfloat16):
    entries = jax.random.normal(key, extent, jnp.float32) * width
    if len(pieces) > 0:
        entries = block_scale(key, extent, pieces, -0.22, 0.18) * entries
    return jnp.clip(entries, min=-most, max=most).astype(kind)


def setup_inputs(seed: int = 0) -> dict:
    arg_keys = jax.random.split(jax.random.key(seed), 14)
    inputs = scatter_about(arg_keys[0], (TOKENS, D), 1.0, 6.0, ((0, 4),))
    targets = scatter_about(arg_keys[1], (TOKENS, D), 1.0, 6.0, ((0, 4),))
    lengths = ragged(arg_keys[2], SEQS, N_DP * LENGTH * 3 // 4, LENGTH, 1).astype(jnp.int32)
    ln_gain = jnp.clip(1.0 + 0.1 * jax.random.normal(arg_keys[3], (D,), jnp.float32), 0.5, 1.5)
    ln_bias = scatter_about(arg_keys[4], (D,), 0.2, 0.8, (), jnp.float32)
    query_weight = scatter_about(arg_keys[5], (D, INNER), D ** -0.5, 0.078125, ((1, 8),))
    w_key = scatter_about(arg_keys[6], (D, INNER), D ** -0.5, 0.078125, ((1, 8),))
    value_weight = scatter_about(arg_keys[7], (D, INNER), D ** -0.5, 0.078125, ((1, 8),))
    w_out = scatter_about(arg_keys[8], (INNER, D), INNER ** -0.5, 0.109375, ((0, 8),))
    down_query = scatter_about(arg_keys[9], (D, R), D ** -0.5, 0.078125)
    down_value = scatter_about(arg_keys[10], (D, R), D ** -0.5, 0.078125)
    query_up_factor = scatter_about(arg_keys[11], (R, INNER), 0.1, 0.6, ((1, 8),), jnp.float32)
    value_up_factor = scatter_about(arg_keys[12], (R, INNER), 0.1, 0.6, ((1, 8),), jnp.float32)
    return dict(inputs=inputs, targets=targets, lengths=lengths, ln_gain=ln_gain, ln_bias=ln_bias, query_weight=query_weight, w_key=w_key, value_weight=value_weight, w_out=w_out, down_query=down_query, down_value=down_value, query_up_factor=query_up_factor, value_up_factor=value_up_factor)


EPS = 1e-05
ADAPTER_SCALE = 2.0
DAMP = 0.05
NEG = -1e+30

def layer_norm(rows, gain, bias):
    rows = rows.astype(jnp.float32)
    centred = rows - lax.optimization_barrier(jnp.mean(rows, axis=-1, keepdims=True))
    spread = lax.optimization_barrier(jnp.mean(centred * centred, axis=-1, keepdims=True))
    return (centred * lax.rsqrt(spread + EPS) * gain + bias).astype(jnp.bfloat16)

def attend(ups, normalized_input, query_weight, w_key, value_weight, w_out, down_query, down_value, live):
    query_up_factor, value_up_factor = ups
    length = normalized_input.shape[0]
    heads = query_weight.shape[1] // HEAD_DIM
    query_down_factor = jnp.dot(normalized_input, down_query, preferred_element_type=jnp.float32)
    value_down_factor = jnp.dot(normalized_input, down_value, preferred_element_type=jnp.float32)
    query_rows = jnp.dot(normalized_input, query_weight, preferred_element_type=jnp.float32) + ADAPTER_SCALE * jnp.dot(query_down_factor, query_up_factor, precision=lax.Precision.HIGHEST)
    value_rows = jnp.dot(normalized_input, value_weight, preferred_element_type=jnp.float32) + ADAPTER_SCALE * jnp.dot(value_down_factor, value_up_factor, precision=lax.Precision.HIGHEST)
    keys = jnp.dot(normalized_input, w_key, preferred_element_type=jnp.float32)
    query_rows = query_rows.astype(jnp.bfloat16).reshape(length, heads, HEAD_DIM)
    value_rows = value_rows.astype(jnp.bfloat16).reshape(length, heads, HEAD_DIM)
    keys = keys.astype(jnp.bfloat16).reshape(length, heads, HEAD_DIM)
    scores = jnp.einsum('qhd,khd->hqk', query_rows.astype(jnp.float32), keys.astype(jnp.float32)) * HEAD_DIM ** (-0.5)
    scores = jnp.where(live[None], scores, NEG)
    top = lax.stop_gradient(lax.optimization_barrier(jnp.max(scores, axis=-1, keepdims=True)))
    weights = jnp.exp(scores - top)
    probs = (weights / lax.optimization_barrier(jnp.sum(weights, axis=-1, keepdims=True))).astype(jnp.bfloat16)
    mixed = jnp.einsum('hqk,khd->qhd', probs.astype(jnp.float32), value_rows.astype(jnp.float32))
    mixed = mixed.astype(jnp.bfloat16).reshape(length, heads * HEAD_DIM)
    return jnp.dot(mixed, w_out, preferred_element_type=jnp.float32)

def linear_parts(apply, ups):
    output, pullback = jax.vjp(apply, ups)

    def backward(cotan):
        return pullback(cotan)[0]

    def forward(vector):
        _, undo = jax.vjp(backward, jnp.zeros_like(output))
        return undo(vector)[0]
    return (output, forward, backward)

def local_dot(first, second):
    return jnp.sum(first[0] * second[0]) + jnp.sum(first[1] * second[1])

def reference(inputs, targets, lengths, ln_gain, ln_bias, query_weight, w_key, value_weight, w_out, down_query, down_value, query_up_factor, value_up_factor):
    places = jnp.arange(LENGTH, dtype=jnp.int32)
    seq_inputs = inputs.reshape(SEQS, LENGTH, D)
    seq_targets = targets.reshape(SEQS, LENGTH, D)
    ups = (query_up_factor, value_up_factor)
    zeros = (jnp.zeros_like(query_up_factor), jnp.zeros_like(value_up_factor))

    def linear_map(x_seq, len_seq):
        normalized_input = layer_norm(x_seq, ln_gain, ln_bias)
        live = (places[None, :] <= places[:, None]) & (places[None, :] < len_seq)
        row_live = (places < len_seq).astype(jnp.float32)

        def apply(weights):
            return attend(weights, normalized_input, query_weight, w_key, value_weight, w_out, down_query, down_value, live)
        output, forward, backward = linear_parts(apply, ups)
        return (output, forward, backward, row_live)

    def grad_step(total, item):
        x_seq, t_seq, len_seq = item
        output, forward, backward, row_live = linear_map(x_seq, len_seq)
        gap = x_seq.astype(jnp.float32) - t_seq.astype(jnp.float32)
        error = row_live[:, None] * (output + gap)
        back = backward(error / TOKENS)
        return ((total[0] + back[0], total[1] + back[1]), None)
    grads, _ = lax.scan(grad_step, zeros, (seq_inputs, seq_targets, lengths))

    def product(vector):

        def step(total, item):
            x_seq, len_seq = item
            output, forward, backward, row_live = linear_map(x_seq, len_seq)
            tangent = row_live[:, None] * forward(vector)
            back = backward(tangent / TOKENS)
            return ((total[0] + back[0], total[1] + back[1]), None)
        summed, _ = lax.scan(step, zeros, (seq_inputs, lengths))
        return (summed[0] + DAMP * vector[0], summed[1] + DAMP * vector[1])
    newton = zeros
    remain = (-grads[0], -grads[1])
    direction = remain
    norm_now = local_dot(remain, remain)
    for index in range(CG_STEPS):
        image = product(direction)
        alpha = norm_now / local_dot(direction, image)
        newton = (newton[0] + alpha * direction[0], newton[1] + alpha * direction[1])
        remain = (remain[0] - alpha * image[0], remain[1] - alpha * image[1])
        norm_next = local_dot(remain, remain)
        ratio = norm_next / norm_now
        direction = (remain[0] + ratio * direction[0], remain[1] + ratio * direction[1])
        norm_now = norm_next
    return (newton[0], newton[1], remain[0], remain[1])
```

```python
import jax
import jax.numpy as jnp
from jax import lax
from jax.sharding import PartitionSpec as P

HEAD_DIM = 128
CG_STEPS = 3
CHUNKS = 8

EPS = 1e-05
ADAPTER_SCALE = 2.0
DAMP = 0.05
NEG = -1e30
F32 = jnp.float32
BF16 = jnp.bfloat16
HIGH = lax.Precision.HIGHEST


def layer_norm(rows, gain, bias):
    rows = rows.astype(F32)
    centred = rows - jnp.mean(rows, axis=-1, keepdims=True)
    spread = jnp.mean(centred * centred, axis=-1, keepdims=True)
    return (centred * lax.rsqrt(spread + EPS) * gain + bias).astype(BF16)


def dot32(first, second):
    return jnp.dot(first, second, preferred_element_type=F32)


def heads_of(rows):
    return rows.reshape(rows.shape[0], -1, HEAD_DIM)


def side_by_side(rows):
    return rows.reshape(rows.shape[0], -1)


def line_hops(chips):
    inward = []
    for step in range(chips // 2 - 1):
        inward.append([(step, step + 1), (chips - 1 - step, chips - 2 - step)])
    middle = [(chips // 2 - 1, chips // 2), (chips // 2, chips // 2 - 1)]
    outward = [[(b, a) for a, b in hop] for hop in reversed(inward)]
    return inward, middle, outward


def on_cores(hop):
    return [(2 * a + core, 2 * b + core) for a, b in hop for core in (0, 1)]


def core_swap(devices):
    return [(place, place ^ 1) for place in range(devices)]


def on_device(
    inputs,
    targets,
    lengths,
    ln_gain,
    ln_bias,
    query_weight,
    w_key,
    value_weight,
    w_out,
    down_query,
    down_value,
    query_up_factor,
    value_up_factor,
):
    length, width = inputs.shape
    n_dp = lax.axis_size("dp")
    n_tensor = lax.axis_size("tensor")
    place = lax.axis_index("tensor")
    chip = place // 2
    core = place % 2
    token_count = length * n_dp
    swap = core_swap(n_tensor)
    inward, middle, outward = line_hops(n_tensor // 2)

    places = jnp.arange(length, dtype=jnp.int32)
    limit = lengths[0]
    live = (places[None, :] <= places[:, None]) & (places[None, :] < limit)
    row_live = (places < limit).astype(F32)[:, None]

    half = width // 2
    w_mine = lax.dynamic_slice_in_dim(w_out, core * half, half, 1)
    w_other = lax.dynamic_slice_in_dim(w_out, (1 - core) * half, half, 1)
    cols = half // CHUNKS
    w_mine = [w_mine[:, k * cols : (k + 1) * cols] for k in range(CHUNKS)]
    w_other = [w_other[:, k * cols : (k + 1) * cols] for k in range(CHUNKS)]

    normed = layer_norm(inputs, ln_gain, ln_bias)
    down_q = dot32(normed, down_query)
    down_v = dot32(normed, down_value)
    query = dot32(normed, query_weight) + ADAPTER_SCALE * jnp.dot(
        down_q, query_up_factor, precision=HIGH
    )
    value = dot32(normed, value_weight) + ADAPTER_SCALE * jnp.dot(
        down_v, value_up_factor, precision=HIGH
    )
    query = heads_of(query.astype(BF16))
    value = heads_of(value.astype(BF16))
    key = heads_of(dot32(normed, w_key).astype(BF16))
    scale = HEAD_DIM ** (-0.5)
    scores = jnp.einsum("qhd,khd->hqk", query, key, preferred_element_type=F32) * scale
    scores = jnp.where(live[None], scores, NEG)
    weights = jnp.exp(scores - jnp.max(scores, axis=-1, keepdims=True))
    soft = weights / jnp.sum(weights, axis=-1, keepdims=True)
    probs = soft.astype(BF16)
    mixed = jnp.einsum("hqk,khd->qhd", probs, value, preferred_element_type=F32)
    mixed = side_by_side(mixed.astype(BF16))

    def tangent(vector):
        d_query = ADAPTER_SCALE * jnp.dot(down_q, vector[0], precision=HIGH)
        d_value = ADAPTER_SCALE * jnp.dot(down_v, vector[1], precision=HIGH)
        d_query = heads_of(d_query.astype(BF16))
        d_value = heads_of(d_value.astype(BF16))
        d_scores = jnp.einsum("qhd,khd->hqk", d_query, key, preferred_element_type=F32) * scale
        d_scores = jnp.where(live[None], d_scores, 0.0)
        d_probs = soft * (d_scores - jnp.sum(soft * d_scores, axis=-1, keepdims=True))
        d_mixed = jnp.einsum(
            "hqk,khd->qhd", d_probs.astype(BF16), value, preferred_element_type=F32
        ) + jnp.einsum("hqk,khd->qhd", probs, d_value, preferred_element_type=F32)
        return side_by_side(d_mixed.astype(BF16))

    def cotangent(pulled):
        pulled = heads_of(pulled.astype(BF16))
        d_probs = jnp.einsum("qhd,khd->hqk", pulled, value, preferred_element_type=F32)
        d_value = jnp.einsum("hqk,qhd->khd", probs, pulled, preferred_element_type=F32)
        d_probs = d_probs.astype(BF16).astype(F32)
        d_scores = soft * (d_probs - jnp.sum(soft * d_probs, axis=-1, keepdims=True))
        d_scores = jnp.where(live[None], d_scores, 0.0) * scale
        d_query = jnp.einsum(
            "hqk,khd->qhd", d_scores.astype(BF16), key, preferred_element_type=F32
        )
        d_query = side_by_side(d_query.astype(BF16)).astype(F32)
        d_value = side_by_side(d_value.astype(BF16)).astype(F32)
        share = ADAPTER_SCALE / token_count
        return (
            share * jnp.dot(down_q.T, d_query, precision=HIGH),
            share * jnp.dot(down_v.T, d_value, precision=HIGH),
        )

    def pulled_sum(rows):
        rows = rows * row_live.astype(BF16)
        stages = 3 + len(inward) + len(outward)
        held = [None] * CHUNKS
        total_of = [None] * CHUNKS
        pulled = jnp.zeros((length, rows.shape[1]), F32)
        squares = jnp.zeros((), F32)
        for tick in range(CHUNKS + stages):
            for stage in reversed(range(stages)):
                k = tick - stage
                if k < 0 or k >= CHUNKS:
                    continue
                if stage == 0:
                    sent = dot32(rows, w_other[k])
                    got = lax.ppermute(sent, "tensor", swap)
                    held[k] = dot32(rows, w_mine[k]) + got
                elif stage <= len(inward):
                    got = lax.ppermute(held[k], "tensor", on_cores(inward[stage - 1]))
                    held[k] = held[k] + got
                elif stage == len(inward) + 1:
                    got = lax.ppermute(held[k], "tensor", on_cores(middle))
                    held[k] = held[k] + got
                elif stage < stages - 1:
                    hop = outward[stage - len(inward) - 2]
                    got = lax.ppermute(held[k], "tensor", on_cores(hop))
                    takes = jnp.zeros((), jnp.bool_)
                    for _, to in hop:
                        takes = takes | (chip == to)
                    held[k] = jnp.where(takes, got, held[k])
                else:
                    other = lax.ppermute(held[k], "tensor", swap)
                    squares = squares + jnp.sum(held[k] * held[k]) + jnp.sum(other * other)
                    pulled = (
                        pulled
                        + lax.dot_general(
                            held[k], w_mine[k].astype(F32), (((1,), (1,)), ((), ()))
                        )
                        + lax.dot_general(
                            other, w_other[k].astype(F32), (((1,), (1,)), ((), ()))
                        )
                    )
        return pulled, squares

    def data_sum(part):
        terms = [part] + [
            lax.ppermute(part, "dp", [(d, d ^ step) for d in range(n_dp)])
            for step in range(1, n_dp)
        ]
        while len(terms) > 1:
            terms = [terms[i] + terms[i + 1] for i in range(0, len(terms), 2)]
        return terms[0]

    def head_sum(part):
        step = 1
        while step < n_tensor:
            part = part + lax.ppermute(part, "tensor", [(t, t ^ step) for t in range(n_tensor)])
            step *= 2
        return part

    def local_dot(first, second):
        return jnp.sum(first[0] * second[0]) + jnp.sum(first[1] * second[1])

    def pack(part, extra):
        rows = jnp.full((8, part[0].shape[1]), extra, F32)
        return jnp.concatenate([part[0], part[1], rows], axis=0)

    rank = query_up_factor.shape[0]

    def unpack(block):
        return (block[:rank], block[rank : 2 * rank]), block[2 * rank, 0]

    gap = row_live * (inputs.astype(F32) - targets.astype(F32))
    gap_pulled = lax.dot_general(gap, w_out.astype(F32), (((1,), (1,)), ((), ())))
    pulled, squares = pulled_sum(mixed)
    grads, _ = unpack(data_sum(pack(cotangent(pulled + gap_pulled), squares)))

    newton = (jnp.zeros_like(query_up_factor), jnp.zeros_like(value_up_factor))
    remain = (-grads[0], -grads[1])
    direction = remain
    image = newton
    norm_before = curv = None
    for index in range(CG_STEPS):
        lane = jnp.arange(128, dtype=jnp.int32)[None, :]
        sums = jnp.where(lane == 0, local_dot(remain, remain), local_dot(remain, image))
        sums = head_sum(jnp.broadcast_to(sums, (8, 128)))
        norm, cross = sums[0, 0], sums[0, 1]
        pulled, squares = pulled_sum(tangent(remain))
        part, squares = unpack(data_sum(pack(cotangent(pulled), squares)))
        own = squares / token_count + DAMP * norm
        ratio = norm / norm_before if index else None
        fresh = (part[0] + DAMP * remain[0], part[1] + DAMP * remain[1])
        if index:
            direction = (remain[0] + ratio * direction[0], remain[1] + ratio * direction[1])
            image = (fresh[0] + ratio * image[0], fresh[1] + ratio * image[1])
            curv = own + 2.0 * ratio * cross + ratio * ratio * curv
        else:
            image, curv = fresh, own
        alpha = norm / curv
        newton = (newton[0] + alpha * direction[0], newton[1] + alpha * direction[1])
        remain = (remain[0] - alpha * image[0], remain[1] - alpha * image[1])
        norm_before = norm
    return (newton[0], newton[1], remain[0], remain[1])


def solution(mesh):
    in_specs = (
        P("dp", None),
        P("dp", None),
        P("dp"),
        P(),
        P(),
        P(None, "tensor"),
        P(None, "tensor"),
        P(None, "tensor"),
        P("tensor", None),
        P(),
        P(),
        P(None, "tensor"),
        P(None, "tensor"),
    )
    out_specs = (P(None, "tensor"), P(None, "tensor"), P(None, "tensor"), P(None, "tensor"))
    return jax.shard_map(
        on_device, mesh=mesh, in_specs=in_specs, out_specs=out_specs, check_vma=False
    )
```

```python
import jax
import jax.numpy as jnp
from jax import lax
from jax.sharding import PartitionSpec as P

HEAD_DIM = 128
CG_STEPS = 3
CHUNKS = 1

EPS = 1e-05
ADAPTER_SCALE = 2.0
DAMP = 0.05
NEG = -1e30
F32 = jnp.float32
BF16 = jnp.bfloat16
HIGH = lax.Precision.HIGHEST


def layer_norm(rows, gain, bias):
    rows = rows.astype(F32)
    centred = rows - jnp.mean(rows, axis=-1, keepdims=True)
    spread = jnp.mean(centred * centred, axis=-1, keepdims=True)
    return (centred * lax.rsqrt(spread + EPS) * gain + bias).astype(BF16)


def dot32(first, second):
    return jnp.dot(first, second, preferred_element_type=F32)


def heads_of(rows):
    return rows.reshape(rows.shape[0], -1, HEAD_DIM)


def side_by_side(rows):
    return rows.reshape(rows.shape[0], -1)


def on_device(
    inputs,
    targets,
    lengths,
    ln_gain,
    ln_bias,
    query_weight,
    w_key,
    value_weight,
    w_out,
    down_query,
    down_value,
    query_up_factor,
    value_up_factor,
):
    length, width = inputs.shape
    n_dp = lax.axis_size("dp")
    n_tensor = lax.axis_size("tensor")
    token_count = length * n_dp

    places = jnp.arange(length, dtype=jnp.int32)
    limit = lengths[0]
    live = (places[None, :] <= places[:, None]) & (places[None, :] < limit)
    row_live = (places < limit).astype(F32)[:, None]

    cols = width // CHUNKS
    w_parts = [w_out[:, k * cols : (k + 1) * cols] for k in range(CHUNKS)]

    normed = layer_norm(inputs, ln_gain, ln_bias)
    down_q = dot32(normed, down_query)
    down_v = dot32(normed, down_value)
    query = dot32(normed, query_weight) + ADAPTER_SCALE * jnp.dot(
        down_q, query_up_factor, precision=HIGH
    )
    value = dot32(normed, value_weight) + ADAPTER_SCALE * jnp.dot(
        down_v, value_up_factor, precision=HIGH
    )
    query = heads_of(query.astype(BF16))
    value = heads_of(value.astype(BF16))
    key = heads_of(dot32(normed, w_key).astype(BF16))
    scale = HEAD_DIM ** (-0.5)
    scores = jnp.einsum("qhd,khd->hqk", query, key, preferred_element_type=F32) * scale
    scores = jnp.where(live[None], scores, NEG)
    weights = jnp.exp(scores - jnp.max(scores, axis=-1, keepdims=True))
    soft = weights / jnp.sum(weights, axis=-1, keepdims=True)
    probs = soft.astype(BF16)
    mixed = jnp.einsum("hqk,khd->qhd", probs, value, preferred_element_type=F32)
    mixed = side_by_side(mixed.astype(BF16))

    def tangent(vector):
        d_query = ADAPTER_SCALE * jnp.dot(down_q, vector[0], precision=HIGH)
        d_value = ADAPTER_SCALE * jnp.dot(down_v, vector[1], precision=HIGH)
        d_query = heads_of(d_query.astype(BF16))
        d_value = heads_of(d_value.astype(BF16))
        d_scores = jnp.einsum("qhd,khd->hqk", d_query, key, preferred_element_type=F32) * scale
        d_scores = jnp.where(live[None], d_scores, 0.0)
        d_probs = soft * (d_scores - jnp.sum(soft * d_scores, axis=-1, keepdims=True))
        d_mixed = jnp.einsum(
            "hqk,khd->qhd", d_probs.astype(BF16), value, preferred_element_type=F32
        ) + jnp.einsum("hqk,khd->qhd", probs, d_value, preferred_element_type=F32)
        return side_by_side(d_mixed.astype(BF16))

    def cotangent(pulled):
        pulled = heads_of(pulled.astype(BF16))
        d_probs = jnp.einsum("qhd,khd->hqk", pulled, value, preferred_element_type=F32)
        d_value = jnp.einsum("hqk,qhd->khd", probs, pulled, preferred_element_type=F32)
        d_probs = d_probs.astype(BF16).astype(F32)
        d_scores = soft * (d_probs - jnp.sum(soft * d_probs, axis=-1, keepdims=True))
        d_scores = jnp.where(live[None], d_scores, 0.0) * scale
        d_query = jnp.einsum(
            "hqk,khd->qhd", d_scores.astype(BF16), key, preferred_element_type=F32
        )
        d_query = side_by_side(d_query.astype(BF16)).astype(F32)
        d_value = side_by_side(d_value.astype(BF16)).astype(F32)
        share = ADAPTER_SCALE / token_count
        return (
            share * jnp.dot(down_q.T, d_query, precision=HIGH),
            share * jnp.dot(down_v.T, d_value, precision=HIGH),
        )

    def pulled_sum(rows):
        rows = rows * row_live.astype(BF16)
        sums = [lax.psum(dot32(rows, w), "tensor") for w in w_parts]
        pulled = jnp.zeros((length, rows.shape[1]), F32)
        squares = jnp.zeros((), F32)
        for total, w in zip(sums, w_parts):
            squares = squares + jnp.sum(total * total)
            pulled = pulled + lax.dot_general(total, w.astype(F32), (((1,), (1,)), ((), ())))
        return pulled, squares

    def data_sum(part):
        terms = [part] + [
            lax.ppermute(part, "dp", [(d, d ^ step) for d in range(n_dp)])
            for step in range(1, n_dp)
        ]
        while len(terms) > 1:
            terms = [terms[i] + terms[i + 1] for i in range(0, len(terms), 2)]
        return terms[0]

    def head_sum(part):
        step = 1
        while step < n_tensor:
            part = part + lax.ppermute(part, "tensor", [(t, t ^ step) for t in range(n_tensor)])
            step *= 2
        return part

    def local_dot(first, second):
        return jnp.sum(first[0] * second[0]) + jnp.sum(first[1] * second[1])

    def pack(part, extra):
        rows = jnp.full((8, part[0].shape[1]), extra, F32)
        return jnp.concatenate([part[0], part[1], rows], axis=0)

    rank = query_up_factor.shape[0]

    def unpack(block):
        return (block[:rank], block[rank : 2 * rank]), block[2 * rank, 0]

    gap = row_live * (inputs.astype(F32) - targets.astype(F32))
    gap_pulled = lax.dot_general(gap, w_out.astype(F32), (((1,), (1,)), ((), ())))
    pulled, squares = pulled_sum(mixed)
    grads, _ = unpack(data_sum(pack(cotangent(pulled + gap_pulled), squares)))

    newton = (jnp.zeros_like(query_up_factor), jnp.zeros_like(value_up_factor))
    remain = (-grads[0], -grads[1])
    direction = remain
    image = newton
    norm_before = curv = None
    for index in range(CG_STEPS):
        lane = jnp.arange(128, dtype=jnp.int32)[None, :]
        sums = jnp.where(lane == 0, local_dot(remain, remain), local_dot(remain, image))
        sums = head_sum(jnp.broadcast_to(sums, (8, 128)))
        norm, cross = sums[0, 0], sums[0, 1]
        pulled, squares = pulled_sum(tangent(remain))
        part, squares = unpack(data_sum(pack(cotangent(pulled), squares)))
        own = squares / token_count + DAMP * norm
        ratio = norm / norm_before if index else None
        fresh = (part[0] + DAMP * remain[0], part[1] + DAMP * remain[1])
        if index:
            direction = (remain[0] + ratio * direction[0], remain[1] + ratio * direction[1])
            image = (fresh[0] + ratio * image[0], fresh[1] + ratio * image[1])
            curv = own + 2.0 * ratio * cross + ratio * ratio * curv
        else:
            image, curv = fresh, own
        alpha = norm / curv
        newton = (newton[0] + alpha * direction[0], newton[1] + alpha * direction[1])
        remain = (remain[0] - alpha * image[0], remain[1] - alpha * image[1])
        norm_before = norm
    return (newton[0], newton[1], remain[0], remain[1])


def solution(mesh):
    in_specs = (
        P("dp", None),
        P("dp", None),
        P("dp"),
        P(),
        P(),
        P(None, "tensor"),
        P(None, "tensor"),
        P(None, "tensor"),
        P("tensor", None),
        P(),
        P(),
        P(None, "tensor"),
        P(None, "tensor"),
    )
    out_specs = (P(None, "tensor"), P(None, "tensor"), P(None, "tensor"), P(None, "tensor"))
    return jax.shard_map(
        on_device, mesh=mesh, in_specs=in_specs, out_specs=out_specs, check_vma=False
    )
```

```python
import functools

import jax
import jax.numpy as jnp
from jax import lax
from jax.experimental import pallas as pl
from jax.experimental.pallas import tpu as pltpu
from jax.sharding import Mesh
from jax.sharding import PartitionSpec as P

HEAD_DIM = 128
CG_STEPS = 3
COLUMNS = 512
DEPTH = 512

EPS = 1e-05
ADAPTER_SCALE = 2.0
DAMP = 0.05
NEG = -1e30
F32 = jnp.float32
BF16 = jnp.bfloat16
HIGH = lax.Precision.HIGHEST
SCALE = HEAD_DIM ** (-0.5)
VMEM = pl.BlockSpec(memory_space=pltpu.VMEM)
SMEM = pl.BlockSpec(memory_space=pltpu.SMEM)
LIMIT = 32 * 1024 * 1024


def dot32(first, second):
    return jnp.dot(first, second, preferred_element_type=F32)


def dot_nt(first, second):
    return lax.dot_general(
        first, second, (((1,), (1,)), ((), ())), preferred_element_type=F32
    )


def dot_tn(first, second):
    return lax.dot_general(
        first, second, (((0,), (0,)), ((), ())), preferred_element_type=F32
    )


def high(first, second):
    return jnp.dot(first, second, precision=HIGH, preferred_element_type=F32)


def head(index):
    return slice(index * HEAD_DIM, (index + 1) * HEAD_DIM)


def rows_below(limit, length, width):
    return lax.broadcasted_iota(jnp.int32, (length, width), 0) < limit


def live_pairs(limit, length):
    row = lax.broadcasted_iota(jnp.int32, (length, length), 0)
    column = lax.broadcasted_iota(jnp.int32, (length, length), 1)
    return (column <= row) & (column < limit)


def project_kernel(
    limit_ref, x_ref, gain_ref, bias_ref, wq_ref, wk_ref, wv_ref, aq_ref, av_ref, bq_ref, bv_ref,
    soft_ref, key_ref, value_ref, down_q_ref, down_v_ref, mixed_ref,
    normed, query_sum, key_sum, value_sum,
):
    step = pl.program_id(0)
    length, width = x_ref.shape
    depth = wq_ref.shape[0]

    @pl.when(step == 0)
    def _():
        rows = x_ref[...].astype(F32)
        centred = rows - jnp.sum(rows, axis=-1, keepdims=True) / width
        spread = jnp.sum(centred * centred, axis=-1, keepdims=True) / width
        full = centred * lax.rsqrt(spread + EPS) * gain_ref[...] + bias_ref[...]
        normed[...] = full.astype(BF16)
        query_sum[...] = jnp.zeros_like(query_sum)
        key_sum[...] = jnp.zeros_like(key_sum)
        value_sum[...] = jnp.zeros_like(value_sum)
        down_q_ref[...] = jnp.zeros_like(down_q_ref)
        down_v_ref[...] = jnp.zeros_like(down_v_ref)

    part = normed[:, pl.ds(pl.multiple_of(step * depth, depth), depth)]
    query_sum[...] += dot32(part, wq_ref[...])
    key_sum[...] += dot32(part, wk_ref[...])
    value_sum[...] += dot32(part, wv_ref[...])
    down_q_ref[...] += dot32(part, aq_ref[...])
    down_v_ref[...] += dot32(part, av_ref[...])

    @pl.when(step == pl.num_programs(0) - 1)
    def _():
        limit = limit_ref[0]
        live = live_pairs(limit, length)
        kept = rows_below(limit, length, HEAD_DIM)
        query = query_sum[...] + ADAPTER_SCALE * high(down_q_ref[...], bq_ref[...])
        value = value_sum[...] + ADAPTER_SCALE * high(down_v_ref[...], bv_ref[...])
        query = query.astype(BF16)
        value = value.astype(BF16)
        key = key_sum[...].astype(BF16)
        key_ref[...] = key
        value_ref[...] = value
        for h in range(key.shape[1] // HEAD_DIM):
            scores = dot_nt(query[:, head(h)], key[:, head(h)]) * SCALE
            scores = jnp.where(live, scores, NEG)
            weights = jnp.exp(scores - jnp.max(scores, axis=-1, keepdims=True))
            soft = weights / jnp.sum(weights, axis=-1, keepdims=True)
            soft_ref[h] = soft
            mixed = dot32(soft.astype(BF16), value[:, head(h)]).astype(BF16)
            mixed_ref[:, head(h)] = jnp.where(kept, mixed.astype(F32), 0.0)


def project(limit, x, gain, bias, wq, wk, wv, aq, av, bq, bv):
    length, width = x.shape
    inner = wq.shape[1]
    rank = aq.shape[1]
    heads = inner // HEAD_DIM
    whole = lambda i: (0, 0)
    deep = lambda i: (i, 0)
    return pl.pallas_call(
        project_kernel,
        grid=(width // DEPTH,),
        in_specs=[
            SMEM,
            pl.BlockSpec((length, width), whole),
            pl.BlockSpec((1, width), whole),
            pl.BlockSpec((1, width), whole),
            pl.BlockSpec((DEPTH, inner), deep),
            pl.BlockSpec((DEPTH, inner), deep),
            pl.BlockSpec((DEPTH, inner), deep),
            pl.BlockSpec((DEPTH, rank), deep),
            pl.BlockSpec((DEPTH, rank), deep),
            pl.BlockSpec((rank, inner), whole),
            pl.BlockSpec((rank, inner), whole),
        ],
        out_specs=[
            pl.BlockSpec((heads, length, length), lambda i: (0, 0, 0)),
            pl.BlockSpec((length, inner), whole),
            pl.BlockSpec((length, inner), whole),
            pl.BlockSpec((length, rank), whole),
            pl.BlockSpec((length, rank), whole),
            pl.BlockSpec((length, inner), whole),
        ],
        out_shape=[
            jax.ShapeDtypeStruct((heads, length, length), F32),
            jax.ShapeDtypeStruct((length, inner), BF16),
            jax.ShapeDtypeStruct((length, inner), BF16),
            jax.ShapeDtypeStruct((length, rank), F32),
            jax.ShapeDtypeStruct((length, rank), F32),
            jax.ShapeDtypeStruct((length, inner), F32),
        ],
        scratch_shapes=[
            pltpu.VMEM((length, width), BF16),
            pltpu.VMEM((length, inner), F32),
            pltpu.VMEM((length, inner), F32),
            pltpu.VMEM((length, inner), F32),
        ],
        compiler_params=pltpu.CompilerParams(vmem_limit_bytes=LIMIT),
        cost_estimate=pl.CostEstimate(
            flops=6 * length * width * inner, bytes_accessed=6 * width * inner, transcendentals=0
        ),
    )(limit, x, gain[None], bias[None], wq, wk, wv, aq, av, bq, bv)


def pair_kernel(core_ref, own_ref, got_ref, out_ref):
    inner = own_ref.shape[0]
    out_ref[:inner] = own_ref[...]
    out_ref[inner:] = got_ref[...].astype(BF16)


def pair_weights(core, w_out, got):
    inner, half = got.shape
    blocks = half // COLUMNS
    return pl.pallas_call(
        pair_kernel,
        grid_spec=pltpu.PrefetchScalarGridSpec(
            num_scalar_prefetch=1,
            grid=(blocks,),
            in_specs=[
                pl.BlockSpec((inner, COLUMNS), lambda i, core: (0, core[0] * blocks + i)),
                pl.BlockSpec((inner, COLUMNS), lambda i, core: (0, i)),
            ],
            out_specs=pl.BlockSpec((2 * inner, COLUMNS), lambda i, core: (0, i)),
        ),
        out_shape=jax.ShapeDtypeStruct((2 * inner, half), BF16),
        compiler_params=pltpu.CompilerParams(vmem_limit_bytes=LIMIT),
    )(core, w_out, got)


def spread_kernel(own_ref, got_ref, w_ref, out_ref):
    inner = own_ref.shape[1]
    out_ref[...] = dot32(own_ref[...].astype(BF16), w_ref[:inner]) + dot32(
        got_ref[...].astype(BF16), w_ref[inner:]
    )


def spread(own, got, pair):
    length, inner = own.shape
    half = pair.shape[1]
    whole = lambda i: (0, 0)
    across = lambda i: (0, i)
    return pl.pallas_call(
        spread_kernel,
        grid=(half // COLUMNS,),
        in_specs=[
            pl.BlockSpec((length, inner), whole),
            pl.BlockSpec((length, inner), whole),
            pl.BlockSpec((2 * inner, COLUMNS), across),
        ],
        out_specs=pl.BlockSpec((length, COLUMNS), across),
        out_shape=jax.ShapeDtypeStruct((length, half), F32),
        compiler_params=pltpu.CompilerParams(vmem_limit_bytes=LIMIT),
    )(own, got, pair)


def gather_kernel(has_gap, core_ref, *refs):
    if has_gap:
        limit_ref, total_ref, x_ref, t_ref, w_ref, own_ref, other_ref = refs
    else:
        total_ref, w_ref, own_ref, other_ref = refs
    step = pl.program_id(0)
    length, inner = own_ref.shape
    total = total_ref[...]
    if has_gap:
        gap = x_ref[...].astype(F32) - t_ref[...].astype(F32)
        kept = rows_below(limit_ref[0], length, total.shape[1])
        total = jnp.where(kept, total + gap, 0.0)

    @pl.when(step == 0)
    def _():
        own_ref[...] = jnp.zeros_like(own_ref)
        other_ref[...] = jnp.zeros_like(other_ref)

    rounded = total.astype(BF16)
    own_ref[...] += dot_nt(rounded, w_ref[:inner])
    other_ref[:length] += dot_nt(rounded, w_ref[inner:])
    other_ref[length:] += jnp.sum(total * total)


def gather(core, total, pair, gap):
    length, half = total.shape
    inner = pair.shape[0] // 2
    blocks = half // COLUMNS
    whole = lambda i, core: (0, 0)
    across = lambda i, core: (0, i)
    chosen = lambda i, core: (0, core[0] * blocks + i)
    specs = [pl.BlockSpec((length, COLUMNS), across)]
    args = [total]
    if gap is not None:
        limit, x, t = gap
        specs = [SMEM] + specs + [pl.BlockSpec((length, COLUMNS), chosen)] * 2
        args = [limit] + args + [x, t]
    specs.append(pl.BlockSpec((2 * inner, COLUMNS), across))
    args.append(pair)
    return pl.pallas_call(
        functools.partial(gather_kernel, gap is not None),
        grid_spec=pltpu.PrefetchScalarGridSpec(
            num_scalar_prefetch=1,
            grid=(blocks,),
            in_specs=specs,
            out_specs=[
                pl.BlockSpec((length, inner), whole),
                pl.BlockSpec((length + 8, inner), whole),
            ],
        ),
        out_shape=[
            jax.ShapeDtypeStruct((length, inner), F32),
            jax.ShapeDtypeStruct((length + 8, inner), F32),
        ],
        compiler_params=pltpu.CompilerParams(vmem_limit_bytes=LIMIT),
    )(core, *args)


def cotangent_kernel(
    share, limit_ref, own_ref, other_ref, got_ref, soft_ref, key_ref, value_ref, down_q_ref,
    down_v_ref, out_ref,
):
    length, inner = own_ref.shape
    rank = down_q_ref.shape[1]
    live = live_pairs(limit_ref[0], length)
    pulled = (own_ref[...] + got_ref[:length]).astype(BF16)
    out_ref[2 * rank :] = other_ref[length:] + got_ref[length:]
    for h in range(inner // HEAD_DIM):
        soft = soft_ref[h]
        rows = pulled[:, head(h)]
        d_probs = dot_nt(rows, value_ref[:, head(h)]).astype(BF16).astype(F32)
        d_value = dot_tn(soft.astype(BF16), rows).astype(BF16).astype(F32)
        d_scores = soft * (d_probs - jnp.sum(soft * d_probs, axis=-1, keepdims=True))
        d_scores = jnp.where(live, d_scores, 0.0) * SCALE
        d_query = dot32(d_scores.astype(BF16), key_ref[:, head(h)]).astype(BF16).astype(F32)
        out_ref[:rank, head(h)] = share * lax.dot_general(
            down_q_ref[...], d_query, (((0,), (0,)), ((), ())), precision=HIGH,
            preferred_element_type=F32,
        )
        out_ref[rank : 2 * rank, head(h)] = share * lax.dot_general(
            down_v_ref[...], d_value, (((0,), (0,)), ((), ())), precision=HIGH,
            preferred_element_type=F32,
        )


def cotangent(share, limit, own, other, got, attention):
    inner = own.shape[1]
    rank = attention[3].shape[1]
    return pl.pallas_call(
        functools.partial(cotangent_kernel, share),
        in_specs=[SMEM] + [VMEM] * 8,
        out_specs=VMEM,
        out_shape=jax.ShapeDtypeStruct((2 * rank + 8, inner), F32),
        compiler_params=pltpu.CompilerParams(vmem_limit_bytes=LIMIT),
    )(limit, own, other, got, *attention)


def tangent_of(vector, limit, soft_ref, key_ref, value_ref, down_q_ref, down_v_ref, out_ref):
    length = key_ref.shape[0]
    rank = down_q_ref.shape[1]
    live = live_pairs(limit, length)
    kept = rows_below(limit, length, HEAD_DIM)
    d_query = (ADAPTER_SCALE * high(down_q_ref[...], vector[:rank])).astype(BF16)
    d_value = (ADAPTER_SCALE * high(down_v_ref[...], vector[rank:])).astype(BF16)
    for h in range(key_ref.shape[1] // HEAD_DIM):
        soft = soft_ref[h]
        d_scores = dot_nt(d_query[:, head(h)], key_ref[:, head(h)]) * SCALE
        d_scores = jnp.where(live, d_scores, 0.0)
        d_probs = soft * (d_scores - jnp.sum(soft * d_scores, axis=-1, keepdims=True))
        d_mixed = dot32(d_probs.astype(BF16), value_ref[:, head(h)]) + dot32(
            soft.astype(BF16), d_value[:, head(h)]
        )
        out_ref[:, head(h)] = jnp.where(kept, d_mixed.astype(BF16).astype(F32), 0.0)


def total_of(terms):
    while len(terms) > 1:
        terms = [terms[i] + terms[i + 1] for i in range(0, len(terms), 2)]
    return terms[0]


def put_sums(sums_ref, remain, image):
    lane = lax.broadcasted_iota(jnp.int32, sums_ref.shape, 1)
    cross = 0.0 if image is None else jnp.sum(remain * image)
    sums_ref[...] = jnp.where(lane == 0, jnp.sum(remain * remain), cross)


def first_kernel(n_dp, *refs):
    terms, refs = refs[:n_dp], refs[n_dp:]
    limit_ref, *attention, remain_ref, sums_ref, out_ref = refs
    grads = total_of([term[...] for term in terms])
    remain = -grads[: remain_ref.shape[0]]
    remain_ref[...] = remain
    put_sums(sums_ref, remain, None)
    tangent_of(remain, limit_ref[0], *attention, out_ref)


def first_step(terms, limit, attention):
    inner = terms[0].shape[1]
    length = attention[1].shape[0]
    rank = attention[3].shape[1]
    return pl.pallas_call(
        functools.partial(first_kernel, len(terms)),
        in_specs=[VMEM] * len(terms) + [SMEM] + [VMEM] * 5,
        out_specs=[VMEM] * 3,
        out_shape=[
            jax.ShapeDtypeStruct((2 * rank, inner), F32),
            jax.ShapeDtypeStruct((8, 128), F32),
            jax.ShapeDtypeStruct((length, inner), F32),
        ],
        compiler_params=pltpu.CompilerParams(vmem_limit_bytes=LIMIT),
    )(*terms, limit, *attention)


def step_kernel(n_dp, token_count, index, last, *refs):
    terms, refs = refs[:n_dp], refs[n_dp:]
    sums_ref, remain_ref, *refs = refs
    if index:
        before_ref, newton_ref, direction_ref, image_ref, *refs = refs
    part = total_of([term[...] for term in terms])
    remain = remain_ref[...]
    rows = remain.shape[0]
    norm, cross = sums_ref[:1, 0:1], sums_ref[:1, 1:2]
    fresh = part[:rows] + DAMP * remain
    curv = part[rows : rows + 1, 0:1] / token_count + DAMP * norm
    if index:
        ratio = norm / before_ref[:1, 0:1]
        curv = curv + 2.0 * ratio * cross + ratio * ratio * before_ref[:1, 1:2]
        direction = remain + ratio * direction_ref[...]
        image = fresh + ratio * image_ref[...]
    else:
        direction, image = remain, fresh
    alpha = norm / curv
    newton = alpha * direction
    if index:
        newton = newton_ref[...] + newton
    remain = remain - alpha * image
    if last:
        step_q_ref, step_v_ref, remain_q_ref, remain_v_ref = refs
        rank = rows // 2
        step_q_ref[...] = newton[:rank]
        step_v_ref[...] = newton[rank:]
        remain_q_ref[...] = remain[:rank]
        remain_v_ref[...] = remain[rank:]
        return
    limit_ref, *refs = refs
    attention, refs = refs[:5], refs[5:]
    next_remain, next_before, next_newton, next_direction, next_image, next_sums, out_ref = refs
    lane = lax.broadcasted_iota(jnp.int32, next_before.shape, 1)
    next_remain[...] = remain
    next_before[...] = jnp.where(lane == 0, norm, curv)
    next_newton[...] = newton
    next_direction[...] = direction
    next_image[...] = image
    put_sums(next_sums, remain, image)
    tangent_of(remain, limit_ref[0], *attention, out_ref)


def cg_step(index, token_count, terms, sums, remain, state, limit, attention):
    last = index == CG_STEPS - 1
    rows, inner = remain.shape
    matrix = jax.ShapeDtypeStruct((rows, inner), F32)
    scalars = jax.ShapeDtypeStruct((8, 128), F32)
    args = [*terms, sums, remain, *state]
    specs = [VMEM] * len(args)
    if last:
        shapes = [jax.ShapeDtypeStruct((rows // 2, inner), F32)] * 4
    else:
        args += [limit, *attention]
        specs += [SMEM] + [VMEM] * 5
        length = attention[1].shape[0]
        shapes = [matrix, scalars, matrix, matrix, matrix, scalars]
        shapes.append(jax.ShapeDtypeStruct((length, inner), F32))
    return pl.pallas_call(
        functools.partial(step_kernel, len(terms), token_count, index, last),
        in_specs=specs,
        out_specs=[VMEM] * len(shapes),
        out_shape=shapes,
        compiler_params=pltpu.CompilerParams(vmem_limit_bytes=LIMIT),
    )(*args)


def on_device(
    inputs,
    targets,
    lengths,
    ln_gain,
    ln_bias,
    query_weight,
    w_key,
    value_weight,
    w_out,
    down_query,
    down_value,
    query_up_factor,
    value_up_factor,
):
    length, width = inputs.shape
    n_dp = lax.axis_size("dp")
    n_chip = lax.axis_size("chip")
    core = lax.axis_index("core")
    token_count = length * n_dp
    half = width // 2

    def swap(part):
        return lax.ppermute(part, "core", [(0, 1), (1, 0)])

    def data_terms(part):
        return [part] + [
            lax.ppermute(part, "dp", [(d, d ^ step) for d in range(n_dp)])
            for step in range(1, n_dp)
        ]

    def head_sum(part):
        part = part + swap(part)
        step = 1
        while step < n_chip:
            part = part + lax.ppermute(part, "chip", [(c, c ^ step) for c in range(n_chip)])
            step *= 2
        return part

    where = core.astype(jnp.int32)[None]
    sent = lax.dynamic_slice_in_dim(w_out, (1 - core) * half, half, 1).astype(F32)
    pair = pair_weights(where, w_out, swap(sent))

    soft, key, value, down_q, down_v, mixed = project(
        lengths, inputs, ln_gain, ln_bias, query_weight, w_key, value_weight, down_query,
        down_value, query_up_factor, value_up_factor,
    )
    attention = (soft, key, value, down_q, down_v)

    def product(rows, gap):
        total = lax.psum(spread(rows, swap(rows), pair), "chip")
        own, other = gather(where, total, pair, gap)
        share = ADAPTER_SCALE / token_count
        return data_terms(cotangent(share, lengths, own, other, swap(other), attention))

    terms = product(mixed, (lengths, inputs, targets))
    remain, sums, rows = first_step(terms, lengths, attention)
    state = ()
    for index in range(CG_STEPS):
        sums = head_sum(sums)
        terms = product(rows, None)
        out = cg_step(index, token_count, terms, sums, remain, state, lengths, attention)
        if index < CG_STEPS - 1:
            remain, *state, sums, rows = out
    return tuple(out)


def solution(mesh):
    fine = Mesh(mesh.devices.reshape(mesh.shape["dp"], -1, 2), ("dp", "chip", "core"))
    tensor = ("chip", "core")
    in_specs = (
        P("dp", None),
        P("dp", None),
        P("dp"),
        P(),
        P(),
        P(None, tensor),
        P(None, tensor),
        P(None, tensor),
        P(tensor, None),
        P(),
        P(),
        P(None, tensor),
        P(None, tensor),
    )
    out_specs = (P(None, tensor),) * 4
    return jax.shard_map(
        on_device, mesh=fine, in_specs=in_specs, out_specs=out_specs, check_vma=False
    )
```

```python
import functools

import jax
import jax.numpy as jnp
from jax import lax
from jax.experimental import pallas as pl
from jax.experimental.pallas import tpu as pltpu
from jax.sharding import Mesh
from jax.sharding import PartitionSpec as P

HEAD_DIM = 128
CG_STEPS = 3
CHUNKS = 4
AHEAD = 2
DEPTH = 512

EPS = 1e-05
ADAPTER_SCALE = 2.0
DAMP = 0.05
NEG = -1e30
F32 = jnp.float32
BF16 = jnp.bfloat16
HIGH = lax.Precision.HIGHEST
SCALE = HEAD_DIM ** (-0.5)
VMEM = pl.BlockSpec(memory_space=pltpu.VMEM)
SMEM = pl.BlockSpec(memory_space=pltpu.SMEM)
LIMIT = 32 * 1024 * 1024
STEP_COST = pl.CostEstimate(flops=10**9, bytes_accessed=10**7, transcendentals=0)
STREAM_LIMIT = 56 * 1024 * 1024


def dot32(first, second):
    return jnp.dot(first, second, preferred_element_type=F32)


def dot_nt(first, second):
    return lax.dot_general(
        first, second, (((1,), (1,)), ((), ())), preferred_element_type=F32
    )


def dot_tn(first, second):
    return lax.dot_general(
        first, second, (((0,), (0,)), ((), ())), preferred_element_type=F32
    )


def high(first, second):
    return jnp.dot(first, second, precision=HIGH, preferred_element_type=F32)


def head(index):
    return slice(index * HEAD_DIM, (index + 1) * HEAD_DIM)


def rows_below(limit, length, width):
    return lax.broadcasted_iota(jnp.int32, (length, width), 0) < limit


def live_pairs(limit, length):
    row = lax.broadcasted_iota(jnp.int32, (length, length), 0)
    column = lax.broadcasted_iota(jnp.int32, (length, length), 1)
    return (column <= row) & (column < limit)


def project_kernel(
    limit_ref, x_ref, gain_ref, bias_ref, wq_ref, wk_ref, wv_ref, aq_ref, av_ref, bq_ref, bv_ref,
    soft_ref, key_ref, value_ref, down_q_ref, down_v_ref, mixed_ref,
    normed, query_sum, key_sum, value_sum,
):
    step = pl.program_id(0)
    length, width = x_ref.shape
    depth = wq_ref.shape[0]

    @pl.when(step == 0)
    def _():
        rows = x_ref[...].astype(F32)
        centred = rows - jnp.sum(rows, axis=-1, keepdims=True) / width
        spread = jnp.sum(centred * centred, axis=-1, keepdims=True) / width
        full = centred * lax.rsqrt(spread + EPS) * gain_ref[...] + bias_ref[...]
        normed[...] = full.astype(BF16)
        query_sum[...] = jnp.zeros_like(query_sum)
        key_sum[...] = jnp.zeros_like(key_sum)
        value_sum[...] = jnp.zeros_like(value_sum)
        down_q_ref[...] = jnp.zeros_like(down_q_ref)
        down_v_ref[...] = jnp.zeros_like(down_v_ref)

    part = normed[:, pl.ds(pl.multiple_of(step * depth, depth), depth)]
    query_sum[...] += dot32(part, wq_ref[...])
    key_sum[...] += dot32(part, wk_ref[...])
    value_sum[...] += dot32(part, wv_ref[...])
    down_q_ref[...] += dot32(part, aq_ref[...])
    down_v_ref[...] += dot32(part, av_ref[...])

    @pl.when(step == pl.num_programs(0) - 1)
    def _():
        limit = limit_ref[0]
        live = live_pairs(limit, length)
        kept = rows_below(limit, length, HEAD_DIM)
        query = query_sum[...] + ADAPTER_SCALE * high(down_q_ref[...], bq_ref[...])
        value = value_sum[...] + ADAPTER_SCALE * high(down_v_ref[...], bv_ref[...])
        query = query.astype(BF16)
        value = value.astype(BF16)
        key = key_sum[...].astype(BF16)
        key_ref[...] = key
        value_ref[...] = value
        for h in range(key.shape[1] // HEAD_DIM):
            scores = dot_nt(query[:, head(h)], key[:, head(h)]) * SCALE
            scores = jnp.where(live, scores, NEG)
            weights = jnp.exp(scores - jnp.max(scores, axis=-1, keepdims=True))
            soft = weights / jnp.sum(weights, axis=-1, keepdims=True)
            soft_ref[h] = soft
            mixed = dot32(soft.astype(BF16), value[:, head(h)]).astype(BF16)
            mixed_ref[:length, head(h)] = jnp.where(kept, mixed.astype(F32), 0.0)
        mixed_ref[length:] = jnp.zeros((8, key.shape[1]), F32)


def project(limit, x, gain, bias, wq, wk, wv, aq, av, bq, bv):
    length, width = x.shape
    inner = wq.shape[1]
    rank = aq.shape[1]
    heads = inner // HEAD_DIM
    whole = lambda i: (0, 0)
    deep = lambda i: (i, 0)
    return pl.pallas_call(
        project_kernel,
        grid=(width // DEPTH,),
        in_specs=[
            SMEM,
            pl.BlockSpec((length, width), whole),
            pl.BlockSpec((1, width), whole),
            pl.BlockSpec((1, width), whole),
            pl.BlockSpec((DEPTH, inner), deep),
            pl.BlockSpec((DEPTH, inner), deep),
            pl.BlockSpec((DEPTH, inner), deep),
            pl.BlockSpec((DEPTH, rank), deep),
            pl.BlockSpec((DEPTH, rank), deep),
            pl.BlockSpec((rank, inner), whole),
            pl.BlockSpec((rank, inner), whole),
        ],
        out_specs=[
            pl.BlockSpec((heads, length, length), lambda i: (0, 0, 0)),
            pl.BlockSpec((length, inner), whole),
            pl.BlockSpec((length, inner), whole),
            pl.BlockSpec((length, rank), whole),
            pl.BlockSpec((length, rank), whole),
            pl.BlockSpec((length + 8, inner), whole),
        ],
        out_shape=[
            jax.ShapeDtypeStruct((heads, length, length), F32),
            jax.ShapeDtypeStruct((length, inner), BF16),
            jax.ShapeDtypeStruct((length, inner), BF16),
            jax.ShapeDtypeStruct((length, rank), F32),
            jax.ShapeDtypeStruct((length, rank), F32),
            jax.ShapeDtypeStruct((length + 8, inner), F32),
        ],
        scratch_shapes=[
            pltpu.VMEM((length, width), BF16),
            pltpu.VMEM((length, inner), F32),
            pltpu.VMEM((length, inner), F32),
            pltpu.VMEM((length, inner), F32),
        ],
        compiler_params=pltpu.CompilerParams(vmem_limit_bytes=STREAM_LIMIT),
        cost_estimate=pl.CostEstimate(
            flops=6 * length * width * inner, bytes_accessed=6 * width * inner, transcendentals=0
        ),
    )(limit, x, gain[None], bias[None], wq, wk, wv, aq, av, bq, bv)


def token_spec():
    return pl.BlockSpec(memory_space=pl.ANY)


def call(kernel, ins, outs, token, scalars=()):
    tokens = [] if token is None else [token]

    def body(*refs):
        count = len(scalars) + len(ins)
        kernel(*refs[:count], *refs[count + len(tokens) :])

    return pl.pallas_call(
        body,
        in_specs=[SMEM] * len(scalars) + [VMEM] * len(ins) + [token_spec()] * len(tokens),
        out_specs=[VMEM] * len(outs),
        out_shape=[jax.ShapeDtypeStruct(shape, kind) for shape, kind in outs],
        compiler_params=pltpu.CompilerParams(vmem_limit_bytes=LIMIT),
        cost_estimate=STEP_COST,
    )(*scalars, *ins, *tokens)


def rows_of(own_ref, got_ref, length):
    return jnp.concatenate(
        [own_ref[:length].astype(BF16), got_ref[:length].astype(BF16)], axis=1
    )


def put_tail(out_ref, own_ref, got_ref, length):
    inner = own_ref.shape[1]
    out_ref[length:, inner:] = jnp.zeros((8, out_ref.shape[1] - inner), F32)
    out_ref[length:, :inner] = own_ref[length:] + got_ref[length:]


def first_spread_kernel(tail, length, core_ref, own_ref, got_ref, w_ref, other_w_ref, *refs):
    out_ref, pair_ref = refs[-2:]
    inner = own_ref.shape[1]
    pair_ref[:inner] = w_ref[...]
    pair_ref[inner:] = other_w_ref[...].astype(BF16)
    out_ref[:length] = dot32(rows_of(own_ref, got_ref, length), pair_ref[...])
    if tail:
        put_tail(out_ref, own_ref, got_ref, length)


def first_spread(index, chunks, length, core, own, got, w_out, other_w, token):
    inner, half = other_w.shape
    cols = half // chunks
    height = length + (8 if index == 0 else 0)
    whole = lambda i, core: (0, 0)
    tokens = [] if token is None else [token]
    return pl.pallas_call(
        functools.partial(first_spread_kernel, index == 0, length),
        grid_spec=pltpu.PrefetchScalarGridSpec(
            num_scalar_prefetch=1,
            grid=(1,),
            in_specs=[
                pl.BlockSpec(own.shape, whole),
                pl.BlockSpec(own.shape, whole),
                pl.BlockSpec((inner, cols), lambda i, core: (0, core[0] * chunks + index)),
                pl.BlockSpec((inner, cols), lambda i, core: (0, index)),
            ] + [token_spec()] * len(tokens),
            out_specs=[
                pl.BlockSpec((height, cols), whole),
                pl.BlockSpec((2 * inner, cols), whole),
            ],
        ),
        out_shape=[
            jax.ShapeDtypeStruct((height, cols), F32),
            jax.ShapeDtypeStruct((2 * inner, cols), BF16),
        ],
        compiler_params=pltpu.CompilerParams(vmem_limit_bytes=LIMIT),
        cost_estimate=STEP_COST,
    )(core, own, got, w_out, other_w, *tokens)


def spread(index, length, own, got, pair, token):
    height = length + (8 if index == 0 else 0)

    def kernel(own_ref, got_ref, pair_ref, out_ref):
        out_ref[:length] = dot32(rows_of(own_ref, got_ref, length), pair_ref[...])
        if index == 0:
            put_tail(out_ref, own_ref, got_ref, length)

    return call(kernel, [own, got, pair], [((height, pair.shape[1]), F32)], token)[0]


def add(first, second, token):
    def kernel(first_ref, second_ref, out_ref):
        out_ref[...] = first_ref[...] + second_ref[...]

    return call(kernel, [first, second], [(first.shape, F32)], token)[0]


def choose(takes, got, held, token):
    def kernel(takes_ref, got_ref, held_ref, out_ref):
        out_ref[...] = jnp.where(takes_ref[0] > 0, got_ref[...], held_ref[...])

    return call(kernel, [got, held], [(held.shape, F32)], token, [takes])[0]


def gather(index, takes, got, held, pair, sums, limit, gap, token):
    inner = pair.shape[0] // 2
    extra = [] if gap is None else [gap]
    length = held.shape[0] - (8 if index == 0 else 0)

    def kernel(takes_ref, limit_ref, got_ref, held_ref, pair_ref, *refs):
        refs = list(refs)
        gap_ref = refs.pop(0) if gap is not None else None
        before = [refs.pop(0), refs.pop(0)] if index else None
        own_ref, other_ref = refs[:2]
        total = jnp.where(takes_ref[0] > 0, got_ref[...], held_ref[...])
        if index == 0:
            refs[2][...] = total[length:, :128]
            total = total[:length]
        if gap_ref is not None:
            kept = rows_below(limit_ref[0], length, total.shape[1])
            total = jnp.where(kept, total + gap_ref[...], 0.0)
        rounded = total.astype(BF16)
        own = dot_nt(rounded, pair_ref[:inner])
        other = dot_nt(rounded, pair_ref[inner:])
        squares = jnp.full((8, inner), jnp.sum(total * total), F32)
        if index:
            own = own + before[0][...]
            other = other + before[1][:length]
            squares = squares + before[1][length:]
        own_ref[...] = own
        other_ref[:length] = other
        other_ref[length:] = squares

    outs = [((length, inner), F32), ((length + 8, inner), F32)]
    if index == 0:
        outs.append(((8, 128), F32))
    return call(kernel, [got, held, pair] + extra + sums, outs, token, [takes, limit])


def line_hops(chips):
    inward = []
    for step in range(chips // 2 - 1):
        inward.append([(step, step + 1), (chips - 1 - step, chips - 2 - step)])
    middle = [(chips // 2 - 1, chips // 2), (chips // 2, chips // 2 - 1)]
    outward = [[(b, a) for a, b in hop] for hop in reversed(inward)]
    return inward + [middle], outward


def cotangent_kernel(
    share, limit_ref, own_ref, other_ref, got_ref, soft_ref, key_ref, value_ref, down_q_ref,
    down_v_ref, out_ref,
):
    length, inner = own_ref.shape
    rank = down_q_ref.shape[1]
    live = live_pairs(limit_ref[0], length)
    pulled = (own_ref[...] + got_ref[:length]).astype(BF16)
    out_ref[2 * rank :] = other_ref[length:] + got_ref[length:]
    for h in range(inner // HEAD_DIM):
        soft = soft_ref[h]
        rows = pulled[:, head(h)]
        d_probs = dot_nt(rows, value_ref[:, head(h)]).astype(BF16).astype(F32)
        d_value = dot_tn(soft.astype(BF16), rows).astype(BF16).astype(F32)
        d_scores = soft * (d_probs - jnp.sum(soft * d_probs, axis=-1, keepdims=True))
        d_scores = jnp.where(live, d_scores, 0.0) * SCALE
        d_query = dot32(d_scores.astype(BF16), key_ref[:, head(h)]).astype(BF16).astype(F32)
        out_ref[:rank, head(h)] = share * lax.dot_general(
            down_q_ref[...], d_query, (((0,), (0,)), ((), ())), precision=HIGH,
            preferred_element_type=F32,
        )
        out_ref[rank : 2 * rank, head(h)] = share * lax.dot_general(
            down_v_ref[...], d_value, (((0,), (0,)), ((), ())), precision=HIGH,
            preferred_element_type=F32,
        )


def cotangent(share, limit, own, other, got, attention):
    inner = own.shape[1]
    rank = attention[3].shape[1]
    return pl.pallas_call(
        functools.partial(cotangent_kernel, share),
        in_specs=[SMEM] + [VMEM] * 8,
        out_specs=VMEM,
        out_shape=jax.ShapeDtypeStruct((2 * rank + 8, inner), F32),
        compiler_params=pltpu.CompilerParams(vmem_limit_bytes=LIMIT),
    )(limit, own, other, got, *attention)


def tangent_of(vector, limit, soft_ref, key_ref, value_ref, down_q_ref, down_v_ref, out_ref):
    length = key_ref.shape[0]
    rank = down_q_ref.shape[1]
    live = live_pairs(limit, length)
    kept = rows_below(limit, length, HEAD_DIM)
    d_query = (ADAPTER_SCALE * high(down_q_ref[...], vector[:rank])).astype(BF16)
    d_value = (ADAPTER_SCALE * high(down_v_ref[...], vector[rank:])).astype(BF16)
    for h in range(key_ref.shape[1] // HEAD_DIM):
        soft = soft_ref[h]
        d_scores = dot_nt(d_query[:, head(h)], key_ref[:, head(h)]) * SCALE
        d_scores = jnp.where(live, d_scores, 0.0)
        d_probs = soft * (d_scores - jnp.sum(soft * d_scores, axis=-1, keepdims=True))
        d_mixed = dot32(d_probs.astype(BF16), value_ref[:, head(h)]) + dot32(
            soft.astype(BF16), d_value[:, head(h)]
        )
        out_ref[:length, head(h)] = jnp.where(kept, d_mixed.astype(BF16).astype(F32), 0.0)


def total_of(terms):
    while len(terms) > 1:
        terms = [terms[i] + terms[i + 1] for i in range(0, len(terms), 2)]
    return terms[0]


def put_sums(out_ref, remain, image):
    lane = lax.broadcasted_iota(jnp.int32, (8, out_ref.shape[1]), 1)
    cross = 0.0 if image is None else jnp.sum(remain * image)
    out_ref[out_ref.shape[0] - 8 :] = jnp.where(lane == 0, jnp.sum(remain * remain), cross)


def first_kernel(n_dp, *refs):
    terms, refs = refs[:n_dp], refs[n_dp:]
    limit_ref, *attention, remain_ref, out_ref = refs
    grads = total_of([term[...] for term in terms])
    remain = -grads[: remain_ref.shape[0]]
    remain_ref[...] = remain
    put_sums(out_ref, remain, None)
    tangent_of(remain, limit_ref[0], *attention, out_ref)


def first_step(terms, limit, attention):
    inner = terms[0].shape[1]
    length = attention[1].shape[0]
    rank = attention[3].shape[1]
    return pl.pallas_call(
        functools.partial(first_kernel, len(terms)),
        in_specs=[VMEM] * len(terms) + [SMEM] + [VMEM] * 5,
        out_specs=[VMEM] * 2,
        out_shape=[
            jax.ShapeDtypeStruct((2 * rank, inner), F32),
            jax.ShapeDtypeStruct((length + 8, inner), F32),
        ],
        compiler_params=pltpu.CompilerParams(vmem_limit_bytes=LIMIT),
    )(*terms, limit, *attention)


def step_kernel(n_dp, token_count, index, last, *refs):
    terms, refs = refs[:n_dp], refs[n_dp:]
    sums_ref, remain_ref, *refs = refs
    if index:
        before_ref, newton_ref, direction_ref, image_ref, *refs = refs
    part = total_of([term[...] for term in terms])
    remain = remain_ref[...]
    rows = remain.shape[0]
    norm, cross = sums_ref[:1, 0:1], sums_ref[:1, 1:2]
    fresh = part[:rows] + DAMP * remain
    curv = part[rows : rows + 1, 0:1] / token_count + DAMP * norm
    if index:
        ratio = norm / before_ref[:1, 0:1]
        curv = curv + 2.0 * ratio * cross + ratio * ratio * before_ref[:1, 1:2]
        direction = remain + ratio * direction_ref[...]
        image = fresh + ratio * image_ref[...]
    else:
        direction, image = remain, fresh
    alpha = norm / curv
    newton = alpha * direction
    if index:
        newton = newton_ref[...] + newton
    remain = remain - alpha * image
    if last:
        step_q_ref, step_v_ref, remain_q_ref, remain_v_ref = refs
        rank = rows // 2
        step_q_ref[...] = newton[:rank]
        step_v_ref[...] = newton[rank:]
        remain_q_ref[...] = remain[:rank]
        remain_v_ref[...] = remain[rank:]
        return
    limit_ref, *refs = refs
    attention, refs = refs[:5], refs[5:]
    next_remain, next_before, next_newton, next_direction, next_image, out_ref = refs
    lane = lax.broadcasted_iota(jnp.int32, next_before.shape, 1)
    next_remain[...] = remain
    next_before[...] = jnp.where(lane == 0, norm, curv)
    next_newton[...] = newton
    next_direction[...] = direction
    next_image[...] = image
    put_sums(out_ref, remain, image)
    tangent_of(remain, limit_ref[0], *attention, out_ref)


def cg_step(index, token_count, terms, sums, remain, state, limit, attention):
    last = index == CG_STEPS - 1
    rows, inner = remain.shape
    matrix = jax.ShapeDtypeStruct((rows, inner), F32)
    scalars = jax.ShapeDtypeStruct((8, 128), F32)
    args = [*terms, sums, remain, *state]
    specs = [VMEM] * len(args)
    if last:
        shapes = [jax.ShapeDtypeStruct((rows // 2, inner), F32)] * 4
    else:
        args += [limit, *attention]
        specs += [SMEM] + [VMEM] * 5
        length = attention[1].shape[0]
        shapes = [matrix, scalars, matrix, matrix, matrix]
        shapes.append(jax.ShapeDtypeStruct((length + 8, inner), F32))
    return pl.pallas_call(
        functools.partial(step_kernel, len(terms), token_count, index, last),
        in_specs=specs,
        out_specs=[VMEM] * len(shapes),
        out_shape=shapes,
        compiler_params=pltpu.CompilerParams(vmem_limit_bytes=LIMIT),
    )(*args)


def on_device(
    inputs,
    targets,
    lengths,
    ln_gain,
    ln_bias,
    query_weight,
    w_key,
    value_weight,
    w_out,
    down_query,
    down_value,
    query_up_factor,
    value_up_factor,
):
    length, width = inputs.shape
    n_dp = lax.axis_size("dp")
    n_chip = lax.axis_size("chip")
    core = lax.axis_index("core")
    chip = lax.axis_index("chip")
    token_count = length * n_dp
    half = width // 2

    def swap(part):
        return lax.ppermute(part, "core", [(0, 1), (1, 0)])

    def data_terms(part):
        step = 1
        while 2 * step < n_dp:
            part = part + lax.ppermute(part, "dp", [(d, d ^ step) for d in range(n_dp)])
            step *= 2
        return [part, lax.ppermute(part, "dp", [(d, d ^ step) for d in range(n_dp)])]

    where = core.astype(jnp.int32)[None]
    sent = lax.dynamic_slice_in_dim(w_out, (1 - core) * half, half, 1).astype(F32)
    other_w = swap(sent)
    cols = half // CHUNKS
    gap = lax.dynamic_slice_in_dim(inputs, core * half, half, 1).astype(F32)
    gap = gap - lax.dynamic_slice_in_dim(targets, core * half, half, 1).astype(F32)

    soft, key, value, down_q, down_v, mixed = project(
        lengths, inputs, ln_gain, ln_bias, query_weight, w_key, value_weight, down_query,
        down_value, query_up_factor, value_up_factor,
    )
    attention = (soft, key, value, down_q, down_v)

    sums_in, sums_out = line_hops(n_chip)
    hops = sums_in + sums_out
    takes = []
    for hop in sums_out:
        inside = jnp.zeros((), jnp.bool_)
        for _, to in hop:
            inside = inside | (chip == to)
        takes.append(inside.astype(jnp.int32)[None])

    def product(rows, pairs):
        got_rows = swap(rows)
        first = not pairs
        held, arriving = {}, {}
        parts, scalars = [], None
        token = None

        def launch(k, hop):
            arriving[k] = lax.ppermute(held[k], "chip", hops[hop])

        def begin(k):
            if first:
                held[k], pair = first_spread(
                    k, CHUNKS, length, where, rows, got_rows, w_out, other_w, token
                )
                pairs.append(pair)
            else:
                held[k] = spread(k, length, rows, got_rows, pairs[k], token)
            launch(k, 0)
            return held[k]

        for k in range(AHEAD):
            token = begin(k)
        for tick in range(CHUNKS + len(hops) - 1):
            for stage in range(len(hops)):
                k = tick - stage
                if 0 <= k < CHUNKS:
                    if stage == len(hops) - 1:
                        out = gather(
                            k, takes[-1], arriving[k], held[k], pairs[k], parts, lengths,
                            gap[:, k * cols : (k + 1) * cols] if first else None, token,
                        )
                        parts = list(out[:2])
                        scalars = out[2] if k == 0 else scalars
                        token = parts[0]
                        continue
                    if stage < len(sums_in):
                        held[k] = add(held[k], arriving[k], token)
                    else:
                        flag = takes[stage - len(sums_in)]
                        held[k] = choose(flag, arriving[k], held[k], token)
                    token = held[k]
                    launch(k, stage + 1)
                if stage == 0 and tick + AHEAD < CHUNKS:
                    token = begin(tick + AHEAD)
        own, other = parts
        share = ADAPTER_SCALE / token_count
        part = cotangent(share, lengths, own, other, swap(other), attention)
        return data_terms(part), scalars

    pairs = []
    terms, _ = product(mixed, pairs)
    remain, rows = first_step(terms, lengths, attention)
    state = ()
    for index in range(CG_STEPS):
        terms, sums = product(rows, pairs)
        out = cg_step(index, token_count, terms, sums, remain, state, lengths, attention)
        if index < CG_STEPS - 1:
            remain, *state, rows = out
    return tuple(out)


def solution(mesh):
    fine = Mesh(mesh.devices.reshape(mesh.shape["dp"], -1, 2), ("dp", "chip", "core"))
    tensor = ("chip", "core")
    in_specs = (
        P("dp", None),
        P("dp", None),
        P("dp"),
        P(),
        P(),
        P(None, tensor),
        P(None, tensor),
        P(None, tensor),
        P(tensor, None),
        P(),
        P(),
        P(None, tensor),
        P(None, tensor),
    )
    out_specs = (P(None, tensor),) * 4
    return jax.shard_map(
        on_device, mesh=fine, in_specs=in_specs, out_specs=out_specs, check_vma=False
    )
```

```python
import functools

import jax
import jax.numpy as jnp
from jax import lax
from jax.experimental import pallas as pl
from jax.experimental.pallas import tpu as pltpu
from jax.sharding import Mesh
from jax.sharding import PartitionSpec as P

HEAD_DIM = 128
CG_STEPS = 3
CHUNKS = 8
AHEAD = 2
DEPTH = 512

EPS = 1e-05
ADAPTER_SCALE = 2.0
DAMP = 0.05
NEG = -1e30
F32 = jnp.float32
BF16 = jnp.bfloat16
HIGH = lax.Precision.HIGHEST
SCALE = HEAD_DIM ** (-0.5)
VMEM = pl.BlockSpec(memory_space=pltpu.VMEM)
SMEM = pl.BlockSpec(memory_space=pltpu.SMEM)
LIMIT = 16 * 1024 * 1024
STEP_COST = pl.CostEstimate(flops=10**9, bytes_accessed=10**7, transcendentals=0)
STREAM_LIMIT = 56 * 1024 * 1024


def dot32(first, second):
    return jnp.dot(first, second, preferred_element_type=F32)


def dot_nt(first, second):
    return lax.dot_general(
        first, second, (((1,), (1,)), ((), ())), preferred_element_type=F32
    )


def dot_tn(first, second):
    return lax.dot_general(
        first, second, (((0,), (0,)), ((), ())), preferred_element_type=F32
    )


def high(first, second):
    return jnp.dot(first, second, precision=HIGH, preferred_element_type=F32)


def head(index):
    return slice(index * HEAD_DIM, (index + 1) * HEAD_DIM)


def rows_below(limit, length, width):
    return lax.broadcasted_iota(jnp.int32, (length, width), 0) < limit


def live_pairs(limit, length):
    row = lax.broadcasted_iota(jnp.int32, (length, length), 0)
    column = lax.broadcasted_iota(jnp.int32, (length, length), 1)
    return (column <= row) & (column < limit)


def project_kernel(
    limit_ref, x_ref, gain_ref, bias_ref, wq_ref, wk_ref, wv_ref, aq_ref, av_ref, bq_ref, bv_ref,
    soft_ref, key_ref, value_ref, down_q_ref, down_v_ref, mixed_ref,
    normed, query_sum, key_sum, value_sum,
):
    step = pl.program_id(0)
    length, width = x_ref.shape
    depth = wq_ref.shape[0]

    @pl.when(step == 0)
    def _():
        rows = x_ref[...].astype(F32)
        centred = rows - jnp.sum(rows, axis=-1, keepdims=True) / width
        spread = jnp.sum(centred * centred, axis=-1, keepdims=True) / width
        full = centred * lax.rsqrt(spread + EPS) * gain_ref[...] + bias_ref[...]
        normed[...] = full.astype(BF16)
        query_sum[...] = jnp.zeros_like(query_sum)
        key_sum[...] = jnp.zeros_like(key_sum)
        value_sum[...] = jnp.zeros_like(value_sum)
        down_q_ref[...] = jnp.zeros_like(down_q_ref)
        down_v_ref[...] = jnp.zeros_like(down_v_ref)

    part = normed[:, pl.ds(pl.multiple_of(step * depth, depth), depth)]
    query_sum[...] += dot32(part, wq_ref[...])
    key_sum[...] += dot32(part, wk_ref[...])
    value_sum[...] += dot32(part, wv_ref[...])
    down_q_ref[...] += dot_nt(part, aq_ref[...])
    down_v_ref[...] += dot_nt(part, av_ref[...])

    @pl.when(step == pl.num_programs(0) - 1)
    def _():
        limit = limit_ref[0]
        live = live_pairs(limit, length)
        kept = rows_below(limit, length, HEAD_DIM)
        query = query_sum[...] + ADAPTER_SCALE * high(down_q_ref[...], bq_ref[...])
        value = value_sum[...] + ADAPTER_SCALE * high(down_v_ref[...], bv_ref[...])
        query = query.astype(BF16)
        value = value.astype(BF16)
        key = key_sum[...].astype(BF16)
        key_ref[...] = key
        value_ref[...] = value
        for h in range(key.shape[1] // HEAD_DIM):
            scores = dot_nt(query[:, head(h)], key[:, head(h)]) * SCALE
            scores = jnp.where(live, scores, NEG)
            weights = jnp.exp(scores - jnp.max(scores, axis=-1, keepdims=True))
            soft = weights / jnp.sum(weights, axis=-1, keepdims=True)
            soft_ref[h] = soft
            mixed = dot32(soft.astype(BF16), value[:, head(h)]).astype(BF16)
            mixed_ref[:length, head(h)] = jnp.where(kept, mixed.astype(F32), 0.0)
        mixed_ref[length:] = jnp.zeros((8, key.shape[1]), F32)


def project(limit, x, gain, bias, wq, wk, wv, aq, av, bq, bv):
    length, width = x.shape
    inner = wq.shape[1]
    rank = aq.shape[1]
    heads = inner // HEAD_DIM
    whole = lambda i: (0, 0)
    deep = lambda i: (i, 0)
    return pl.pallas_call(
        project_kernel,
        grid=(width // DEPTH,),
        in_specs=[
            SMEM,
            pl.BlockSpec((length, width), whole),
            pl.BlockSpec((1, width), whole),
            pl.BlockSpec((1, width), whole),
            pl.BlockSpec((DEPTH, inner), deep),
            pl.BlockSpec((DEPTH, inner), deep),
            pl.BlockSpec((DEPTH, inner), deep),
            pl.BlockSpec((rank, DEPTH), lambda i: (0, i)),
            pl.BlockSpec((rank, DEPTH), lambda i: (0, i)),
            pl.BlockSpec((rank, inner), whole),
            pl.BlockSpec((rank, inner), whole),
        ],
        out_specs=[
            pl.BlockSpec((heads, length, length), lambda i: (0, 0, 0)),
            pl.BlockSpec((length, inner), whole),
            pl.BlockSpec((length, inner), whole),
            pl.BlockSpec((length, rank), whole),
            pl.BlockSpec((length, rank), whole),
            pl.BlockSpec((length + 8, inner), whole),
        ],
        out_shape=[
            jax.ShapeDtypeStruct((heads, length, length), F32),
            jax.ShapeDtypeStruct((length, inner), BF16),
            jax.ShapeDtypeStruct((length, inner), BF16),
            jax.ShapeDtypeStruct((length, rank), F32),
            jax.ShapeDtypeStruct((length, rank), F32),
            jax.ShapeDtypeStruct((length + 8, inner), F32),
        ],
        scratch_shapes=[
            pltpu.VMEM((length, width), BF16),
            pltpu.VMEM((length, inner), F32),
            pltpu.VMEM((length, inner), F32),
            pltpu.VMEM((length, inner), F32),
        ],
        compiler_params=pltpu.CompilerParams(vmem_limit_bytes=STREAM_LIMIT),
        cost_estimate=pl.CostEstimate(
            flops=6 * length * width * inner, bytes_accessed=6 * width * inner, transcendentals=0
        ),
    )(limit, x, gain[None], bias[None], wq, wk, wv, aq.T, av.T, bq, bv)


def token_spec():
    return pl.BlockSpec(memory_space=pl.ANY)


def call(kernel, ins, outs, token, scalars=()):
    tokens = [] if token is None else [token]

    def body(*refs):
        count = len(scalars) + len(ins)
        kernel(*refs[:count], *refs[count + len(tokens) :])

    return pl.pallas_call(
        body,
        in_specs=[SMEM] * len(scalars) + [VMEM] * len(ins) + [token_spec()] * len(tokens),
        out_specs=[VMEM] * len(outs),
        out_shape=[jax.ShapeDtypeStruct(shape, kind) for shape, kind in outs],
        compiler_params=pltpu.CompilerParams(vmem_limit_bytes=LIMIT),
        cost_estimate=STEP_COST,
    )(*scalars, *ins, *tokens)


def rows_of(own_ref, got_ref, length):
    return jnp.concatenate(
        [own_ref[:length].astype(BF16), got_ref[:length].astype(BF16)], axis=1
    )


def put_tail(out_ref, own_ref, got_ref, length):
    out_ref[length:] = jnp.zeros((8, out_ref.shape[1]), F32)
    out_ref[length:, :HEAD_DIM] = own_ref[length:, :HEAD_DIM] + got_ref[length:, :HEAD_DIM]


def first_spread_kernel(tail, length, core_ref, own_ref, got_ref, w_ref, other_w_ref, *refs):
    out_ref, pair_ref = refs[-2:]
    inner = own_ref.shape[1]
    pair_ref[:inner] = w_ref[...]
    pair_ref[inner:] = other_w_ref[...].astype(BF16)
    out_ref[:length] = dot32(rows_of(own_ref, got_ref, length), pair_ref[...])
    if tail:
        put_tail(out_ref, own_ref, got_ref, length)


def first_spread(index, chunks, length, core, own, got, w_out, other_w, token):
    inner, half = other_w.shape
    cols = half // chunks
    height = length + (8 if index == 0 else 0)
    whole = lambda i, core: (0, 0)
    tokens = [] if token is None else [token]
    return pl.pallas_call(
        functools.partial(first_spread_kernel, index == 0, length),
        grid_spec=pltpu.PrefetchScalarGridSpec(
            num_scalar_prefetch=1,
            grid=(1,),
            in_specs=[
                pl.BlockSpec(own.shape, whole),
                pl.BlockSpec(own.shape, whole),
                pl.BlockSpec((inner, cols), lambda i, core: (0, core[0] * chunks + index)),
                pl.BlockSpec((inner, cols), lambda i, core: (0, index)),
            ] + [token_spec()] * len(tokens),
            out_specs=[
                pl.BlockSpec((height, cols), whole),
                pl.BlockSpec((2 * inner, cols), whole),
            ],
        ),
        out_shape=[
            jax.ShapeDtypeStruct((height, cols), F32),
            jax.ShapeDtypeStruct((2 * inner, cols), BF16),
        ],
        compiler_params=pltpu.CompilerParams(vmem_limit_bytes=LIMIT),
        cost_estimate=STEP_COST,
    )(core, own, got, w_out, other_w, *tokens)


def spread(index, length, own, got, pair, token):
    height = length + (8 if index == 0 else 0)

    def kernel(own_ref, got_ref, pair_ref, out_ref):
        out_ref[:length] = dot32(rows_of(own_ref, got_ref, length), pair_ref[...])
        if index == 0:
            put_tail(out_ref, own_ref, got_ref, length)

    return call(kernel, [own, got, pair], [((height, pair.shape[1]), F32)], token)[0]


def add(first, second, token):
    def kernel(first_ref, second_ref, out_ref):
        out_ref[...] = first_ref[...] + second_ref[...]

    return call(kernel, [first, second], [(first.shape, F32)], token)[0]


def choose(takes, got, held, token):
    def kernel(takes_ref, got_ref, held_ref, out_ref):
        out_ref[...] = jnp.where(takes_ref[0] > 0, got_ref[...], held_ref[...])

    return call(kernel, [got, held], [(held.shape, F32)], token, [takes])[0]


def gather(index, takes, got, held, pair, sums, limit, gap, token):
    inner = pair.shape[0] // 2
    extra = [] if gap is None else [gap]
    length = held.shape[0] - (8 if index == 0 else 0)

    def kernel(takes_ref, limit_ref, got_ref, held_ref, pair_ref, *refs):
        refs = list(refs)
        gap_ref = refs.pop(0) if gap is not None else None
        before = [refs.pop(0), refs.pop(0)] if index else None
        own_ref, other_ref = refs[:2]
        total = jnp.where(takes_ref[0] > 0, got_ref[...], held_ref[...])
        if index == 0:
            refs[2][...] = total[length:, :128]
            total = total[:length]
        if gap_ref is not None:
            kept = rows_below(limit_ref[0], length, total.shape[1])
            total = jnp.where(kept, total + gap_ref[...], 0.0)
        rounded = total.astype(BF16)
        own = dot_nt(rounded, pair_ref[:inner])
        other = dot_nt(rounded, pair_ref[inner:])
        squares = jnp.full((8, inner), jnp.sum(total * total), F32)
        if index:
            own = own + before[0][...]
            other = other + before[1][:length]
            squares = squares + before[1][length:]
        own_ref[...] = own
        other_ref[:length] = other
        other_ref[length:] = squares

    outs = [((length, inner), F32), ((length + 8, inner), F32)]
    if index == 0:
        outs.append(((8, 128), F32))
    return call(kernel, [got, held, pair] + extra + sums, outs, token, [takes, limit])


def line_hops(chips):
    inward = []
    for step in range(chips // 2 - 1):
        inward.append([(step, step + 1), (chips - 1 - step, chips - 2 - step)])
    middle = [(chips // 2 - 1, chips // 2), (chips // 2, chips // 2 - 1)]
    outward = [[(b, a) for a, b in hop] for hop in reversed(inward)]
    return inward + [middle], outward


def cotangent_kernel(
    share, limit_ref, own_ref, other_ref, got_ref, soft_ref, key_ref, value_ref, down_q_ref,
    down_v_ref, out_ref,
):
    length, inner = own_ref.shape
    rank = down_q_ref.shape[1]
    live = live_pairs(limit_ref[0], length)
    pulled = (own_ref[...] + got_ref[:length]).astype(BF16)
    out_ref[2 * rank :] = other_ref[length:] + got_ref[length:]
    for h in range(inner // HEAD_DIM):
        soft = soft_ref[h]
        rows = pulled[:, head(h)]
        d_probs = dot_nt(rows, value_ref[:, head(h)]).astype(BF16).astype(F32)
        d_value = dot_tn(soft.astype(BF16), rows).astype(BF16).astype(F32)
        d_scores = soft * (d_probs - jnp.sum(soft * d_probs, axis=-1, keepdims=True))
        d_scores = jnp.where(live, d_scores, 0.0) * SCALE
        d_query = dot32(d_scores.astype(BF16), key_ref[:, head(h)]).astype(BF16).astype(F32)
        out_ref[:rank, head(h)] = share * lax.dot_general(
            down_q_ref[...], d_query, (((0,), (0,)), ((), ())), precision=HIGH,
            preferred_element_type=F32,
        )
        out_ref[rank : 2 * rank, head(h)] = share * lax.dot_general(
            down_v_ref[...], d_value, (((0,), (0,)), ((), ())), precision=HIGH,
            preferred_element_type=F32,
        )


def cotangent(share, limit, own, other, got, attention):
    inner = own.shape[1]
    rank = attention[3].shape[1]
    return pl.pallas_call(
        functools.partial(cotangent_kernel, share),
        in_specs=[SMEM] + [VMEM] * 8,
        out_specs=VMEM,
        out_shape=jax.ShapeDtypeStruct((2 * rank + 8, inner), F32),
        compiler_params=pltpu.CompilerParams(vmem_limit_bytes=LIMIT),
    )(limit, own, other, got, *attention)


def tangent_of(vector, limit, soft_ref, key_ref, value_ref, down_q_ref, down_v_ref, out_ref):
    length = key_ref.shape[0]
    rank = down_q_ref.shape[1]
    live = live_pairs(limit, length)
    kept = rows_below(limit, length, HEAD_DIM)
    d_query = (ADAPTER_SCALE * high(down_q_ref[...], vector[:rank])).astype(BF16)
    d_value = (ADAPTER_SCALE * high(down_v_ref[...], vector[rank:])).astype(BF16)
    for h in range(key_ref.shape[1] // HEAD_DIM):
        soft = soft_ref[h]
        d_scores = dot_nt(d_query[:, head(h)], key_ref[:, head(h)]) * SCALE
        d_scores = jnp.where(live, d_scores, 0.0)
        d_probs = soft * (d_scores - jnp.sum(soft * d_scores, axis=-1, keepdims=True))
        d_mixed = dot32(d_probs.astype(BF16), value_ref[:, head(h)]) + dot32(
            soft.astype(BF16), d_value[:, head(h)]
        )
        out_ref[:length, head(h)] = jnp.where(kept, d_mixed.astype(BF16).astype(F32), 0.0)


def total_of(terms):
    while len(terms) > 1:
        terms = [terms[i] + terms[i + 1] for i in range(0, len(terms), 2)]
    return terms[0]


def put_sums(out_ref, remain, image):
    lane = lax.broadcasted_iota(jnp.int32, (8, out_ref.shape[1]), 1)
    cross = 0.0 if image is None else jnp.sum(remain * image)
    out_ref[out_ref.shape[0] - 8 :] = jnp.where(lane == 0, jnp.sum(remain * remain), cross)


def first_kernel(n_dp, *refs):
    terms, refs = refs[:n_dp], refs[n_dp:]
    limit_ref, *attention, remain_ref, out_ref = refs
    grads = total_of([term[...] for term in terms])
    remain = -grads[: remain_ref.shape[0]]
    remain_ref[...] = remain
    put_sums(out_ref, remain, None)
    tangent_of(remain, limit_ref[0], *attention, out_ref)


def first_step(terms, limit, attention):
    inner = terms[0].shape[1]
    length = attention[1].shape[0]
    rank = attention[3].shape[1]
    return pl.pallas_call(
        functools.partial(first_kernel, len(terms)),
        in_specs=[VMEM] * len(terms) + [SMEM] + [VMEM] * 5,
        out_specs=[VMEM] * 2,
        out_shape=[
            jax.ShapeDtypeStruct((2 * rank, inner), F32),
            jax.ShapeDtypeStruct((length + 8, inner), F32),
        ],
        compiler_params=pltpu.CompilerParams(vmem_limit_bytes=LIMIT),
    )(*terms, limit, *attention)


def step_kernel(n_dp, token_count, index, last, *refs):
    terms, refs = refs[:n_dp], refs[n_dp:]
    sums_ref, remain_ref, *refs = refs
    if index:
        before_ref, newton_ref, direction_ref, image_ref, *refs = refs
    part = total_of([term[...] for term in terms])
    remain = remain_ref[...]
    rows = remain.shape[0]
    norm, cross = sums_ref[:1, 0:1], sums_ref[:1, 1:2]
    fresh = part[:rows] + DAMP * remain
    curv = part[rows : rows + 1, 0:1] / token_count + DAMP * norm
    if index:
        ratio = norm / before_ref[:1, 0:1]
        curv = curv + 2.0 * ratio * cross + ratio * ratio * before_ref[:1, 1:2]
        direction = remain + ratio * direction_ref[...]
        image = fresh + ratio * image_ref[...]
    else:
        direction, image = remain, fresh
    alpha = norm / curv
    newton = alpha * direction
    if index:
        newton = newton_ref[...] + newton
    remain = remain - alpha * image
    if last:
        step_q_ref, step_v_ref, remain_q_ref, remain_v_ref = refs
        rank = rows // 2
        step_q_ref[...] = newton[:rank]
        step_v_ref[...] = newton[rank:]
        remain_q_ref[...] = remain[:rank]
        remain_v_ref[...] = remain[rank:]
        return
    limit_ref, *refs = refs
    attention, refs = refs[:5], refs[5:]
    next_remain, next_before, next_newton, next_direction, next_image, out_ref = refs
    lane = lax.broadcasted_iota(jnp.int32, next_before.shape, 1)
    next_remain[...] = remain
    next_before[...] = jnp.where(lane == 0, norm, curv)
    next_newton[...] = newton
    next_direction[...] = direction
    next_image[...] = image
    put_sums(out_ref, remain, image)
    tangent_of(remain, limit_ref[0], *attention, out_ref)


def cg_step(index, token_count, terms, sums, remain, state, limit, attention):
    last = index == CG_STEPS - 1
    rows, inner = remain.shape
    matrix = jax.ShapeDtypeStruct((rows, inner), F32)
    scalars = jax.ShapeDtypeStruct((8, 128), F32)
    args = [*terms, sums, remain, *state]
    specs = [VMEM] * len(args)
    if last:
        shapes = [jax.ShapeDtypeStruct((rows // 2, inner), F32)] * 4
    else:
        args += [limit, *attention]
        specs += [SMEM] + [VMEM] * 5
        length = attention[1].shape[0]
        shapes = [matrix, scalars, matrix, matrix, matrix]
        shapes.append(jax.ShapeDtypeStruct((length + 8, inner), F32))
    return pl.pallas_call(
        functools.partial(step_kernel, len(terms), token_count, index, last),
        in_specs=specs,
        out_specs=[VMEM] * len(shapes),
        out_shape=shapes,
        compiler_params=pltpu.CompilerParams(vmem_limit_bytes=LIMIT),
    )(*args)


def on_device(
    inputs,
    targets,
    lengths,
    ln_gain,
    ln_bias,
    query_weight,
    w_key,
    value_weight,
    w_out,
    down_query,
    down_value,
    query_up_factor,
    value_up_factor,
):
    length, width = inputs.shape
    n_dp = lax.axis_size("dp")
    n_chip = lax.axis_size("chip")
    core = lax.axis_index("core")
    chip = lax.axis_index("chip")
    token_count = length * n_dp
    half = width // 2

    def swap(part):
        return lax.ppermute(part, "core", [(0, 1), (1, 0)])

    def data_terms(part):
        step = 1
        while 2 * step < n_dp:
            part = part + lax.ppermute(part, "dp", [(d, d ^ step) for d in range(n_dp)])
            step *= 2
        return [part, lax.ppermute(part, "dp", [(d, d ^ step) for d in range(n_dp)])]

    where = core.astype(jnp.int32)[None]
    sent = lax.dynamic_slice_in_dim(w_out, (1 - core) * half, half, 1).astype(F32)
    other_w = swap(sent)
    cols = half // CHUNKS
    gap = lax.dynamic_slice_in_dim(inputs, core * half, half, 1).astype(F32)
    gap = gap - lax.dynamic_slice_in_dim(targets, core * half, half, 1).astype(F32)

    soft, key, value, down_q, down_v, mixed = project(
        lengths, inputs, ln_gain, ln_bias, query_weight, w_key, value_weight, down_query,
        down_value, query_up_factor, value_up_factor,
    )
    attention = (soft, key, value, down_q, down_v)

    sums_in, sums_out = line_hops(n_chip)
    hops = sums_in + sums_out
    takes = []
    for hop in sums_out:
        inside = jnp.zeros((), jnp.bool_)
        for _, to in hop:
            inside = inside | (chip == to)
        takes.append(inside.astype(jnp.int32)[None])

    def product(rows, pairs):
        got_rows = swap(rows)
        first = not pairs
        held, arriving = {}, {}
        parts, scalars = [], None
        token = None

        def launch(k, hop):
            arriving[k] = lax.ppermute(held[k], "chip", hops[hop])

        def begin(k):
            if first:
                held[k], pair = first_spread(
                    k, CHUNKS, length, where, rows, got_rows, w_out, other_w, token
                )
                pairs.append(pair)
            else:
                held[k] = spread(k, length, rows, got_rows, pairs[k], token)
            launch(k, 0)
            return held[k]

        for k in range(AHEAD):
            token = begin(k)
        for tick in range(CHUNKS + len(hops) - 1):
            for stage in range(len(hops)):
                k = tick - stage
                if 0 <= k < CHUNKS:
                    if stage == len(hops) - 1:
                        out = gather(
                            k, takes[-1], arriving[k], held[k], pairs[k], parts, lengths,
                            gap[:, k * cols : (k + 1) * cols] if first else None, token,
                        )
                        parts = list(out[:2])
                        scalars = out[2] if k == 0 else scalars
                        token = parts[0]
                        continue
                    if stage < len(sums_in):
                        held[k] = add(held[k], arriving[k], token)
                    else:
                        flag = takes[stage - len(sums_in)]
                        held[k] = choose(flag, arriving[k], held[k], token)
                    token = held[k]
                    launch(k, stage + 1)
                if stage == 0 and tick + AHEAD < CHUNKS:
                    token = begin(tick + AHEAD)
        own, other = parts
        share = ADAPTER_SCALE / token_count
        part = cotangent(share, lengths, own, other, swap(other), attention)
        return data_terms(part), scalars

    pairs = []
    terms, _ = product(mixed, pairs)
    remain, rows = first_step(terms, lengths, attention)
    state = ()
    for index in range(CG_STEPS):
        terms, sums = product(rows, pairs)
        out = cg_step(index, token_count, terms, sums, remain, state, lengths, attention)
        if index < CG_STEPS - 1:
            remain, *state, rows = out
    return tuple(out)


def solution(mesh):
    fine = Mesh(mesh.devices.reshape(mesh.shape["dp"], -1, 2), ("dp", "chip", "core"))
    tensor = ("chip", "core")
    in_specs = (
        P("dp", None),
        P("dp", None),
        P("dp"),
        P(),
        P(),
        P(None, tensor),
        P(None, tensor),
        P(None, tensor),
        P(tensor, None),
        P(),
        P(),
        P(None, tensor),
        P(None, tensor),
    )
    out_specs = (P(None, tensor),) * 4
    return jax.shard_map(
        on_device, mesh=fine, in_specs=in_specs, out_specs=out_specs, check_vma=False
    )
```

```python
import functools

import jax
import jax.numpy as jnp
from jax import lax
from jax.experimental import pallas as pl
from jax.experimental.pallas import tpu as pltpu
from jax.sharding import Mesh
from jax.sharding import PartitionSpec as P

HEAD_DIM = 128
CG_STEPS = 3
CHUNKS = 6
DEPTH = 512

EPS = 1e-05
ADAPTER_SCALE = 2.0
DAMP = 0.05
NEG = -1e30
F32 = jnp.float32
BF16 = jnp.bfloat16
HIGH = lax.Precision.HIGHEST
SCALE = HEAD_DIM ** (-0.5)
VMEM = pl.BlockSpec(memory_space=pltpu.VMEM)
SMEM = pl.BlockSpec(memory_space=pltpu.SMEM)
LIMIT = 16 * 1024 * 1024
STEP_COST = pl.CostEstimate(flops=10**9, bytes_accessed=10**7, transcendentals=0)
STREAM_LIMIT = 56 * 1024 * 1024


def dot32(first, second):
    return jnp.dot(first, second, preferred_element_type=F32)


def dot_nt(first, second):
    return lax.dot_general(
        first, second, (((1,), (1,)), ((), ())), preferred_element_type=F32
    )


def dot_tn(first, second):
    return lax.dot_general(
        first, second, (((0,), (0,)), ((), ())), preferred_element_type=F32
    )


def high(first, second):
    return jnp.dot(first, second, precision=HIGH, preferred_element_type=F32)


def head(index):
    return slice(index * HEAD_DIM, (index + 1) * HEAD_DIM)


def rows_below(limit, length, width):
    return lax.broadcasted_iota(jnp.int32, (length, width), 0) < limit


def live_pairs(limit, length):
    row = lax.broadcasted_iota(jnp.int32, (length, length), 0)
    column = lax.broadcasted_iota(jnp.int32, (length, length), 1)
    return (column <= row) & (column < limit)


def project_kernel(
    limit_ref, x_ref, gain_ref, bias_ref, wq_ref, wk_ref, wv_ref, aq_ref, av_ref, bq_ref, bv_ref,
    soft_ref, key_ref, value_ref, down_q_ref, down_v_ref, mixed_ref,
    normed, query_sum, key_sum, value_sum,
):
    step = pl.program_id(0)
    length, width = x_ref.shape
    depth = wq_ref.shape[0]

    @pl.when(step == 0)
    def _():
        rows = x_ref[...].astype(F32)
        centred = rows - jnp.sum(rows, axis=-1, keepdims=True) / width
        spread = jnp.sum(centred * centred, axis=-1, keepdims=True) / width
        full = centred * lax.rsqrt(spread + EPS) * gain_ref[...] + bias_ref[...]
        normed[...] = full.astype(BF16)
        query_sum[...] = jnp.zeros_like(query_sum)
        key_sum[...] = jnp.zeros_like(key_sum)
        value_sum[...] = jnp.zeros_like(value_sum)
        down_q_ref[...] = jnp.zeros_like(down_q_ref)
        down_v_ref[...] = jnp.zeros_like(down_v_ref)

    part = normed[:, pl.ds(pl.multiple_of(step * depth, depth), depth)]
    query_sum[...] += dot32(part, wq_ref[...])
    key_sum[...] += dot32(part, wk_ref[...])
    value_sum[...] += dot32(part, wv_ref[...])
    down_q_ref[...] += dot_nt(part, aq_ref[...])
    down_v_ref[...] += dot_nt(part, av_ref[...])

    @pl.when(step == pl.num_programs(0) - 1)
    def _():
        limit = limit_ref[0]
        live = live_pairs(limit, length)
        kept = rows_below(limit, length, HEAD_DIM)
        query = query_sum[...] + ADAPTER_SCALE * high(down_q_ref[...], bq_ref[...])
        value = value_sum[...] + ADAPTER_SCALE * high(down_v_ref[...], bv_ref[...])
        query = query.astype(BF16)
        value = value.astype(BF16)
        key = key_sum[...].astype(BF16)
        key_ref[...] = key
        value_ref[...] = value
        for h in range(key.shape[1] // HEAD_DIM):
            scores = dot_nt(query[:, head(h)], key[:, head(h)]) * SCALE
            scores = jnp.where(live, scores, NEG)
            weights = jnp.exp(scores - jnp.max(scores, axis=-1, keepdims=True))
            soft = weights / jnp.sum(weights, axis=-1, keepdims=True)
            soft_ref[h] = soft
            mixed = dot32(soft.astype(BF16), value[:, head(h)]).astype(BF16)
            mixed_ref[:length, head(h)] = jnp.where(kept, mixed.astype(F32), 0.0)
        mixed_ref[length:] = jnp.zeros((8, key.shape[1]), F32)


def project(limit, x, gain, bias, wq, wk, wv, aq, av, bq, bv):
    length, width = x.shape
    inner = wq.shape[1]
    rank = aq.shape[1]
    heads = inner // HEAD_DIM
    whole = lambda i: (0, 0)
    deep = lambda i: (i, 0)
    return pl.pallas_call(
        project_kernel,
        grid=(width // DEPTH,),
        in_specs=[
            SMEM,
            pl.BlockSpec((length, width), whole),
            pl.BlockSpec((1, width), whole),
            pl.BlockSpec((1, width), whole),
            pl.BlockSpec((DEPTH, inner), deep),
            pl.BlockSpec((DEPTH, inner), deep),
            pl.BlockSpec((DEPTH, inner), deep),
            pl.BlockSpec((rank, DEPTH), lambda i: (0, i)),
            pl.BlockSpec((rank, DEPTH), lambda i: (0, i)),
            pl.BlockSpec((rank, inner), whole),
            pl.BlockSpec((rank, inner), whole),
        ],
        out_specs=[
            pl.BlockSpec((heads, length, length), lambda i: (0, 0, 0)),
            pl.BlockSpec((length, inner), whole),
            pl.BlockSpec((length, inner), whole),
            pl.BlockSpec((length, rank), whole),
            pl.BlockSpec((length, rank), whole),
            pl.BlockSpec((length + 8, inner), whole),
        ],
        out_shape=[
            jax.ShapeDtypeStruct((heads, length, length), F32),
            jax.ShapeDtypeStruct((length, inner), BF16),
            jax.ShapeDtypeStruct((length, inner), BF16),
            jax.ShapeDtypeStruct((length, rank), F32),
            jax.ShapeDtypeStruct((length, rank), F32),
            jax.ShapeDtypeStruct((length + 8, inner), F32),
        ],
        scratch_shapes=[
            pltpu.VMEM((length, width), BF16),
            pltpu.VMEM((length, inner), F32),
            pltpu.VMEM((length, inner), F32),
            pltpu.VMEM((length, inner), F32),
        ],
        compiler_params=pltpu.CompilerParams(vmem_limit_bytes=STREAM_LIMIT),
        cost_estimate=pl.CostEstimate(
            flops=6 * length * width * inner, bytes_accessed=6 * width * inner, transcendentals=0
        ),
    )(limit, x, gain[None], bias[None], wq, wk, wv, aq.T, av.T, bq, bv)


def token_spec():
    return pl.BlockSpec(memory_space=pl.ANY)


def call(kernel, ins, outs, token, scalars=()):
    tokens = [] if token is None else [token]

    def body(*refs):
        count = len(scalars) + len(ins)
        kernel(*refs[:count], *refs[count + len(tokens) :])

    return pl.pallas_call(
        body,
        in_specs=[SMEM] * len(scalars) + [VMEM] * len(ins) + [token_spec()] * len(tokens),
        out_specs=[VMEM] * len(outs),
        out_shape=[jax.ShapeDtypeStruct(shape, kind) for shape, kind in outs],
        compiler_params=pltpu.CompilerParams(vmem_limit_bytes=LIMIT),
        cost_estimate=STEP_COST,
    )(*scalars, *ins, *tokens)


def rows_of(own_ref, got_ref, length):
    return jnp.concatenate(
        [own_ref[:length].astype(BF16), got_ref[:length].astype(BF16)], axis=1
    )


def put_tail(out_ref, own_ref, got_ref, length):
    out_ref[length:] = jnp.zeros((8, out_ref.shape[1]), F32)
    out_ref[length:, :HEAD_DIM] = own_ref[length:, :HEAD_DIM] + got_ref[length:, :HEAD_DIM]


def first_spread_kernel(tail, length, core_ref, own_ref, got_ref, w_ref, other_w_ref, *refs):
    out_ref, pair_ref = refs[-2:]
    inner = own_ref.shape[1]
    pair_ref[:inner] = w_ref[...]
    pair_ref[inner:] = other_w_ref[...].astype(BF16)
    out_ref[:length] = dot32(rows_of(own_ref, got_ref, length), pair_ref[...])
    if tail:
        put_tail(out_ref, own_ref, got_ref, length)


def first_spread(index, chunks, length, core, own, got, w_out, other_w, token):
    inner, half = other_w.shape
    cols = half // chunks
    height = length + (8 if index == 0 else 0)
    whole = lambda i, core: (0, 0)
    tokens = [] if token is None else [token]
    return pl.pallas_call(
        functools.partial(first_spread_kernel, index == 0, length),
        grid_spec=pltpu.PrefetchScalarGridSpec(
            num_scalar_prefetch=1,
            grid=(1,),
            in_specs=[
                pl.BlockSpec(own.shape, whole),
                pl.BlockSpec(own.shape, whole),
                pl.BlockSpec((inner, cols), lambda i, core: (0, core[0] * chunks + index)),
                pl.BlockSpec((inner, cols), lambda i, core: (0, index)),
            ] + [token_spec()] * len(tokens),
            out_specs=[
                pl.BlockSpec((height, cols), whole),
                pl.BlockSpec((2 * inner, cols), whole),
            ],
        ),
        out_shape=[
            jax.ShapeDtypeStruct((height, cols), F32),
            jax.ShapeDtypeStruct((2 * inner, cols), BF16),
        ],
        compiler_params=pltpu.CompilerParams(vmem_limit_bytes=LIMIT),
        cost_estimate=STEP_COST,
    )(core, own, got, w_out, other_w, *tokens)


def spread(index, length, own, got, pair, token):
    height = length + (8 if index == 0 else 0)

    def kernel(own_ref, got_ref, pair_ref, out_ref):
        out_ref[:length] = dot32(rows_of(own_ref, got_ref, length), pair_ref[...])
        if index == 0:
            put_tail(out_ref, own_ref, got_ref, length)

    return call(kernel, [own, got, pair], [((height, pair.shape[1]), F32)], token)[0]


def add(first, second, token):
    def kernel(first_ref, second_ref, out_ref):
        out_ref[...] = first_ref[...] + second_ref[: first_ref.shape[0]]

    return call(kernel, [first, second], [(first.shape, F32)], token)[0]


def add_and_pick(first, second, ends, outer, token):
    def kernel(ends_ref, first_ref, second_ref, outer_ref, sum_ref, sent_ref):
        total = first_ref[...] + second_ref[...]
        sum_ref[...] = total
        rows = outer_ref.shape[0]
        sent_ref[:rows] = jnp.where(ends_ref[0] > 0, outer_ref[...], total[:rows])
        if total.shape[0] > rows:
            sent_ref[rows:] = total[rows:]

    outs = [(first.shape, F32)] * 2
    return call(kernel, [first, second, outer], outs, token, [ends])


def gather(index, ends, got, held, pair, sums, limit, gap, token):
    inner = pair.shape[0] // 2
    extra = [] if gap is None else [gap]
    length = held.shape[0] - (8 if index == 0 else 0)

    def kernel(ends_ref, limit_ref, got_ref, held_ref, pair_ref, *refs):
        refs = list(refs)
        gap_ref = refs.pop(0) if gap is not None else None
        before = [refs.pop(0), refs.pop(0)] if index else None
        own_ref, other_ref = refs[:2]
        total = jnp.where(ends_ref[0] > 0, got_ref[...], held_ref[...])
        if index == 0:
            refs[2][...] = total[length:, :128]
            total = total[:length]
        if gap_ref is not None:
            kept = rows_below(limit_ref[0], length, total.shape[1])
            total = jnp.where(kept, total + gap_ref[...], 0.0)
        rounded = total.astype(BF16)
        own = dot_nt(rounded, pair_ref[:inner])
        other = dot_nt(rounded, pair_ref[inner:])
        squares = jnp.full((8, inner), jnp.sum(total * total), F32)
        if index:
            own = own + before[0][...]
            other = other + before[1][:length]
            squares = squares + before[1][length:]
        own_ref[...] = own
        other_ref[:length] = other
        other_ref[length:] = squares

    outs = [((length, inner), F32), ((length + 8, inner), F32)]
    if index == 0:
        outs.append(((8, 128), F32))
    return call(kernel, [got, held, pair] + extra + sums, outs, token, [ends, limit])


def cotangent_kernel(
    share, limit_ref, own_ref, other_ref, got_ref, soft_ref, key_ref, value_ref, down_q_ref,
    down_v_ref, out_ref,
):
    length, inner = own_ref.shape
    rank = down_q_ref.shape[1]
    live = live_pairs(limit_ref[0], length)
    pulled = (own_ref[...] + got_ref[:length]).astype(BF16)
    out_ref[2 * rank :] = other_ref[length:] + got_ref[length:]
    for h in range(inner // HEAD_DIM):
        soft = soft_ref[h]
        rows = pulled[:, head(h)]
        d_probs = dot_nt(rows, value_ref[:, head(h)]).astype(BF16).astype(F32)
        d_value = dot_tn(soft.astype(BF16), rows).astype(BF16).astype(F32)
        d_scores = soft * (d_probs - jnp.sum(soft * d_probs, axis=-1, keepdims=True))
        d_scores = jnp.where(live, d_scores, 0.0) * SCALE
        d_query = dot32(d_scores.astype(BF16), key_ref[:, head(h)]).astype(BF16).astype(F32)
        out_ref[:rank, head(h)] = share * lax.dot_general(
            down_q_ref[...], d_query, (((0,), (0,)), ((), ())), precision=HIGH,
            preferred_element_type=F32,
        )
        out_ref[rank : 2 * rank, head(h)] = share * lax.dot_general(
            down_v_ref[...], d_value, (((0,), (0,)), ((), ())), precision=HIGH,
            preferred_element_type=F32,
        )


def cotangent(share, limit, own, other, got, attention):
    inner = own.shape[1]
    rank = attention[3].shape[1]
    return pl.pallas_call(
        functools.partial(cotangent_kernel, share),
        in_specs=[SMEM] + [VMEM] * 8,
        out_specs=VMEM,
        out_shape=jax.ShapeDtypeStruct((2 * rank + 8, inner), F32),
        compiler_params=pltpu.CompilerParams(vmem_limit_bytes=LIMIT),
    )(limit, own, other, got, *attention)


def tangent_of(vector, limit, soft_ref, key_ref, value_ref, down_q_ref, down_v_ref, out_ref):
    length = key_ref.shape[0]
    rank = down_q_ref.shape[1]
    live = live_pairs(limit, length)
    kept = rows_below(limit, length, HEAD_DIM)
    d_query = (ADAPTER_SCALE * high(down_q_ref[...], vector[:rank])).astype(BF16)
    d_value = (ADAPTER_SCALE * high(down_v_ref[...], vector[rank:])).astype(BF16)
    for h in range(key_ref.shape[1] // HEAD_DIM):
        soft = soft_ref[h]
        d_scores = dot_nt(d_query[:, head(h)], key_ref[:, head(h)]) * SCALE
        d_scores = jnp.where(live, d_scores, 0.0)
        d_probs = soft * (d_scores - jnp.sum(soft * d_scores, axis=-1, keepdims=True))
        d_mixed = dot32(d_probs.astype(BF16), value_ref[:, head(h)]) + dot32(
            soft.astype(BF16), d_value[:, head(h)]
        )
        out_ref[:length, head(h)] = jnp.where(kept, d_mixed.astype(BF16).astype(F32), 0.0)


def total_of(terms):
    while len(terms) > 1:
        terms = [terms[i] + terms[i + 1] for i in range(0, len(terms), 2)]
    return terms[0]


def put_sums(out_ref, remain, image):
    lane = lax.broadcasted_iota(jnp.int32, (8, out_ref.shape[1]), 1)
    cross = 0.0 if image is None else jnp.sum(remain * image)
    out_ref[out_ref.shape[0] - 8 :] = jnp.where(lane == 0, jnp.sum(remain * remain), cross)


def first_kernel(n_dp, *refs):
    terms, refs = refs[:n_dp], refs[n_dp:]
    limit_ref, *attention, remain_ref, out_ref = refs
    grads = total_of([term[...] for term in terms])
    remain = -grads[: remain_ref.shape[0]]
    remain_ref[...] = remain
    put_sums(out_ref, remain, None)
    tangent_of(remain, limit_ref[0], *attention, out_ref)


def first_step(terms, limit, attention):
    inner = terms[0].shape[1]
    length = attention[1].shape[0]
    rank = attention[3].shape[1]
    return pl.pallas_call(
        functools.partial(first_kernel, len(terms)),
        in_specs=[VMEM] * len(terms) + [SMEM] + [VMEM] * 5,
        out_specs=[VMEM] * 2,
        out_shape=[
            jax.ShapeDtypeStruct((2 * rank, inner), F32),
            jax.ShapeDtypeStruct((length + 8, inner), F32),
        ],
        compiler_params=pltpu.CompilerParams(vmem_limit_bytes=LIMIT),
    )(*terms, limit, *attention)


def step_kernel(n_dp, token_count, index, last, *refs):
    terms, refs = refs[:n_dp], refs[n_dp:]
    sums_ref, remain_ref, *refs = refs
    if index:
        before_ref, newton_ref, direction_ref, image_ref, *refs = refs
    part = total_of([term[...] for term in terms])
    remain = remain_ref[...]
    rows = remain.shape[0]
    norm, cross = sums_ref[:1, 0:1], sums_ref[:1, 1:2]
    fresh = part[:rows] + DAMP * remain
    curv = part[rows : rows + 1, 0:1] / token_count + DAMP * norm
    if index:
        ratio = norm / before_ref[:1, 0:1]
        curv = curv + 2.0 * ratio * cross + ratio * ratio * before_ref[:1, 1:2]
        direction = remain + ratio * direction_ref[...]
        image = fresh + ratio * image_ref[...]
    else:
        direction, image = remain, fresh
    alpha = norm / curv
    newton = alpha * direction
    if index:
        newton = newton_ref[...] + newton
    remain = remain - alpha * image
    if last:
        step_q_ref, step_v_ref, remain_q_ref, remain_v_ref = refs
        rank = rows // 2
        step_q_ref[...] = newton[:rank]
        step_v_ref[...] = newton[rank:]
        remain_q_ref[...] = remain[:rank]
        remain_v_ref[...] = remain[rank:]
        return
    limit_ref, *refs = refs
    attention, refs = refs[:5], refs[5:]
    next_remain, next_before, next_newton, next_direction, next_image, out_ref = refs
    lane = lax.broadcasted_iota(jnp.int32, next_before.shape, 1)
    next_remain[...] = remain
    next_before[...] = jnp.where(lane == 0, norm, curv)
    next_newton[...] = newton
    next_direction[...] = direction
    next_image[...] = image
    put_sums(out_ref, remain, image)
    tangent_of(remain, limit_ref[0], *attention, out_ref)


def cg_step(index, token_count, terms, sums, remain, state, limit, attention):
    last = index == CG_STEPS - 1
    rows, inner = remain.shape
    matrix = jax.ShapeDtypeStruct((rows, inner), F32)
    scalars = jax.ShapeDtypeStruct((8, 128), F32)
    args = [*terms, sums, remain, *state]
    specs = [VMEM] * len(args)
    if last:
        shapes = [jax.ShapeDtypeStruct((rows // 2, inner), F32)] * 4
    else:
        args += [limit, *attention]
        specs += [SMEM] + [VMEM] * 5
        length = attention[1].shape[0]
        shapes = [matrix, scalars, matrix, matrix, matrix]
        shapes.append(jax.ShapeDtypeStruct((length + 8, inner), F32))
    return pl.pallas_call(
        functools.partial(step_kernel, len(terms), token_count, index, last),
        in_specs=specs,
        out_specs=[VMEM] * len(shapes),
        out_shape=shapes,
        compiler_params=pltpu.CompilerParams(vmem_limit_bytes=LIMIT),
    )(*args)


def on_device(
    inputs,
    targets,
    lengths,
    ln_gain,
    ln_bias,
    query_weight,
    w_key,
    value_weight,
    w_out,
    down_query,
    down_value,
    query_up_factor,
    value_up_factor,
):
    length, width = inputs.shape
    n_dp = lax.axis_size("dp")
    n_chip = lax.axis_size("chip")
    core = lax.axis_index("core")
    chip = lax.axis_index("chip")
    token_count = length * n_dp
    half = width // 2

    def swap(part):
        return lax.ppermute(part, "core", [(0, 1), (1, 0)])

    def data_terms(part):
        step = 1
        while 2 * step < n_dp:
            part = part + lax.ppermute(part, "dp", [(d, d ^ step) for d in range(n_dp)])
            step *= 2
        return [part, lax.ppermute(part, "dp", [(d, d ^ step) for d in range(n_dp)])]

    where = core.astype(jnp.int32)[None]
    sent = lax.dynamic_slice_in_dim(w_out, (1 - core) * half, half, 1).astype(F32)
    other_w = swap(sent)
    cols = half // CHUNKS
    gap = lax.dynamic_slice_in_dim(inputs, core * half, half, 1).astype(F32)
    gap = gap - lax.dynamic_slice_in_dim(targets, core * half, half, 1).astype(F32)

    soft, key, value, down_q, down_v, mixed = project(
        lengths, inputs, ln_gain, ln_bias, query_weight, w_key, value_weight, down_query,
        down_value, query_up_factor, value_up_factor,
    )
    attention = (soft, key, value, down_q, down_v)

    ends = ((chip == 0) | (chip == n_chip - 1)).astype(jnp.int32)[None]

    def outer_swap(part):
        return lax.ppermute(part, "chip", [(0, 1), (1, 0), (2, 3), (3, 2)])

    def inner_swap(part):
        return lax.ppermute(part, "chip", [(0, 0), (1, 2), (2, 1), (3, 3)])

    def product(rows, pairs):
        got_rows = swap(rows)
        first = not pairs
        pairs.extend([None] * (CHUNKS - len(pairs)))
        parts, scalars = [], None
        own_part, total, outer, inner = {}, {}, {}, {}
        token = None

        def begin(k):
            if first:
                own_part[k], pairs[k] = first_spread(
                    k, CHUNKS, length, where, rows, got_rows, w_out, other_w, token
                )
            else:
                own_part[k] = spread(k, length, rows, got_rows, pairs[k], token)
            return own_part[k]

        def finish(k, got):
            gap_part = gap[:, k * cols : (k + 1) * cols] if first else None
            return gather(k, ends, got, total[k], pairs[k], parts, lengths, gap_part, token)

        if n_chip != 4:
            for k in range(CHUNKS):
                token = begin(k)
            for k in range(CHUNKS):
                total[k] = lax.psum(own_part[k], "chip")
                out = finish(k, total[k])
                parts, scalars = list(out[:2]), out[2] if k == 0 else scalars
        else:
            for k in [0, 1, 2] if first else [0, *range(2, CHUNKS), 1]:
                token = begin(k)
            for k in (0, 1):
                outer[k] = outer_swap(own_part[k])
            for tick in range(CHUNKS + 3):
                if tick < CHUNKS:
                    own_part[tick] = add(own_part[tick], outer[tick], token)
                    token = own_part[tick]
                    inner[tick] = inner_swap(token)
                later = tick + 2
                if 1 <= tick <= CHUNKS:
                    k = tick - 1
                    if later < CHUNKS:
                        total[k], sent = add_and_pick(
                            own_part[k], inner[k], ends, own_part[later], token
                        )
                    else:
                        total[k] = sent = add(own_part[k], inner[k], token)
                    token = sent
                    outer[later] = outer_swap(sent)
                elif tick == 0:
                    outer[later] = outer_swap(own_part[later])
                if tick + 3 < CHUNKS and first:
                    token = begin(tick + 3)
                if tick >= 3:
                    out = finish(tick - 3, outer[tick])
                    parts, scalars = list(out[:2]), out[2] if tick == 3 else scalars
                    token = parts[0]
        own, other = parts
        share = ADAPTER_SCALE / token_count
        part = cotangent(share, lengths, own, other, swap(other), attention)
        return data_terms(part), scalars

    pairs = []
    terms, _ = product(mixed, pairs)
    remain, rows = first_step(terms, lengths, attention)
    state = ()
    for index in range(CG_STEPS):
        terms, sums = product(rows, pairs)
        out = cg_step(index, token_count, terms, sums, remain, state, lengths, attention)
        if index < CG_STEPS - 1:
            remain, *state, rows = out
    return tuple(out)


def solution(mesh):
    fine = Mesh(mesh.devices.reshape(mesh.shape["dp"], -1, 2), ("dp", "chip", "core"))
    tensor = ("chip", "core")
    in_specs = (
        P("dp", None),
        P("dp", None),
        P("dp"),
        P(),
        P(),
        P(None, tensor),
        P(None, tensor),
        P(None, tensor),
        P(tensor, None),
        P(),
        P(),
        P(None, tensor),
        P(None, tensor),
    )
    out_specs = (P(None, tensor),) * 4
    return jax.shard_map(
        on_device, mesh=fine, in_specs=in_specs, out_specs=out_specs, check_vma=False
    )
```

```python
import functools

import jax
import jax.numpy as jnp
from jax import lax
from jax.experimental import pallas as pl
from jax.experimental.pallas import tpu as pltpu
from jax.sharding import Mesh
from jax.sharding import PartitionSpec as P

HEAD_DIM = 128
CG_STEPS = 3
CHUNKS = 8
DEPTH = 1024

EPS = 1e-05
ADAPTER_SCALE = 2.0
DAMP = 0.05
NEG = -1e30
F32 = jnp.float32
BF16 = jnp.bfloat16
HIGH = lax.Precision.HIGHEST
SCALE = HEAD_DIM ** (-0.5)
VMEM = pl.BlockSpec(memory_space=pltpu.VMEM)
SMEM = pl.BlockSpec(memory_space=pltpu.SMEM)
LIMIT = 16 * 1024 * 1024
STEP_COST = pl.CostEstimate(flops=10**9, bytes_accessed=10**7, transcendentals=0)
STREAM_LIMIT = 50 * 1024 * 1024


def dot32(first, second):
    return jnp.dot(first, second, preferred_element_type=F32)


def dot_nt(first, second):
    return lax.dot_general(
        first, second, (((1,), (1,)), ((), ())), preferred_element_type=F32
    )


def dot_tn(first, second):
    return lax.dot_general(
        first, second, (((0,), (0,)), ((), ())), preferred_element_type=F32
    )


def high(first, second):
    return jnp.dot(first, second, precision=HIGH, preferred_element_type=F32)


def head(index):
    return slice(index * HEAD_DIM, (index + 1) * HEAD_DIM)


def rows_below(limit, length, width):
    return lax.broadcasted_iota(jnp.int32, (length, width), 0) < limit


def live_pairs(limit, length):
    row = lax.broadcasted_iota(jnp.int32, (length, length), 0)
    column = lax.broadcasted_iota(jnp.int32, (length, length), 1)
    return (column <= row) & (column < limit)


def split_kernel(core_ref, w_ref, own_ref, other_ref, landed, own_sem, other_sem):
    half = own_ref.shape[1]
    cols = half // CHUNKS
    core = core_ref[0]

    def own_copy(k):
        start = pl.multiple_of(core * half + k * cols, HEAD_DIM)
        place = slice(k * cols, (k + 1) * cols)
        return pltpu.make_async_copy(
            w_ref.at[:, pl.ds(start, cols)], own_ref.at[:, place], own_sem.at[k]
        )

    def other_copy(k):
        start = pl.multiple_of((1 - core) * half + k * cols, HEAD_DIM)
        place = slice(k * cols, (k + 1) * cols)
        return pltpu.make_async_copy(
            w_ref.at[:, pl.ds(start, cols)], landed.at[:, place], other_sem.at[k]
        )

    for k in range(CHUNKS):
        other_copy(k).start()
    for k in range(CHUNKS):
        own_copy(k).start()
    for k in range(CHUNKS):
        other_copy(k).wait()
        place = slice(k * cols, (k + 1) * cols)
        other_ref[:, place] = landed[:, place].astype(F32)
    for k in range(CHUNKS):
        own_copy(k).wait()


def split(core, w_out):
    inner, width = w_out.shape
    half = width // 2
    return pl.pallas_call(
        split_kernel,
        in_specs=[SMEM, pl.BlockSpec(memory_space=pltpu.HBM)],
        out_specs=[VMEM, VMEM],
        out_shape=[
            jax.ShapeDtypeStruct((inner, half), BF16),
            jax.ShapeDtypeStruct((inner, half), F32),
        ],
        scratch_shapes=[
            pltpu.VMEM((inner, half), BF16),
            pltpu.SemaphoreType.DMA((CHUNKS,)),
            pltpu.SemaphoreType.DMA((CHUNKS,)),
        ],
        compiler_params=pltpu.CompilerParams(vmem_limit_bytes=LIMIT),
    )(core, w_out)


def project_kernel(
    limit_ref, x_ref, wq_ref, wk_ref, wv_ref, gain_ref, bias_ref, aq_ref, av_ref, bq_ref, bv_ref,
    soft_ref, key_ref, value_ref, down_q_ref, down_v_ref, mixed_ref,
    rows_in, normed, wq_in, wk_in, wv_in, rows_sem, weight_sem,
):
    length, width = normed.shape
    inner = key_ref.shape[1]
    blocks = [slice(i, i + DEPTH) for i in range(0, width, DEPTH)]
    rows_copy = pltpu.make_async_copy(x_ref, rows_in, rows_sem)
    rows_copy.start()
    copies = []
    for i, block in enumerate(blocks):
        for j, (source, target) in enumerate(
            [(wq_ref, wq_in), (wk_ref, wk_in), (wv_ref, wv_in)]
        ):
            copies.append(
                pltpu.make_async_copy(
                    source.at[block], target.at[block], weight_sem.at[3 * i + j]
                )
            )
            copies[-1].start()
    rows_copy.wait()
    total = jnp.zeros((length, 1), F32)
    for block in blocks:
        total = total + jnp.sum(rows_in[:, block].astype(F32), axis=-1, keepdims=True)
    mean = total / width
    total = jnp.zeros((length, 1), F32)
    for block in blocks:
        centred = rows_in[:, block].astype(F32) - mean
        total = total + jnp.sum(centred * centred, axis=-1, keepdims=True)
    spread = lax.rsqrt(total / width + EPS)
    for block in blocks:
        centred = rows_in[:, block].astype(F32) - mean
        full = centred * spread * gain_ref[:, block] + bias_ref[:, block]
        normed[:, block] = full.astype(BF16)
    query = jnp.zeros((length, inner), F32)
    key = jnp.zeros((length, inner), F32)
    value = jnp.zeros((length, inner), F32)
    for i, block in enumerate(blocks):
        part = normed[:, block]
        for j in range(3):
            copies[3 * i + j].wait()
        query = query + dot32(part, wq_in[block])
        key = key + dot32(part, wk_in[block])
        value = value + dot32(part, wv_in[block])
    down_q = dot_nt(normed[...], aq_ref[...])
    down_v = dot_nt(normed[...], av_ref[...])
    down_q_ref[...] = down_q
    down_v_ref[...] = down_v
    limit = limit_ref[0]
    live = live_pairs(limit, length)
    kept = rows_below(limit, length, HEAD_DIM)
    query = (query + ADAPTER_SCALE * high(down_q, bq_ref[...])).astype(BF16)
    value = (value + ADAPTER_SCALE * high(down_v, bv_ref[...])).astype(BF16)
    key = key.astype(BF16)
    key_ref[...] = key
    value_ref[...] = value
    for h in range(inner // HEAD_DIM):
        scores = dot_nt(query[:, head(h)], key[:, head(h)]) * SCALE
        scores = jnp.where(live, scores, NEG)
        weights = jnp.exp(scores - jnp.max(scores, axis=-1, keepdims=True))
        soft = weights / jnp.sum(weights, axis=-1, keepdims=True)
        soft_ref[h] = soft
        mixed = dot32(soft.astype(BF16), value[:, head(h)]).astype(BF16)
        mixed_ref[:length, head(h)] = jnp.where(kept, mixed.astype(F32), 0.0)
    mixed_ref[length:] = jnp.zeros((8, inner), F32)


def project(limit, x, gain, bias, wq, wk, wv, aq, av, bq, bv):
    length, width = x.shape
    inner = wq.shape[1]
    rank = aq.shape[1]
    heads = inner // HEAD_DIM
    hbm = pl.BlockSpec(memory_space=pltpu.HBM)
    return pl.pallas_call(
        project_kernel,
        in_specs=[SMEM] + [hbm] * 4 + [VMEM] * 6,
        out_specs=[VMEM] * 6,
        out_shape=[
            jax.ShapeDtypeStruct((heads, length, length), F32),
            jax.ShapeDtypeStruct((length, inner), BF16),
            jax.ShapeDtypeStruct((length, inner), BF16),
            jax.ShapeDtypeStruct((length, rank), F32),
            jax.ShapeDtypeStruct((length, rank), F32),
            jax.ShapeDtypeStruct((length + 8, inner), F32),
        ],
        scratch_shapes=[
            pltpu.VMEM((length, width), BF16),
            pltpu.VMEM((length, width), BF16),
            pltpu.VMEM((width, inner), BF16),
            pltpu.VMEM((width, inner), BF16),
            pltpu.VMEM((width, inner), BF16),
            pltpu.SemaphoreType.DMA,
            pltpu.SemaphoreType.DMA((3 * (width // DEPTH),)),
        ],
        compiler_params=pltpu.CompilerParams(vmem_limit_bytes=STREAM_LIMIT),
        cost_estimate=pl.CostEstimate(
            flops=6 * length * width * inner, bytes_accessed=6 * width * inner, transcendentals=0
        ),
    )(limit, x, wq, wk, wv, gain[None], bias[None], aq.T, av.T, bq, bv)


def token_spec():
    return pl.BlockSpec(memory_space=pl.ANY)


def call(kernel, ins, outs, token, scalars=()):
    tokens = [] if token is None else [token]

    def body(*refs):
        count = len(scalars) + len(ins)
        kernel(*refs[:count], *refs[count + len(tokens) :])

    return pl.pallas_call(
        body,
        in_specs=[SMEM] * len(scalars) + [VMEM] * len(ins) + [token_spec()] * len(tokens),
        out_specs=[VMEM] * len(outs),
        out_shape=[jax.ShapeDtypeStruct(shape, kind) for shape, kind in outs],
        compiler_params=pltpu.CompilerParams(vmem_limit_bytes=LIMIT),
        cost_estimate=STEP_COST,
    )(*scalars, *ins, *tokens)


def rows_of(own_ref, got_ref, length):
    return jnp.concatenate(
        [own_ref[:length].astype(BF16), got_ref[:length].astype(BF16)], axis=1
    )


def put_tail(out_ref, own_ref, got_ref, length):
    out_ref[length:] = jnp.zeros((8, out_ref.shape[1]), F32)
    out_ref[length:, :HEAD_DIM] = own_ref[length:, :HEAD_DIM] + got_ref[length:, :HEAD_DIM]


def first_spread(index, chunks, length, own, got, own_w, other_w, token):
    inner, half = own_w.shape
    cols = half // chunks
    place = slice(index * cols, (index + 1) * cols)
    height = length + (8 if index == 0 else 0)

    def kernel(own_ref, got_ref, own_w_ref, other_w_ref, out_ref, pair_ref):
        pair_ref[:inner] = own_w_ref[:, place]
        pair_ref[inner:] = other_w_ref[:, place].astype(BF16)
        out_ref[:length] = dot32(rows_of(own_ref, got_ref, length), pair_ref[...])
        if index == 0:
            put_tail(out_ref, own_ref, got_ref, length)

    outs = [((height, cols), F32), ((2 * inner, cols), BF16)]
    return call(kernel, [own, got, own_w, other_w], outs, token)


def spread(index, length, own, got, pair, token):
    height = length + (8 if index == 0 else 0)

    def kernel(own_ref, got_ref, pair_ref, out_ref):
        out_ref[:length] = dot32(rows_of(own_ref, got_ref, length), pair_ref[...])
        if index == 0:
            put_tail(out_ref, own_ref, got_ref, length)

    return call(kernel, [own, got, pair], [((height, pair.shape[1]), F32)], token)[0]


def add(first, second, token):
    def kernel(first_ref, second_ref, out_ref):
        out_ref[...] = first_ref[...] + second_ref[: first_ref.shape[0]]

    return call(kernel, [first, second], [(first.shape, F32)], token)[0]


def add_and_pick(first, second, ends, outer, token):
    def kernel(ends_ref, first_ref, second_ref, outer_ref, sum_ref, sent_ref):
        total = first_ref[...] + second_ref[...]
        sum_ref[...] = total
        rows = outer_ref.shape[0]
        sent_ref[:rows] = jnp.where(ends_ref[0] > 0, outer_ref[...], total[:rows])
        if total.shape[0] > rows:
            sent_ref[rows:] = total[rows:]

    outs = [(first.shape, F32)] * 2
    return call(kernel, [first, second, outer], outs, token, [ends])


def gather(index, ends, got, held, pair, sums, limit, gap, token):
    inner = pair.shape[0] // 2
    extra = [] if gap is None else [gap]
    length = held.shape[0] - (8 if index == 0 else 0)

    def kernel(ends_ref, limit_ref, got_ref, held_ref, pair_ref, *refs):
        refs = list(refs)
        gap_ref = refs.pop(0) if gap is not None else None
        before = [refs.pop(0), refs.pop(0)] if index else None
        own_ref, other_ref = refs[:2]
        total = jnp.where(ends_ref[0] > 0, got_ref[...], held_ref[...])
        if index == 0:
            refs[2][...] = total[length:, :128]
            total = total[:length]
        if gap_ref is not None:
            kept = rows_below(limit_ref[0], length, total.shape[1])
            total = jnp.where(kept, total + gap_ref[...], 0.0)
        rounded = total.astype(BF16)
        own = dot_nt(rounded, pair_ref[:inner])
        other = dot_nt(rounded, pair_ref[inner:])
        squares = jnp.full((8, inner), jnp.sum(total * total), F32)
        if index:
            own = own + before[0][...]
            other = other + before[1][:length]
            squares = squares + before[1][length:]
        own_ref[...] = own
        other_ref[:length] = other
        other_ref[length:] = squares

    outs = [((length, inner), F32), ((length + 8, inner), F32)]
    if index == 0:
        outs.append(((8, 128), F32))
    return call(kernel, [got, held, pair] + extra + sums, outs, token, [ends, limit])


def cotangent_kernel(
    share, limit_ref, own_ref, other_ref, got_ref, soft_ref, key_ref, value_ref, down_q_ref,
    down_v_ref, out_ref,
):
    length, inner = own_ref.shape
    rank = down_q_ref.shape[1]
    live = live_pairs(limit_ref[0], length)
    pulled = (own_ref[...] + got_ref[:length]).astype(BF16)
    out_ref[2 * rank :] = other_ref[length:] + got_ref[length:]
    for h in range(inner // HEAD_DIM):
        soft = soft_ref[h]
        rows = pulled[:, head(h)]
        d_probs = dot_nt(rows, value_ref[:, head(h)]).astype(BF16).astype(F32)
        d_value = dot_tn(soft.astype(BF16), rows).astype(BF16).astype(F32)
        d_scores = soft * (d_probs - jnp.sum(soft * d_probs, axis=-1, keepdims=True))
        d_scores = jnp.where(live, d_scores, 0.0) * SCALE
        d_query = dot32(d_scores.astype(BF16), key_ref[:, head(h)]).astype(BF16).astype(F32)
        out_ref[:rank, head(h)] = share * lax.dot_general(
            down_q_ref[...], d_query, (((0,), (0,)), ((), ())), precision=HIGH,
            preferred_element_type=F32,
        )
        out_ref[rank : 2 * rank, head(h)] = share * lax.dot_general(
            down_v_ref[...], d_value, (((0,), (0,)), ((), ())), precision=HIGH,
            preferred_element_type=F32,
        )


def cotangent(share, limit, own, other, got, attention):
    inner = own.shape[1]
    rank = attention[3].shape[1]
    return pl.pallas_call(
        functools.partial(cotangent_kernel, share),
        in_specs=[SMEM] + [VMEM] * 8,
        out_specs=VMEM,
        out_shape=jax.ShapeDtypeStruct((2 * rank + 8, inner), F32),
        compiler_params=pltpu.CompilerParams(vmem_limit_bytes=LIMIT),
    )(limit, own, other, got, *attention)


def tangent_of(vector, limit, soft_ref, key_ref, value_ref, down_q_ref, down_v_ref, out_ref):
    length = key_ref.shape[0]
    rank = down_q_ref.shape[1]
    live = live_pairs(limit, length)
    kept = rows_below(limit, length, HEAD_DIM)
    d_query = (ADAPTER_SCALE * high(down_q_ref[...], vector[:rank])).astype(BF16)
    d_value = (ADAPTER_SCALE * high(down_v_ref[...], vector[rank:])).astype(BF16)
    for h in range(key_ref.shape[1] // HEAD_DIM):
        soft = soft_ref[h]
        d_scores = dot_nt(d_query[:, head(h)], key_ref[:, head(h)]) * SCALE
        d_scores = jnp.where(live, d_scores, 0.0)
        d_probs = soft * (d_scores - jnp.sum(soft * d_scores, axis=-1, keepdims=True))
        d_mixed = dot32(d_probs.astype(BF16), value_ref[:, head(h)]) + dot32(
            soft.astype(BF16), d_value[:, head(h)]
        )
        out_ref[:length, head(h)] = jnp.where(kept, d_mixed.astype(BF16).astype(F32), 0.0)


def total_of(terms):
    while len(terms) > 1:
        terms = [terms[i] + terms[i + 1] for i in range(0, len(terms), 2)]
    return terms[0]


def put_sums(out_ref, remain, image):
    lane = lax.broadcasted_iota(jnp.int32, (8, out_ref.shape[1]), 1)
    cross = 0.0 if image is None else jnp.sum(remain * image)
    out_ref[out_ref.shape[0] - 8 :] = jnp.where(lane == 0, jnp.sum(remain * remain), cross)


def first_kernel(n_dp, *refs):
    terms, refs = refs[:n_dp], refs[n_dp:]
    limit_ref, *attention, remain_ref, out_ref = refs
    grads = total_of([term[...] for term in terms])
    remain = -grads[: remain_ref.shape[0]]
    remain_ref[...] = remain
    put_sums(out_ref, remain, None)
    tangent_of(remain, limit_ref[0], *attention, out_ref)


def first_step(terms, limit, attention):
    inner = terms[0].shape[1]
    length = attention[1].shape[0]
    rank = attention[3].shape[1]
    return pl.pallas_call(
        functools.partial(first_kernel, len(terms)),
        in_specs=[VMEM] * len(terms) + [SMEM] + [VMEM] * 5,
        out_specs=[VMEM] * 2,
        out_shape=[
            jax.ShapeDtypeStruct((2 * rank, inner), F32),
            jax.ShapeDtypeStruct((length + 8, inner), F32),
        ],
        compiler_params=pltpu.CompilerParams(vmem_limit_bytes=LIMIT),
    )(*terms, limit, *attention)


def step_kernel(n_dp, token_count, index, last, *refs):
    terms, refs = refs[:n_dp], refs[n_dp:]
    sums_ref, remain_ref, *refs = refs
    if index:
        before_ref, newton_ref, direction_ref, image_ref, *refs = refs
    part = total_of([term[...] for term in terms])
    remain = remain_ref[...]
    rows = remain.shape[0]
    norm, cross = sums_ref[:1, 0:1], sums_ref[:1, 1:2]
    fresh = part[:rows] + DAMP * remain
    curv = part[rows : rows + 1, 0:1] / token_count + DAMP * norm
    if index:
        ratio = norm / before_ref[:1, 0:1]
        curv = curv + 2.0 * ratio * cross + ratio * ratio * before_ref[:1, 1:2]
        direction = remain + ratio * direction_ref[...]
        image = fresh + ratio * image_ref[...]
    else:
        direction, image = remain, fresh
    alpha = norm / curv
    newton = alpha * direction
    if index:
        newton = newton_ref[...] + newton
    remain = remain - alpha * image
    if last:
        step_q_ref, step_v_ref, remain_q_ref, remain_v_ref = refs
        rank = rows // 2
        step_q_ref[...] = newton[:rank]
        step_v_ref[...] = newton[rank:]
        remain_q_ref[...] = remain[:rank]
        remain_v_ref[...] = remain[rank:]
        return
    limit_ref, *refs = refs
    attention, refs = refs[:5], refs[5:]
    next_remain, next_before, next_newton, next_direction, next_image, out_ref = refs
    lane = lax.broadcasted_iota(jnp.int32, next_before.shape, 1)
    next_remain[...] = remain
    next_before[...] = jnp.where(lane == 0, norm, curv)
    next_newton[...] = newton
    next_direction[...] = direction
    next_image[...] = image
    put_sums(out_ref, remain, image)
    tangent_of(remain, limit_ref[0], *attention, out_ref)


def cg_step(index, token_count, terms, sums, remain, state, limit, attention):
    last = index == CG_STEPS - 1
    rows, inner = remain.shape
    matrix = jax.ShapeDtypeStruct((rows, inner), F32)
    scalars = jax.ShapeDtypeStruct((8, 128), F32)
    args = [*terms, sums, remain, *state]
    specs = [VMEM] * len(args)
    if last:
        shapes = [jax.ShapeDtypeStruct((rows // 2, inner), F32)] * 4
    else:
        args += [limit, *attention]
        specs += [SMEM] + [VMEM] * 5
        length = attention[1].shape[0]
        shapes = [matrix, scalars, matrix, matrix, matrix]
        shapes.append(jax.ShapeDtypeStruct((length + 8, inner), F32))
    return pl.pallas_call(
        functools.partial(step_kernel, len(terms), token_count, index, last),
        in_specs=specs,
        out_specs=[VMEM] * len(shapes),
        out_shape=shapes,
        compiler_params=pltpu.CompilerParams(vmem_limit_bytes=LIMIT),
    )(*args)


def on_device(
    inputs,
    targets,
    lengths,
    ln_gain,
    ln_bias,
    query_weight,
    w_key,
    value_weight,
    w_out,
    down_query,
    down_value,
    query_up_factor,
    value_up_factor,
):
    length, width = inputs.shape
    n_dp = lax.axis_size("dp")
    n_chip = lax.axis_size("chip")
    core = lax.axis_index("core")
    chip = lax.axis_index("chip")
    token_count = length * n_dp
    half = width // 2

    def swap(part):
        return lax.ppermute(part, "core", [(0, 1), (1, 0)])

    def data_terms(part):
        step = 1
        while 2 * step < n_dp:
            part = part + lax.ppermute(part, "dp", [(d, d ^ step) for d in range(n_dp)])
            step *= 2
        return [part, lax.ppermute(part, "dp", [(d, d ^ step) for d in range(n_dp)])]

    where = core.astype(jnp.int32)[None]
    own_w, other_w = split(where, w_out)
    other_w = swap(other_w)
    cols = half // CHUNKS
    gap = lax.dynamic_slice_in_dim(inputs, core * half, half, 1).astype(F32)
    gap = gap - lax.dynamic_slice_in_dim(targets, core * half, half, 1).astype(F32)

    soft, key, value, down_q, down_v, mixed = project(
        lengths, inputs, ln_gain, ln_bias, query_weight, w_key, value_weight, down_query,
        down_value, query_up_factor, value_up_factor,
    )
    attention = (soft, key, value, down_q, down_v)

    ends = ((chip == 0) | (chip == n_chip - 1)).astype(jnp.int32)[None]

    def outer_swap(part):
        return lax.ppermute(part, "chip", [(0, 1), (1, 0), (2, 3), (3, 2)])

    def inner_swap(part):
        return lax.ppermute(part, "chip", [(0, 0), (1, 2), (2, 1), (3, 3)])

    def product(rows, pairs):
        got_rows = swap(rows)
        first = not pairs
        pairs.extend([None] * (CHUNKS - len(pairs)))
        parts, scalars = [], None
        own_part, total, outer, inner = {}, {}, {}, {}
        token = None

        def begin(k):
            if first:
                own_part[k], pairs[k] = first_spread(
                    k, CHUNKS, length, rows, got_rows, own_w, other_w, token
                )
            else:
                own_part[k] = spread(k, length, rows, got_rows, pairs[k], token)
            return own_part[k]

        def finish(k, got):
            gap_part = gap[:, k * cols : (k + 1) * cols] if first else None
            return gather(k, ends, got, total[k], pairs[k], parts, lengths, gap_part, token)

        if n_chip != 4:
            for k in range(CHUNKS):
                token = begin(k)
            for k in range(CHUNKS):
                total[k] = lax.psum(own_part[k], "chip")
                out = finish(k, total[k])
                parts, scalars = list(out[:2]), out[2] if k == 0 else scalars
        else:
            for k in [0, 1, 2] if first else [0, *range(2, CHUNKS), 1]:
                token = begin(k)
            for k in (0, 1):
                outer[k] = outer_swap(own_part[k])
            for tick in range(CHUNKS + 3):
                if tick < CHUNKS:
                    own_part[tick] = add(own_part[tick], outer[tick], token)
                    token = own_part[tick]
                    inner[tick] = inner_swap(token)
                later = tick + 2
                if 1 <= tick <= CHUNKS:
                    k = tick - 1
                    if later < CHUNKS:
                        total[k], sent = add_and_pick(
                            own_part[k], inner[k], ends, own_part[later], token
                        )
                    else:
                        total[k] = sent = add(own_part[k], inner[k], token)
                    token = sent
                    outer[later] = outer_swap(sent)
                elif tick == 0:
                    outer[later] = outer_swap(own_part[later])
                if tick + 3 < CHUNKS and first:
                    token = begin(tick + 3)
                if tick >= 3:
                    out = finish(tick - 3, outer[tick])
                    parts, scalars = list(out[:2]), out[2] if tick == 3 else scalars
                    token = parts[0]
        own, other = parts
        share = ADAPTER_SCALE / token_count
        part = cotangent(share, lengths, own, other, swap(other), attention)
        return data_terms(part), scalars

    pairs = []
    terms, _ = product(mixed, pairs)
    remain, rows = first_step(terms, lengths, attention)
    state = ()
    for index in range(CG_STEPS):
        terms, sums = product(rows, pairs)
        out = cg_step(index, token_count, terms, sums, remain, state, lengths, attention)
        if index < CG_STEPS - 1:
            remain, *state, rows = out
    return tuple(out)


def solution(mesh):
    fine = Mesh(mesh.devices.reshape(mesh.shape["dp"], -1, 2), ("dp", "chip", "core"))
    tensor = ("chip", "core")
    in_specs = (
        P("dp", None),
        P("dp", None),
        P("dp"),
        P(),
        P(),
        P(None, tensor),
        P(None, tensor),
        P(None, tensor),
        P(tensor, None),
        P(),
        P(),
        P(None, tensor),
        P(None, tensor),
    )
    out_specs = (P(None, tensor),) * 4
    return jax.shard_map(
        on_device, mesh=fine, in_specs=in_specs, out_specs=out_specs, check_vma=False
    )
```

```python
import functools

import jax
import jax.numpy as jnp
from jax import lax
from jax.experimental import pallas as pl
from jax.experimental.pallas import tpu as pltpu
from jax.sharding import Mesh
from jax.sharding import PartitionSpec as P

HEAD_DIM = 128
CG_STEPS = 3
CHUNKS = 6
DEPTH = 1024

EPS = 1e-05
ADAPTER_SCALE = 2.0
DAMP = 0.05
NEG = -1e30
F32 = jnp.float32
BF16 = jnp.bfloat16
HIGH = lax.Precision.HIGHEST
SCALE = HEAD_DIM ** (-0.5)
VMEM = pl.BlockSpec(memory_space=pltpu.VMEM)
SMEM = pl.BlockSpec(memory_space=pltpu.SMEM)
LIMIT = 16 * 1024 * 1024
STEP_COST = pl.CostEstimate(flops=10**9, bytes_accessed=10**7, transcendentals=0)
STREAM_LIMIT = 50 * 1024 * 1024


def dot32(first, second):
    return jnp.dot(first, second, preferred_element_type=F32)


def dot_nt(first, second):
    return lax.dot_general(
        first, second, (((1,), (1,)), ((), ())), preferred_element_type=F32
    )


def dot_tn(first, second):
    return lax.dot_general(
        first, second, (((0,), (0,)), ((), ())), preferred_element_type=F32
    )


def high(first, second):
    return jnp.dot(first, second, precision=HIGH, preferred_element_type=F32)


def head(index):
    return slice(index * HEAD_DIM, (index + 1) * HEAD_DIM)


def rows_below(limit, length, width):
    return lax.broadcasted_iota(jnp.int32, (length, width), 0) < limit


def live_pairs(limit, length):
    row = lax.broadcasted_iota(jnp.int32, (length, length), 0)
    column = lax.broadcasted_iota(jnp.int32, (length, length), 1)
    return (column <= row) & (column < limit)


def split_kernel(core_ref, w_ref, *refs):
    own_refs, other_refs = refs[:CHUNKS], refs[CHUNKS : 2 * CHUNKS]
    landed, own_sem, other_sem = refs[2 * CHUNKS :]
    cols = own_refs[0].shape[1]
    half = CHUNKS * cols
    core = core_ref[0]

    def own_copy(k):
        start = pl.multiple_of(core * half + k * cols, HEAD_DIM)
        return pltpu.make_async_copy(
            w_ref.at[:, pl.ds(start, cols)], own_refs[k], own_sem.at[k]
        )

    def other_copy(k):
        start = pl.multiple_of((1 - core) * half + k * cols, HEAD_DIM)
        return pltpu.make_async_copy(
            w_ref.at[:, pl.ds(start, cols)], landed.at[k], other_sem.at[k]
        )

    for k in range(CHUNKS):
        other_copy(k).start()
    for k in range(CHUNKS):
        own_copy(k).start()
    for k in range(CHUNKS):
        other_copy(k).wait()
        other_refs[k][...] = landed[k].astype(F32)
    for k in range(CHUNKS):
        own_copy(k).wait()


def split(core, w_out):
    inner, width = w_out.shape
    cols = width // 2 // CHUNKS
    out = pl.pallas_call(
        split_kernel,
        in_specs=[SMEM, pl.BlockSpec(memory_space=pltpu.HBM)],
        out_specs=[VMEM] * (2 * CHUNKS),
        out_shape=[jax.ShapeDtypeStruct((inner, cols), BF16)] * CHUNKS
        + [jax.ShapeDtypeStruct((inner, cols), F32)] * CHUNKS,
        scratch_shapes=[
            pltpu.VMEM((CHUNKS, inner, cols), BF16),
            pltpu.SemaphoreType.DMA((CHUNKS,)),
            pltpu.SemaphoreType.DMA((CHUNKS,)),
        ],
        compiler_params=pltpu.CompilerParams(vmem_limit_bytes=LIMIT),
    )(core, w_out)
    return out[:CHUNKS], out[CHUNKS:]


def project_kernel(
    limit_ref, x_ref, wq_ref, wk_ref, wv_ref, gain_ref, bias_ref, aq_ref, av_ref, bq_ref, bv_ref,
    soft_ref, key_ref, value_ref, down_q_ref, down_v_ref, mixed_ref,
    rows_in, normed, wq_in, wk_in, wv_in, rows_sem, weight_sem,
):
    length, width = normed.shape
    inner = key_ref.shape[1]
    blocks = [slice(i, i + DEPTH) for i in range(0, width, DEPTH)]
    rows_copy = pltpu.make_async_copy(x_ref, rows_in, rows_sem)
    rows_copy.start()
    copies = []
    for i, block in enumerate(blocks):
        for j, (source, target) in enumerate(
            [(wq_ref, wq_in), (wk_ref, wk_in), (wv_ref, wv_in)]
        ):
            copies.append(
                pltpu.make_async_copy(
                    source.at[block], target.at[block], weight_sem.at[3 * i + j]
                )
            )
            copies[-1].start()
    rows_copy.wait()
    total = jnp.zeros((length, 1), F32)
    for block in blocks:
        total = total + jnp.sum(rows_in[:, block].astype(F32), axis=-1, keepdims=True)
    mean = total / width
    total = jnp.zeros((length, 1), F32)
    for block in blocks:
        centred = rows_in[:, block].astype(F32) - mean
        total = total + jnp.sum(centred * centred, axis=-1, keepdims=True)
    spread = lax.rsqrt(total / width + EPS)
    for block in blocks:
        centred = rows_in[:, block].astype(F32) - mean
        full = centred * spread * gain_ref[:, block] + bias_ref[:, block]
        normed[:, block] = full.astype(BF16)
    query = jnp.zeros((length, inner), F32)
    key = jnp.zeros((length, inner), F32)
    value = jnp.zeros((length, inner), F32)
    for i, block in enumerate(blocks):
        part = normed[:, block]
        for j in range(3):
            copies[3 * i + j].wait()
        query = query + dot32(part, wq_in[block])
        key = key + dot32(part, wk_in[block])
        value = value + dot32(part, wv_in[block])
    down_q = dot_nt(normed[...], aq_ref[...])
    down_v = dot_nt(normed[...], av_ref[...])
    down_q_ref[...] = down_q
    down_v_ref[...] = down_v
    limit = limit_ref[0]
    live = live_pairs(limit, length)
    kept = rows_below(limit, length, HEAD_DIM)
    query = (query + ADAPTER_SCALE * high(down_q, bq_ref[...])).astype(BF16)
    value = (value + ADAPTER_SCALE * high(down_v, bv_ref[...])).astype(BF16)
    key = key.astype(BF16)
    key_ref[...] = key
    value_ref[...] = value
    for h in range(inner // HEAD_DIM):
        scores = dot_nt(query[:, head(h)], key[:, head(h)]) * SCALE
        scores = jnp.where(live, scores, NEG)
        weights = jnp.exp(scores - jnp.max(scores, axis=-1, keepdims=True))
        soft = weights / jnp.sum(weights, axis=-1, keepdims=True)
        soft_ref[h] = soft
        mixed = dot32(soft.astype(BF16), value[:, head(h)]).astype(BF16)
        mixed_ref[:length, head(h)] = jnp.where(kept, mixed.astype(F32), 0.0)
    mixed_ref[length:] = jnp.zeros((8, inner), F32)


def project(limit, x, gain, bias, wq, wk, wv, aq, av, bq, bv):
    length, width = x.shape
    inner = wq.shape[1]
    rank = aq.shape[1]
    heads = inner // HEAD_DIM
    hbm = pl.BlockSpec(memory_space=pltpu.HBM)
    return pl.pallas_call(
        project_kernel,
        in_specs=[SMEM] + [hbm] * 4 + [VMEM] * 6,
        out_specs=[VMEM] * 6,
        out_shape=[
            jax.ShapeDtypeStruct((heads, length, length), F32),
            jax.ShapeDtypeStruct((length, inner), BF16),
            jax.ShapeDtypeStruct((length, inner), BF16),
            jax.ShapeDtypeStruct((length, rank), F32),
            jax.ShapeDtypeStruct((length, rank), F32),
            jax.ShapeDtypeStruct((length + 8, inner), F32),
        ],
        scratch_shapes=[
            pltpu.VMEM((length, width), BF16),
            pltpu.VMEM((length, width), BF16),
            pltpu.VMEM((width, inner), BF16),
            pltpu.VMEM((width, inner), BF16),
            pltpu.VMEM((width, inner), BF16),
            pltpu.SemaphoreType.DMA,
            pltpu.SemaphoreType.DMA((3 * (width // DEPTH),)),
        ],
        compiler_params=pltpu.CompilerParams(vmem_limit_bytes=STREAM_LIMIT),
        cost_estimate=pl.CostEstimate(
            flops=6 * length * width * inner, bytes_accessed=6 * width * inner, transcendentals=0
        ),
    )(limit, x, wq, wk, wv, gain[None], bias[None], aq.T, av.T, bq, bv)


def token_spec():
    return pl.BlockSpec(memory_space=pl.ANY)


def call(kernel, ins, outs, token, scalars=()):
    tokens = [] if token is None else [token]

    def body(*refs):
        count = len(scalars) + len(ins)
        kernel(*refs[:count], *refs[count + len(tokens) :])

    return pl.pallas_call(
        body,
        in_specs=[SMEM] * len(scalars) + [VMEM] * len(ins) + [token_spec()] * len(tokens),
        out_specs=[VMEM] * len(outs),
        out_shape=[jax.ShapeDtypeStruct(shape, kind) for shape, kind in outs],
        compiler_params=pltpu.CompilerParams(vmem_limit_bytes=LIMIT),
        cost_estimate=STEP_COST,
    )(*scalars, *ins, *tokens)


def rows_of(own_ref, got_ref, length):
    return jnp.concatenate(
        [own_ref[:length].astype(BF16), got_ref[:length].astype(BF16)], axis=1
    )


def put_tail(out_ref, own_ref, got_ref, length):
    out_ref[length:] = jnp.zeros((8, out_ref.shape[1]), F32)
    out_ref[length:, :HEAD_DIM] = own_ref[length:, :HEAD_DIM] + got_ref[length:, :HEAD_DIM]


def first_spread(index, length, own, got, own_w, other_w, token):
    inner, cols = own_w.shape
    height = length + (8 if index == 0 else 0)

    def kernel(own_ref, got_ref, own_w_ref, other_w_ref, out_ref, pair_ref):
        pair_ref[:inner] = own_w_ref[...]
        pair_ref[inner:] = other_w_ref[...].astype(BF16)
        out_ref[:length] = dot32(rows_of(own_ref, got_ref, length), pair_ref[...])
        if index == 0:
            put_tail(out_ref, own_ref, got_ref, length)

    outs = [((height, cols), F32), ((2 * inner, cols), BF16)]
    return call(kernel, [own, got, own_w, other_w], outs, token)


def spread(index, length, own, got, pair, token):
    height = length + (8 if index == 0 else 0)

    def kernel(own_ref, got_ref, pair_ref, out_ref):
        out_ref[:length] = dot32(rows_of(own_ref, got_ref, length), pair_ref[...])
        if index == 0:
            put_tail(out_ref, own_ref, got_ref, length)

    return call(kernel, [own, got, pair], [((height, pair.shape[1]), F32)], token)[0]


def add(first, second, token):
    def kernel(first_ref, second_ref, out_ref):
        out_ref[...] = first_ref[...] + second_ref[: first_ref.shape[0]]

    return call(kernel, [first, second], [(first.shape, F32)], token)[0]


def add_and_pick(first, second, ends, outer, token):
    def kernel(ends_ref, first_ref, second_ref, outer_ref, sum_ref, sent_ref):
        total = first_ref[...] + second_ref[...]
        sum_ref[...] = total
        rows = outer_ref.shape[0]
        sent_ref[:rows] = jnp.where(ends_ref[0] > 0, outer_ref[...], total[:rows])
        if total.shape[0] > rows:
            sent_ref[rows:] = total[rows:]

    outs = [(first.shape, F32)] * 2
    return call(kernel, [first, second, outer], outs, token, [ends])


def gather(index, length, ends, got, held, pair, sums, limit, gap, token):
    inner = pair.shape[0] // 2
    extra = [] if gap is None else [gap]

    def kernel(ends_ref, limit_ref, got_ref, held_ref, pair_ref, *refs):
        refs = list(refs)
        gap_ref = refs.pop(0) if gap is not None else None
        before = [refs.pop(0), refs.pop(0)] if index else None
        own_ref, other_ref = refs[:2]
        total = jnp.where(ends_ref[0] > 0, got_ref[...], held_ref[...])
        total = total[: length + (8 if index == 0 else 0)]
        if index == 0:
            refs[2][...] = total[length:, :128]
            total = total[:length]
        if gap_ref is not None:
            kept = rows_below(limit_ref[0], length, total.shape[1])
            total = jnp.where(kept, total + gap_ref[...], 0.0)
        rounded = total.astype(BF16)
        own = dot_nt(rounded, pair_ref[:inner])
        other = dot_nt(rounded, pair_ref[inner:])
        squares = jnp.full((8, inner), jnp.sum(total * total), F32)
        if index:
            own = own + before[0][...]
            other = other + before[1][:length]
            squares = squares + before[1][length:]
        own_ref[...] = own
        other_ref[:length] = other
        other_ref[length:] = squares

    outs = [((length, inner), F32), ((length + 8, inner), F32)]
    if index == 0:
        outs.append(((8, 128), F32))
    return call(kernel, [got, held, pair] + extra + sums, outs, token, [ends, limit])


def cotangent_kernel(
    share, limit_ref, own_ref, other_ref, got_ref, soft_ref, key_ref, value_ref, down_q_ref,
    down_v_ref, out_ref,
):
    length, inner = own_ref.shape
    rank = down_q_ref.shape[1]
    live = live_pairs(limit_ref[0], length)
    pulled = (own_ref[...] + got_ref[:length]).astype(BF16)
    out_ref[2 * rank :] = other_ref[length:] + got_ref[length:]
    for h in range(inner // HEAD_DIM):
        soft = soft_ref[h]
        rows = pulled[:, head(h)]
        d_probs = dot_nt(rows, value_ref[:, head(h)]).astype(BF16).astype(F32)
        d_value = dot_tn(soft.astype(BF16), rows).astype(BF16).astype(F32)
        d_scores = soft * (d_probs - jnp.sum(soft * d_probs, axis=-1, keepdims=True))
        d_scores = jnp.where(live, d_scores, 0.0) * SCALE
        d_query = dot32(d_scores.astype(BF16), key_ref[:, head(h)]).astype(BF16).astype(F32)
        out_ref[:rank, head(h)] = share * lax.dot_general(
            down_q_ref[...], d_query, (((0,), (0,)), ((), ())), precision=HIGH,
            preferred_element_type=F32,
        )
        out_ref[rank : 2 * rank, head(h)] = share * lax.dot_general(
            down_v_ref[...], d_value, (((0,), (0,)), ((), ())), precision=HIGH,
            preferred_element_type=F32,
        )


def cotangent(share, limit, own, other, got, attention):
    inner = own.shape[1]
    rank = attention[3].shape[1]
    return pl.pallas_call(
        functools.partial(cotangent_kernel, share),
        in_specs=[SMEM] + [VMEM] * 8,
        out_specs=VMEM,
        out_shape=jax.ShapeDtypeStruct((2 * rank + 8, inner), F32),
        compiler_params=pltpu.CompilerParams(vmem_limit_bytes=LIMIT),
    )(limit, own, other, got, *attention)


def tangent_of(vector, limit, soft_ref, key_ref, value_ref, down_q_ref, down_v_ref, out_ref):
    length = key_ref.shape[0]
    rank = down_q_ref.shape[1]
    live = live_pairs(limit, length)
    kept = rows_below(limit, length, HEAD_DIM)
    d_query = (ADAPTER_SCALE * high(down_q_ref[...], vector[:rank])).astype(BF16)
    d_value = (ADAPTER_SCALE * high(down_v_ref[...], vector[rank:])).astype(BF16)
    for h in range(key_ref.shape[1] // HEAD_DIM):
        soft = soft_ref[h]
        d_scores = dot_nt(d_query[:, head(h)], key_ref[:, head(h)]) * SCALE
        d_scores = jnp.where(live, d_scores, 0.0)
        d_probs = soft * (d_scores - jnp.sum(soft * d_scores, axis=-1, keepdims=True))
        d_mixed = dot32(d_probs.astype(BF16), value_ref[:, head(h)]) + dot32(
            soft.astype(BF16), d_value[:, head(h)]
        )
        out_ref[:length, head(h)] = jnp.where(kept, d_mixed.astype(BF16).astype(F32), 0.0)


def total_of(terms):
    while len(terms) > 1:
        terms = [terms[i] + terms[i + 1] for i in range(0, len(terms), 2)]
    return terms[0]


def put_sums(out_ref, remain, image):
    lane = lax.broadcasted_iota(jnp.int32, (8, out_ref.shape[1]), 1)
    cross = 0.0 if image is None else jnp.sum(remain * image)
    out_ref[out_ref.shape[0] - 8 :] = jnp.where(lane == 0, jnp.sum(remain * remain), cross)


def first_kernel(n_dp, *refs):
    terms, refs = refs[:n_dp], refs[n_dp:]
    limit_ref, *attention, remain_ref, out_ref = refs
    grads = total_of([term[...] for term in terms])
    remain = -grads[: remain_ref.shape[0]]
    remain_ref[...] = remain
    put_sums(out_ref, remain, None)
    tangent_of(remain, limit_ref[0], *attention, out_ref)


def first_step(terms, limit, attention):
    inner = terms[0].shape[1]
    length = attention[1].shape[0]
    rank = attention[3].shape[1]
    return pl.pallas_call(
        functools.partial(first_kernel, len(terms)),
        in_specs=[VMEM] * len(terms) + [SMEM] + [VMEM] * 5,
        out_specs=[VMEM] * 2,
        out_shape=[
            jax.ShapeDtypeStruct((2 * rank, inner), F32),
            jax.ShapeDtypeStruct((length + 8, inner), F32),
        ],
        compiler_params=pltpu.CompilerParams(vmem_limit_bytes=LIMIT),
    )(*terms, limit, *attention)


def step_kernel(n_dp, token_count, index, last, *refs):
    terms, refs = refs[:n_dp], refs[n_dp:]
    sums_ref, remain_ref, *refs = refs
    if index:
        before_ref, newton_ref, direction_ref, image_ref, *refs = refs
    part = total_of([term[...] for term in terms])
    remain = remain_ref[...]
    rows = remain.shape[0]
    norm, cross = sums_ref[:1, 0:1], sums_ref[:1, 1:2]
    fresh = part[:rows] + DAMP * remain
    curv = part[rows : rows + 1, 0:1] / token_count + DAMP * norm
    if index:
        ratio = norm / before_ref[:1, 0:1]
        curv = curv + 2.0 * ratio * cross + ratio * ratio * before_ref[:1, 1:2]
        direction = remain + ratio * direction_ref[...]
        image = fresh + ratio * image_ref[...]
    else:
        direction, image = remain, fresh
    alpha = norm / curv
    newton = alpha * direction
    if index:
        newton = newton_ref[...] + newton
    remain = remain - alpha * image
    if last:
        step_q_ref, step_v_ref, remain_q_ref, remain_v_ref = refs
        rank = rows // 2
        step_q_ref[...] = newton[:rank]
        step_v_ref[...] = newton[rank:]
        remain_q_ref[...] = remain[:rank]
        remain_v_ref[...] = remain[rank:]
        return
    limit_ref, *refs = refs
    attention, refs = refs[:5], refs[5:]
    next_remain, next_before, next_newton, next_direction, next_image, out_ref = refs
    lane = lax.broadcasted_iota(jnp.int32, next_before.shape, 1)
    next_remain[...] = remain
    next_before[...] = jnp.where(lane == 0, norm, curv)
    next_newton[...] = newton
    next_direction[...] = direction
    next_image[...] = image
    put_sums(out_ref, remain, image)
    tangent_of(remain, limit_ref[0], *attention, out_ref)


def cg_step(index, token_count, terms, sums, remain, state, limit, attention):
    last = index == CG_STEPS - 1
    rows, inner = remain.shape
    matrix = jax.ShapeDtypeStruct((rows, inner), F32)
    scalars = jax.ShapeDtypeStruct((8, 128), F32)
    args = [*terms, sums, remain, *state]
    specs = [VMEM] * len(args)
    if last:
        shapes = [jax.ShapeDtypeStruct((rows // 2, inner), F32)] * 4
    else:
        args += [limit, *attention]
        specs += [SMEM] + [VMEM] * 5
        length = attention[1].shape[0]
        shapes = [matrix, scalars, matrix, matrix, matrix]
        shapes.append(jax.ShapeDtypeStruct((length + 8, inner), F32))
    return pl.pallas_call(
        functools.partial(step_kernel, len(terms), token_count, index, last),
        in_specs=specs,
        out_specs=[VMEM] * len(shapes),
        out_shape=shapes,
        compiler_params=pltpu.CompilerParams(vmem_limit_bytes=LIMIT),
    )(*args)


def on_device(
    inputs,
    targets,
    lengths,
    ln_gain,
    ln_bias,
    query_weight,
    w_key,
    value_weight,
    w_out,
    down_query,
    down_value,
    query_up_factor,
    value_up_factor,
):
    length, width = inputs.shape
    n_dp = lax.axis_size("dp")
    n_chip = lax.axis_size("chip")
    core = lax.axis_index("core")
    chip = lax.axis_index("chip")
    token_count = length * n_dp
    half = width // 2

    def swap(part):
        return lax.ppermute(part, "core", [(0, 1), (1, 0)])

    def data_terms(part):
        step = 1
        while 2 * step < n_dp:
            part = part + lax.ppermute(part, "dp", [(d, d ^ step) for d in range(n_dp)])
            step *= 2
        return [part, lax.ppermute(part, "dp", [(d, d ^ step) for d in range(n_dp)])]

    where = core.astype(jnp.int32)[None]
    own_w, other_w = split(where, w_out)
    other_w = [swap(part) for part in other_w]
    cols = half // CHUNKS
    gap = lax.dynamic_slice_in_dim(inputs, core * half, half, 1).astype(F32)
    gap = gap - lax.dynamic_slice_in_dim(targets, core * half, half, 1).astype(F32)

    soft, key, value, down_q, down_v, mixed = project(
        lengths, inputs, ln_gain, ln_bias, query_weight, w_key, value_weight, down_query,
        down_value, query_up_factor, value_up_factor,
    )
    attention = (soft, key, value, down_q, down_v)

    ends = ((chip == 0) | (chip == n_chip - 1)).astype(jnp.int32)[None]

    def outer_swap(part):
        return lax.ppermute(part, "chip", [(0, 1), (1, 0), (2, 3), (3, 2)])

    def inner_swap(part):
        return lax.ppermute(part, "chip", [(0, 0), (1, 2), (2, 1), (3, 3)])

    def product(rows, pairs):
        got_rows = swap(rows)
        first = not pairs
        pairs.extend([None] * (CHUNKS - len(pairs)))
        parts, scalars = [], None
        own_part, total, outer, inner = {}, {}, {}, {}
        token = None

        def begin(k):
            if first:
                own_part[k], pairs[k] = first_spread(
                    k, length, rows, got_rows, own_w[k], other_w[k], token
                )
            else:
                own_part[k] = spread(k, length, rows, got_rows, pairs[k], token)
            return own_part[k]

        def finish(k, got):
            gap_part = gap[:, k * cols : (k + 1) * cols] if first else None
            return gather(k, length, ends, got, total[k], pairs[k], parts, lengths, gap_part, token)

        if n_chip != 4:
            for k in range(CHUNKS):
                token = begin(k)
            for k in range(CHUNKS):
                total[k] = lax.psum(own_part[k], "chip")
                out = finish(k, total[k])
                parts, scalars = list(out[:2]), out[2] if k == 0 else scalars
        else:
            for k in [0, 1, 2] if first else [0, *range(2, CHUNKS), 1]:
                token = begin(k)
            for k in (0, 1):
                outer[k] = outer_swap(own_part[k])
            for tick in range(CHUNKS + 3):
                if tick < CHUNKS:
                    own_part[tick] = add(own_part[tick], outer[tick], token)
                    token = own_part[tick]
                    inner[tick] = inner_swap(token)
                later = tick + 2
                if tick == CHUNKS:
                    out = finish(tick - 3, outer[tick])
                    parts = list(out[:2])
                    token = parts[0]
                if 1 <= tick <= CHUNKS:
                    k = tick - 1
                    if later < CHUNKS:
                        total[k], sent = add_and_pick(
                            own_part[k], inner[k], ends, own_part[later], token
                        )
                    else:
                        total[k] = sent = add(own_part[k], inner[k], token)
                    token = sent
                    outer[later] = outer_swap(sent)
                elif tick == 0:
                    outer[later] = outer_swap(own_part[later])
                if tick + 3 < CHUNKS and first:
                    token = begin(tick + 3)
                if tick >= 3 and tick != CHUNKS:
                    out = finish(tick - 3, outer[tick])
                    parts, scalars = list(out[:2]), out[2] if tick == 3 else scalars
                    token = parts[0]
        own, other = parts
        share = ADAPTER_SCALE / token_count
        part = cotangent(share, lengths, own, other, swap(other), attention)
        return data_terms(part), scalars

    pairs = []
    terms, _ = product(mixed, pairs)
    remain, rows = first_step(terms, lengths, attention)
    state = ()
    for index in range(CG_STEPS):
        terms, sums = product(rows, pairs)
        out = cg_step(index, token_count, terms, sums, remain, state, lengths, attention)
        if index < CG_STEPS - 1:
            remain, *state, rows = out
    return tuple(out)


def solution(mesh):
    fine = Mesh(mesh.devices.reshape(mesh.shape["dp"], -1, 2), ("dp", "chip", "core"))
    tensor = ("chip", "core")
    in_specs = (
        P("dp", None),
        P("dp", None),
        P("dp"),
        P(),
        P(),
        P(None, tensor),
        P(None, tensor),
        P(None, tensor),
        P(tensor, None),
        P(),
        P(),
        P(None, tensor),
        P(None, tensor),
    )
    out_specs = (P(None, tensor),) * 4
    return jax.shard_map(
        on_device, mesh=fine, in_specs=in_specs, out_specs=out_specs, check_vma=False
    )
```

```python
import functools

import jax
import jax.numpy as jnp
from jax import lax
from jax.experimental import pallas as pl
from jax.experimental.pallas import tpu as pltpu
from jax.sharding import Mesh
from jax.sharding import PartitionSpec as P

HEAD_DIM = 128
CG_STEPS = 3
CHUNKS = 6
LAG = 4
DEPTH = 1024

EPS = 1e-05
ADAPTER_SCALE = 2.0
DAMP = 0.05
NEG = -1e30
F32 = jnp.float32
BF16 = jnp.bfloat16
HIGH = lax.Precision.HIGHEST
SCALE = HEAD_DIM ** (-0.5)
VMEM = pl.BlockSpec(memory_space=pltpu.VMEM)
SMEM = pl.BlockSpec(memory_space=pltpu.SMEM)
LIMIT = 16 * 1024 * 1024
STEP_COST = pl.CostEstimate(flops=10**9, bytes_accessed=10**7, transcendentals=0)
STREAM_LIMIT = 50 * 1024 * 1024


def dot32(first, second):
    return jnp.dot(first, second, preferred_element_type=F32)


def dot_nt(first, second):
    return lax.dot_general(
        first, second, (((1,), (1,)), ((), ())), preferred_element_type=F32
    )


def dot_tn(first, second):
    return lax.dot_general(
        first, second, (((0,), (0,)), ((), ())), preferred_element_type=F32
    )


def high(first, second):
    return jnp.dot(first, second, precision=HIGH, preferred_element_type=F32)


def head(index):
    return slice(index * HEAD_DIM, (index + 1) * HEAD_DIM)


def rows_below(limit, length, width):
    return lax.broadcasted_iota(jnp.int32, (length, width), 0) < limit


def live_pairs(limit, length):
    row = lax.broadcasted_iota(jnp.int32, (length, length), 0)
    column = lax.broadcasted_iota(jnp.int32, (length, length), 1)
    return (column <= row) & (column < limit)


def split_kernel(core_ref, w_ref, *refs):
    own_refs, other_refs = refs[:CHUNKS], refs[CHUNKS : 2 * CHUNKS]
    landed, own_sem, other_sem = refs[2 * CHUNKS :]
    cols = own_refs[0].shape[1]
    half = CHUNKS * cols
    core = core_ref[0]

    def own_copy(k):
        start = pl.multiple_of(core * half + k * cols, HEAD_DIM)
        return pltpu.make_async_copy(
            w_ref.at[:, pl.ds(start, cols)], own_refs[k], own_sem.at[k]
        )

    def other_copy(k):
        start = pl.multiple_of((1 - core) * half + k * cols, HEAD_DIM)
        return pltpu.make_async_copy(
            w_ref.at[:, pl.ds(start, cols)], landed.at[k], other_sem.at[k]
        )

    for k in range(CHUNKS):
        other_copy(k).start()
    for k in range(CHUNKS):
        own_copy(k).start()
    for k in range(CHUNKS):
        other_copy(k).wait()
        other_refs[k][...] = landed[k].astype(F32)
    for k in range(CHUNKS):
        own_copy(k).wait()


def split(core, w_out):
    inner, width = w_out.shape
    cols = width // 2 // CHUNKS
    out = pl.pallas_call(
        split_kernel,
        in_specs=[SMEM, pl.BlockSpec(memory_space=pltpu.HBM)],
        out_specs=[VMEM] * (2 * CHUNKS),
        out_shape=[jax.ShapeDtypeStruct((inner, cols), BF16)] * CHUNKS
        + [jax.ShapeDtypeStruct((inner, cols), F32)] * CHUNKS,
        scratch_shapes=[
            pltpu.VMEM((CHUNKS, inner, cols), BF16),
            pltpu.SemaphoreType.DMA((CHUNKS,)),
            pltpu.SemaphoreType.DMA((CHUNKS,)),
        ],
        compiler_params=pltpu.CompilerParams(vmem_limit_bytes=LIMIT),
    )(core, w_out)
    return out[:CHUNKS], out[CHUNKS:]


def project_kernel(
    limit_ref, x_ref, wq_ref, wk_ref, wv_ref, gain_ref, bias_ref, aq_ref, av_ref, bq_ref, bv_ref,
    soft_ref, key_ref, value_ref, down_q_ref, down_v_ref, mixed_ref,
    rows_in, normed, wq_in, wk_in, wv_in, rows_sem, weight_sem,
):
    length, width = normed.shape
    inner = key_ref.shape[1]
    blocks = [slice(i, i + DEPTH) for i in range(0, width, DEPTH)]
    rows_copy = pltpu.make_async_copy(x_ref, rows_in, rows_sem)
    rows_copy.start()
    copies = []
    for i, block in enumerate(blocks):
        for j, (source, target) in enumerate(
            [(wq_ref, wq_in), (wk_ref, wk_in), (wv_ref, wv_in)]
        ):
            copies.append(
                pltpu.make_async_copy(
                    source.at[block], target.at[block], weight_sem.at[3 * i + j]
                )
            )
            copies[-1].start()
    rows_copy.wait()
    total = jnp.zeros((length, 1), F32)
    for block in blocks:
        total = total + jnp.sum(rows_in[:, block].astype(F32), axis=-1, keepdims=True)
    mean = total / width
    total = jnp.zeros((length, 1), F32)
    for block in blocks:
        centred = rows_in[:, block].astype(F32) - mean
        total = total + jnp.sum(centred * centred, axis=-1, keepdims=True)
    spread = lax.rsqrt(total / width + EPS)
    for block in blocks:
        centred = rows_in[:, block].astype(F32) - mean
        full = centred * spread * gain_ref[:, block] + bias_ref[:, block]
        normed[:, block] = full.astype(BF16)
    query = jnp.zeros((length, inner), F32)
    key = jnp.zeros((length, inner), F32)
    value = jnp.zeros((length, inner), F32)
    for i, block in enumerate(blocks):
        part = normed[:, block]
        for j in range(3):
            copies[3 * i + j].wait()
        query = query + dot32(part, wq_in[block])
        key = key + dot32(part, wk_in[block])
        value = value + dot32(part, wv_in[block])
    down_q = dot_nt(normed[...], aq_ref[...])
    down_v = dot_nt(normed[...], av_ref[...])
    down_q_ref[...] = down_q
    down_v_ref[...] = down_v
    limit = limit_ref[0]
    live = live_pairs(limit, length)
    kept = rows_below(limit, length, HEAD_DIM)
    query = (query + ADAPTER_SCALE * high(down_q, bq_ref[...])).astype(BF16)
    value = (value + ADAPTER_SCALE * high(down_v, bv_ref[...])).astype(BF16)
    key = key.astype(BF16)
    key_ref[...] = key
    value_ref[...] = value
    for h in range(inner // HEAD_DIM):
        scores = dot_nt(query[:, head(h)], key[:, head(h)]) * SCALE
        scores = jnp.where(live, scores, NEG)
        weights = jnp.exp(scores - jnp.max(scores, axis=-1, keepdims=True))
        soft = weights / jnp.sum(weights, axis=-1, keepdims=True)
        soft_ref[h] = soft
        mixed = dot32(soft.astype(BF16), value[:, head(h)]).astype(BF16)
        mixed_ref[:length, head(h)] = jnp.where(kept, mixed.astype(F32), 0.0)
    mixed_ref[length:] = jnp.zeros((8, inner), F32)


def project(limit, x, gain, bias, wq, wk, wv, aq, av, bq, bv):
    length, width = x.shape
    inner = wq.shape[1]
    rank = aq.shape[1]
    heads = inner // HEAD_DIM
    hbm = pl.BlockSpec(memory_space=pltpu.HBM)
    return pl.pallas_call(
        project_kernel,
        in_specs=[SMEM] + [hbm] * 4 + [VMEM] * 6,
        out_specs=[VMEM] * 6,
        out_shape=[
            jax.ShapeDtypeStruct((heads, length, length), F32),
            jax.ShapeDtypeStruct((length, inner), BF16),
            jax.ShapeDtypeStruct((length, inner), BF16),
            jax.ShapeDtypeStruct((length, rank), F32),
            jax.ShapeDtypeStruct((length, rank), F32),
            jax.ShapeDtypeStruct((length + 8, inner), F32),
        ],
        scratch_shapes=[
            pltpu.VMEM((length, width), BF16),
            pltpu.VMEM((length, width), BF16),
            pltpu.VMEM((width, inner), BF16),
            pltpu.VMEM((width, inner), BF16),
            pltpu.VMEM((width, inner), BF16),
            pltpu.SemaphoreType.DMA,
            pltpu.SemaphoreType.DMA((3 * (width // DEPTH),)),
        ],
        compiler_params=pltpu.CompilerParams(vmem_limit_bytes=STREAM_LIMIT),
        cost_estimate=pl.CostEstimate(
            flops=6 * length * width * inner, bytes_accessed=6 * width * inner, transcendentals=0
        ),
    )(limit, x, wq, wk, wv, gain[None], bias[None], aq.T, av.T, bq, bv)


def token_spec():
    return pl.BlockSpec(memory_space=pl.ANY)


def call(kernel, ins, outs, token, scalars=()):
    tokens = [] if token is None else [token]

    def body(*refs):
        count = len(scalars) + len(ins)
        kernel(*refs[:count], *refs[count + len(tokens) :])

    return pl.pallas_call(
        body,
        in_specs=[SMEM] * len(scalars) + [VMEM] * len(ins) + [token_spec()] * len(tokens),
        out_specs=[VMEM] * len(outs),
        out_shape=[jax.ShapeDtypeStruct(shape, kind) for shape, kind in outs],
        compiler_params=pltpu.CompilerParams(vmem_limit_bytes=LIMIT),
        cost_estimate=STEP_COST,
    )(*scalars, *ins, *tokens)


def rows_of(own_ref, got_ref, length):
    return jnp.concatenate(
        [own_ref[:length].astype(BF16), got_ref[:length].astype(BF16)], axis=1
    )


def put_tail(out_ref, own_ref, got_ref, length):
    out_ref[length:] = jnp.zeros((8, out_ref.shape[1]), F32)
    out_ref[length:, :HEAD_DIM] = own_ref[length:, :HEAD_DIM] + got_ref[length:, :HEAD_DIM]


def first_spread(index, length, own, got, own_w, other_w, token):
    inner, cols = own_w.shape
    height = length + (8 if index == 0 else 0)

    def kernel(own_ref, got_ref, own_w_ref, other_w_ref, out_ref, pair_ref):
        pair_ref[:inner] = own_w_ref[...]
        pair_ref[inner:] = other_w_ref[...].astype(BF16)
        out_ref[:length] = dot32(rows_of(own_ref, got_ref, length), pair_ref[...])
        if index == 0:
            put_tail(out_ref, own_ref, got_ref, length)

    outs = [((height, cols), F32), ((2 * inner, cols), BF16)]
    return call(kernel, [own, got, own_w, other_w], outs, token)


def spread(index, length, own, got, pair, token):
    height = length + (8 if index == 0 else 0)

    def kernel(own_ref, got_ref, pair_ref, out_ref):
        out_ref[:length] = dot32(rows_of(own_ref, got_ref, length), pair_ref[...])
        if index == 0:
            put_tail(out_ref, own_ref, got_ref, length)

    return call(kernel, [own, got, pair], [((height, pair.shape[1]), F32)], token)[0]


def add(first, second, token):
    def kernel(first_ref, second_ref, out_ref):
        out_ref[...] = first_ref[...] + second_ref[: first_ref.shape[0]]

    return call(kernel, [first, second], [(first.shape, F32)], token)[0]


def copy(part, token):
    def kernel(part_ref, out_ref):
        out_ref[...] = part_ref[...]

    return call(kernel, [part], [(part.shape, F32)], token)[0]


def add_and_pick(first, second, ends, outer, token):
    rows = outer.shape[0]

    def kernel(ends_ref, first_ref, second_ref, outer_ref, sum_ref, sent_ref):
        total = first_ref[...] + second_ref[...]
        sum_ref[...] = total
        sent_ref[:rows] = jnp.where(ends_ref[0] > 0, outer_ref[...], total[:rows])
        if total.shape[0] > rows:
            sent_ref[rows:] = total[rows:]

    outs = [(first.shape, F32)] * 2
    return call(kernel, [first, second, outer], outs, token, [ends])


def gather(index, length, ends, got, held, pair, sums, limit, gap, token):
    inner = pair.shape[0] // 2
    extra = [] if gap is None else [gap]

    def kernel(ends_ref, limit_ref, got_ref, held_ref, pair_ref, *refs):
        refs = list(refs)
        gap_ref = refs.pop(0) if gap is not None else None
        before = [refs.pop(0), refs.pop(0)] if index else None
        own_ref, other_ref = refs[:2]
        total = jnp.where(ends_ref[0] > 0, got_ref[...], held_ref[...])
        total = total[: length + (8 if index == 0 else 0)]
        if index == 0:
            refs[2][...] = total[length:, :128]
            total = total[:length]
        if gap_ref is not None:
            kept = rows_below(limit_ref[0], length, total.shape[1])
            total = jnp.where(kept, total + gap_ref[...], 0.0)
        rounded = total.astype(BF16)
        own = dot_nt(rounded, pair_ref[:inner])
        other = dot_nt(rounded, pair_ref[inner:])
        squares = jnp.full((8, inner), jnp.sum(total * total), F32)
        if index:
            own = own + before[0][...]
            other = other + before[1][:length]
            squares = squares + before[1][length:]
        own_ref[...] = own
        other_ref[:length] = other
        other_ref[length:] = squares

    outs = [((length, inner), F32), ((length + 8, inner), F32)]
    if index == 0:
        outs.append(((8, 128), F32))
    return call(kernel, [got, held, pair] + extra + sums, outs, token, [ends, limit])


def cotangent_kernel(
    share, limit_ref, own_ref, other_ref, got_ref, soft_ref, key_ref, value_ref, down_q_ref,
    down_v_ref, out_ref,
):
    length, inner = own_ref.shape
    rank = down_q_ref.shape[1]
    live = live_pairs(limit_ref[0], length)
    pulled = (own_ref[...] + got_ref[:length]).astype(BF16)
    out_ref[2 * rank :] = other_ref[length:] + got_ref[length:]
    for h in range(inner // HEAD_DIM):
        soft = soft_ref[h]
        rows = pulled[:, head(h)]
        d_probs = dot_nt(rows, value_ref[:, head(h)]).astype(BF16).astype(F32)
        d_value = dot_tn(soft.astype(BF16), rows).astype(BF16).astype(F32)
        d_scores = soft * (d_probs - jnp.sum(soft * d_probs, axis=-1, keepdims=True))
        d_scores = jnp.where(live, d_scores, 0.0) * SCALE
        d_query = dot32(d_scores.astype(BF16), key_ref[:, head(h)]).astype(BF16).astype(F32)
        out_ref[:rank, head(h)] = share * lax.dot_general(
            down_q_ref[...], d_query, (((0,), (0,)), ((), ())), precision=HIGH,
            preferred_element_type=F32,
        )
        out_ref[rank : 2 * rank, head(h)] = share * lax.dot_general(
            down_v_ref[...], d_value, (((0,), (0,)), ((), ())), precision=HIGH,
            preferred_element_type=F32,
        )


def cotangent(share, limit, own, other, got, attention):
    inner = own.shape[1]
    rank = attention[3].shape[1]
    return pl.pallas_call(
        functools.partial(cotangent_kernel, share),
        in_specs=[SMEM] + [VMEM] * 8,
        out_specs=VMEM,
        out_shape=jax.ShapeDtypeStruct((2 * rank + 8, inner), F32),
        compiler_params=pltpu.CompilerParams(vmem_limit_bytes=LIMIT),
    )(limit, own, other, got, *attention)


def tangent_of(vector, limit, soft_ref, key_ref, value_ref, down_q_ref, down_v_ref, out_ref):
    length = key_ref.shape[0]
    rank = down_q_ref.shape[1]
    live = live_pairs(limit, length)
    kept = rows_below(limit, length, HEAD_DIM)
    d_query = (ADAPTER_SCALE * high(down_q_ref[...], vector[:rank])).astype(BF16)
    d_value = (ADAPTER_SCALE * high(down_v_ref[...], vector[rank:])).astype(BF16)
    for h in range(key_ref.shape[1] // HEAD_DIM):
        soft = soft_ref[h]
        d_scores = dot_nt(d_query[:, head(h)], key_ref[:, head(h)]) * SCALE
        d_scores = jnp.where(live, d_scores, 0.0)
        d_probs = soft * (d_scores - jnp.sum(soft * d_scores, axis=-1, keepdims=True))
        d_mixed = dot32(d_probs.astype(BF16), value_ref[:, head(h)]) + dot32(
            soft.astype(BF16), d_value[:, head(h)]
        )
        out_ref[:length, head(h)] = jnp.where(kept, d_mixed.astype(BF16).astype(F32), 0.0)


def total_of(terms):
    while len(terms) > 1:
        terms = [terms[i] + terms[i + 1] for i in range(0, len(terms), 2)]
    return terms[0]


def put_sums(out_ref, remain, image):
    lane = lax.broadcasted_iota(jnp.int32, (8, out_ref.shape[1]), 1)
    cross = 0.0 if image is None else jnp.sum(remain * image)
    out_ref[out_ref.shape[0] - 8 :] = jnp.where(lane == 0, jnp.sum(remain * remain), cross)


def first_kernel(n_dp, *refs):
    terms, refs = refs[:n_dp], refs[n_dp:]
    limit_ref, *attention, remain_ref, out_ref = refs
    grads = total_of([term[...] for term in terms])
    remain = -grads[: remain_ref.shape[0]]
    remain_ref[...] = remain
    put_sums(out_ref, remain, None)
    tangent_of(remain, limit_ref[0], *attention, out_ref)


def first_step(terms, limit, attention):
    inner = terms[0].shape[1]
    length = attention[1].shape[0]
    rank = attention[3].shape[1]
    return pl.pallas_call(
        functools.partial(first_kernel, len(terms)),
        in_specs=[VMEM] * len(terms) + [SMEM] + [VMEM] * 5,
        out_specs=[VMEM] * 2,
        out_shape=[
            jax.ShapeDtypeStruct((2 * rank, inner), F32),
            jax.ShapeDtypeStruct((length + 8, inner), F32),
        ],
        compiler_params=pltpu.CompilerParams(vmem_limit_bytes=LIMIT),
    )(*terms, limit, *attention)


def step_kernel(n_dp, token_count, index, last, *refs):
    terms, refs = refs[:n_dp], refs[n_dp:]
    sums_ref, remain_ref, *refs = refs
    if index:
        before_ref, newton_ref, direction_ref, image_ref, *refs = refs
    part = total_of([term[...] for term in terms])
    remain = remain_ref[...]
    rows = remain.shape[0]
    norm, cross = sums_ref[:1, 0:1], sums_ref[:1, 1:2]
    fresh = part[:rows] + DAMP * remain
    curv = part[rows : rows + 1, 0:1] / token_count + DAMP * norm
    if index:
        ratio = norm / before_ref[:1, 0:1]
        curv = curv + 2.0 * ratio * cross + ratio * ratio * before_ref[:1, 1:2]
        direction = remain + ratio * direction_ref[...]
        image = fresh + ratio * image_ref[...]
    else:
        direction, image = remain, fresh
    alpha = norm / curv
    newton = alpha * direction
    if index:
        newton = newton_ref[...] + newton
    remain = remain - alpha * image
    if last:
        step_q_ref, step_v_ref, remain_q_ref, remain_v_ref = refs
        rank = rows // 2
        step_q_ref[...] = newton[:rank]
        step_v_ref[...] = newton[rank:]
        remain_q_ref[...] = remain[:rank]
        remain_v_ref[...] = remain[rank:]
        return
    limit_ref, *refs = refs
    attention, refs = refs[:5], refs[5:]
    next_remain, next_before, next_newton, next_direction, next_image, out_ref = refs
    lane = lax.broadcasted_iota(jnp.int32, next_before.shape, 1)
    next_remain[...] = remain
    next_before[...] = jnp.where(lane == 0, norm, curv)
    next_newton[...] = newton
    next_direction[...] = direction
    next_image[...] = image
    put_sums(out_ref, remain, image)
    tangent_of(remain, limit_ref[0], *attention, out_ref)


def cg_step(index, token_count, terms, sums, remain, state, limit, attention):
    last = index == CG_STEPS - 1
    rows, inner = remain.shape
    matrix = jax.ShapeDtypeStruct((rows, inner), F32)
    scalars = jax.ShapeDtypeStruct((8, 128), F32)
    args = [*terms, sums, remain, *state]
    specs = [VMEM] * len(args)
    if last:
        shapes = [jax.ShapeDtypeStruct((rows // 2, inner), F32)] * 4
    else:
        args += [limit, *attention]
        specs += [SMEM] + [VMEM] * 5
        length = attention[1].shape[0]
        shapes = [matrix, scalars, matrix, matrix, matrix]
        shapes.append(jax.ShapeDtypeStruct((length + 8, inner), F32))
    return pl.pallas_call(
        functools.partial(step_kernel, len(terms), token_count, index, last),
        in_specs=specs,
        out_specs=[VMEM] * len(shapes),
        out_shape=shapes,
        compiler_params=pltpu.CompilerParams(vmem_limit_bytes=LIMIT),
    )(*args)


def on_device(
    inputs,
    targets,
    lengths,
    ln_gain,
    ln_bias,
    query_weight,
    w_key,
    value_weight,
    w_out,
    down_query,
    down_value,
    query_up_factor,
    value_up_factor,
):
    length, width = inputs.shape
    n_dp = lax.axis_size("dp")
    n_chip = lax.axis_size("chip")
    core = lax.axis_index("core")
    chip = lax.axis_index("chip")
    token_count = length * n_dp
    half = width // 2

    def swap(part):
        return lax.ppermute(part, "core", [(0, 1), (1, 0)])

    def data_terms(part):
        step = 1
        while 2 * step < n_dp:
            part = part + lax.ppermute(part, "dp", [(d, d ^ step) for d in range(n_dp)])
            step *= 2
        return [part, lax.ppermute(part, "dp", [(d, d ^ step) for d in range(n_dp)])]

    where = core.astype(jnp.int32)[None]
    own_w, other_w = split(where, w_out)
    other_w = [swap(part) for part in other_w]
    cols = half // CHUNKS
    gap = lax.dynamic_slice_in_dim(inputs, core * half, half, 1).astype(F32)
    gap = gap - lax.dynamic_slice_in_dim(targets, core * half, half, 1).astype(F32)

    soft, key, value, down_q, down_v, mixed = project(
        lengths, inputs, ln_gain, ln_bias, query_weight, w_key, value_weight, down_query,
        down_value, query_up_factor, value_up_factor,
    )
    attention = (soft, key, value, down_q, down_v)

    ends = ((chip == 0) | (chip == n_chip - 1)).astype(jnp.int32)[None]

    def outer_swap(part):
        return lax.ppermute(part, "chip", [(0, 1), (1, 0), (2, 3), (3, 2)])

    def inner_swap(part):
        return lax.ppermute(part, "chip", [(0, 0), (1, 2), (2, 1), (3, 3)])

    def product(rows, pairs):
        got_rows = swap(rows)
        first = not pairs
        pairs.extend([None] * (CHUNKS - len(pairs)))
        parts, scalars = [], None
        own_part, total, outer, inner = {}, {}, {}, {}
        token = None

        def begin(k):
            if first:
                own_part[k], pairs[k] = first_spread(
                    k, length, rows, got_rows, own_w[k], other_w[k], token
                )
            else:
                own_part[k] = spread(k, length, rows, got_rows, pairs[k], token)
            return own_part[k]

        def take_in(k, got):
            nonlocal parts, scalars
            gap_part = gap[:, k * cols : (k + 1) * cols] if first else None
            out = gather(k, length, ends, got, total[k], pairs[k], parts, lengths, gap_part, token)
            parts = list(out[:2])
            scalars = out[2] if k == 0 else scalars
            return parts[0]

        if n_chip != 4:
            for k in range(CHUNKS):
                token = begin(k)
            for k in range(CHUNKS):
                total[k] = lax.psum(own_part[k], "chip")
                token = take_in(k, total[k])
        else:
            for k in (0, 2, 1):
                token = begin(k)
            for k in (0, 1):
                outer[k] = outer_swap(own_part[k])
            for tick in range(CHUNKS + LAG):
                if LAG <= tick != CHUNKS + 1:
                    token = take_in(tick - LAG, outer[tick])
                else:
                    token = outer.get(tick, token)
                if tick < CHUNKS:
                    later, back = tick + 2, tick - 2
                    if back < 0:
                        sent = copy(own_part[later], token)
                    elif later < CHUNKS:
                        total[back], sent = add_and_pick(
                            own_part[back], inner[back], ends, own_part[later], token
                        )
                    else:
                        sent = total[back] = add(own_part[back], inner[back], token)
                    outer[later] = outer_swap(sent)
                    own_part[tick] = add(own_part[tick], outer[tick], sent)
                    token = own_part[tick]
                    inner[tick] = inner_swap(token)
                    if tick + 3 < CHUNKS:
                        token = begin(tick + 3)
                if tick == CHUNKS:
                    token = take_in(tick + 1 - LAG, outer[tick + 1])
                if tick in (CHUNKS - 1, CHUNKS):
                    k = tick - 1
                    token = total[k] = add(own_part[k], inner[k], token)
                    outer[k + LAG] = outer_swap(token)
        own, other = parts
        share = ADAPTER_SCALE / token_count
        part = cotangent(share, lengths, own, other, swap(other), attention)
        return data_terms(part), scalars

    pairs = []
    terms, _ = product(mixed, pairs)
    remain, rows = first_step(terms, lengths, attention)
    state = ()
    for index in range(CG_STEPS):
        terms, sums = product(rows, pairs)
        out = cg_step(index, token_count, terms, sums, remain, state, lengths, attention)
        if index < CG_STEPS - 1:
            remain, *state, rows = out
    return tuple(out)


def solution(mesh):
    fine = Mesh(mesh.devices.reshape(mesh.shape["dp"], -1, 2), ("dp", "chip", "core"))
    tensor = ("chip", "core")
    in_specs = (
        P("dp", None),
        P("dp", None),
        P("dp"),
        P(),
        P(),
        P(None, tensor),
        P(None, tensor),
        P(None, tensor),
        P(tensor, None),
        P(),
        P(),
        P(None, tensor),
        P(None, tensor),
    )
    out_specs = (P(None, tensor),) * 4
    return jax.shard_map(
        on_device, mesh=fine, in_specs=in_specs, out_specs=out_specs, check_vma=False
    )
```

```python
import functools

import jax
import jax.numpy as jnp
from jax import lax
from jax.experimental import pallas as pl
from jax.experimental.pallas import tpu as pltpu
from jax.sharding import Mesh
from jax.sharding import PartitionSpec as P

HEAD_DIM = 128
CG_STEPS = 3
WIDTHS = (2, 5, 4, 4, 5, 4)
CHUNKS = len(WIDTHS)
DEPTH = 1024

EPS = 1e-05
ADAPTER_SCALE = 2.0
DAMP = 0.05
NEG = -1e30
F32 = jnp.float32
BF16 = jnp.bfloat16
HIGH = lax.Precision.HIGHEST
SCALE = HEAD_DIM ** (-0.5)
VMEM = pl.BlockSpec(memory_space=pltpu.VMEM)
SMEM = pl.BlockSpec(memory_space=pltpu.SMEM)
LIMIT = 16 * 1024 * 1024
STEP_COST = pl.CostEstimate(flops=10**9, bytes_accessed=10**7, transcendentals=0)
STREAM_LIMIT = 50 * 1024 * 1024


def dot32(first, second):
    return jnp.dot(first, second, preferred_element_type=F32)


def dot_nt(first, second):
    return lax.dot_general(
        first, second, (((1,), (1,)), ((), ())), preferred_element_type=F32
    )


def dot_tn(first, second):
    return lax.dot_general(
        first, second, (((0,), (0,)), ((), ())), preferred_element_type=F32
    )


def high(first, second):
    return jnp.dot(first, second, precision=HIGH, preferred_element_type=F32)


def chunks_of(half):
    unit = half // sum(WIDTHS)
    ends = [unit * sum(WIDTHS[:k]) for k in range(CHUNKS + 1)]
    return [slice(first, last) for first, last in zip(ends[:-1], ends[1:])]


def head(index):
    return slice(index * HEAD_DIM, (index + 1) * HEAD_DIM)


def rows_below(limit, length, width):
    return lax.broadcasted_iota(jnp.int32, (length, width), 0) < limit


def live_pairs(limit, length):
    row = lax.broadcasted_iota(jnp.int32, (length, length), 0)
    column = lax.broadcasted_iota(jnp.int32, (length, length), 1)
    return (column <= row) & (column < limit)


def split_kernel(core_ref, w_ref, *refs):
    own_refs, other_refs = refs[:CHUNKS], refs[CHUNKS : 2 * CHUNKS]
    landed, own_sem, other_sem = refs[2 * CHUNKS :]
    half = w_ref.shape[1] // 2
    places = chunks_of(half)
    core = core_ref[0]

    def own_copy(k):
        start = pl.multiple_of(core * half + places[k].start, HEAD_DIM)
        return pltpu.make_async_copy(
            w_ref.at[:, pl.ds(start, own_refs[k].shape[1])], own_refs[k], own_sem.at[k]
        )

    def other_copy(k):
        start = pl.multiple_of((1 - core) * half + places[k].start, HEAD_DIM)
        return pltpu.make_async_copy(
            w_ref.at[:, pl.ds(start, other_refs[k].shape[1])],
            landed.at[:, places[k]],
            other_sem.at[k],
        )

    for k in range(CHUNKS):
        other_copy(k).start()
    for k in range(CHUNKS):
        own_copy(k).start()
    for k in range(CHUNKS):
        other_copy(k).wait()
        other_refs[k][...] = landed[:, places[k]].astype(F32)
    for k in range(CHUNKS):
        own_copy(k).wait()


def split(core, w_out):
    inner, width = w_out.shape
    half = width // 2
    cols = [place.stop - place.start for place in chunks_of(half)]
    out = pl.pallas_call(
        split_kernel,
        in_specs=[SMEM, pl.BlockSpec(memory_space=pltpu.HBM)],
        out_specs=[VMEM] * (2 * CHUNKS),
        out_shape=[jax.ShapeDtypeStruct((inner, wide), BF16) for wide in cols]
        + [jax.ShapeDtypeStruct((inner, wide), F32) for wide in cols],
        scratch_shapes=[
            pltpu.VMEM((inner, half), BF16),
            pltpu.SemaphoreType.DMA((CHUNKS,)),
            pltpu.SemaphoreType.DMA((CHUNKS,)),
        ],
        compiler_params=pltpu.CompilerParams(vmem_limit_bytes=LIMIT),
    )(core, w_out)
    return out[:CHUNKS], out[CHUNKS:]


def project_kernel(
    limit_ref, x_ref, wq_ref, wk_ref, wv_ref, gain_ref, bias_ref, aq_ref, av_ref, bq_ref, bv_ref,
    soft_ref, key_ref, value_ref, down_q_ref, down_v_ref, mixed_ref,
    rows_in, normed, wq_in, wk_in, wv_in, rows_sem, weight_sem,
):
    length, width = normed.shape
    inner = key_ref.shape[1]
    blocks = [slice(i, i + DEPTH) for i in range(0, width, DEPTH)]
    rows_copy = pltpu.make_async_copy(x_ref, rows_in, rows_sem)
    rows_copy.start()
    copies = []
    for i, block in enumerate(blocks):
        for j, (source, target) in enumerate(
            [(wq_ref, wq_in), (wk_ref, wk_in), (wv_ref, wv_in)]
        ):
            copies.append(
                pltpu.make_async_copy(
                    source.at[block], target.at[block], weight_sem.at[3 * i + j]
                )
            )
            copies[-1].start()
    rows_copy.wait()
    total = jnp.zeros((length, 1), F32)
    for block in blocks:
        total = total + jnp.sum(rows_in[:, block].astype(F32), axis=-1, keepdims=True)
    mean = total / width
    total = jnp.zeros((length, 1), F32)
    for block in blocks:
        centred = rows_in[:, block].astype(F32) - mean
        total = total + jnp.sum(centred * centred, axis=-1, keepdims=True)
    spread = lax.rsqrt(total / width + EPS)
    for block in blocks:
        centred = rows_in[:, block].astype(F32) - mean
        full = centred * spread * gain_ref[:, block] + bias_ref[:, block]
        normed[:, block] = full.astype(BF16)
    query = jnp.zeros((length, inner), F32)
    key = jnp.zeros((length, inner), F32)
    value = jnp.zeros((length, inner), F32)
    for i, block in enumerate(blocks):
        part = normed[:, block]
        for j in range(3):
            copies[3 * i + j].wait()
        query = query + dot32(part, wq_in[block])
        key = key + dot32(part, wk_in[block])
        value = value + dot32(part, wv_in[block])
    down_q = dot_nt(normed[...], aq_ref[...])
    down_v = dot_nt(normed[...], av_ref[...])
    down_q_ref[...] = down_q
    down_v_ref[...] = down_v
    limit = limit_ref[0]
    live = live_pairs(limit, length)
    kept = rows_below(limit, length, HEAD_DIM)
    query = (query + ADAPTER_SCALE * high(down_q, bq_ref[...])).astype(BF16)
    value = (value + ADAPTER_SCALE * high(down_v, bv_ref[...])).astype(BF16)
    key = key.astype(BF16)
    key_ref[...] = key
    value_ref[...] = value
    for h in range(inner // HEAD_DIM):
        scores = dot_nt(query[:, head(h)], key[:, head(h)]) * SCALE
        scores = jnp.where(live, scores, NEG)
        weights = jnp.exp(scores - jnp.max(scores, axis=-1, keepdims=True))
        soft = weights / jnp.sum(weights, axis=-1, keepdims=True)
        soft_ref[h] = soft
        mixed = dot32(soft.astype(BF16), value[:, head(h)]).astype(BF16)
        mixed_ref[:length, head(h)] = jnp.where(kept, mixed.astype(F32), 0.0)
    mixed_ref[length:] = jnp.zeros((8, inner), F32)


def project(limit, x, gain, bias, wq, wk, wv, aq, av, bq, bv):
    length, width = x.shape
    inner = wq.shape[1]
    rank = aq.shape[1]
    heads = inner // HEAD_DIM
    hbm = pl.BlockSpec(memory_space=pltpu.HBM)
    return pl.pallas_call(
        project_kernel,
        in_specs=[SMEM] + [hbm] * 4 + [VMEM] * 6,
        out_specs=[VMEM] * 6,
        out_shape=[
            jax.ShapeDtypeStruct((heads, length, length), F32),
            jax.ShapeDtypeStruct((length, inner), BF16),
            jax.ShapeDtypeStruct((length, inner), BF16),
            jax.ShapeDtypeStruct((length, rank), F32),
            jax.ShapeDtypeStruct((length, rank), F32),
            jax.ShapeDtypeStruct((length + 8, inner), F32),
        ],
        scratch_shapes=[
            pltpu.VMEM((length, width), BF16),
            pltpu.VMEM((length, width), BF16),
            pltpu.VMEM((width, inner), BF16),
            pltpu.VMEM((width, inner), BF16),
            pltpu.VMEM((width, inner), BF16),
            pltpu.SemaphoreType.DMA,
            pltpu.SemaphoreType.DMA((3 * (width // DEPTH),)),
        ],
        compiler_params=pltpu.CompilerParams(vmem_limit_bytes=STREAM_LIMIT),
        cost_estimate=pl.CostEstimate(
            flops=6 * length * width * inner, bytes_accessed=6 * width * inner, transcendentals=0
        ),
    )(limit, x, wq, wk, wv, gain[None], bias[None], aq.T, av.T, bq, bv)


def token_spec():
    return pl.BlockSpec(memory_space=pl.ANY)


def call(kernel, ins, outs, token, scalars=()):
    tokens = [] if token is None else [token]

    def body(*refs):
        count = len(scalars) + len(ins)
        kernel(*refs[:count], *refs[count + len(tokens) :])

    return pl.pallas_call(
        body,
        in_specs=[SMEM] * len(scalars) + [VMEM] * len(ins) + [token_spec()] * len(tokens),
        out_specs=[VMEM] * len(outs),
        out_shape=[jax.ShapeDtypeStruct(shape, kind) for shape, kind in outs],
        compiler_params=pltpu.CompilerParams(vmem_limit_bytes=LIMIT),
        cost_estimate=STEP_COST,
    )(*scalars, *ins, *tokens)


def rows_of(own_ref, got_ref, length):
    return jnp.concatenate(
        [own_ref[:length].astype(BF16), got_ref[:length].astype(BF16)], axis=1
    )


def put_tail(out_ref, own_ref, got_ref, length):
    out_ref[length:] = jnp.zeros((8, out_ref.shape[1]), F32)
    out_ref[length:, :HEAD_DIM] = own_ref[length:, :HEAD_DIM] + got_ref[length:, :HEAD_DIM]


def first_spread(index, length, own, got, own_w, other_w, token):
    inner, cols = own_w.shape
    height = length + (8 if index == 0 else 0)

    def kernel(own_ref, got_ref, own_w_ref, other_w_ref, out_ref, pair_ref):
        pair_ref[:inner] = own_w_ref[...]
        pair_ref[inner:] = other_w_ref[...].astype(BF16)
        out_ref[:length] = dot32(rows_of(own_ref, got_ref, length), pair_ref[...])
        if index == 0:
            put_tail(out_ref, own_ref, got_ref, length)

    outs = [((height, cols), F32), ((2 * inner, cols), BF16)]
    return call(kernel, [own, got, own_w, other_w], outs, token)


def spread(index, length, own, got, pair, token):
    height = length + (8 if index == 0 else 0)

    def kernel(own_ref, got_ref, pair_ref, out_ref):
        out_ref[:length] = dot32(rows_of(own_ref, got_ref, length), pair_ref[...])
        if index == 0:
            put_tail(out_ref, own_ref, got_ref, length)

    return call(kernel, [own, got, pair], [((height, pair.shape[1]), F32)], token)[0]


def add(first, second, token):
    rows, cols = first.shape

    def kernel(first_ref, second_ref, out_ref):
        out_ref[...] = first_ref[...] + second_ref[:rows, :cols]

    return call(kernel, [first, second], [(first.shape, F32)], token)[0]


def copy(part, token):
    def kernel(part_ref, out_ref):
        out_ref[...] = part_ref[...]

    return call(kernel, [part], [(part.shape, F32)], token)[0]


def add_and_pick(first, second, ends, outer, token):
    rows, cols = first.shape
    high, wide = outer.shape

    def kernel(ends_ref, first_ref, second_ref, outer_ref, sum_ref, sent_ref):
        total = first_ref[...] + second_ref[...]
        sum_ref[...] = total
        sent_ref[:high, :cols] = jnp.where(ends_ref[0] > 0, outer_ref[:, :cols], total[:high])
        if wide > cols:
            sent_ref[:high, cols:] = outer_ref[:, cols:]
        if rows > high:
            sent_ref[high:] = jnp.zeros((rows - high, wide), F32)
            sent_ref[high:, :cols] = total[high:]

    outs = [(first.shape, F32), ((rows, wide), F32)]
    return call(kernel, [first, second, outer], outs, token, [ends])


def gather(index, length, ends, got, held, pair, sums, limit, gap, token):
    inner = pair.shape[0] // 2
    extra = [] if gap is None else [gap]

    def kernel(ends_ref, limit_ref, got_ref, held_ref, pair_ref, *refs):
        refs = list(refs)
        gap_ref = refs.pop(0) if gap is not None else None
        before = [refs.pop(0), refs.pop(0)] if index else None
        own_ref, other_ref = refs[:2]
        total = jnp.where(ends_ref[0] > 0, got_ref[:, : held.shape[1]], held_ref[...])
        total = total[: length + (8 if index == 0 else 0)]
        if index == 0:
            refs[2][...] = total[length:, :128]
            total = total[:length]
        if gap_ref is not None:
            kept = rows_below(limit_ref[0], length, total.shape[1])
            total = jnp.where(kept, total + gap_ref[...], 0.0)
        rounded = total.astype(BF16)
        own = dot_nt(rounded, pair_ref[:inner])
        other = dot_nt(rounded, pair_ref[inner:])
        squares = jnp.full((8, inner), jnp.sum(total * total), F32)
        if index:
            own = own + before[0][...]
            other = other + before[1][:length]
            squares = squares + before[1][length:]
        own_ref[...] = own
        other_ref[:length] = other
        other_ref[length:] = squares

    outs = [((length, inner), F32), ((length + 8, inner), F32)]
    if index == 0:
        outs.append(((8, 128), F32))
    return call(kernel, [got, held, pair] + extra + sums, outs, token, [ends, limit])


def cotangent_kernel(
    share, limit_ref, own_ref, other_ref, got_ref, soft_ref, key_ref, value_ref, down_q_ref,
    down_v_ref, out_ref,
):
    length, inner = own_ref.shape
    rank = down_q_ref.shape[1]
    live = live_pairs(limit_ref[0], length)
    pulled = (own_ref[...] + got_ref[:length]).astype(BF16)
    out_ref[2 * rank :] = other_ref[length:] + got_ref[length:]
    for h in range(inner // HEAD_DIM):
        soft = soft_ref[h]
        rows = pulled[:, head(h)]
        d_probs = dot_nt(rows, value_ref[:, head(h)]).astype(BF16).astype(F32)
        d_value = dot_tn(soft.astype(BF16), rows).astype(BF16).astype(F32)
        d_scores = soft * (d_probs - jnp.sum(soft * d_probs, axis=-1, keepdims=True))
        d_scores = jnp.where(live, d_scores, 0.0) * SCALE
        d_query = dot32(d_scores.astype(BF16), key_ref[:, head(h)]).astype(BF16).astype(F32)
        out_ref[:rank, head(h)] = share * lax.dot_general(
            down_q_ref[...], d_query, (((0,), (0,)), ((), ())), precision=HIGH,
            preferred_element_type=F32,
        )
        out_ref[rank : 2 * rank, head(h)] = share * lax.dot_general(
            down_v_ref[...], d_value, (((0,), (0,)), ((), ())), precision=HIGH,
            preferred_element_type=F32,
        )


def cotangent(share, limit, own, other, got, attention):
    inner = own.shape[1]
    rank = attention[3].shape[1]
    return pl.pallas_call(
        functools.partial(cotangent_kernel, share),
        in_specs=[SMEM] + [VMEM] * 8,
        out_specs=VMEM,
        out_shape=jax.ShapeDtypeStruct((2 * rank + 8, inner), F32),
        compiler_params=pltpu.CompilerParams(vmem_limit_bytes=LIMIT),
    )(limit, own, other, got, *attention)


def tangent_of(vector, limit, soft_ref, key_ref, value_ref, down_q_ref, down_v_ref, out_ref):
    length = key_ref.shape[0]
    rank = down_q_ref.shape[1]
    live = live_pairs(limit, length)
    kept = rows_below(limit, length, HEAD_DIM)
    d_query = (ADAPTER_SCALE * high(down_q_ref[...], vector[:rank])).astype(BF16)
    d_value = (ADAPTER_SCALE * high(down_v_ref[...], vector[rank:])).astype(BF16)
    for h in range(key_ref.shape[1] // HEAD_DIM):
        soft = soft_ref[h]
        d_scores = dot_nt(d_query[:, head(h)], key_ref[:, head(h)]) * SCALE
        d_scores = jnp.where(live, d_scores, 0.0)
        d_probs = soft * (d_scores - jnp.sum(soft * d_scores, axis=-1, keepdims=True))
        d_mixed = dot32(d_probs.astype(BF16), value_ref[:, head(h)]) + dot32(
            soft.astype(BF16), d_value[:, head(h)]
        )
        out_ref[:length, head(h)] = jnp.where(kept, d_mixed.astype(BF16).astype(F32), 0.0)


def total_of(terms):
    while len(terms) > 1:
        terms = [terms[i] + terms[i + 1] for i in range(0, len(terms), 2)]
    return terms[0]


def put_sums(out_ref, remain, image):
    lane = lax.broadcasted_iota(jnp.int32, (8, out_ref.shape[1]), 1)
    cross = 0.0 if image is None else jnp.sum(remain * image)
    out_ref[out_ref.shape[0] - 8 :] = jnp.where(lane == 0, jnp.sum(remain * remain), cross)


def first_kernel(n_dp, *refs):
    terms, refs = refs[:n_dp], refs[n_dp:]
    limit_ref, *attention, remain_ref, out_ref = refs
    grads = total_of([term[...] for term in terms])
    remain = -grads[: remain_ref.shape[0]]
    remain_ref[...] = remain
    put_sums(out_ref, remain, None)
    tangent_of(remain, limit_ref[0], *attention, out_ref)


def first_step(terms, limit, attention):
    inner = terms[0].shape[1]
    length = attention[1].shape[0]
    rank = attention[3].shape[1]
    return pl.pallas_call(
        functools.partial(first_kernel, len(terms)),
        in_specs=[VMEM] * len(terms) + [SMEM] + [VMEM] * 5,
        out_specs=[VMEM] * 2,
        out_shape=[
            jax.ShapeDtypeStruct((2 * rank, inner), F32),
            jax.ShapeDtypeStruct((length + 8, inner), F32),
        ],
        compiler_params=pltpu.CompilerParams(vmem_limit_bytes=LIMIT),
    )(*terms, limit, *attention)


def step_kernel(n_dp, token_count, index, last, *refs):
    terms, refs = refs[:n_dp], refs[n_dp:]
    sums_ref, remain_ref, *refs = refs
    if index:
        before_ref, newton_ref, direction_ref, image_ref, *refs = refs
    part = total_of([term[...] for term in terms])
    remain = remain_ref[...]
    rows = remain.shape[0]
    norm, cross = sums_ref[:1, 0:1], sums_ref[:1, 1:2]
    fresh = part[:rows] + DAMP * remain
    curv = part[rows : rows + 1, 0:1] / token_count + DAMP * norm
    if index:
        ratio = norm / before_ref[:1, 0:1]
        curv = curv + 2.0 * ratio * cross + ratio * ratio * before_ref[:1, 1:2]
        direction = remain + ratio * direction_ref[...]
        image = fresh + ratio * image_ref[...]
    else:
        direction, image = remain, fresh
    alpha = norm / curv
    newton = alpha * direction
    if index:
        newton = newton_ref[...] + newton
    remain = remain - alpha * image
    if last:
        step_q_ref, step_v_ref, remain_q_ref, remain_v_ref = refs
        rank = rows // 2
        step_q_ref[...] = newton[:rank]
        step_v_ref[...] = newton[rank:]
        remain_q_ref[...] = remain[:rank]
        remain_v_ref[...] = remain[rank:]
        return
    limit_ref, *refs = refs
    attention, refs = refs[:5], refs[5:]
    next_remain, next_before, next_newton, next_direction, next_image, out_ref = refs
    lane = lax.broadcasted_iota(jnp.int32, next_before.shape, 1)
    next_remain[...] = remain
    next_before[...] = jnp.where(lane == 0, norm, curv)
    next_newton[...] = newton
    next_direction[...] = direction
    next_image[...] = image
    put_sums(out_ref, remain, image)
    tangent_of(remain, limit_ref[0], *attention, out_ref)


def cg_step(index, token_count, terms, sums, remain, state, limit, attention):
    last = index == CG_STEPS - 1
    rows, inner = remain.shape
    matrix = jax.ShapeDtypeStruct((rows, inner), F32)
    scalars = jax.ShapeDtypeStruct((8, 128), F32)
    args = [*terms, sums, remain, *state]
    specs = [VMEM] * len(args)
    if last:
        shapes = [jax.ShapeDtypeStruct((rows // 2, inner), F32)] * 4
    else:
        args += [limit, *attention]
        specs += [SMEM] + [VMEM] * 5
        length = attention[1].shape[0]
        shapes = [matrix, scalars, matrix, matrix, matrix]
        shapes.append(jax.ShapeDtypeStruct((length + 8, inner), F32))
    return pl.pallas_call(
        functools.partial(step_kernel, len(terms), token_count, index, last),
        in_specs=specs,
        out_specs=[VMEM] * len(shapes),
        out_shape=shapes,
        compiler_params=pltpu.CompilerParams(vmem_limit_bytes=LIMIT),
    )(*args)


def on_device(
    inputs,
    targets,
    lengths,
    ln_gain,
    ln_bias,
    query_weight,
    w_key,
    value_weight,
    w_out,
    down_query,
    down_value,
    query_up_factor,
    value_up_factor,
):
    length, width = inputs.shape
    n_dp = lax.axis_size("dp")
    n_chip = lax.axis_size("chip")
    core = lax.axis_index("core")
    chip = lax.axis_index("chip")
    token_count = length * n_dp
    half = width // 2

    def swap(part):
        return lax.ppermute(part, "core", [(0, 1), (1, 0)])

    def data_terms(part):
        step = 1
        while 2 * step < n_dp:
            part = part + lax.ppermute(part, "dp", [(d, d ^ step) for d in range(n_dp)])
            step *= 2
        return [part, lax.ppermute(part, "dp", [(d, d ^ step) for d in range(n_dp)])]

    where = core.astype(jnp.int32)[None]
    own_w, other_w = split(where, w_out)
    other_w = [swap(part) for part in other_w]
    places = chunks_of(half)
    gap = lax.dynamic_slice_in_dim(inputs, core * half, half, 1).astype(F32)
    gap = gap - lax.dynamic_slice_in_dim(targets, core * half, half, 1).astype(F32)

    soft, key, value, down_q, down_v, mixed = project(
        lengths, inputs, ln_gain, ln_bias, query_weight, w_key, value_weight, down_query,
        down_value, query_up_factor, value_up_factor,
    )
    attention = (soft, key, value, down_q, down_v)

    ends = ((chip == 0) | (chip == n_chip - 1)).astype(jnp.int32)[None]

    def outer_swap(part):
        return lax.ppermute(part, "chip", [(0, 1), (1, 0), (2, 3), (3, 2)])

    def inner_swap(part):
        return lax.ppermute(part, "chip", [(0, 0), (1, 2), (2, 1), (3, 3)])

    def product(rows, pairs):
        got_rows = swap(rows)
        first = not pairs
        pairs.extend([None] * (CHUNKS - len(pairs)))
        parts, scalars = [], None
        own_part, total, outer, inner = {}, {}, {}, {}
        token = None

        def begin(k):
            if first:
                own_part[k], pairs[k] = first_spread(
                    k, length, rows, got_rows, own_w[k], other_w[k], token
                )
            else:
                own_part[k] = spread(k, length, rows, got_rows, pairs[k], token)
            return own_part[k]

        def take_in(k, got):
            nonlocal parts, scalars
            gap_part = gap[:, places[k]] if first else None
            out = gather(k, length, ends, got, total[k], pairs[k], parts, lengths, gap_part, token)
            parts = list(out[:2])
            scalars = out[2] if k == 0 else scalars
            return parts[0]

        if n_chip != 4:
            for k in range(CHUNKS):
                token = begin(k)
            for k in range(CHUNKS):
                total[k] = lax.psum(own_part[k], "chip")
                token = take_in(k, total[k])
        else:
            for k in (0, 1, 2) if first else (0,):
                token = begin(k)
            outer[0] = outer_swap(own_part[0])
            for tick in range(CHUNKS + 3):
                later = tick + 2
                if tick == 0:
                    token = outer[0]
                    token = copy(own_part[1], token) if first else begin(1)
                    outer[1] = outer_swap(token)
                if tick < CHUNKS:
                    own_part[tick] = add(own_part[tick], outer[tick], token)
                    token = own_part[tick]
                    inner[tick] = inner_swap(token)
                if tick == CHUNKS:
                    token = take_in(tick - 3, outer[tick])
                if tick == 0:
                    token = copy(own_part[2], token) if first else begin(2)
                    outer[2] = outer_swap(token)
                elif tick <= CHUNKS:
                    k = tick - 1
                    if later < CHUNKS:
                        total[k], token = add_and_pick(
                            own_part[k], inner[k], ends, own_part[later], token
                        )
                    else:
                        token = total[k] = add(own_part[k], inner[k], token)
                    outer[later] = outer_swap(token)
                if tick + 3 < CHUNKS:
                    token = begin(tick + 3)
                if tick >= 3 and tick != CHUNKS:
                    token = take_in(tick - 3, outer[tick])
        own, other = parts
        share = ADAPTER_SCALE / token_count
        part = cotangent(share, lengths, own, other, swap(other), attention)
        return data_terms(part), scalars

    pairs = []
    terms, _ = product(mixed, pairs)
    remain, rows = first_step(terms, lengths, attention)
    state = ()
    for index in range(CG_STEPS):
        terms, sums = product(rows, pairs)
        out = cg_step(index, token_count, terms, sums, remain, state, lengths, attention)
        if index < CG_STEPS - 1:
            remain, *state, rows = out
    return tuple(out)


def solution(mesh):
    fine = Mesh(mesh.devices.reshape(mesh.shape["dp"], -1, 2), ("dp", "chip", "core"))
    tensor = ("chip", "core")
    in_specs = (
        P("dp", None),
        P("dp", None),
        P("dp"),
        P(),
        P(),
        P(None, tensor),
        P(None, tensor),
        P(None, tensor),
        P(tensor, None),
        P(),
        P(),
        P(None, tensor),
        P(None, tensor),
    )
    out_specs = (P(None, tensor),) * 4
    return jax.shard_map(
        on_device, mesh=fine, in_specs=in_specs, out_specs=out_specs, check_vma=False
    )
```

```python
import functools

import jax
import jax.numpy as jnp
from jax import lax
from jax.experimental import pallas as pl
from jax.experimental.pallas import tpu as pltpu
from jax.sharding import Mesh
from jax.sharding import PartitionSpec as P

HEAD_DIM = 128
CG_STEPS = 3
CHUNKS = 6
DEPTH = 1024

EPS = 1e-05
ADAPTER_SCALE = 2.0
DAMP = 0.05
NEG = -1e30
F32 = jnp.float32
BF16 = jnp.bfloat16
HIGH = lax.Precision.HIGHEST
SCALE = HEAD_DIM ** (-0.5)
VMEM = pl.BlockSpec(memory_space=pltpu.VMEM)
SMEM = pl.BlockSpec(memory_space=pltpu.SMEM)
LIMIT = 16 * 1024 * 1024
STEP_COST = pl.CostEstimate(flops=10**9, bytes_accessed=10**7, transcendentals=0)
STREAM_LIMIT = 50 * 1024 * 1024


def dot32(first, second):
    return jnp.dot(first, second, preferred_element_type=F32)


def dot_nt(first, second):
    return lax.dot_general(
        first, second, (((1,), (1,)), ((), ())), preferred_element_type=F32
    )


def dot_tn(first, second):
    return lax.dot_general(
        first, second, (((0,), (0,)), ((), ())), preferred_element_type=F32
    )


def high(first, second):
    return jnp.dot(first, second, precision=HIGH, preferred_element_type=F32)


def head(index):
    return slice(index * HEAD_DIM, (index + 1) * HEAD_DIM)


def rows_below(limit, length, width):
    return lax.broadcasted_iota(jnp.int32, (length, width), 0) < limit


def live_pairs(limit, length):
    row = lax.broadcasted_iota(jnp.int32, (length, length), 0)
    column = lax.broadcasted_iota(jnp.int32, (length, length), 1)
    return (column <= row) & (column < limit)


def split_kernel(core_ref, w_ref, token_ref, *refs):
    own_refs, other_refs = refs[:CHUNKS], refs[CHUNKS : 2 * CHUNKS]
    landed, own_sem, other_sem = refs[2 * CHUNKS :]
    cols = own_refs[0].shape[1]
    half = CHUNKS * cols
    core = core_ref[0]

    def own_copy(k):
        start = pl.multiple_of(core * half + k * cols, HEAD_DIM)
        return pltpu.make_async_copy(
            w_ref.at[:, pl.ds(start, cols)], own_refs[k], own_sem.at[k]
        )

    def other_copy(k):
        start = pl.multiple_of((1 - core) * half + k * cols, HEAD_DIM)
        return pltpu.make_async_copy(
            w_ref.at[:, pl.ds(start, cols)], landed.at[k], other_sem.at[k]
        )

    for k in range(CHUNKS):
        other_copy(k).start()
    for k in range(CHUNKS):
        own_copy(k).start()
    for k in range(CHUNKS):
        other_copy(k).wait()
        other_refs[k][...] = landed[k].astype(F32)
    for k in range(CHUNKS):
        own_copy(k).wait()


def split(core, w_out, token):
    inner, width = w_out.shape
    cols = width // 2 // CHUNKS
    out = pl.pallas_call(
        split_kernel,
        in_specs=[SMEM, pl.BlockSpec(memory_space=pltpu.HBM), token_spec()],
        out_specs=[VMEM] * (2 * CHUNKS),
        out_shape=[jax.ShapeDtypeStruct((inner, cols), BF16)] * CHUNKS
        + [jax.ShapeDtypeStruct((inner, cols), F32)] * CHUNKS,
        scratch_shapes=[
            pltpu.VMEM((CHUNKS, inner, cols), BF16),
            pltpu.SemaphoreType.DMA((CHUNKS,)),
            pltpu.SemaphoreType.DMA((CHUNKS,)),
        ],
        compiler_params=pltpu.CompilerParams(vmem_limit_bytes=LIMIT),
    )(core, w_out, token)
    return out[:CHUNKS], out[CHUNKS:]


def norm_kernel(x_ref, gain_ref, bias_ref, out_ref):
    length, width = x_ref.shape
    blocks = [slice(i, i + DEPTH) for i in range(0, width, DEPTH)]
    total = jnp.zeros((length, 1), F32)
    for block in blocks:
        total = total + jnp.sum(x_ref[:, block].astype(F32), axis=-1, keepdims=True)
    mean = total / width
    total = jnp.zeros((length, 1), F32)
    for block in blocks:
        centred = x_ref[:, block].astype(F32) - mean
        total = total + jnp.sum(centred * centred, axis=-1, keepdims=True)
    spread = lax.rsqrt(total / width + EPS)
    for block in blocks:
        centred = x_ref[:, block].astype(F32) - mean
        full = centred * spread * gain_ref[:, block] + bias_ref[:, block]
        out_ref[:, block] = full.astype(BF16)


def layer_norm(x, gain, bias):
    return pl.pallas_call(
        norm_kernel,
        in_specs=[VMEM] * 3,
        out_specs=VMEM,
        out_shape=jax.ShapeDtypeStruct(x.shape, BF16),
        compiler_params=pltpu.CompilerParams(vmem_limit_bytes=LIMIT),
        cost_estimate=STEP_COST,
    )(x, gain[None], bias[None])


def project_kernel(
    limit_ref, normed, wq_ref, wk_ref, wv_ref, aq_ref, av_ref, bq_ref, bv_ref,
    soft_ref, key_ref, value_ref, down_q_ref, down_v_ref, mixed_ref,
    wq_in, wk_in, wv_in, weight_sem,
):
    length, width = normed.shape
    inner = key_ref.shape[1]
    blocks = [slice(i, i + DEPTH) for i in range(0, width, DEPTH)]
    copies = []
    for i, block in enumerate(blocks):
        for j, (source, target) in enumerate(
            [(wq_ref, wq_in), (wk_ref, wk_in), (wv_ref, wv_in)]
        ):
            copies.append(
                pltpu.make_async_copy(
                    source.at[block], target.at[block], weight_sem.at[3 * i + j]
                )
            )
            copies[-1].start()
    query = jnp.zeros((length, inner), F32)
    key = jnp.zeros((length, inner), F32)
    value = jnp.zeros((length, inner), F32)
    for i, block in enumerate(blocks):
        part = normed[:, block]
        for j in range(3):
            copies[3 * i + j].wait()
        query = query + dot32(part, wq_in[block])
        key = key + dot32(part, wk_in[block])
        value = value + dot32(part, wv_in[block])
    down_q = dot_nt(normed[...], aq_ref[...])
    down_v = dot_nt(normed[...], av_ref[...])
    down_q_ref[...] = down_q
    down_v_ref[...] = down_v
    limit = limit_ref[0]
    live = live_pairs(limit, length)
    kept = rows_below(limit, length, HEAD_DIM)
    query = (query + ADAPTER_SCALE * high(down_q, bq_ref[...])).astype(BF16)
    value = (value + ADAPTER_SCALE * high(down_v, bv_ref[...])).astype(BF16)
    key = key.astype(BF16)
    key_ref[...] = key
    value_ref[...] = value
    for h in range(inner // HEAD_DIM):
        scores = dot_nt(query[:, head(h)], key[:, head(h)]) * SCALE
        scores = jnp.where(live, scores, NEG)
        weights = jnp.exp(scores - jnp.max(scores, axis=-1, keepdims=True))
        soft = weights / jnp.sum(weights, axis=-1, keepdims=True)
        soft_ref[h] = soft
        mixed = dot32(soft.astype(BF16), value[:, head(h)]).astype(BF16)
        mixed_ref[:length, head(h)] = jnp.where(kept, mixed.astype(F32), 0.0)
    mixed_ref[length:] = jnp.zeros((8, inner), F32)


def project(limit, normed, wq, wk, wv, aq, av, bq, bv):
    length, width = normed.shape
    inner = wq.shape[1]
    rank = aq.shape[1]
    heads = inner // HEAD_DIM
    hbm = pl.BlockSpec(memory_space=pltpu.HBM)
    return pl.pallas_call(
        project_kernel,
        in_specs=[SMEM, VMEM] + [hbm] * 3 + [VMEM] * 4,
        out_specs=[VMEM] * 6,
        out_shape=[
            jax.ShapeDtypeStruct((heads, length, length), F32),
            jax.ShapeDtypeStruct((length, inner), BF16),
            jax.ShapeDtypeStruct((length, inner), BF16),
            jax.ShapeDtypeStruct((length, rank), F32),
            jax.ShapeDtypeStruct((length, rank), F32),
            jax.ShapeDtypeStruct((length + 8, inner), F32),
        ],
        scratch_shapes=[
            pltpu.VMEM((width, inner), BF16),
            pltpu.VMEM((width, inner), BF16),
            pltpu.VMEM((width, inner), BF16),
            pltpu.SemaphoreType.DMA((3 * (width // DEPTH),)),
        ],
        compiler_params=pltpu.CompilerParams(vmem_limit_bytes=STREAM_LIMIT),
        cost_estimate=pl.CostEstimate(
            flops=6 * length * width * inner, bytes_accessed=6 * width * inner, transcendentals=0
        ),
    )(limit, normed, wq, wk, wv, aq.T, av.T, bq, bv)


def token_spec():
    return pl.BlockSpec(memory_space=pl.ANY)


def call(kernel, ins, outs, token, scalars=()):
    tokens = [] if token is None else [token]

    def body(*refs):
        count = len(scalars) + len(ins)
        kernel(*refs[:count], *refs[count + len(tokens) :])

    return pl.pallas_call(
        body,
        in_specs=[SMEM] * len(scalars) + [VMEM] * len(ins) + [token_spec()] * len(tokens),
        out_specs=[VMEM] * len(outs),
        out_shape=[jax.ShapeDtypeStruct(shape, kind) for shape, kind in outs],
        compiler_params=pltpu.CompilerParams(vmem_limit_bytes=LIMIT),
        cost_estimate=STEP_COST,
    )(*scalars, *ins, *tokens)


def rows_of(own_ref, got_ref, length):
    return jnp.concatenate(
        [own_ref[:length].astype(BF16), got_ref[:length].astype(BF16)], axis=1
    )


def put_tail(out_ref, own_ref, got_ref, length):
    out_ref[length:] = jnp.zeros((8, out_ref.shape[1]), F32)
    out_ref[length:, :HEAD_DIM] = own_ref[length:, :HEAD_DIM] + got_ref[length:, :HEAD_DIM]


def first_spread(index, length, own, got, own_w, other_w, token):
    inner, cols = own_w.shape
    height = length + (8 if index == 0 else 0)

    def kernel(own_ref, got_ref, own_w_ref, other_w_ref, out_ref, pair_ref):
        pair_ref[:inner] = own_w_ref[...]
        pair_ref[inner:] = other_w_ref[...].astype(BF16)
        out_ref[:length] = dot32(rows_of(own_ref, got_ref, length), pair_ref[...])
        if index == 0:
            put_tail(out_ref, own_ref, got_ref, length)

    outs = [((height, cols), F32), ((2 * inner, cols), BF16)]
    return call(kernel, [own, got, own_w, other_w], outs, token)


def spread(index, length, own, got, pair, token):
    height = length + (8 if index == 0 else 0)

    def kernel(own_ref, got_ref, pair_ref, out_ref):
        out_ref[:length] = dot32(rows_of(own_ref, got_ref, length), pair_ref[...])
        if index == 0:
            put_tail(out_ref, own_ref, got_ref, length)

    return call(kernel, [own, got, pair], [((height, pair.shape[1]), F32)], token)[0]


def add(first, second, token):
    def kernel(first_ref, second_ref, out_ref):
        out_ref[...] = first_ref[...] + second_ref[: first_ref.shape[0]]

    return call(kernel, [first, second], [(first.shape, F32)], token)[0]


def add_and_pick(first, second, ends, outer, token):
    def kernel(ends_ref, first_ref, second_ref, outer_ref, sum_ref, sent_ref):
        total = first_ref[...] + second_ref[...]
        sum_ref[...] = total
        rows = outer_ref.shape[0]
        sent_ref[:rows] = jnp.where(ends_ref[0] > 0, outer_ref[...], total[:rows])
        if total.shape[0] > rows:
            sent_ref[rows:] = total[rows:]

    outs = [(first.shape, F32)] * 2
    return call(kernel, [first, second, outer], outs, token, [ends])


def gather(index, length, ends, got, held, pair, sums, limit, gap, token):
    inner = pair.shape[0] // 2
    extra = [] if gap is None else [gap]

    def kernel(ends_ref, limit_ref, got_ref, held_ref, pair_ref, *refs):
        refs = list(refs)
        gap_ref = refs.pop(0) if gap is not None else None
        before = [refs.pop(0), refs.pop(0)] if index else None
        own_ref, other_ref = refs[:2]
        total = jnp.where(ends_ref[0] > 0, got_ref[...], held_ref[...])
        total = total[: length + (8 if index == 0 else 0)]
        if index == 0:
            refs[2][...] = total[length:, :128]
            total = total[:length]
        if gap_ref is not None:
            kept = rows_below(limit_ref[0], length, total.shape[1])
            total = jnp.where(kept, total + gap_ref[...], 0.0)
        rounded = total.astype(BF16)
        own = dot_nt(rounded, pair_ref[:inner])
        other = dot_nt(rounded, pair_ref[inner:])
        squares = jnp.full((8, inner), jnp.sum(total * total), F32)
        if index:
            own = own + before[0][...]
            other = other + before[1][:length]
            squares = squares + before[1][length:]
        own_ref[...] = own
        other_ref[:length] = other
        other_ref[length:] = squares

    outs = [((length, inner), F32), ((length + 8, inner), F32)]
    if index == 0:
        outs.append(((8, 128), F32))
    return call(kernel, [got, held, pair] + extra + sums, outs, token, [ends, limit])


def cotangent_kernel(
    share, limit_ref, own_ref, other_ref, got_ref, soft_ref, key_ref, value_ref, down_q_ref,
    down_v_ref, out_ref,
):
    length, inner = own_ref.shape
    rank = down_q_ref.shape[1]
    live = live_pairs(limit_ref[0], length)
    pulled = (own_ref[...] + got_ref[:length]).astype(BF16)
    out_ref[2 * rank :] = other_ref[length:] + got_ref[length:]
    for h in range(inner // HEAD_DIM):
        soft = soft_ref[h]
        rows = pulled[:, head(h)]
        d_probs = dot_nt(rows, value_ref[:, head(h)]).astype(BF16).astype(F32)
        d_value = dot_tn(soft.astype(BF16), rows).astype(BF16).astype(F32)
        d_scores = soft * (d_probs - jnp.sum(soft * d_probs, axis=-1, keepdims=True))
        d_scores = jnp.where(live, d_scores, 0.0) * SCALE
        d_query = dot32(d_scores.astype(BF16), key_ref[:, head(h)]).astype(BF16).astype(F32)
        out_ref[:rank, head(h)] = share * lax.dot_general(
            down_q_ref[...], d_query, (((0,), (0,)), ((), ())), precision=HIGH,
            preferred_element_type=F32,
        )
        out_ref[rank : 2 * rank, head(h)] = share * lax.dot_general(
            down_v_ref[...], d_value, (((0,), (0,)), ((), ())), precision=HIGH,
            preferred_element_type=F32,
        )


def cotangent(share, limit, own, other, got, attention):
    inner = own.shape[1]
    rank = attention[3].shape[1]
    return pl.pallas_call(
        functools.partial(cotangent_kernel, share),
        in_specs=[SMEM] + [VMEM] * 8,
        out_specs=VMEM,
        out_shape=jax.ShapeDtypeStruct((2 * rank + 8, inner), F32),
        compiler_params=pltpu.CompilerParams(vmem_limit_bytes=LIMIT),
    )(limit, own, other, got, *attention)


def tangent_of(vector, limit, soft_ref, key_ref, value_ref, down_q_ref, down_v_ref, out_ref):
    length = key_ref.shape[0]
    rank = down_q_ref.shape[1]
    live = live_pairs(limit, length)
    kept = rows_below(limit, length, HEAD_DIM)
    d_query = (ADAPTER_SCALE * high(down_q_ref[...], vector[:rank])).astype(BF16)
    d_value = (ADAPTER_SCALE * high(down_v_ref[...], vector[rank:])).astype(BF16)
    for h in range(key_ref.shape[1] // HEAD_DIM):
        soft = soft_ref[h]
        d_scores = dot_nt(d_query[:, head(h)], key_ref[:, head(h)]) * SCALE
        d_scores = jnp.where(live, d_scores, 0.0)
        d_probs = soft * (d_scores - jnp.sum(soft * d_scores, axis=-1, keepdims=True))
        d_mixed = dot32(d_probs.astype(BF16), value_ref[:, head(h)]) + dot32(
            soft.astype(BF16), d_value[:, head(h)]
        )
        out_ref[:length, head(h)] = jnp.where(kept, d_mixed.astype(BF16).astype(F32), 0.0)


def total_of(terms):
    while len(terms) > 1:
        terms = [terms[i] + terms[i + 1] for i in range(0, len(terms), 2)]
    return terms[0]


def put_sums(out_ref, remain, image):
    lane = lax.broadcasted_iota(jnp.int32, (8, out_ref.shape[1]), 1)
    cross = 0.0 if image is None else jnp.sum(remain * image)
    out_ref[out_ref.shape[0] - 8 :] = jnp.where(lane == 0, jnp.sum(remain * remain), cross)


def first_kernel(n_dp, *refs):
    terms, refs = refs[:n_dp], refs[n_dp:]
    limit_ref, *attention, remain_ref, out_ref = refs
    grads = total_of([term[...] for term in terms])
    remain = -grads[: remain_ref.shape[0]]
    remain_ref[...] = remain
    put_sums(out_ref, remain, None)
    tangent_of(remain, limit_ref[0], *attention, out_ref)


def first_step(terms, limit, attention):
    inner = terms[0].shape[1]
    length = attention[1].shape[0]
    rank = attention[3].shape[1]
    return pl.pallas_call(
        functools.partial(first_kernel, len(terms)),
        in_specs=[VMEM] * len(terms) + [SMEM] + [VMEM] * 5,
        out_specs=[VMEM] * 2,
        out_shape=[
            jax.ShapeDtypeStruct((2 * rank, inner), F32),
            jax.ShapeDtypeStruct((length + 8, inner), F32),
        ],
        compiler_params=pltpu.CompilerParams(vmem_limit_bytes=LIMIT),
    )(*terms, limit, *attention)


def step_kernel(n_dp, token_count, index, last, *refs):
    terms, refs = refs[:n_dp], refs[n_dp:]
    sums_ref, remain_ref, *refs = refs
    if index:
        before_ref, newton_ref, direction_ref, image_ref, *refs = refs
    part = total_of([term[...] for term in terms])
    remain = remain_ref[...]
    rows = remain.shape[0]
    norm, cross = sums_ref[:1, 0:1], sums_ref[:1, 1:2]
    fresh = part[:rows] + DAMP * remain
    curv = part[rows : rows + 1, 0:1] / token_count + DAMP * norm
    if index:
        ratio = norm / before_ref[:1, 0:1]
        curv = curv + 2.0 * ratio * cross + ratio * ratio * before_ref[:1, 1:2]
        direction = remain + ratio * direction_ref[...]
        image = fresh + ratio * image_ref[...]
    else:
        direction, image = remain, fresh
    alpha = norm / curv
    newton = alpha * direction
    if index:
        newton = newton_ref[...] + newton
    remain = remain - alpha * image
    if last:
        step_q_ref, step_v_ref, remain_q_ref, remain_v_ref = refs
        rank = rows // 2
        step_q_ref[...] = newton[:rank]
        step_v_ref[...] = newton[rank:]
        remain_q_ref[...] = remain[:rank]
        remain_v_ref[...] = remain[rank:]
        return
    limit_ref, *refs = refs
    attention, refs = refs[:5], refs[5:]
    next_remain, next_before, next_newton, next_direction, next_image, out_ref = refs
    lane = lax.broadcasted_iota(jnp.int32, next_before.shape, 1)
    next_remain[...] = remain
    next_before[...] = jnp.where(lane == 0, norm, curv)
    next_newton[...] = newton
    next_direction[...] = direction
    next_image[...] = image
    put_sums(out_ref, remain, image)
    tangent_of(remain, limit_ref[0], *attention, out_ref)


def cg_step(index, token_count, terms, sums, remain, state, limit, attention):
    last = index == CG_STEPS - 1
    rows, inner = remain.shape
    matrix = jax.ShapeDtypeStruct((rows, inner), F32)
    scalars = jax.ShapeDtypeStruct((8, 128), F32)
    args = [*terms, sums, remain, *state]
    specs = [VMEM] * len(args)
    if last:
        shapes = [jax.ShapeDtypeStruct((rows // 2, inner), F32)] * 4
    else:
        args += [limit, *attention]
        specs += [SMEM] + [VMEM] * 5
        length = attention[1].shape[0]
        shapes = [matrix, scalars, matrix, matrix, matrix]
        shapes.append(jax.ShapeDtypeStruct((length + 8, inner), F32))
    return pl.pallas_call(
        functools.partial(step_kernel, len(terms), token_count, index, last),
        in_specs=specs,
        out_specs=[VMEM] * len(shapes),
        out_shape=shapes,
        compiler_params=pltpu.CompilerParams(vmem_limit_bytes=LIMIT),
    )(*args)


def on_device(
    inputs,
    targets,
    lengths,
    ln_gain,
    ln_bias,
    query_weight,
    w_key,
    value_weight,
    w_out,
    down_query,
    down_value,
    query_up_factor,
    value_up_factor,
):
    length, width = inputs.shape
    n_dp = lax.axis_size("dp")
    n_chip = lax.axis_size("chip")
    core = lax.axis_index("core")
    chip = lax.axis_index("chip")
    token_count = length * n_dp
    half = width // 2

    def swap(part):
        return lax.ppermute(part, "core", [(0, 1), (1, 0)])

    def data_terms(part):
        step = 1
        while 2 * step < n_dp:
            part = part + lax.ppermute(part, "dp", [(d, d ^ step) for d in range(n_dp)])
            step *= 2
        return [part, lax.ppermute(part, "dp", [(d, d ^ step) for d in range(n_dp)])]

    where = core.astype(jnp.int32)[None]
    normed = layer_norm(inputs, ln_gain, ln_bias)
    own_w, other_w = split(where, w_out, normed)
    other_w = [swap(part) for part in other_w]
    cols = half // CHUNKS
    gap = lax.dynamic_slice_in_dim(inputs, core * half, half, 1).astype(F32)
    gap = gap - lax.dynamic_slice_in_dim(targets, core * half, half, 1).astype(F32)

    soft, key, value, down_q, down_v, mixed = project(
        lengths, normed, query_weight, w_key, value_weight, down_query, down_value,
        query_up_factor, value_up_factor,
    )
    attention = (soft, key, value, down_q, down_v)

    ends = ((chip == 0) | (chip == n_chip - 1)).astype(jnp.int32)[None]

    def outer_swap(part):
        return lax.ppermute(part, "chip", [(0, 1), (1, 0), (2, 3), (3, 2)])

    def inner_swap(part):
        return lax.ppermute(part, "chip", [(0, 0), (1, 2), (2, 1), (3, 3)])

    def product(rows, pairs):
        got_rows = swap(rows)
        first = not pairs
        pairs.extend([None] * (CHUNKS - len(pairs)))
        parts, scalars = [], None
        own_part, total, outer, inner = {}, {}, {}, {}
        token = None

        def begin(k):
            if first:
                own_part[k], pairs[k] = first_spread(
                    k, length, rows, got_rows, own_w[k], other_w[k], token
                )
            else:
                own_part[k] = spread(k, length, rows, got_rows, pairs[k], token)
            return own_part[k]

        def take_in(k, got):
            nonlocal parts, scalars
            gap_part = gap[:, k * cols : (k + 1) * cols] if first else None
            out = gather(k, length, ends, got, total[k], pairs[k], parts, lengths, gap_part, token)
            parts = list(out[:2])
            scalars = out[2] if k == 0 else scalars
            return parts[0]

        if n_chip != 4:
            for k in range(CHUNKS):
                token = begin(k)
            for k in range(CHUNKS):
                total[k] = lax.psum(own_part[k], "chip")
                token = take_in(k, total[k])
        else:
            for k in [0, 1, 2] if first else [0, *range(2, CHUNKS), 1]:
                token = begin(k)
            for k in (0, 1):
                outer[k] = outer_swap(own_part[k])
            for tick in range(CHUNKS + 3):
                later = tick + 2
                if tick == CHUNKS - 1:
                    token = total[tick - 2] = add(own_part[tick - 2], inner[tick - 2], outer[tick])
                    outer[later - 1] = outer_swap(token)
                if tick < CHUNKS:
                    own_part[tick] = add(own_part[tick], outer[tick], token)
                    token = own_part[tick]
                    inner[tick] = inner_swap(token)
                if tick == CHUNKS:
                    token = take_in(tick - 3, outer[tick])
                if tick == 0:
                    outer[later] = outer_swap(own_part[later])
                elif tick <= CHUNKS and later != CHUNKS:
                    k = tick - 1
                    if later < CHUNKS:
                        total[k], token = add_and_pick(
                            own_part[k], inner[k], ends, own_part[later], token
                        )
                    else:
                        token = total[k] = add(own_part[k], inner[k], token)
                    outer[later] = outer_swap(token)
                if tick + 3 < CHUNKS and first:
                    token = begin(tick + 3)
                if tick >= 3 and tick != CHUNKS:
                    token = take_in(tick - 3, outer[tick])
        own, other = parts
        share = ADAPTER_SCALE / token_count
        part = cotangent(share, lengths, own, other, swap(other), attention)
        return data_terms(part), scalars

    pairs = []
    terms, _ = product(mixed, pairs)
    remain, rows = first_step(terms, lengths, attention)
    state = ()
    for index in range(CG_STEPS):
        terms, sums = product(rows, pairs)
        out = cg_step(index, token_count, terms, sums, remain, state, lengths, attention)
        if index < CG_STEPS - 1:
            remain, *state, rows = out
    return tuple(out)


def solution(mesh):
    fine = Mesh(mesh.devices.reshape(mesh.shape["dp"], -1, 2), ("dp", "chip", "core"))
    tensor = ("chip", "core")
    in_specs = (
        P("dp", None),
        P("dp", None),
        P("dp"),
        P(),
        P(),
        P(None, tensor),
        P(None, tensor),
        P(None, tensor),
        P(tensor, None),
        P(),
        P(),
        P(None, tensor),
        P(None, tensor),
    )
    out_specs = (P(None, tensor),) * 4
    return jax.shard_map(
        on_device, mesh=fine, in_specs=in_specs, out_specs=out_specs, check_vma=False
    )
```

```python
import functools

import jax
import jax.numpy as jnp
from jax import lax
from jax.experimental import pallas as pl
from jax.experimental.pallas import tpu as pltpu
from jax.sharding import Mesh
from jax.sharding import PartitionSpec as P

HEAD_DIM = 128
CG_STEPS = 3
CHUNKS = 6
DEPTH = 1024

EPS = 1e-05
ADAPTER_SCALE = 2.0
DAMP = 0.05
NEG = -1e30
F32 = jnp.float32
BF16 = jnp.bfloat16
HIGH = lax.Precision.HIGHEST
SCALE = HEAD_DIM ** (-0.5)
VMEM = pl.BlockSpec(memory_space=pltpu.VMEM)
SMEM = pl.BlockSpec(memory_space=pltpu.SMEM)
LIMIT = 16 * 1024 * 1024
STEP_COST = pl.CostEstimate(flops=10**9, bytes_accessed=10**7, transcendentals=0)
STREAM_LIMIT = 45 * 1024 * 1024


def dot32(first, second):
    return jnp.dot(first, second, preferred_element_type=F32)


def dot_nt(first, second):
    return lax.dot_general(
        first, second, (((1,), (1,)), ((), ())), preferred_element_type=F32
    )


def dot_tn(first, second):
    return lax.dot_general(
        first, second, (((0,), (0,)), ((), ())), preferred_element_type=F32
    )


def high(first, second):
    return jnp.dot(first, second, precision=HIGH, preferred_element_type=F32)


def head(index):
    return slice(index * HEAD_DIM, (index + 1) * HEAD_DIM)


def rows_below(limit, length, width):
    return lax.broadcasted_iota(jnp.int32, (length, width), 0) < limit


def live_pairs(limit, length):
    row = lax.broadcasted_iota(jnp.int32, (length, length), 0)
    column = lax.broadcasted_iota(jnp.int32, (length, length), 1)
    return (column <= row) & (column < limit)


def split_kernel(core_ref, w_ref, *refs):
    own_refs, other_refs = refs[:CHUNKS], refs[CHUNKS : 2 * CHUNKS]
    landed, own_sem, other_sem = refs[2 * CHUNKS :]
    cols = own_refs[0].shape[1]
    half = CHUNKS * cols
    core = core_ref[0]

    def own_copy(k):
        start = pl.multiple_of(core * half + k * cols, HEAD_DIM)
        return pltpu.make_async_copy(
            w_ref.at[:, pl.ds(start, cols)], own_refs[k], own_sem.at[k]
        )

    def other_copy(k):
        start = pl.multiple_of((1 - core) * half + k * cols, HEAD_DIM)
        return pltpu.make_async_copy(
            w_ref.at[:, pl.ds(start, cols)], landed.at[k], other_sem.at[k]
        )

    for k in range(CHUNKS):
        other_copy(k).start()
    for k in range(CHUNKS):
        own_copy(k).start()
    for k in range(CHUNKS):
        other_copy(k).wait()
        other_refs[k][...] = landed[k].astype(F32)
    for k in range(CHUNKS):
        own_copy(k).wait()


def split(core, w_out):
    inner, width = w_out.shape
    cols = width // 2 // CHUNKS
    out = pl.pallas_call(
        split_kernel,
        in_specs=[SMEM, pl.BlockSpec(memory_space=pltpu.HBM)],
        out_specs=[VMEM] * (2 * CHUNKS),
        out_shape=[jax.ShapeDtypeStruct((inner, cols), BF16)] * CHUNKS
        + [jax.ShapeDtypeStruct((inner, cols), F32)] * CHUNKS,
        scratch_shapes=[
            pltpu.VMEM((CHUNKS, inner, cols), BF16),
            pltpu.SemaphoreType.DMA((CHUNKS,)),
            pltpu.SemaphoreType.DMA((CHUNKS,)),
        ],
        compiler_params=pltpu.CompilerParams(vmem_limit_bytes=LIMIT),
    )(core, w_out)
    return out[:CHUNKS], out[CHUNKS:]


def project_kernel(
    limit_ref, x_ref, wq_ref, wk_ref, wv_ref, gain_ref, bias_ref, aq_ref, av_ref, bq_ref, bv_ref,
    soft_ref, key_ref, value_ref, down_q_ref, down_v_ref, mixed_ref,
    rows_in, normed, wq_in, wk_in, wv_in, rows_sem, weight_sem,
):
    length, width = normed.shape
    inner = key_ref.shape[1]
    blocks = [slice(i, i + DEPTH) for i in range(0, width, DEPTH)]
    rows_copy = pltpu.make_async_copy(x_ref, rows_in, rows_sem)
    rows_copy.start()
    copies = []
    for i, block in enumerate(blocks):
        for j, (source, target) in enumerate(
            [(wq_ref, wq_in), (wk_ref, wk_in), (wv_ref, wv_in)]
        ):
            copies.append(
                pltpu.make_async_copy(
                    source.at[block], target.at[block], weight_sem.at[3 * i + j]
                )
            )
            copies[-1].start()
    rows_copy.wait()
    total = jnp.zeros((length, 1), F32)
    for block in blocks:
        total = total + jnp.sum(rows_in[:, block].astype(F32), axis=-1, keepdims=True)
    mean = total / width
    total = jnp.zeros((length, 1), F32)
    for block in blocks:
        centred = rows_in[:, block].astype(F32) - mean
        total = total + jnp.sum(centred * centred, axis=-1, keepdims=True)
    spread = lax.rsqrt(total / width + EPS)
    for block in blocks:
        centred = rows_in[:, block].astype(F32) - mean
        full = centred * spread * gain_ref[:, block] + bias_ref[:, block]
        normed[:, block] = full.astype(BF16)
    query = jnp.zeros((length, inner), F32)
    key = jnp.zeros((length, inner), F32)
    value = jnp.zeros((length, inner), F32)
    for i, block in enumerate(blocks):
        part = normed[:, block]
        for j in range(3):
            copies[3 * i + j].wait()
        query = query + dot32(part, wq_in[block])
        key = key + dot32(part, wk_in[block])
        value = value + dot32(part, wv_in[block])
    down_q = dot_nt(normed[...], aq_ref[...])
    down_v = dot_nt(normed[...], av_ref[...])
    down_q_ref[...] = down_q
    down_v_ref[...] = down_v
    limit = limit_ref[0]
    live = live_pairs(limit, length)
    kept = rows_below(limit, length, HEAD_DIM)
    query = (query + ADAPTER_SCALE * high(down_q, bq_ref[...])).astype(BF16)
    value = (value + ADAPTER_SCALE * high(down_v, bv_ref[...])).astype(BF16)
    key = key.astype(BF16)
    key_ref[...] = key
    value_ref[...] = value
    for h in range(inner // HEAD_DIM):
        scores = dot_nt(query[:, head(h)], key[:, head(h)]) * SCALE
        scores = jnp.where(live, scores, NEG)
        weights = jnp.exp(scores - jnp.max(scores, axis=-1, keepdims=True))
        soft = weights / jnp.sum(weights, axis=-1, keepdims=True)
        soft_ref[h] = soft
        mixed = dot32(soft.astype(BF16), value[:, head(h)]).astype(BF16)
        mixed_ref[:length, head(h)] = jnp.where(kept, mixed.astype(F32), 0.0)
    mixed_ref[length:] = jnp.zeros((8, inner), F32)


def project(limit, x, gain, bias, wq, wk, wv, aq, av, bq, bv):
    length, width = x.shape
    inner = wq.shape[1]
    rank = aq.shape[1]
    heads = inner // HEAD_DIM
    hbm = pl.BlockSpec(memory_space=pltpu.HBM)
    return pl.pallas_call(
        project_kernel,
        in_specs=[SMEM] + [hbm] * 4 + [VMEM] * 6,
        out_specs=[VMEM] * 6,
        out_shape=[
            jax.ShapeDtypeStruct((heads, length, length), F32),
            jax.ShapeDtypeStruct((length, inner), BF16),
            jax.ShapeDtypeStruct((length, inner), BF16),
            jax.ShapeDtypeStruct((length, rank), F32),
            jax.ShapeDtypeStruct((length, rank), F32),
            jax.ShapeDtypeStruct((length + 8, inner), F32),
        ],
        scratch_shapes=[
            pltpu.VMEM((length, width), BF16),
            pltpu.VMEM((length, width), BF16),
            pltpu.VMEM((width, inner), BF16),
            pltpu.VMEM((width, inner), BF16),
            pltpu.VMEM((width, inner), BF16),
            pltpu.SemaphoreType.DMA,
            pltpu.SemaphoreType.DMA((3 * (width // DEPTH),)),
        ],
        compiler_params=pltpu.CompilerParams(vmem_limit_bytes=STREAM_LIMIT),
        cost_estimate=pl.CostEstimate(
            flops=6 * length * width * inner, bytes_accessed=6 * width * inner, transcendentals=0
        ),
    )(limit, x, wq, wk, wv, gain[None], bias[None], aq.T, av.T, bq, bv)


def token_spec():
    return pl.BlockSpec(memory_space=pl.ANY)


def call(kernel, ins, outs, token, scalars=()):
    tokens = [] if token is None else [token]

    def body(*refs):
        count = len(scalars) + len(ins)
        kernel(*refs[:count], *refs[count + len(tokens) :])

    return pl.pallas_call(
        body,
        in_specs=[SMEM] * len(scalars) + [VMEM] * len(ins) + [token_spec()] * len(tokens),
        out_specs=[VMEM] * len(outs),
        out_shape=[jax.ShapeDtypeStruct(shape, kind) for shape, kind in outs],
        compiler_params=pltpu.CompilerParams(vmem_limit_bytes=LIMIT),
        cost_estimate=STEP_COST,
    )(*scalars, *ins, *tokens)


def rows_of(own_ref, got_ref, length):
    return jnp.concatenate(
        [own_ref[:length].astype(BF16), got_ref[:length].astype(BF16)], axis=1
    )


def put_tail(out_ref, own_ref, got_ref, length):
    out_ref[length:] = jnp.zeros((8, out_ref.shape[1]), F32)
    out_ref[length:, :HEAD_DIM] = own_ref[length:, :HEAD_DIM] + got_ref[length:, :HEAD_DIM]


def first_spread(index, length, own, got, own_w, other_w, token):
    inner, cols = own_w.shape
    height = length + (8 if index == 0 else 0)

    def kernel(own_ref, got_ref, own_w_ref, other_w_ref, out_ref, pair_ref):
        pair_ref[:inner] = own_w_ref[...]
        pair_ref[inner:] = other_w_ref[...].astype(BF16)
        out_ref[:length] = dot32(rows_of(own_ref, got_ref, length), pair_ref[...])
        if index == 0:
            put_tail(out_ref, own_ref, got_ref, length)

    outs = [((height, cols), F32), ((2 * inner, cols), BF16)]
    return call(kernel, [own, got, own_w, other_w], outs, token)


def spread(index, length, own, got, pair, token):
    height = length + (8 if index == 0 else 0)

    def kernel(own_ref, got_ref, pair_ref, out_ref):
        out_ref[:length] = dot32(rows_of(own_ref, got_ref, length), pair_ref[...])
        if index == 0:
            put_tail(out_ref, own_ref, got_ref, length)

    return call(kernel, [own, got, pair], [((height, pair.shape[1]), F32)], token)[0]


def add(first, second, token):
    def kernel(first_ref, second_ref, out_ref):
        out_ref[...] = first_ref[...] + second_ref[: first_ref.shape[0]]

    return call(kernel, [first, second], [(first.shape, F32)], token)[0]


def add_and_pick(first, second, ends, outer, token):
    def kernel(ends_ref, first_ref, second_ref, outer_ref, sum_ref, sent_ref):
        total = first_ref[...] + second_ref[...]
        sum_ref[...] = total
        rows = outer_ref.shape[0]
        sent_ref[:rows] = jnp.where(ends_ref[0] > 0, outer_ref[...], total[:rows])
        if total.shape[0] > rows:
            sent_ref[rows:] = total[rows:]

    outs = [(first.shape, F32)] * 2
    return call(kernel, [first, second, outer], outs, token, [ends])


def gather(index, length, ends, got, held, pair, sums, limit, gap, token):
    inner = pair.shape[0] // 2
    extra = [] if gap is None else [gap]

    def kernel(ends_ref, limit_ref, got_ref, held_ref, pair_ref, *refs):
        refs = list(refs)
        gap_ref = refs.pop(0) if gap is not None else None
        before = [refs.pop(0), refs.pop(0)] if index else None
        own_ref, other_ref = refs[:2]
        total = jnp.where(ends_ref[0] > 0, got_ref[...], held_ref[...])
        total = total[: length + (8 if index == 0 else 0)]
        if index == 0:
            refs[2][...] = total[length:, :128]
            total = total[:length]
        if gap_ref is not None:
            kept = rows_below(limit_ref[0], length, total.shape[1])
            total = jnp.where(kept, total + gap_ref[...], 0.0)
        rounded = total.astype(BF16)
        own = dot_nt(rounded, pair_ref[:inner])
        other = dot_nt(rounded, pair_ref[inner:])
        squares = jnp.full((8, inner), jnp.sum(total * total), F32)
        if index:
            own = own + before[0][...]
            other = other + before[1][:length]
            squares = squares + before[1][length:]
        own_ref[...] = own
        other_ref[:length] = other
        other_ref[length:] = squares

    outs = [((length, inner), F32), ((length + 8, inner), F32)]
    if index == 0:
        outs.append(((8, 128), F32))
    return call(kernel, [got, held, pair] + extra + sums, outs, token, [ends, limit])


def cotangent_kernel(
    share, limit_ref, own_ref, other_ref, got_ref, soft_ref, key_ref, value_ref, down_q_ref,
    down_v_ref, out_ref,
):
    length, inner = own_ref.shape
    rank = down_q_ref.shape[1]
    live = live_pairs(limit_ref[0], length)
    pulled = (own_ref[...] + got_ref[:length]).astype(BF16)
    out_ref[2 * rank :] = other_ref[length:] + got_ref[length:]
    for h in range(inner // HEAD_DIM):
        soft = soft_ref[h]
        rows = pulled[:, head(h)]
        d_probs = dot_nt(rows, value_ref[:, head(h)]).astype(BF16).astype(F32)
        d_value = dot_tn(soft.astype(BF16), rows).astype(BF16).astype(F32)
        d_scores = soft * (d_probs - jnp.sum(soft * d_probs, axis=-1, keepdims=True))
        d_scores = jnp.where(live, d_scores, 0.0) * SCALE
        d_query = dot32(d_scores.astype(BF16), key_ref[:, head(h)]).astype(BF16).astype(F32)
        out_ref[:rank, head(h)] = share * lax.dot_general(
            down_q_ref[...], d_query, (((0,), (0,)), ((), ())), precision=HIGH,
            preferred_element_type=F32,
        )
        out_ref[rank : 2 * rank, head(h)] = share * lax.dot_general(
            down_v_ref[...], d_value, (((0,), (0,)), ((), ())), precision=HIGH,
            preferred_element_type=F32,
        )


def cotangent(share, limit, own, other, got, attention):
    inner = own.shape[1]
    rank = attention[3].shape[1]
    return pl.pallas_call(
        functools.partial(cotangent_kernel, share),
        in_specs=[SMEM] + [VMEM] * 8,
        out_specs=VMEM,
        out_shape=jax.ShapeDtypeStruct((2 * rank + 8, inner), F32),
        compiler_params=pltpu.CompilerParams(vmem_limit_bytes=LIMIT),
    )(limit, own, other, got, *attention)


def tangent_of(vector, limit, soft_ref, key_ref, value_ref, down_q_ref, down_v_ref, out_ref):
    length = key_ref.shape[0]
    rank = down_q_ref.shape[1]
    live = live_pairs(limit, length)
    kept = rows_below(limit, length, HEAD_DIM)
    d_query = (ADAPTER_SCALE * high(down_q_ref[...], vector[:rank])).astype(BF16)
    d_value = (ADAPTER_SCALE * high(down_v_ref[...], vector[rank:])).astype(BF16)
    for h in range(key_ref.shape[1] // HEAD_DIM):
        soft = soft_ref[h]
        d_scores = dot_nt(d_query[:, head(h)], key_ref[:, head(h)]) * SCALE
        d_scores = jnp.where(live, d_scores, 0.0)
        d_probs = soft * (d_scores - jnp.sum(soft * d_scores, axis=-1, keepdims=True))
        d_mixed = dot32(d_probs.astype(BF16), value_ref[:, head(h)]) + dot32(
            soft.astype(BF16), d_value[:, head(h)]
        )
        out_ref[:length, head(h)] = jnp.where(kept, d_mixed.astype(BF16).astype(F32), 0.0)


def total_of(terms):
    while len(terms) > 1:
        terms = [terms[i] + terms[i + 1] for i in range(0, len(terms), 2)]
    return terms[0]


def put_sums(out_ref, remain, image):
    lane = lax.broadcasted_iota(jnp.int32, (8, out_ref.shape[1]), 1)
    cross = 0.0 if image is None else jnp.sum(remain * image)
    out_ref[out_ref.shape[0] - 8 :] = jnp.where(lane == 0, jnp.sum(remain * remain), cross)


def first_kernel(n_dp, *refs):
    terms, refs = refs[:n_dp], refs[n_dp:]
    limit_ref, *attention, remain_ref, out_ref = refs
    grads = total_of([term[...] for term in terms])
    remain = -grads[: remain_ref.shape[0]]
    remain_ref[...] = remain
    put_sums(out_ref, remain, None)
    tangent_of(remain, limit_ref[0], *attention, out_ref)


def first_step(terms, limit, attention):
    inner = terms[0].shape[1]
    length = attention[1].shape[0]
    rank = attention[3].shape[1]
    return pl.pallas_call(
        functools.partial(first_kernel, len(terms)),
        in_specs=[VMEM] * len(terms) + [SMEM] + [VMEM] * 5,
        out_specs=[VMEM] * 2,
        out_shape=[
            jax.ShapeDtypeStruct((2 * rank, inner), F32),
            jax.ShapeDtypeStruct((length + 8, inner), F32),
        ],
        compiler_params=pltpu.CompilerParams(vmem_limit_bytes=LIMIT),
    )(*terms, limit, *attention)


def step_kernel(n_dp, token_count, index, last, *refs):
    terms, refs = refs[:n_dp], refs[n_dp:]
    sums_ref, remain_ref, *refs = refs
    if index:
        before_ref, newton_ref, direction_ref, image_ref, *refs = refs
    part = total_of([term[...] for term in terms])
    remain = remain_ref[...]
    rows = remain.shape[0]
    norm, cross = sums_ref[:1, 0:1], sums_ref[:1, 1:2]
    fresh = part[:rows] + DAMP * remain
    curv = part[rows : rows + 1, 0:1] / token_count + DAMP * norm
    if index:
        ratio = norm / before_ref[:1, 0:1]
        curv = curv + 2.0 * ratio * cross + ratio * ratio * before_ref[:1, 1:2]
        direction = remain + ratio * direction_ref[...]
        image = fresh + ratio * image_ref[...]
    else:
        direction, image = remain, fresh
    alpha = norm / curv
    newton = alpha * direction
    if index:
        newton = newton_ref[...] + newton
    remain = remain - alpha * image
    if last:
        step_q_ref, step_v_ref, remain_q_ref, remain_v_ref = refs
        rank = rows // 2
        step_q_ref[...] = newton[:rank]
        step_v_ref[...] = newton[rank:]
        remain_q_ref[...] = remain[:rank]
        remain_v_ref[...] = remain[rank:]
        return
    limit_ref, *refs = refs
    attention, refs = refs[:5], refs[5:]
    next_remain, next_before, next_newton, next_direction, next_image, out_ref = refs
    lane = lax.broadcasted_iota(jnp.int32, next_before.shape, 1)
    next_remain[...] = remain
    next_before[...] = jnp.where(lane == 0, norm, curv)
    next_newton[...] = newton
    next_direction[...] = direction
    next_image[...] = image
    put_sums(out_ref, remain, image)
    tangent_of(remain, limit_ref[0], *attention, out_ref)


def cg_step(index, token_count, terms, sums, remain, state, limit, attention):
    last = index == CG_STEPS - 1
    rows, inner = remain.shape
    matrix = jax.ShapeDtypeStruct((rows, inner), F32)
    scalars = jax.ShapeDtypeStruct((8, 128), F32)
    args = [*terms, sums, remain, *state]
    specs = [VMEM] * len(args)
    if last:
        shapes = [jax.ShapeDtypeStruct((rows // 2, inner), F32)] * 4
    else:
        args += [limit, *attention]
        specs += [SMEM] + [VMEM] * 5
        length = attention[1].shape[0]
        shapes = [matrix, scalars, matrix, matrix, matrix]
        shapes.append(jax.ShapeDtypeStruct((length + 8, inner), F32))
    return pl.pallas_call(
        functools.partial(step_kernel, len(terms), token_count, index, last),
        in_specs=specs,
        out_specs=[VMEM] * len(shapes),
        out_shape=shapes,
        compiler_params=pltpu.CompilerParams(vmem_limit_bytes=LIMIT),
    )(*args)


def on_device(
    inputs,
    targets,
    lengths,
    ln_gain,
    ln_bias,
    query_weight,
    w_key,
    value_weight,
    w_out,
    down_query,
    down_value,
    query_up_factor,
    value_up_factor,
):
    length, width = inputs.shape
    n_dp = lax.axis_size("dp")
    n_chip = lax.axis_size("chip")
    core = lax.axis_index("core")
    chip = lax.axis_index("chip")
    token_count = length * n_dp
    half = width // 2

    def swap(part):
        return lax.ppermute(part, "core", [(0, 1), (1, 0)])

    def data_terms(part):
        step = 1
        while 2 * step < n_dp:
            part = part + lax.ppermute(part, "dp", [(d, d ^ step) for d in range(n_dp)])
            step *= 2
        return [part, lax.ppermute(part, "dp", [(d, d ^ step) for d in range(n_dp)])]

    where = core.astype(jnp.int32)[None]
    own_w, other_w = split(where, w_out)
    other_w = [swap(part) for part in other_w]
    cols = half // CHUNKS
    gap = lax.dynamic_slice_in_dim(inputs, core * half, half, 1).astype(F32)
    gap = gap - lax.dynamic_slice_in_dim(targets, core * half, half, 1).astype(F32)

    soft, key, value, down_q, down_v, mixed = project(
        lengths, inputs, ln_gain, ln_bias, query_weight, w_key, value_weight, down_query,
        down_value, query_up_factor, value_up_factor,
    )
    attention = (soft, key, value, down_q, down_v)

    ends = ((chip == 0) | (chip == n_chip - 1)).astype(jnp.int32)[None]

    def outer_swap(part):
        return lax.ppermute(part, "chip", [(0, 1), (1, 0), (2, 3), (3, 2)])

    def send_back(part):
        return lax.ppermute(part, "chip", [(1, 0), (2, 3)])

    def inner_swap(part):
        return lax.ppermute(part, "chip", [(0, 0), (1, 2), (2, 1), (3, 3)])

    def product(rows, pairs):
        got_rows = swap(rows)
        first = not pairs
        pairs.extend([None] * (CHUNKS - len(pairs)))
        parts, scalars = [], None
        own_part, total, outer, inner = {}, {}, {}, {}
        token = None

        def begin(k):
            if first:
                own_part[k], pairs[k] = first_spread(
                    k, length, rows, got_rows, own_w[k], other_w[k], token
                )
            else:
                own_part[k] = spread(k, length, rows, got_rows, pairs[k], token)
            return own_part[k]

        def finish(k, got):
            gap_part = gap[:, k * cols : (k + 1) * cols] if first else None
            return gather(k, length, ends, got, total[k], pairs[k], parts, lengths, gap_part, token)

        if n_chip != 4:
            for k in range(CHUNKS):
                token = begin(k)
            for k in range(CHUNKS):
                total[k] = lax.psum(own_part[k], "chip")
                out = finish(k, total[k])
                parts, scalars = list(out[:2]), out[2] if k == 0 else scalars
        else:
            for k in [0, 1, 2] if first else [0, *range(2, CHUNKS), 1]:
                token = begin(k)
            for k in (0, 1):
                outer[k] = outer_swap(own_part[k])
            for tick in range(CHUNKS + 3):
                if tick < CHUNKS:
                    own_part[tick] = add(own_part[tick], outer[tick], token)
                    token = own_part[tick]
                    inner[tick] = inner_swap(token)
                later = tick + 2
                if tick == CHUNKS:
                    out = finish(tick - 3, outer[tick])
                    parts = list(out[:2])
                    token = parts[0]
                if 1 <= tick <= CHUNKS:
                    k = tick - 1
                    if later < CHUNKS:
                        total[k], sent = add_and_pick(
                            own_part[k], inner[k], ends, own_part[later], token
                        )
                    else:
                        total[k] = sent = add(own_part[k], inner[k], token)
                    token = sent
                    outer[later] = send_back(sent) if later == CHUNKS else outer_swap(sent)
                elif tick == 0:
                    outer[later] = outer_swap(own_part[later])
                if tick + 3 < CHUNKS and first:
                    token = begin(tick + 3)
                if tick >= 3 and tick != CHUNKS:
                    out = finish(tick - 3, outer[tick])
                    parts, scalars = list(out[:2]), out[2] if tick == 3 else scalars
                    token = parts[0]
        own, other = parts
        share = ADAPTER_SCALE / token_count
        part = cotangent(share, lengths, own, other, swap(other), attention)
        return data_terms(part), scalars

    pairs = []
    terms, _ = product(mixed, pairs)
    remain, rows = first_step(terms, lengths, attention)
    state = ()
    for index in range(CG_STEPS):
        terms, sums = product(rows, pairs)
        out = cg_step(index, token_count, terms, sums, remain, state, lengths, attention)
        if index < CG_STEPS - 1:
            remain, *state, rows = out
    return tuple(out)


def solution(mesh):
    fine = Mesh(mesh.devices.reshape(mesh.shape["dp"], -1, 2), ("dp", "chip", "core"))
    tensor = ("chip", "core")
    in_specs = (
        P("dp", None),
        P("dp", None),
        P("dp"),
        P(),
        P(),
        P(None, tensor),
        P(None, tensor),
        P(None, tensor),
        P(tensor, None),
        P(),
        P(),
        P(None, tensor),
        P(None, tensor),
    )
    out_specs = (P(None, tensor),) * 4
    return jax.shard_map(
        on_device, mesh=fine, in_specs=in_specs, out_specs=out_specs, check_vma=False
    )
```

```python
import functools

import jax
import jax.numpy as jnp
from jax import lax
from jax.experimental import pallas as pl
from jax.experimental.pallas import tpu as pltpu
from jax.sharding import Mesh
from jax.sharding import PartitionSpec as P

HEAD_DIM = 128
CG_STEPS = 3
CHUNKS = 6
DEPTH = 1024

EPS = 1e-05
ADAPTER_SCALE = 2.0
DAMP = 0.05
NEG = -1e30
F32 = jnp.float32
BF16 = jnp.bfloat16
HIGH = lax.Precision.HIGHEST
SCALE = HEAD_DIM ** (-0.5)
VMEM = pl.BlockSpec(memory_space=pltpu.VMEM)
SMEM = pl.BlockSpec(memory_space=pltpu.SMEM)
LIMIT = 16 * 1024 * 1024
STEP_COST = pl.CostEstimate(flops=10**9, bytes_accessed=10**7, transcendentals=0)
STREAM_LIMIT = 50 * 1024 * 1024


def dot32(first, second):
    return jnp.dot(first, second, preferred_element_type=F32)


def dot_nt(first, second):
    return lax.dot_general(
        first, second, (((1,), (1,)), ((), ())), preferred_element_type=F32
    )


def dot_tn(first, second):
    return lax.dot_general(
        first, second, (((0,), (0,)), ((), ())), preferred_element_type=F32
    )


def high(first, second):
    return jnp.dot(first, second, precision=HIGH, preferred_element_type=F32)


def head(index):
    return slice(index * HEAD_DIM, (index + 1) * HEAD_DIM)


def rows_below(limit, length, width):
    return lax.broadcasted_iota(jnp.int32, (length, width), 0) < limit


def live_pairs(limit, length):
    row = lax.broadcasted_iota(jnp.int32, (length, length), 0)
    column = lax.broadcasted_iota(jnp.int32, (length, length), 1)
    return (column <= row) & (column < limit)


def split_kernel(core_ref, w_ref, *refs):
    own_refs, other_refs = refs[:CHUNKS], refs[CHUNKS : 2 * CHUNKS]
    landed, own_sem, other_sem = refs[2 * CHUNKS :]
    cols = own_refs[0].shape[1]
    half = CHUNKS * cols
    core = core_ref[0]

    def own_copy(k):
        start = pl.multiple_of(core * half + k * cols, HEAD_DIM)
        return pltpu.make_async_copy(
            w_ref.at[:, pl.ds(start, cols)], own_refs[k], own_sem.at[k]
        )

    def other_copy(k):
        start = pl.multiple_of((1 - core) * half + k * cols, HEAD_DIM)
        return pltpu.make_async_copy(
            w_ref.at[:, pl.ds(start, cols)], landed.at[k], other_sem.at[k]
        )

    for k in range(CHUNKS):
        other_copy(k).start()
    for k in range(CHUNKS):
        own_copy(k).start()
    for k in range(CHUNKS):
        other_copy(k).wait()
        other_refs[k][...] = landed[k].astype(F32)
    for k in range(CHUNKS):
        own_copy(k).wait()


def split(core, w_out):
    inner, width = w_out.shape
    cols = width // 2 // CHUNKS
    out = pl.pallas_call(
        split_kernel,
        in_specs=[SMEM, pl.BlockSpec(memory_space=pltpu.HBM)],
        out_specs=[VMEM] * (2 * CHUNKS),
        out_shape=[jax.ShapeDtypeStruct((inner, cols), BF16)] * CHUNKS
        + [jax.ShapeDtypeStruct((inner, cols), F32)] * CHUNKS,
        scratch_shapes=[
            pltpu.VMEM((CHUNKS, inner, cols), BF16),
            pltpu.SemaphoreType.DMA((CHUNKS,)),
            pltpu.SemaphoreType.DMA((CHUNKS,)),
        ],
        compiler_params=pltpu.CompilerParams(vmem_limit_bytes=LIMIT),
    )(core, w_out)
    return out[:CHUNKS], out[CHUNKS:]


def project_kernel(
    limit_ref, x_ref, wq_ref, wk_ref, wv_ref, gain_ref, bias_ref, aq_ref, av_ref, bq_ref, bv_ref,
    soft_ref, key_ref, value_ref, down_q_ref, down_v_ref, mixed_ref,
    rows_in, normed, wq_in, wk_in, wv_in, rows_sem, weight_sem,
):
    length, width = normed.shape
    inner = key_ref.shape[1]
    blocks = [slice(i, i + DEPTH) for i in range(0, width, DEPTH)]
    rows_copy = pltpu.make_async_copy(x_ref, rows_in, rows_sem)
    rows_copy.start()
    copies = []
    for i, block in enumerate(blocks):
        for j, (source, target) in enumerate(
            [(wq_ref, wq_in), (wk_ref, wk_in), (wv_ref, wv_in)]
        ):
            copies.append(
                pltpu.make_async_copy(
                    source.at[block], target.at[block], weight_sem.at[3 * i + j]
                )
            )
            copies[-1].start()
    rows_copy.wait()
    total = jnp.zeros((length, 1), F32)
    for block in blocks:
        total = total + jnp.sum(rows_in[:, block].astype(F32), axis=-1, keepdims=True)
    mean = total / width
    total = jnp.zeros((length, 1), F32)
    for block in blocks:
        centred = rows_in[:, block].astype(F32) - mean
        total = total + jnp.sum(centred * centred, axis=-1, keepdims=True)
    spread = lax.rsqrt(total / width + EPS)
    for block in blocks:
        centred = rows_in[:, block].astype(F32) - mean
        full = centred * spread * gain_ref[:, block] + bias_ref[:, block]
        normed[:, block] = full.astype(BF16)
    query = jnp.zeros((length, inner), F32)
    key = jnp.zeros((length, inner), F32)
    value = jnp.zeros((length, inner), F32)
    for i, block in enumerate(blocks):
        part = normed[:, block]
        for j in range(3):
            copies[3 * i + j].wait()
        query = query + dot32(part, wq_in[block])
        key = key + dot32(part, wk_in[block])
        value = value + dot32(part, wv_in[block])
    down_q = dot_nt(normed[...], aq_ref[...])
    down_v = dot_nt(normed[...], av_ref[...])
    down_q_ref[...] = down_q
    down_v_ref[...] = down_v
    limit = limit_ref[0]
    live = live_pairs(limit, length)
    kept = rows_below(limit, length, HEAD_DIM)
    query = (query + ADAPTER_SCALE * high(down_q, bq_ref[...])).astype(BF16)
    value = (value + ADAPTER_SCALE * high(down_v, bv_ref[...])).astype(BF16)
    key = key.astype(BF16)
    key_ref[...] = key
    value_ref[...] = value
    for h in range(inner // HEAD_DIM):
        scores = dot_nt(query[:, head(h)], key[:, head(h)]) * SCALE
        scores = jnp.where(live, scores, NEG)
        weights = jnp.exp(scores - jnp.max(scores, axis=-1, keepdims=True))
        soft = weights / jnp.sum(weights, axis=-1, keepdims=True)
        soft_ref[h] = soft
        mixed = dot32(soft.astype(BF16), value[:, head(h)]).astype(BF16)
        mixed_ref[:length, head(h)] = jnp.where(kept, mixed.astype(F32), 0.0)
    mixed_ref[length:] = jnp.zeros((8, inner), F32)


def project(limit, x, gain, bias, wq, wk, wv, aq, av, bq, bv):
    length, width = x.shape
    inner = wq.shape[1]
    rank = aq.shape[1]
    heads = inner // HEAD_DIM
    hbm = pl.BlockSpec(memory_space=pltpu.HBM)
    return pl.pallas_call(
        project_kernel,
        in_specs=[SMEM] + [hbm] * 4 + [VMEM] * 6,
        out_specs=[VMEM] * 6,
        out_shape=[
            jax.ShapeDtypeStruct((heads, length, length), F32),
            jax.ShapeDtypeStruct((length, inner), BF16),
            jax.ShapeDtypeStruct((length, inner), BF16),
            jax.ShapeDtypeStruct((length, rank), F32),
            jax.ShapeDtypeStruct((length, rank), F32),
            jax.ShapeDtypeStruct((length + 8, inner), F32),
        ],
        scratch_shapes=[
            pltpu.VMEM((length, width), BF16),
            pltpu.VMEM((length, width), BF16),
            pltpu.VMEM((width, inner), BF16),
            pltpu.VMEM((width, inner), BF16),
            pltpu.VMEM((width, inner), BF16),
            pltpu.SemaphoreType.DMA,
            pltpu.SemaphoreType.DMA((3 * (width // DEPTH),)),
        ],
        compiler_params=pltpu.CompilerParams(vmem_limit_bytes=STREAM_LIMIT),
        cost_estimate=pl.CostEstimate(
            flops=6 * length * width * inner, bytes_accessed=6 * width * inner, transcendentals=0
        ),
    )(limit, x, wq, wk, wv, gain[None], bias[None], aq.T, av.T, bq, bv)


def token_spec():
    return pl.BlockSpec(memory_space=pl.ANY)


def call(kernel, ins, outs, token, scalars=()):
    tokens = [] if token is None else [token]

    def body(*refs):
        count = len(scalars) + len(ins)
        kernel(*refs[:count], *refs[count + len(tokens) :])

    return pl.pallas_call(
        body,
        in_specs=[SMEM] * len(scalars) + [VMEM] * len(ins) + [token_spec()] * len(tokens),
        out_specs=[VMEM] * len(outs),
        out_shape=[jax.ShapeDtypeStruct(shape, kind) for shape, kind in outs],
        compiler_params=pltpu.CompilerParams(vmem_limit_bytes=LIMIT),
        cost_estimate=STEP_COST,
    )(*scalars, *ins, *tokens)


def rows_of(own_ref, got_ref, length):
    return jnp.concatenate(
        [own_ref[:length].astype(BF16), got_ref[:length].astype(BF16)], axis=1
    )


def put_tail(out_ref, own_ref, got_ref, length):
    out_ref[length:] = jnp.zeros((8, out_ref.shape[1]), F32)
    out_ref[length:, :HEAD_DIM] = own_ref[length:, :HEAD_DIM] + got_ref[length:, :HEAD_DIM]


def first_spread(index, length, own, got, own_w, other_w, token):
    inner, cols = own_w.shape
    height = length + (8 if index == 0 else 0)

    def kernel(own_ref, got_ref, own_w_ref, other_w_ref, out_ref, pair_ref):
        pair_ref[:inner] = own_w_ref[...]
        pair_ref[inner:] = other_w_ref[...].astype(BF16)
        out_ref[:length] = dot32(rows_of(own_ref, got_ref, length), pair_ref[...])
        if index == 0:
            put_tail(out_ref, own_ref, got_ref, length)

    outs = [((height, cols), F32), ((2 * inner, cols), BF16)]
    return call(kernel, [own, got, own_w, other_w], outs, token)


def spread(index, length, own, got, pair, token):
    height = length + (8 if index == 0 else 0)

    def kernel(own_ref, got_ref, pair_ref, out_ref):
        out_ref[:length] = dot32(rows_of(own_ref, got_ref, length), pair_ref[...])
        if index == 0:
            put_tail(out_ref, own_ref, got_ref, length)

    return call(kernel, [own, got, pair], [((height, pair.shape[1]), F32)], token)[0]


def add(first, second, token):
    def kernel(first_ref, second_ref, out_ref):
        out_ref[...] = first_ref[...] + second_ref[: first_ref.shape[0]]

    return call(kernel, [first, second], [(first.shape, F32)], token)[0]


def add_and_pick(first, second, ends, outer, token):
    def kernel(ends_ref, first_ref, second_ref, outer_ref, sum_ref, sent_ref):
        total = first_ref[...] + second_ref[...]
        sum_ref[...] = total
        rows = outer_ref.shape[0]
        sent_ref[:rows] = jnp.where(ends_ref[0] > 0, outer_ref[...], total[:rows])
        if total.shape[0] > rows:
            sent_ref[rows:] = total[rows:]

    outs = [(first.shape, F32)] * 2
    return call(kernel, [first, second, outer], outs, token, [ends])


def gather(index, length, ends, got, held, pair, sums, limit, gap, token):
    inner = pair.shape[0] // 2
    extra = [] if gap is None else [gap]

    def kernel(ends_ref, limit_ref, got_ref, held_ref, pair_ref, *refs):
        refs = list(refs)
        gap_ref = refs.pop(0) if gap is not None else None
        before = [refs.pop(0), refs.pop(0)] if index else None
        own_ref, other_ref = refs[:2]
        total = jnp.where(ends_ref[0] > 0, got_ref[...], held_ref[...])
        total = total[: length + (8 if index == 0 else 0)]
        if index == 0:
            refs[2][...] = total[length:, :128]
            total = total[:length]
        if gap_ref is not None:
            kept = rows_below(limit_ref[0], length, total.shape[1])
            total = jnp.where(kept, total + gap_ref[...], 0.0)
        rounded = total.astype(BF16)
        own = dot_nt(rounded, pair_ref[:inner])
        other = dot_nt(rounded, pair_ref[inner:])
        squares = jnp.full((8, inner), jnp.sum(total * total), F32)
        if index:
            own = own + before[0][...]
            other = other + before[1][:length]
            squares = squares + before[1][length:]
        own_ref[...] = own
        other_ref[:length] = other
        other_ref[length:] = squares

    outs = [((length, inner), F32), ((length + 8, inner), F32)]
    if index == 0:
        outs.append(((8, 128), F32))
    return call(kernel, [got, held, pair] + extra + sums, outs, token, [ends, limit])


def cotangent_kernel(
    share, limit_ref, own_ref, other_ref, got_ref, soft_ref, key_ref, value_ref, down_q_ref,
    down_v_ref, out_ref,
):
    length, inner = own_ref.shape
    rank = down_q_ref.shape[1]
    live = live_pairs(limit_ref[0], length)
    pulled = (own_ref[...] + got_ref[:length]).astype(BF16)
    out_ref[2 * rank :] = other_ref[length:] + got_ref[length:]
    for h in range(inner // HEAD_DIM):
        soft = soft_ref[h]
        rows = pulled[:, head(h)]
        d_probs = dot_nt(rows, value_ref[:, head(h)]).astype(BF16).astype(F32)
        d_value = dot_tn(soft.astype(BF16), rows).astype(BF16).astype(F32)
        d_scores = soft * (d_probs - jnp.sum(soft * d_probs, axis=-1, keepdims=True))
        d_scores = jnp.where(live, d_scores, 0.0) * SCALE
        d_query = dot32(d_scores.astype(BF16), key_ref[:, head(h)]).astype(BF16).astype(F32)
        out_ref[:rank, head(h)] = share * lax.dot_general(
            down_q_ref[...], d_query, (((0,), (0,)), ((), ())), precision=HIGH,
            preferred_element_type=F32,
        )
        out_ref[rank : 2 * rank, head(h)] = share * lax.dot_general(
            down_v_ref[...], d_value, (((0,), (0,)), ((), ())), precision=HIGH,
            preferred_element_type=F32,
        )


def cotangent(share, limit, own, other, got, attention):
    inner = own.shape[1]
    rank = attention[3].shape[1]
    return pl.pallas_call(
        functools.partial(cotangent_kernel, share),
        in_specs=[SMEM] + [VMEM] * 8,
        out_specs=VMEM,
        out_shape=jax.ShapeDtypeStruct((2 * rank + 8, inner), F32),
        compiler_params=pltpu.CompilerParams(vmem_limit_bytes=LIMIT),
    )(limit, own, other, got, *attention)


def tangent_of(vector, limit, soft_ref, key_ref, value_ref, down_q_ref, down_v_ref, out_ref):
    length = key_ref.shape[0]
    rank = down_q_ref.shape[1]
    live = live_pairs(limit, length)
    kept = rows_below(limit, length, HEAD_DIM)
    d_query = (ADAPTER_SCALE * high(down_q_ref[...], vector[:rank])).astype(BF16)
    d_value = (ADAPTER_SCALE * high(down_v_ref[...], vector[rank:])).astype(BF16)
    for h in range(key_ref.shape[1] // HEAD_DIM):
        soft = soft_ref[h]
        d_scores = dot_nt(d_query[:, head(h)], key_ref[:, head(h)]) * SCALE
        d_scores = jnp.where(live, d_scores, 0.0)
        d_probs = soft * (d_scores - jnp.sum(soft * d_scores, axis=-1, keepdims=True))
        d_mixed = dot32(d_probs.astype(BF16), value_ref[:, head(h)]) + dot32(
            soft.astype(BF16), d_value[:, head(h)]
        )
        out_ref[:length, head(h)] = jnp.where(kept, d_mixed.astype(BF16).astype(F32), 0.0)


def total_of(terms):
    while len(terms) > 1:
        terms = [terms[i] + terms[i + 1] for i in range(0, len(terms), 2)]
    return terms[0]


def put_sums(out_ref, remain, image):
    lane = lax.broadcasted_iota(jnp.int32, (8, out_ref.shape[1]), 1)
    cross = 0.0 if image is None else jnp.sum(remain * image)
    out_ref[out_ref.shape[0] - 8 :] = jnp.where(lane == 0, jnp.sum(remain * remain), cross)


def first_kernel(n_dp, *refs):
    terms, refs = refs[:n_dp], refs[n_dp:]
    limit_ref, *attention, remain_ref, out_ref = refs
    grads = total_of([term[...] for term in terms])
    remain = -grads[: remain_ref.shape[0]]
    remain_ref[...] = remain
    put_sums(out_ref, remain, None)
    tangent_of(remain, limit_ref[0], *attention, out_ref)


def first_step(terms, limit, attention):
    inner = terms[0].shape[1]
    length = attention[1].shape[0]
    rank = attention[3].shape[1]
    return pl.pallas_call(
        functools.partial(first_kernel, len(terms)),
        in_specs=[VMEM] * len(terms) + [SMEM] + [VMEM] * 5,
        out_specs=[VMEM] * 2,
        out_shape=[
            jax.ShapeDtypeStruct((2 * rank, inner), F32),
            jax.ShapeDtypeStruct((length + 8, inner), F32),
        ],
        compiler_params=pltpu.CompilerParams(vmem_limit_bytes=LIMIT),
    )(*terms, limit, *attention)


def step_kernel(n_dp, token_count, index, last, *refs):
    terms, refs = refs[:n_dp], refs[n_dp:]
    sums_ref, remain_ref, *refs = refs
    if index:
        before_ref, newton_ref, direction_ref, image_ref, *refs = refs
    part = total_of([term[...] for term in terms])
    remain = remain_ref[...]
    rows = remain.shape[0]
    norm, cross = sums_ref[:1, 0:1], sums_ref[:1, 1:2]
    fresh = part[:rows] + DAMP * remain
    curv = part[rows : rows + 1, 0:1] / token_count + DAMP * norm
    if index:
        ratio = norm / before_ref[:1, 0:1]
        curv = curv + 2.0 * ratio * cross + ratio * ratio * before_ref[:1, 1:2]
        direction = remain + ratio * direction_ref[...]
        image = fresh + ratio * image_ref[...]
    else:
        direction, image = remain, fresh
    alpha = norm / curv
    newton = alpha * direction
    if index:
        newton = newton_ref[...] + newton
    remain = remain - alpha * image
    if last:
        step_q_ref, step_v_ref, remain_q_ref, remain_v_ref = refs
        rank = rows // 2
        step_q_ref[...] = newton[:rank]
        step_v_ref[...] = newton[rank:]
        remain_q_ref[...] = remain[:rank]
        remain_v_ref[...] = remain[rank:]
        return
    limit_ref, *refs = refs
    attention, refs = refs[:5], refs[5:]
    next_remain, next_before, next_newton, next_direction, next_image, out_ref = refs
    lane = lax.broadcasted_iota(jnp.int32, next_before.shape, 1)
    next_remain[...] = remain
    next_before[...] = jnp.where(lane == 0, norm, curv)
    next_newton[...] = newton
    next_direction[...] = direction
    next_image[...] = image
    put_sums(out_ref, remain, image)
    tangent_of(remain, limit_ref[0], *attention, out_ref)


def cg_step(index, token_count, terms, sums, remain, state, limit, attention):
    last = index == CG_STEPS - 1
    rows, inner = remain.shape
    matrix = jax.ShapeDtypeStruct((rows, inner), F32)
    scalars = jax.ShapeDtypeStruct((8, 128), F32)
    args = [*terms, sums, remain, *state]
    specs = [VMEM] * len(args)
    if last:
        shapes = [jax.ShapeDtypeStruct((rows // 2, inner), F32)] * 4
    else:
        args += [limit, *attention]
        specs += [SMEM] + [VMEM] * 5
        length = attention[1].shape[0]
        shapes = [matrix, scalars, matrix, matrix, matrix]
        shapes.append(jax.ShapeDtypeStruct((length + 8, inner), F32))
    return pl.pallas_call(
        functools.partial(step_kernel, len(terms), token_count, index, last),
        in_specs=specs,
        out_specs=[VMEM] * len(shapes),
        out_shape=shapes,
        compiler_params=pltpu.CompilerParams(vmem_limit_bytes=LIMIT),
    )(*args)


def on_device(
    inputs,
    targets,
    lengths,
    ln_gain,
    ln_bias,
    query_weight,
    w_key,
    value_weight,
    w_out,
    down_query,
    down_value,
    query_up_factor,
    value_up_factor,
):
    length, width = inputs.shape
    n_dp = lax.axis_size("dp")
    n_chip = lax.axis_size("chip")
    core = lax.axis_index("core")
    chip = lax.axis_index("chip")
    token_count = length * n_dp
    half = width // 2

    def swap(part):
        return lax.ppermute(part, "core", [(0, 1), (1, 0)])

    def data_terms(part):
        step = 1
        while 2 * step < n_dp:
            part = part + lax.ppermute(part, "dp", [(d, d ^ step) for d in range(n_dp)])
            step *= 2
        return [part, lax.ppermute(part, "dp", [(d, d ^ step) for d in range(n_dp)])]

    where = core.astype(jnp.int32)[None]
    own_w, other_w = split(where, w_out)
    other_w = [swap(part) for part in other_w]
    cols = half // CHUNKS
    gap = lax.dynamic_slice_in_dim(inputs, core * half, half, 1).astype(F32)
    gap = gap - lax.dynamic_slice_in_dim(targets, core * half, half, 1).astype(F32)

    soft, key, value, down_q, down_v, mixed = project(
        lengths, inputs, ln_gain, ln_bias, query_weight, w_key, value_weight, down_query,
        down_value, query_up_factor, value_up_factor,
    )
    attention = (soft, key, value, down_q, down_v)

    ends = ((chip == 0) | (chip == n_chip - 1)).astype(jnp.int32)[None]

    def outer_swap(part):
        return lax.ppermute(part, "chip", [(0, 1), (1, 0), (2, 3), (3, 2)])

    def inner_swap(part):
        hops = [(2, 4), (4, 2), (3, 5), (5, 3), (0, 1), (1, 0), (6, 7), (7, 6)]
        return lax.ppermute(part, ("chip", "core"), hops)

    def product(rows, pairs):
        got_rows = swap(rows)
        first = not pairs
        pairs.extend([None] * (CHUNKS - len(pairs)))
        parts, scalars = [], None
        own_part, total, outer, inner = {}, {}, {}, {}
        token = None

        def begin(k):
            if first:
                own_part[k], pairs[k] = first_spread(
                    k, length, rows, got_rows, own_w[k], other_w[k], token
                )
            else:
                own_part[k] = spread(k, length, rows, got_rows, pairs[k], token)
            return own_part[k]

        def finish(k, got):
            gap_part = gap[:, k * cols : (k + 1) * cols] if first else None
            return gather(k, length, ends, got, total[k], pairs[k], parts, lengths, gap_part, token)

        if n_chip != 4:
            for k in range(CHUNKS):
                token = begin(k)
            for k in range(CHUNKS):
                total[k] = lax.psum(own_part[k], "chip")
                out = finish(k, total[k])
                parts, scalars = list(out[:2]), out[2] if k == 0 else scalars
        else:
            for k in [0, 1, 2] if first else [0, *range(2, CHUNKS), 1]:
                token = begin(k)
            for k in (0, 1):
                outer[k] = outer_swap(own_part[k])
            for tick in range(CHUNKS + 3):
                if tick < CHUNKS:
                    own_part[tick] = add(own_part[tick], outer[tick], token)
                    token = own_part[tick]
                    inner[tick] = inner_swap(token)
                later = tick + 2
                if tick == CHUNKS:
                    out = finish(tick - 3, outer[tick])
                    parts = list(out[:2])
                    token = parts[0]
                if 1 <= tick <= CHUNKS:
                    k = tick - 1
                    if later < CHUNKS:
                        total[k], sent = add_and_pick(
                            own_part[k], inner[k], ends, own_part[later], token
                        )
                    else:
                        total[k] = sent = add(own_part[k], inner[k], token)
                    token = sent
                    outer[later] = outer_swap(sent)
                elif tick == 0:
                    outer[later] = outer_swap(own_part[later])
                if tick + 3 < CHUNKS and first:
                    token = begin(tick + 3)
                if tick >= 3 and tick != CHUNKS:
                    out = finish(tick - 3, outer[tick])
                    parts, scalars = list(out[:2]), out[2] if tick == 3 else scalars
                    token = parts[0]
        own, other = parts
        share = ADAPTER_SCALE / token_count
        part = cotangent(share, lengths, own, other, swap(other), attention)
        return data_terms(part), scalars

    pairs = []
    terms, _ = product(mixed, pairs)
    remain, rows = first_step(terms, lengths, attention)
    state = ()
    for index in range(CG_STEPS):
        terms, sums = product(rows, pairs)
        out = cg_step(index, token_count, terms, sums, remain, state, lengths, attention)
        if index < CG_STEPS - 1:
            remain, *state, rows = out
    return tuple(out)


def solution(mesh):
    fine = Mesh(mesh.devices.reshape(mesh.shape["dp"], -1, 2), ("dp", "chip", "core"))
    tensor = ("chip", "core")
    in_specs = (
        P("dp", None),
        P("dp", None),
        P("dp"),
        P(),
        P(),
        P(None, tensor),
        P(None, tensor),
        P(None, tensor),
        P(tensor, None),
        P(),
        P(),
        P(None, tensor),
        P(None, tensor),
    )
    out_specs = (P(None, tensor),) * 4
    return jax.shard_map(
        on_device, mesh=fine, in_specs=in_specs, out_specs=out_specs, check_vma=False
    )
```

```python
import functools

import jax
import jax.numpy as jnp
from jax import lax
from jax.experimental import pallas as pl
from jax.experimental.pallas import tpu as pltpu
from jax.sharding import Mesh
from jax.sharding import PartitionSpec as P

HEAD_DIM = 128
CG_STEPS = 3
CHUNKS = 8
DEPTH = 1024

EPS = 1e-05
ADAPTER_SCALE = 2.0
DAMP = 0.05
NEG = -1e30
F32 = jnp.float32
BF16 = jnp.bfloat16
HIGH = lax.Precision.HIGHEST
SCALE = HEAD_DIM ** (-0.5)
VMEM = pl.BlockSpec(memory_space=pltpu.VMEM)
SMEM = pl.BlockSpec(memory_space=pltpu.SMEM)
LIMIT = 16 * 1024 * 1024
STEP_COST = pl.CostEstimate(flops=10**9, bytes_accessed=10**7, transcendentals=0)
STREAM_LIMIT = 50 * 1024 * 1024


def dot32(first, second):
    return jnp.dot(first, second, preferred_element_type=F32)


def dot_nt(first, second):
    return lax.dot_general(
        first, second, (((1,), (1,)), ((), ())), preferred_element_type=F32
    )


def dot_tn(first, second):
    return lax.dot_general(
        first, second, (((0,), (0,)), ((), ())), preferred_element_type=F32
    )


def high(first, second):
    return jnp.dot(first, second, precision=HIGH, preferred_element_type=F32)


def head(index):
    return slice(index * HEAD_DIM, (index + 1) * HEAD_DIM)


def rows_below(limit, length, width):
    return lax.broadcasted_iota(jnp.int32, (length, width), 0) < limit


def live_pairs(limit, length):
    row = lax.broadcasted_iota(jnp.int32, (length, length), 0)
    column = lax.broadcasted_iota(jnp.int32, (length, length), 1)
    return (column <= row) & (column < limit)


def split_kernel(core_ref, w_ref, *refs):
    own_refs, other_refs = refs[:CHUNKS], refs[CHUNKS : 2 * CHUNKS]
    landed, own_sem, other_sem = refs[2 * CHUNKS :]
    cols = own_refs[0].shape[1]
    half = CHUNKS * cols
    core = core_ref[0]

    def own_copy(k):
        start = pl.multiple_of(core * half + k * cols, HEAD_DIM)
        return pltpu.make_async_copy(
            w_ref.at[:, pl.ds(start, cols)], own_refs[k], own_sem.at[k]
        )

    def other_copy(k):
        start = pl.multiple_of((1 - core) * half + k * cols, HEAD_DIM)
        return pltpu.make_async_copy(
            w_ref.at[:, pl.ds(start, cols)], landed.at[k], other_sem.at[k]
        )

    for k in range(CHUNKS):
        other_copy(k).start()
    for k in range(CHUNKS):
        own_copy(k).start()
    for k in range(CHUNKS):
        other_copy(k).wait()
        other_refs[k][...] = landed[k].astype(F32)
    for k in range(CHUNKS):
        own_copy(k).wait()


def split(core, w_out):
    inner, width = w_out.shape
    cols = width // 2 // CHUNKS
    out = pl.pallas_call(
        split_kernel,
        in_specs=[SMEM, pl.BlockSpec(memory_space=pltpu.HBM)],
        out_specs=[VMEM] * (2 * CHUNKS),
        out_shape=[jax.ShapeDtypeStruct((inner, cols), BF16)] * CHUNKS
        + [jax.ShapeDtypeStruct((inner, cols), F32)] * CHUNKS,
        scratch_shapes=[
            pltpu.VMEM((CHUNKS, inner, cols), BF16),
            pltpu.SemaphoreType.DMA((CHUNKS,)),
            pltpu.SemaphoreType.DMA((CHUNKS,)),
        ],
        compiler_params=pltpu.CompilerParams(vmem_limit_bytes=LIMIT),
    )(core, w_out)
    return out[:CHUNKS], out[CHUNKS:]


def project_kernel(
    limit_ref, x_ref, wq_ref, wk_ref, wv_ref, gain_ref, bias_ref, aq_ref, av_ref, bq_ref, bv_ref,
    soft_ref, key_ref, value_ref, down_q_ref, down_v_ref, mixed_ref,
    rows_in, normed, wq_in, wk_in, wv_in, rows_sem, weight_sem,
):
    length, width = normed.shape
    inner = key_ref.shape[1]
    blocks = [slice(i, i + DEPTH) for i in range(0, width, DEPTH)]
    rows_copy = pltpu.make_async_copy(x_ref, rows_in, rows_sem)
    rows_copy.start()
    copies = []
    for i, block in enumerate(blocks):
        for j, (source, target) in enumerate(
            [(wq_ref, wq_in), (wk_ref, wk_in), (wv_ref, wv_in)]
        ):
            copies.append(
                pltpu.make_async_copy(
                    source.at[block], target.at[block], weight_sem.at[3 * i + j]
                )
            )
            copies[-1].start()
    rows_copy.wait()
    total = jnp.zeros((length, 1), F32)
    for block in blocks:
        total = total + jnp.sum(rows_in[:, block].astype(F32), axis=-1, keepdims=True)
    mean = total / width
    total = jnp.zeros((length, 1), F32)
    for block in blocks:
        centred = rows_in[:, block].astype(F32) - mean
        total = total + jnp.sum(centred * centred, axis=-1, keepdims=True)
    spread = lax.rsqrt(total / width + EPS)
    for block in blocks:
        centred = rows_in[:, block].astype(F32) - mean
        full = centred * spread * gain_ref[:, block] + bias_ref[:, block]
        normed[:, block] = full.astype(BF16)
    query = jnp.zeros((length, inner), F32)
    key = jnp.zeros((length, inner), F32)
    value = jnp.zeros((length, inner), F32)
    for i, block in enumerate(blocks):
        part = normed[:, block]
        for j in range(3):
            copies[3 * i + j].wait()
        query = query + dot32(part, wq_in[block])
        key = key + dot32(part, wk_in[block])
        value = value + dot32(part, wv_in[block])
    down_q = dot_nt(normed[...], aq_ref[...])
    down_v = dot_nt(normed[...], av_ref[...])
    down_q_ref[...] = down_q
    down_v_ref[...] = down_v
    limit = limit_ref[0]
    live = live_pairs(limit, length)
    kept = rows_below(limit, length, HEAD_DIM)
    query = (query + ADAPTER_SCALE * high(down_q, bq_ref[...])).astype(BF16)
    value = (value + ADAPTER_SCALE * high(down_v, bv_ref[...])).astype(BF16)
    key = key.astype(BF16)
    key_ref[...] = key
    value_ref[...] = value
    for h in range(inner // HEAD_DIM):
        scores = dot_nt(query[:, head(h)], key[:, head(h)]) * SCALE
        scores = jnp.where(live, scores, NEG)
        weights = jnp.exp(scores - jnp.max(scores, axis=-1, keepdims=True))
        soft = weights / jnp.sum(weights, axis=-1, keepdims=True)
        soft_ref[h] = soft
        mixed = dot32(soft.astype(BF16), value[:, head(h)]).astype(BF16)
        mixed_ref[:length, head(h)] = jnp.where(kept, mixed.astype(F32), 0.0)
    mixed_ref[length:] = jnp.zeros((8, inner), F32)


def project(limit, x, gain, bias, wq, wk, wv, aq, av, bq, bv):
    length, width = x.shape
    inner = wq.shape[1]
    rank = aq.shape[1]
    heads = inner // HEAD_DIM
    hbm = pl.BlockSpec(memory_space=pltpu.HBM)
    return pl.pallas_call(
        project_kernel,
        in_specs=[SMEM] + [hbm] * 4 + [VMEM] * 6,
        out_specs=[VMEM] * 6,
        out_shape=[
            jax.ShapeDtypeStruct((heads, length, length), F32),
            jax.ShapeDtypeStruct((length, inner), BF16),
            jax.ShapeDtypeStruct((length, inner), BF16),
            jax.ShapeDtypeStruct((length, rank), F32),
            jax.ShapeDtypeStruct((length, rank), F32),
            jax.ShapeDtypeStruct((length + 8, inner), F32),
        ],
        scratch_shapes=[
            pltpu.VMEM((length, width), BF16),
            pltpu.VMEM((length, width), BF16),
            pltpu.VMEM((width, inner), BF16),
            pltpu.VMEM((width, inner), BF16),
            pltpu.VMEM((width, inner), BF16),
            pltpu.SemaphoreType.DMA,
            pltpu.SemaphoreType.DMA((3 * (width // DEPTH),)),
        ],
        compiler_params=pltpu.CompilerParams(vmem_limit_bytes=STREAM_LIMIT),
        cost_estimate=pl.CostEstimate(
            flops=6 * length * width * inner, bytes_accessed=6 * width * inner, transcendentals=0
        ),
    )(limit, x, wq, wk, wv, gain[None], bias[None], aq.T, av.T, bq, bv)


def token_spec():
    return pl.BlockSpec(memory_space=pl.ANY)


def call(kernel, ins, outs, token, scalars=()):
    tokens = [] if token is None else [token]

    def body(*refs):
        count = len(scalars) + len(ins)
        kernel(*refs[:count], *refs[count + len(tokens) :])

    return pl.pallas_call(
        body,
        in_specs=[SMEM] * len(scalars) + [VMEM] * len(ins) + [token_spec()] * len(tokens),
        out_specs=[VMEM] * len(outs),
        out_shape=[jax.ShapeDtypeStruct(shape, kind) for shape, kind in outs],
        compiler_params=pltpu.CompilerParams(vmem_limit_bytes=LIMIT),
        cost_estimate=STEP_COST,
    )(*scalars, *ins, *tokens)


def rows_of(own_ref, got_ref, length):
    return jnp.concatenate(
        [own_ref[:length].astype(BF16), got_ref[:length].astype(BF16)], axis=1
    )


def put_tail(out_ref, own_ref, got_ref, length):
    out_ref[length:] = jnp.zeros((8, out_ref.shape[1]), F32)
    out_ref[length:, :HEAD_DIM] = own_ref[length:, :HEAD_DIM] + got_ref[length:, :HEAD_DIM]


def first_spread(index, length, own, got, own_w, other_w, token):
    inner, cols = own_w.shape
    height = length + (8 if index == 0 else 0)

    def kernel(own_ref, got_ref, own_w_ref, other_w_ref, out_ref, pair_ref):
        pair_ref[:inner] = own_w_ref[...]
        pair_ref[inner:] = other_w_ref[...].astype(BF16)
        out_ref[:length] = dot32(rows_of(own_ref, got_ref, length), pair_ref[...])
        if index == 0:
            put_tail(out_ref, own_ref, got_ref, length)

    outs = [((height, cols), F32), ((2 * inner, cols), BF16)]
    return call(kernel, [own, got, own_w, other_w], outs, token)


def spread(index, length, own, got, pair, token):
    height = length + (8 if index == 0 else 0)

    def kernel(own_ref, got_ref, pair_ref, out_ref):
        out_ref[:length] = dot32(rows_of(own_ref, got_ref, length), pair_ref[...])
        if index == 0:
            put_tail(out_ref, own_ref, got_ref, length)

    return call(kernel, [own, got, pair], [((height, pair.shape[1]), F32)], token)[0]


def add(first, second, token):
    def kernel(first_ref, second_ref, out_ref):
        out_ref[...] = first_ref[...] + second_ref[: first_ref.shape[0]]

    return call(kernel, [first, second], [(first.shape, F32)], token)[0]


def add_and_pick(first, second, ends, outer, token):
    def kernel(ends_ref, first_ref, second_ref, outer_ref, sum_ref, sent_ref):
        total = first_ref[...] + second_ref[...]
        sum_ref[...] = total
        rows = outer_ref.shape[0]
        sent_ref[:rows] = jnp.where(ends_ref[0] > 0, outer_ref[...], total[:rows])
        if total.shape[0] > rows:
            sent_ref[rows:] = total[rows:]

    outs = [(first.shape, F32)] * 2
    return call(kernel, [first, second, outer], outs, token, [ends])


def gather(index, length, ends, got, held, pair, sums, limit, gap, token):
    inner = pair.shape[0] // 2
    extra = [] if gap is None else [gap]

    def kernel(ends_ref, limit_ref, got_ref, held_ref, pair_ref, *refs):
        refs = list(refs)
        gap_ref = refs.pop(0) if gap is not None else None
        before = [refs.pop(0), refs.pop(0)] if index else None
        own_ref, other_ref = refs[:2]
        total = jnp.where(ends_ref[0] > 0, got_ref[...], held_ref[...])
        total = total[: length + (8 if index == 0 else 0)]
        if index == 0:
            refs[2][...] = total[length:, :128]
            total = total[:length]
        if gap_ref is not None:
            kept = rows_below(limit_ref[0], length, total.shape[1])
            total = jnp.where(kept, total + gap_ref[...], 0.0)
        rounded = total.astype(BF16)
        own = dot_nt(rounded, pair_ref[:inner])
        other = dot_nt(rounded, pair_ref[inner:])
        squares = jnp.full((8, inner), jnp.sum(total * total), F32)
        if index:
            own = own + before[0][...]
            other = other + before[1][:length]
            squares = squares + before[1][length:]
        own_ref[...] = own
        other_ref[:length] = other
        other_ref[length:] = squares

    outs = [((length, inner), F32), ((length + 8, inner), F32)]
    if index == 0:
        outs.append(((8, 128), F32))
    return call(kernel, [got, held, pair] + extra + sums, outs, token, [ends, limit])


def cotangent_kernel(
    share, limit_ref, own_ref, other_ref, got_ref, soft_ref, key_ref, value_ref, down_q_ref,
    down_v_ref, out_ref,
):
    length, inner = own_ref.shape
    rank = down_q_ref.shape[1]
    live = live_pairs(limit_ref[0], length)
    pulled = (own_ref[...] + got_ref[:length]).astype(BF16)
    out_ref[2 * rank :] = other_ref[length:] + got_ref[length:]
    for h in range(inner // HEAD_DIM):
        soft = soft_ref[h]
        rows = pulled[:, head(h)]
        d_probs = dot_nt(rows, value_ref[:, head(h)]).astype(BF16).astype(F32)
        d_value = dot_tn(soft.astype(BF16), rows).astype(BF16).astype(F32)
        d_scores = soft * (d_probs - jnp.sum(soft * d_probs, axis=-1, keepdims=True))
        d_scores = jnp.where(live, d_scores, 0.0) * SCALE
        d_query = dot32(d_scores.astype(BF16), key_ref[:, head(h)]).astype(BF16).astype(F32)
        out_ref[:rank, head(h)] = share * lax.dot_general(
            down_q_ref[...], d_query, (((0,), (0,)), ((), ())), precision=HIGH,
            preferred_element_type=F32,
        )
        out_ref[rank : 2 * rank, head(h)] = share * lax.dot_general(
            down_v_ref[...], d_value, (((0,), (0,)), ((), ())), precision=HIGH,
            preferred_element_type=F32,
        )


def cotangent(share, limit, own, other, got, attention):
    inner = own.shape[1]
    rank = attention[3].shape[1]
    return pl.pallas_call(
        functools.partial(cotangent_kernel, share),
        in_specs=[SMEM] + [VMEM] * 8,
        out_specs=VMEM,
        out_shape=jax.ShapeDtypeStruct((2 * rank + 8, inner), F32),
        compiler_params=pltpu.CompilerParams(vmem_limit_bytes=LIMIT),
    )(limit, own, other, got, *attention)


def tangent_of(vector, limit, soft_ref, key_ref, value_ref, down_q_ref, down_v_ref, out_ref):
    length = key_ref.shape[0]
    rank = down_q_ref.shape[1]
    live = live_pairs(limit, length)
    kept = rows_below(limit, length, HEAD_DIM)
    d_query = (ADAPTER_SCALE * high(down_q_ref[...], vector[:rank])).astype(BF16)
    d_value = (ADAPTER_SCALE * high(down_v_ref[...], vector[rank:])).astype(BF16)
    for h in range(key_ref.shape[1] // HEAD_DIM):
        soft = soft_ref[h]
        d_scores = dot_nt(d_query[:, head(h)], key_ref[:, head(h)]) * SCALE
        d_scores = jnp.where(live, d_scores, 0.0)
        d_probs = soft * (d_scores - jnp.sum(soft * d_scores, axis=-1, keepdims=True))
        d_mixed = dot32(d_probs.astype(BF16), value_ref[:, head(h)]) + dot32(
            soft.astype(BF16), d_value[:, head(h)]
        )
        out_ref[:length, head(h)] = jnp.where(kept, d_mixed.astype(BF16).astype(F32), 0.0)


def total_of(terms):
    while len(terms) > 1:
        terms = [terms[i] + terms[i + 1] for i in range(0, len(terms), 2)]
    return terms[0]


def put_sums(out_ref, remain, image):
    lane = lax.broadcasted_iota(jnp.int32, (8, out_ref.shape[1]), 1)
    cross = 0.0 if image is None else jnp.sum(remain * image)
    out_ref[out_ref.shape[0] - 8 :] = jnp.where(lane == 0, jnp.sum(remain * remain), cross)


def first_kernel(n_dp, *refs):
    terms, refs = refs[:n_dp], refs[n_dp:]
    limit_ref, *attention, remain_ref, out_ref = refs
    grads = total_of([term[...] for term in terms])
    remain = -grads[: remain_ref.shape[0]]
    remain_ref[...] = remain
    put_sums(out_ref, remain, None)
    tangent_of(remain, limit_ref[0], *attention, out_ref)


def first_step(terms, limit, attention):
    inner = terms[0].shape[1]
    length = attention[1].shape[0]
    rank = attention[3].shape[1]
    return pl.pallas_call(
        functools.partial(first_kernel, len(terms)),
        in_specs=[VMEM] * len(terms) + [SMEM] + [VMEM] * 5,
        out_specs=[VMEM] * 2,
        out_shape=[
            jax.ShapeDtypeStruct((2 * rank, inner), F32),
            jax.ShapeDtypeStruct((length + 8, inner), F32),
        ],
        compiler_params=pltpu.CompilerParams(vmem_limit_bytes=LIMIT),
    )(*terms, limit, *attention)


def step_kernel(n_dp, token_count, index, last, *refs):
    terms, refs = refs[:n_dp], refs[n_dp:]
    sums_ref, remain_ref, *refs = refs
    if index:
        before_ref, newton_ref, direction_ref, image_ref, *refs = refs
    part = total_of([term[...] for term in terms])
    remain = remain_ref[...]
    rows = remain.shape[0]
    norm, cross = sums_ref[:1, 0:1], sums_ref[:1, 1:2]
    fresh = part[:rows] + DAMP * remain
    curv = part[rows : rows + 1, 0:1] / token_count + DAMP * norm
    if index:
        ratio = norm / before_ref[:1, 0:1]
        curv = curv + 2.0 * ratio * cross + ratio * ratio * before_ref[:1, 1:2]
        direction = remain + ratio * direction_ref[...]
        image = fresh + ratio * image_ref[...]
    else:
        direction, image = remain, fresh
    alpha = norm / curv
    newton = alpha * direction
    if index:
        newton = newton_ref[...] + newton
    remain = remain - alpha * image
    if last:
        step_q_ref, step_v_ref, remain_q_ref, remain_v_ref = refs
        rank = rows // 2
        step_q_ref[...] = newton[:rank]
        step_v_ref[...] = newton[rank:]
        remain_q_ref[...] = remain[:rank]
        remain_v_ref[...] = remain[rank:]
        return
    limit_ref, *refs = refs
    attention, refs = refs[:5], refs[5:]
    next_remain, next_before, next_newton, next_direction, next_image, out_ref = refs
    lane = lax.broadcasted_iota(jnp.int32, next_before.shape, 1)
    next_remain[...] = remain
    next_before[...] = jnp.where(lane == 0, norm, curv)
    next_newton[...] = newton
    next_direction[...] = direction
    next_image[...] = image
    put_sums(out_ref, remain, image)
    tangent_of(remain, limit_ref[0], *attention, out_ref)


def cg_step(index, token_count, terms, sums, remain, state, limit, attention):
    last = index == CG_STEPS - 1
    rows, inner = remain.shape
    matrix = jax.ShapeDtypeStruct((rows, inner), F32)
    scalars = jax.ShapeDtypeStruct((8, 128), F32)
    args = [*terms, sums, remain, *state]
    specs = [VMEM] * len(args)
    if last:
        shapes = [jax.ShapeDtypeStruct((rows // 2, inner), F32)] * 4
    else:
        args += [limit, *attention]
        specs += [SMEM] + [VMEM] * 5
        length = attention[1].shape[0]
        shapes = [matrix, scalars, matrix, matrix, matrix]
        shapes.append(jax.ShapeDtypeStruct((length + 8, inner), F32))
    return pl.pallas_call(
        functools.partial(step_kernel, len(terms), token_count, index, last),
        in_specs=specs,
        out_specs=[VMEM] * len(shapes),
        out_shape=shapes,
        compiler_params=pltpu.CompilerParams(vmem_limit_bytes=LIMIT),
    )(*args)


def on_device(
    inputs,
    targets,
    lengths,
    ln_gain,
    ln_bias,
    query_weight,
    w_key,
    value_weight,
    w_out,
    down_query,
    down_value,
    query_up_factor,
    value_up_factor,
):
    length, width = inputs.shape
    n_dp = lax.axis_size("dp")
    n_chip = lax.axis_size("chip")
    core = lax.axis_index("core")
    chip = lax.axis_index("chip")
    token_count = length * n_dp
    half = width // 2

    def swap(part):
        return lax.ppermute(part, "core", [(0, 1), (1, 0)])

    def data_terms(part):
        step = 1
        while 2 * step < n_dp:
            part = part + lax.ppermute(part, "dp", [(d, d ^ step) for d in range(n_dp)])
            step *= 2
        return [part, lax.ppermute(part, "dp", [(d, d ^ step) for d in range(n_dp)])]

    where = core.astype(jnp.int32)[None]
    own_w, other_w = split(where, w_out)
    other_w = [swap(part) for part in other_w]
    cols = half // CHUNKS
    gap = lax.dynamic_slice_in_dim(inputs, core * half, half, 1).astype(F32)
    gap = gap - lax.dynamic_slice_in_dim(targets, core * half, half, 1).astype(F32)

    soft, key, value, down_q, down_v, mixed = project(
        lengths, inputs, ln_gain, ln_bias, query_weight, w_key, value_weight, down_query,
        down_value, query_up_factor, value_up_factor,
    )
    attention = (soft, key, value, down_q, down_v)

    ends = ((chip == 0) | (chip == n_chip - 1)).astype(jnp.int32)[None]

    def outer_swap(part):
        return lax.ppermute(part, "chip", [(0, 1), (1, 0), (2, 3), (3, 2)])

    def inner_swap(part):
        hops = [(2, 4), (4, 2), (3, 5), (5, 3), (0, 1), (1, 0), (6, 7), (7, 6)]
        return lax.ppermute(part, ("chip", "core"), hops)

    def product(rows, pairs):
        got_rows = swap(rows)
        first = not pairs
        pairs.extend([None] * (CHUNKS - len(pairs)))
        parts, scalars = [], None
        own_part, total, outer, inner = {}, {}, {}, {}
        token = None

        def begin(k):
            if first:
                own_part[k], pairs[k] = first_spread(
                    k, length, rows, got_rows, own_w[k], other_w[k], token
                )
            else:
                own_part[k] = spread(k, length, rows, got_rows, pairs[k], token)
            return own_part[k]

        def finish(k, got):
            gap_part = gap[:, k * cols : (k + 1) * cols] if first else None
            return gather(k, length, ends, got, total[k], pairs[k], parts, lengths, gap_part, token)

        if n_chip != 4:
            for k in range(CHUNKS):
                token = begin(k)
            for k in range(CHUNKS):
                total[k] = lax.psum(own_part[k], "chip")
                out = finish(k, total[k])
                parts, scalars = list(out[:2]), out[2] if k == 0 else scalars
        else:
            for k in [0, 1, 2] if first else [0, *range(2, CHUNKS), 1]:
                token = begin(k)
            for k in (0, 1):
                outer[k] = outer_swap(own_part[k])
            for tick in range(CHUNKS + 3):
                if tick < CHUNKS:
                    own_part[tick] = add(own_part[tick], outer[tick], token)
                    token = own_part[tick]
                    inner[tick] = inner_swap(token)
                later = tick + 2
                if tick == CHUNKS:
                    out = finish(tick - 3, outer[tick])
                    parts = list(out[:2])
                    token = parts[0]
                if 1 <= tick <= CHUNKS:
                    k = tick - 1
                    if later < CHUNKS:
                        total[k], sent = add_and_pick(
                            own_part[k], inner[k], ends, own_part[later], token
                        )
                    else:
                        total[k] = sent = add(own_part[k], inner[k], token)
                    token = sent
                    outer[later] = outer_swap(sent)
                elif tick == 0:
                    outer[later] = outer_swap(own_part[later])
                if tick + 3 < CHUNKS and first:
                    token = begin(tick + 3)
                if tick >= 3 and tick != CHUNKS:
                    out = finish(tick - 3, outer[tick])
                    parts, scalars = list(out[:2]), out[2] if tick == 3 else scalars
                    token = parts[0]
        own, other = parts
        share = ADAPTER_SCALE / token_count
        part = cotangent(share, lengths, own, other, swap(other), attention)
        return data_terms(part), scalars

    pairs = []
    terms, _ = product(mixed, pairs)
    remain, rows = first_step(terms, lengths, attention)
    state = ()
    for index in range(CG_STEPS):
        terms, sums = product(rows, pairs)
        out = cg_step(index, token_count, terms, sums, remain, state, lengths, attention)
        if index < CG_STEPS - 1:
            remain, *state, rows = out
    return tuple(out)


def solution(mesh):
    fine = Mesh(mesh.devices.reshape(mesh.shape["dp"], -1, 2), ("dp", "chip", "core"))
    tensor = ("chip", "core")
    in_specs = (
        P("dp", None),
        P("dp", None),
        P("dp"),
        P(),
        P(),
        P(None, tensor),
        P(None, tensor),
        P(None, tensor),
        P(tensor, None),
        P(),
        P(),
        P(None, tensor),
        P(None, tensor),
    )
    out_specs = (P(None, tensor),) * 4
    return jax.shard_map(
        on_device, mesh=fine, in_specs=in_specs, out_specs=out_specs, check_vma=False
    )
```

```python
import functools

import jax
import jax.numpy as jnp
from jax import lax
from jax.experimental import pallas as pl
from jax.experimental.pallas import tpu as pltpu
from jax.sharding import Mesh
from jax.sharding import PartitionSpec as P

HEAD_DIM = 128
CG_STEPS = 3
CHUNKS = 6
DEPTH = 1024

EPS = 1e-05
ADAPTER_SCALE = 2.0
DAMP = 0.05
NEG = -1e30
F32 = jnp.float32
BF16 = jnp.bfloat16
HIGH = lax.Precision.HIGHEST
SCALE = HEAD_DIM ** (-0.5)
VMEM = pl.BlockSpec(memory_space=pltpu.VMEM)
SMEM = pl.BlockSpec(memory_space=pltpu.SMEM)
LIMIT = 16 * 1024 * 1024
STEP_COST = pl.CostEstimate(flops=10**9, bytes_accessed=10**7, transcendentals=0)
STREAM_LIMIT = 54 * 1024 * 1024


def dot32(first, second):
    return jnp.dot(first, second, preferred_element_type=F32)


def dot_nt(first, second):
    return lax.dot_general(
        first, second, (((1,), (1,)), ((), ())), preferred_element_type=F32
    )


def dot_tn(first, second):
    return lax.dot_general(
        first, second, (((0,), (0,)), ((), ())), preferred_element_type=F32
    )


def high(first, second):
    return jnp.dot(first, second, precision=HIGH, preferred_element_type=F32)


def head(index):
    return slice(index * HEAD_DIM, (index + 1) * HEAD_DIM)


def rows_below(limit, length, width):
    return lax.broadcasted_iota(jnp.int32, (length, width), 0) < limit


def live_pairs(limit, length):
    row = lax.broadcasted_iota(jnp.int32, (length, length), 0)
    column = lax.broadcasted_iota(jnp.int32, (length, length), 1)
    return (column <= row) & (column < limit)


def split_kernel(chunks, half, core_ref, w_ref, token_ref, *refs):
    count = len(chunks)
    own_refs, other_refs = refs[:count], refs[count : 2 * count]
    landed, own_sem, other_sem = refs[2 * count :]
    cols = own_refs[0].shape[1]
    core = core_ref[0]

    def own_copy(i):
        start = pl.multiple_of(core * half + chunks[i] * cols, HEAD_DIM)
        return pltpu.make_async_copy(
            w_ref.at[:, pl.ds(start, cols)], own_refs[i], own_sem.at[i]
        )

    def other_copy(i):
        start = pl.multiple_of((1 - core) * half + chunks[i] * cols, HEAD_DIM)
        return pltpu.make_async_copy(
            w_ref.at[:, pl.ds(start, cols)], landed.at[i], other_sem.at[i]
        )

    for i in range(count):
        other_copy(i).start()
    for i in range(count):
        own_copy(i).start()
    for i in range(count):
        other_copy(i).wait()
        other_refs[i][...] = landed[i].astype(F32)
    for i in range(count):
        own_copy(i).wait()


def split(core, w_out, chunks, token):
    inner, width = w_out.shape
    half = width // 2
    cols = half // CHUNKS
    count = len(chunks)
    out = pl.pallas_call(
        functools.partial(split_kernel, tuple(chunks), half),
        in_specs=[SMEM, pl.BlockSpec(memory_space=pltpu.HBM), token_spec()],
        out_specs=[VMEM] * (2 * count),
        out_shape=[jax.ShapeDtypeStruct((inner, cols), BF16)] * count
        + [jax.ShapeDtypeStruct((inner, cols), F32)] * count,
        scratch_shapes=[
            pltpu.VMEM((count, inner, cols), BF16),
            pltpu.SemaphoreType.DMA((count,)),
            pltpu.SemaphoreType.DMA((count,)),
        ],
        compiler_params=pltpu.CompilerParams(vmem_limit_bytes=LIMIT),
        cost_estimate=STEP_COST,
    )(core, w_out, token)
    return out[:count], out[count:]


def project_kernel(
    limit_ref, x_ref, wq_ref, wk_ref, wv_ref, gain_ref, bias_ref, aq_ref, av_ref, bq_ref, bv_ref,
    soft_ref, key_ref, value_ref, down_q_ref, down_v_ref, mixed_ref,
    rows_in, normed, wq_in, wk_in, wv_in, rows_sem, weight_sem,
):
    length, width = normed.shape
    inner = key_ref.shape[1]
    blocks = [slice(i, i + DEPTH) for i in range(0, width, DEPTH)]
    rows_copy = pltpu.make_async_copy(x_ref, rows_in, rows_sem)
    rows_copy.start()
    copies = []
    for i, block in enumerate(blocks):
        for j, (source, target) in enumerate(
            [(wq_ref, wq_in), (wk_ref, wk_in), (wv_ref, wv_in)]
        ):
            copies.append(
                pltpu.make_async_copy(
                    source.at[block], target.at[block], weight_sem.at[3 * i + j]
                )
            )
            copies[-1].start()
    rows_copy.wait()
    total = jnp.zeros((length, 1), F32)
    for block in blocks:
        total = total + jnp.sum(rows_in[:, block].astype(F32), axis=-1, keepdims=True)
    mean = total / width
    total = jnp.zeros((length, 1), F32)
    for block in blocks:
        centred = rows_in[:, block].astype(F32) - mean
        total = total + jnp.sum(centred * centred, axis=-1, keepdims=True)
    spread = lax.rsqrt(total / width + EPS)
    for block in blocks:
        centred = rows_in[:, block].astype(F32) - mean
        full = centred * spread * gain_ref[:, block] + bias_ref[:, block]
        normed[:, block] = full.astype(BF16)
    down_q = dot_nt(normed[...], aq_ref[...])
    down_v = dot_nt(normed[...], av_ref[...])
    query = jnp.zeros((length, inner), F32)
    key = jnp.zeros((length, inner), F32)
    value = jnp.zeros((length, inner), F32)
    for i, block in enumerate(blocks):
        part = normed[:, block]
        for j in range(3):
            copies[3 * i + j].wait()
        query = query + dot32(part, wq_in[block])
        key = key + dot32(part, wk_in[block])
        value = value + dot32(part, wv_in[block])
    down_q_ref[...] = down_q
    down_v_ref[...] = down_v
    limit = limit_ref[0]
    live = live_pairs(limit, length)
    kept = rows_below(limit, length, HEAD_DIM)
    query = (query + ADAPTER_SCALE * high(down_q, bq_ref[...])).astype(BF16)
    value = (value + ADAPTER_SCALE * high(down_v, bv_ref[...])).astype(BF16)
    key = key.astype(BF16)
    key_ref[...] = key
    value_ref[...] = value
    for h in range(inner // HEAD_DIM):
        scores = dot_nt(query[:, head(h)], key[:, head(h)]) * SCALE
        scores = jnp.where(live, scores, NEG)
        weights = jnp.exp(scores - jnp.max(scores, axis=-1, keepdims=True))
        soft = weights / jnp.sum(weights, axis=-1, keepdims=True)
        soft_ref[h] = soft
        mixed = dot32(soft.astype(BF16), value[:, head(h)]).astype(BF16)
        mixed_ref[:length, head(h)] = jnp.where(kept, mixed.astype(F32), 0.0)
    mixed_ref[length:] = jnp.zeros((8, inner), F32)


def project(limit, x, gain, bias, wq, wk, wv, aq, av, bq, bv):
    length, width = x.shape
    inner = wq.shape[1]
    rank = aq.shape[1]
    heads = inner // HEAD_DIM
    hbm = pl.BlockSpec(memory_space=pltpu.HBM)
    return pl.pallas_call(
        project_kernel,
        in_specs=[SMEM] + [hbm] * 4 + [VMEM] * 6,
        out_specs=[VMEM] * 6,
        out_shape=[
            jax.ShapeDtypeStruct((heads, length, length), F32),
            jax.ShapeDtypeStruct((length, inner), BF16),
            jax.ShapeDtypeStruct((length, inner), BF16),
            jax.ShapeDtypeStruct((length, rank), F32),
            jax.ShapeDtypeStruct((length, rank), F32),
            jax.ShapeDtypeStruct((length + 8, inner), F32),
        ],
        scratch_shapes=[
            pltpu.VMEM((length, width), BF16),
            pltpu.VMEM((length, width), BF16),
            pltpu.VMEM((width, inner), BF16),
            pltpu.VMEM((width, inner), BF16),
            pltpu.VMEM((width, inner), BF16),
            pltpu.SemaphoreType.DMA,
            pltpu.SemaphoreType.DMA((3 * (width // DEPTH),)),
        ],
        compiler_params=pltpu.CompilerParams(vmem_limit_bytes=STREAM_LIMIT),
        cost_estimate=pl.CostEstimate(
            flops=6 * length * width * inner, bytes_accessed=6 * width * inner, transcendentals=0
        ),
    )(limit, x, wq, wk, wv, gain[None], bias[None], aq.T, av.T, bq, bv)


def token_spec():
    return pl.BlockSpec(memory_space=pl.ANY)


def call(kernel, ins, outs, token, scalars=()):
    tokens = [] if token is None else [token]

    def body(*refs):
        count = len(scalars) + len(ins)
        kernel(*refs[:count], *refs[count + len(tokens) :])

    return pl.pallas_call(
        body,
        in_specs=[SMEM] * len(scalars) + [VMEM] * len(ins) + [token_spec()] * len(tokens),
        out_specs=[VMEM] * len(outs),
        out_shape=[jax.ShapeDtypeStruct(shape, kind) for shape, kind in outs],
        compiler_params=pltpu.CompilerParams(vmem_limit_bytes=LIMIT),
        cost_estimate=STEP_COST,
    )(*scalars, *ins, *tokens)


def rows_of(own_ref, got_ref, length):
    return jnp.concatenate(
        [own_ref[:length].astype(BF16), got_ref[:length].astype(BF16)], axis=1
    )


def put_tail(out_ref, own_ref, got_ref, length):
    out_ref[length:] = jnp.zeros((8, out_ref.shape[1]), F32)
    out_ref[length:, :HEAD_DIM] = own_ref[length:, :HEAD_DIM] + got_ref[length:, :HEAD_DIM]


def first_spread(index, length, own, got, own_w, other_w, token):
    inner, cols = own_w.shape
    height = length + (8 if index == 0 else 0)

    def kernel(own_ref, got_ref, own_w_ref, other_w_ref, out_ref, pair_ref):
        pair_ref[:inner] = own_w_ref[...]
        pair_ref[inner:] = other_w_ref[...].astype(BF16)
        out_ref[:length] = dot32(rows_of(own_ref, got_ref, length), pair_ref[...])
        if index == 0:
            put_tail(out_ref, own_ref, got_ref, length)

    outs = [((height, cols), F32), ((2 * inner, cols), BF16)]
    return call(kernel, [own, got, own_w, other_w], outs, token)


def spread(index, length, own, got, pair, token):
    height = length + (8 if index == 0 else 0)

    def kernel(own_ref, got_ref, pair_ref, out_ref):
        out_ref[:length] = dot32(rows_of(own_ref, got_ref, length), pair_ref[...])
        if index == 0:
            put_tail(out_ref, own_ref, got_ref, length)

    return call(kernel, [own, got, pair], [((height, pair.shape[1]), F32)], token)[0]


def add(first, second, token):
    def kernel(first_ref, second_ref, out_ref):
        out_ref[...] = first_ref[...] + second_ref[: first_ref.shape[0]]

    return call(kernel, [first, second], [(first.shape, F32)], token)[0]


def add_and_pick(first, second, ends, outer, token):
    def kernel(ends_ref, first_ref, second_ref, outer_ref, sum_ref, sent_ref):
        total = first_ref[...] + second_ref[...]
        sum_ref[...] = total
        rows = outer_ref.shape[0]
        sent_ref[:rows] = jnp.where(ends_ref[0] > 0, outer_ref[...], total[:rows])
        if total.shape[0] > rows:
            sent_ref[rows:] = total[rows:]

    outs = [(first.shape, F32)] * 2
    return call(kernel, [first, second, outer], outs, token, [ends])


def gather(index, length, ends, got, held, pair, sums, limit, gap, token):
    inner = pair.shape[0] // 2
    extra = [] if gap is None else [gap]

    def kernel(ends_ref, limit_ref, got_ref, held_ref, pair_ref, *refs):
        refs = list(refs)
        gap_ref = refs.pop(0) if gap is not None else None
        before = [refs.pop(0), refs.pop(0)] if index else None
        own_ref, other_ref = refs[:2]
        total = jnp.where(ends_ref[0] > 0, got_ref[...], held_ref[...])
        total = total[: length + (8 if index == 0 else 0)]
        if index == 0:
            refs[2][...] = total[length:, :128]
            total = total[:length]
        if gap_ref is not None:
            kept = rows_below(limit_ref[0], length, total.shape[1])
            total = jnp.where(kept, total + gap_ref[...], 0.0)
        rounded = total.astype(BF16)
        own = dot_nt(rounded, pair_ref[:inner])
        other = dot_nt(rounded, pair_ref[inner:])
        squares = jnp.full((8, inner), jnp.sum(total * total), F32)
        if index:
            own = own + before[0][...]
            other = other + before[1][:length]
            squares = squares + before[1][length:]
        own_ref[...] = own
        other_ref[:length] = other
        other_ref[length:] = squares

    outs = [((length, inner), F32), ((length + 8, inner), F32)]
    if index == 0:
        outs.append(((8, 128), F32))
    return call(kernel, [got, held, pair] + extra + sums, outs, token, [ends, limit])


def cotangent_kernel(
    share, limit_ref, own_ref, other_ref, got_ref, soft_ref, key_ref, value_ref, down_q_ref,
    down_v_ref, out_ref,
):
    length, inner = own_ref.shape
    rank = down_q_ref.shape[1]
    live = live_pairs(limit_ref[0], length)
    pulled = (own_ref[...] + got_ref[:length]).astype(BF16)
    out_ref[2 * rank :] = other_ref[length:] + got_ref[length:]
    for h in range(inner // HEAD_DIM):
        soft = soft_ref[h]
        rows = pulled[:, head(h)]
        d_probs = dot_nt(rows, value_ref[:, head(h)]).astype(BF16).astype(F32)
        d_value = dot_tn(soft.astype(BF16), rows).astype(BF16).astype(F32)
        d_scores = soft * (d_probs - jnp.sum(soft * d_probs, axis=-1, keepdims=True))
        d_scores = jnp.where(live, d_scores, 0.0) * SCALE
        d_query = dot32(d_scores.astype(BF16), key_ref[:, head(h)]).astype(BF16).astype(F32)
        out_ref[:rank, head(h)] = share * lax.dot_general(
            down_q_ref[...], d_query, (((0,), (0,)), ((), ())), precision=HIGH,
            preferred_element_type=F32,
        )
        out_ref[rank : 2 * rank, head(h)] = share * lax.dot_general(
            down_v_ref[...], d_value, (((0,), (0,)), ((), ())), precision=HIGH,
            preferred_element_type=F32,
        )


def cotangent(share, limit, own, other, got, attention):
    inner = own.shape[1]
    rank = attention[3].shape[1]
    return pl.pallas_call(
        functools.partial(cotangent_kernel, share),
        in_specs=[SMEM] + [VMEM] * 8,
        out_specs=VMEM,
        out_shape=jax.ShapeDtypeStruct((2 * rank + 8, inner), F32),
        compiler_params=pltpu.CompilerParams(vmem_limit_bytes=LIMIT),
    )(limit, own, other, got, *attention)


def tangent_of(vector, limit, soft_ref, key_ref, value_ref, down_q_ref, down_v_ref, out_ref):
    length = key_ref.shape[0]
    rank = down_q_ref.shape[1]
    live = live_pairs(limit, length)
    kept = rows_below(limit, length, HEAD_DIM)
    d_query = (ADAPTER_SCALE * high(down_q_ref[...], vector[:rank])).astype(BF16)
    d_value = (ADAPTER_SCALE * high(down_v_ref[...], vector[rank:])).astype(BF16)
    for h in range(key_ref.shape[1] // HEAD_DIM):
        soft = soft_ref[h]
        d_scores = dot_nt(d_query[:, head(h)], key_ref[:, head(h)]) * SCALE
        d_scores = jnp.where(live, d_scores, 0.0)
        d_probs = soft * (d_scores - jnp.sum(soft * d_scores, axis=-1, keepdims=True))
        d_mixed = dot32(d_probs.astype(BF16), value_ref[:, head(h)]) + dot32(
            soft.astype(BF16), d_value[:, head(h)]
        )
        out_ref[:length, head(h)] = jnp.where(kept, d_mixed.astype(BF16).astype(F32), 0.0)


def total_of(terms):
    while len(terms) > 1:
        terms = [terms[i] + terms[i + 1] for i in range(0, len(terms), 2)]
    return terms[0]


def put_sums(out_ref, remain, image):
    lane = lax.broadcasted_iota(jnp.int32, (8, out_ref.shape[1]), 1)
    cross = 0.0 if image is None else jnp.sum(remain * image)
    out_ref[out_ref.shape[0] - 8 :] = jnp.where(lane == 0, jnp.sum(remain * remain), cross)


def first_kernel(n_dp, *refs):
    terms, refs = refs[:n_dp], refs[n_dp:]
    limit_ref, *attention, remain_ref, out_ref = refs
    grads = total_of([term[...] for term in terms])
    remain = -grads[: remain_ref.shape[0]]
    remain_ref[...] = remain
    put_sums(out_ref, remain, None)
    tangent_of(remain, limit_ref[0], *attention, out_ref)


def first_step(terms, limit, attention):
    inner = terms[0].shape[1]
    length = attention[1].shape[0]
    rank = attention[3].shape[1]
    return pl.pallas_call(
        functools.partial(first_kernel, len(terms)),
        in_specs=[VMEM] * len(terms) + [SMEM] + [VMEM] * 5,
        out_specs=[VMEM] * 2,
        out_shape=[
            jax.ShapeDtypeStruct((2 * rank, inner), F32),
            jax.ShapeDtypeStruct((length + 8, inner), F32),
        ],
        compiler_params=pltpu.CompilerParams(vmem_limit_bytes=LIMIT),
    )(*terms, limit, *attention)


def step_kernel(n_dp, token_count, index, last, *refs):
    terms, refs = refs[:n_dp], refs[n_dp:]
    sums_ref, remain_ref, *refs = refs
    if index:
        before_ref, newton_ref, direction_ref, image_ref, *refs = refs
    part = total_of([term[...] for term in terms])
    remain = remain_ref[...]
    rows = remain.shape[0]
    norm, cross = sums_ref[:1, 0:1], sums_ref[:1, 1:2]
    fresh = part[:rows] + DAMP * remain
    curv = part[rows : rows + 1, 0:1] / token_count + DAMP * norm
    if index:
        ratio = norm / before_ref[:1, 0:1]
        curv = curv + 2.0 * ratio * cross + ratio * ratio * before_ref[:1, 1:2]
        direction = remain + ratio * direction_ref[...]
        image = fresh + ratio * image_ref[...]
    else:
        direction, image = remain, fresh
    alpha = norm / curv
    newton = alpha * direction
    if index:
        newton = newton_ref[...] + newton
    remain = remain - alpha * image
    if last:
        step_q_ref, step_v_ref, remain_q_ref, remain_v_ref = refs
        rank = rows // 2
        step_q_ref[...] = newton[:rank]
        step_v_ref[...] = newton[rank:]
        remain_q_ref[...] = remain[:rank]
        remain_v_ref[...] = remain[rank:]
        return
    limit_ref, *refs = refs
    attention, refs = refs[:5], refs[5:]
    next_remain, next_before, next_newton, next_direction, next_image, out_ref = refs
    lane = lax.broadcasted_iota(jnp.int32, next_before.shape, 1)
    next_remain[...] = remain
    next_before[...] = jnp.where(lane == 0, norm, curv)
    next_newton[...] = newton
    next_direction[...] = direction
    next_image[...] = image
    put_sums(out_ref, remain, image)
    tangent_of(remain, limit_ref[0], *attention, out_ref)


def cg_step(index, token_count, terms, sums, remain, state, limit, attention):
    last = index == CG_STEPS - 1
    rows, inner = remain.shape
    matrix = jax.ShapeDtypeStruct((rows, inner), F32)
    scalars = jax.ShapeDtypeStruct((8, 128), F32)
    args = [*terms, sums, remain, *state]
    specs = [VMEM] * len(args)
    if last:
        shapes = [jax.ShapeDtypeStruct((rows // 2, inner), F32)] * 4
    else:
        args += [limit, *attention]
        specs += [SMEM] + [VMEM] * 5
        length = attention[1].shape[0]
        shapes = [matrix, scalars, matrix, matrix, matrix]
        shapes.append(jax.ShapeDtypeStruct((length + 8, inner), F32))
    return pl.pallas_call(
        functools.partial(step_kernel, len(terms), token_count, index, last),
        in_specs=specs,
        out_specs=[VMEM] * len(shapes),
        out_shape=shapes,
        compiler_params=pltpu.CompilerParams(vmem_limit_bytes=LIMIT),
    )(*args)


def on_device(
    inputs,
    targets,
    lengths,
    ln_gain,
    ln_bias,
    query_weight,
    w_key,
    value_weight,
    w_out,
    down_query,
    down_value,
    query_up_factor,
    value_up_factor,
):
    length, width = inputs.shape
    n_dp = lax.axis_size("dp")
    n_chip = lax.axis_size("chip")
    core = lax.axis_index("core")
    chip = lax.axis_index("chip")
    token_count = length * n_dp
    half = width // 2

    def swap(part):
        return lax.ppermute(part, "core", [(0, 1), (1, 0)])

    def data_terms(part):
        step = 1
        while 2 * step < n_dp:
            part = part + lax.ppermute(part, "dp", [(d, d ^ step) for d in range(n_dp)])
            step *= 2
        return [part, lax.ppermute(part, "dp", [(d, d ^ step) for d in range(n_dp)])]

    where = core.astype(jnp.int32)[None]
    cols = half // CHUNKS
    gap = lax.dynamic_slice_in_dim(inputs, core * half, half, 1).astype(F32)
    gap = gap - lax.dynamic_slice_in_dim(targets, core * half, half, 1).astype(F32)

    soft, key, value, down_q, down_v, mixed = project(
        lengths, inputs, ln_gain, ln_bias, query_weight, w_key, value_weight, down_query,
        down_value, query_up_factor, value_up_factor,
    )
    attention = (soft, key, value, down_q, down_v)
    own_first, other_first = split(where, w_out, [0], mixed)
    own_w, other_w = list(own_first), [swap(part) for part in other_first]

    ends = ((chip == 0) | (chip == n_chip - 1)).astype(jnp.int32)[None]

    def outer_swap(part):
        return lax.ppermute(part, "chip", [(0, 1), (1, 0), (2, 3), (3, 2)])

    def inner_swap(part):
        hops = [(2, 4), (4, 2), (3, 5), (5, 3), (0, 1), (1, 0), (6, 7), (7, 6)]
        return lax.ppermute(part, ("chip", "core"), hops)

    def product(rows, pairs):
        got_rows = swap(rows)
        first = not pairs
        pairs.extend([None] * (CHUNKS - len(pairs)))
        parts, scalars = [], None
        own_part, total, outer, inner = {}, {}, {}, {}
        token = None

        def begin(k):
            if first:
                own_part[k], pairs[k] = first_spread(
                    k, length, rows, got_rows, own_w[k], other_w[k], token
                )
                if k == 0:
                    own, other = split(where, w_out, range(1, CHUNKS), own_part[k])
                    own_w.extend(own)
                    other_w.extend([swap(part) for part in other])
            else:
                own_part[k] = spread(k, length, rows, got_rows, pairs[k], token)
            return own_part[k]

        def finish(k, got):
            gap_part = gap[:, k * cols : (k + 1) * cols] if first else None
            return gather(k, length, ends, got, total[k], pairs[k], parts, lengths, gap_part, token)

        if n_chip != 4:
            for k in range(CHUNKS):
                token = begin(k)
            for k in range(CHUNKS):
                total[k] = lax.psum(own_part[k], "chip")
                out = finish(k, total[k])
                parts, scalars = list(out[:2]), out[2] if k == 0 else scalars
        else:
            for k in [0, 1, 2] if first else [0, *range(2, CHUNKS), 1]:
                token = begin(k)
            for k in (0, 1):
                outer[k] = outer_swap(own_part[k])
            for tick in range(CHUNKS + 3):
                if tick < CHUNKS:
                    own_part[tick] = add(own_part[tick], outer[tick], token)
                    token = own_part[tick]
                    inner[tick] = inner_swap(token)
                later = tick + 2
                if tick == CHUNKS:
                    out = finish(tick - 3, outer[tick])
                    parts = list(out[:2])
                    token = parts[0]
                if 1 <= tick <= CHUNKS:
                    k = tick - 1
                    if later < CHUNKS:
                        total[k], sent = add_and_pick(
                            own_part[k], inner[k], ends, own_part[later], token
                        )
                    else:
                        total[k] = sent = add(own_part[k], inner[k], token)
                    token = sent
                    outer[later] = outer_swap(sent)
                elif tick == 0:
                    outer[later] = outer_swap(own_part[later])
                if tick + 3 < CHUNKS and first:
                    token = begin(tick + 3)
                if tick >= 3 and tick != CHUNKS:
                    out = finish(tick - 3, outer[tick])
                    parts, scalars = list(out[:2]), out[2] if tick == 3 else scalars
                    token = parts[0]
        own, other = parts
        share = ADAPTER_SCALE / token_count
        part = cotangent(share, lengths, own, other, swap(other), attention)
        return data_terms(part), scalars

    pairs = []
    terms, _ = product(mixed, pairs)
    remain, rows = first_step(terms, lengths, attention)
    state = ()
    for index in range(CG_STEPS):
        terms, sums = product(rows, pairs)
        out = cg_step(index, token_count, terms, sums, remain, state, lengths, attention)
        if index < CG_STEPS - 1:
            remain, *state, rows = out
    return tuple(out)


def solution(mesh):
    fine = Mesh(mesh.devices.reshape(mesh.shape["dp"], -1, 2), ("dp", "chip", "core"))
    tensor = ("chip", "core")
    in_specs = (
        P("dp", None),
        P("dp", None),
        P("dp"),
        P(),
        P(),
        P(None, tensor),
        P(None, tensor),
        P(None, tensor),
        P(tensor, None),
        P(),
        P(),
        P(None, tensor),
        P(None, tensor),
    )
    out_specs = (P(None, tensor),) * 4
    return jax.shard_map(
        on_device, mesh=fine, in_specs=in_specs, out_specs=out_specs, check_vma=False
    )
```

```python
import functools

import jax
import jax.numpy as jnp
from jax import lax
from jax.experimental import pallas as pl
from jax.experimental.pallas import tpu as pltpu
from jax.sharding import Mesh
from jax.sharding import PartitionSpec as P

HEAD_DIM = 128
CG_STEPS = 3
CHUNKS = 6
DEPTH = 1024

EPS = 1e-05
ADAPTER_SCALE = 2.0
DAMP = 0.05
NEG = -1e30
F32 = jnp.float32
BF16 = jnp.bfloat16
HIGH = lax.Precision.HIGHEST
SCALE = HEAD_DIM ** (-0.5)
VMEM = pl.BlockSpec(memory_space=pltpu.VMEM)
SMEM = pl.BlockSpec(memory_space=pltpu.SMEM)
LIMIT = 16 * 1024 * 1024
STEP_COST = pl.CostEstimate(flops=10**9, bytes_accessed=10**7, transcendentals=0)
STREAM_LIMIT = 50 * 1024 * 1024


def dot32(first, second):
    return jnp.dot(first, second, preferred_element_type=F32)


def dot_nt(first, second):
    return lax.dot_general(
        first, second, (((1,), (1,)), ((), ())), preferred_element_type=F32
    )


def dot_tn(first, second):
    return lax.dot_general(
        first, second, (((0,), (0,)), ((), ())), preferred_element_type=F32
    )


def high(first, second):
    return jnp.dot(first, second, precision=HIGH, preferred_element_type=F32)


def head(index):
    return slice(index * HEAD_DIM, (index + 1) * HEAD_DIM)


def rows_below(limit, length, width):
    return lax.broadcasted_iota(jnp.int32, (length, width), 0) < limit


def live_pairs(limit, length):
    row = lax.broadcasted_iota(jnp.int32, (length, length), 0)
    column = lax.broadcasted_iota(jnp.int32, (length, length), 1)
    return (column <= row) & (column < limit)


def split_kernel(core_ref, w_ref, *refs):
    own_refs, other_refs = refs[:CHUNKS], refs[CHUNKS : 2 * CHUNKS]
    landed, own_sem, other_sem = refs[2 * CHUNKS :]
    cols = own_refs[0].shape[1]
    half = CHUNKS * cols
    core = core_ref[0]

    def own_copy(k):
        start = pl.multiple_of(core * half + k * cols, HEAD_DIM)
        return pltpu.make_async_copy(
            w_ref.at[:, pl.ds(start, cols)], own_refs[k], own_sem.at[k]
        )

    def other_copy(k):
        start = pl.multiple_of((1 - core) * half + k * cols, HEAD_DIM)
        return pltpu.make_async_copy(
            w_ref.at[:, pl.ds(start, cols)], landed.at[k], other_sem.at[k]
        )

    for k in range(CHUNKS):
        other_copy(k).start()
    for k in range(CHUNKS):
        own_copy(k).start()
    for k in range(CHUNKS):
        other_copy(k).wait()
        other_refs[k][...] = landed[k].astype(F32)
    for k in range(CHUNKS):
        own_copy(k).wait()


def split(core, w_out):
    inner, width = w_out.shape
    cols = width // 2 // CHUNKS
    out = pl.pallas_call(
        split_kernel,
        in_specs=[SMEM, pl.BlockSpec(memory_space=pltpu.HBM)],
        out_specs=[VMEM] * (2 * CHUNKS),
        out_shape=[jax.ShapeDtypeStruct((inner, cols), BF16)] * CHUNKS
        + [jax.ShapeDtypeStruct((inner, cols), F32)] * CHUNKS,
        scratch_shapes=[
            pltpu.VMEM((CHUNKS, inner, cols), BF16),
            pltpu.SemaphoreType.DMA((CHUNKS,)),
            pltpu.SemaphoreType.DMA((CHUNKS,)),
        ],
        compiler_params=pltpu.CompilerParams(vmem_limit_bytes=LIMIT),
    )(core, w_out)
    return out[:CHUNKS], out[CHUNKS:]


def project_kernel(
    limit_ref, x_ref, wq_ref, wk_ref, wv_ref, gain_ref, bias_ref, aq_ref, av_ref, bq_ref, bv_ref,
    soft_ref, key_ref, value_ref, down_q_ref, down_v_ref, mixed_ref,
    rows_in, normed, wq_in, wk_in, wv_in, rows_sem, weight_sem,
):
    length, width = normed.shape
    inner = key_ref.shape[1]
    blocks = [slice(i, i + DEPTH) for i in range(0, width, DEPTH)]
    rows_copy = pltpu.make_async_copy(x_ref, rows_in, rows_sem)
    rows_copy.start()
    copies = []
    for i, block in enumerate(blocks):
        for j, (source, target) in enumerate(
            [(wq_ref, wq_in), (wk_ref, wk_in), (wv_ref, wv_in)]
        ):
            copies.append(
                pltpu.make_async_copy(
                    source.at[block], target.at[block], weight_sem.at[3 * i + j]
                )
            )
            copies[-1].start()
    rows_copy.wait()
    total = jnp.zeros((length, 1), F32)
    for block in blocks:
        total = total + jnp.sum(rows_in[:, block].astype(F32), axis=-1, keepdims=True)
    mean = total / width
    total = jnp.zeros((length, 1), F32)
    for block in blocks:
        centred = rows_in[:, block].astype(F32) - mean
        total = total + jnp.sum(centred * centred, axis=-1, keepdims=True)
    spread = lax.rsqrt(total / width + EPS)
    for block in blocks:
        centred = rows_in[:, block].astype(F32) - mean
        full = centred * spread * gain_ref[:, block] + bias_ref[:, block]
        normed[:, block] = full.astype(BF16)
    down_q = dot_nt(normed[...], aq_ref[...])
    down_v = dot_nt(normed[...], av_ref[...])
    query = jnp.zeros((length, inner), F32)
    key = jnp.zeros((length, inner), F32)
    value = jnp.zeros((length, inner), F32)
    for i, block in enumerate(blocks):
        part = normed[:, block]
        for j in range(3):
            copies[3 * i + j].wait()
        query = query + dot32(part, wq_in[block])
        key = key + dot32(part, wk_in[block])
        value = value + dot32(part, wv_in[block])
    down_q_ref[...] = down_q
    down_v_ref[...] = down_v
    limit = limit_ref[0]
    live = live_pairs(limit, length)
    kept = rows_below(limit, length, HEAD_DIM)
    query = (query + ADAPTER_SCALE * high(down_q, bq_ref[...])).astype(BF16)
    value = (value + ADAPTER_SCALE * high(down_v, bv_ref[...])).astype(BF16)
    key = key.astype(BF16)
    key_ref[...] = key
    value_ref[...] = value
    for h in range(inner // HEAD_DIM):
        scores = dot_nt(query[:, head(h)], key[:, head(h)]) * SCALE
        scores = jnp.where(live, scores, NEG)
        weights = jnp.exp(scores - jnp.max(scores, axis=-1, keepdims=True))
        soft = weights / jnp.sum(weights, axis=-1, keepdims=True)
        soft_ref[h] = soft
        mixed = dot32(soft.astype(BF16), value[:, head(h)]).astype(BF16)
        mixed_ref[:length, head(h)] = jnp.where(kept, mixed.astype(F32), 0.0)
    mixed_ref[length:] = jnp.zeros((8, inner), F32)


def project(limit, x, gain, bias, wq, wk, wv, aq, av, bq, bv):
    length, width = x.shape
    inner = wq.shape[1]
    rank = aq.shape[1]
    heads = inner // HEAD_DIM
    hbm = pl.BlockSpec(memory_space=pltpu.HBM)
    return pl.pallas_call(
        project_kernel,
        in_specs=[SMEM] + [hbm] * 4 + [VMEM] * 6,
        out_specs=[VMEM] * 6,
        out_shape=[
            jax.ShapeDtypeStruct((heads, length, length), F32),
            jax.ShapeDtypeStruct((length, inner), BF16),
            jax.ShapeDtypeStruct((length, inner), BF16),
            jax.ShapeDtypeStruct((length, rank), F32),
            jax.ShapeDtypeStruct((length, rank), F32),
            jax.ShapeDtypeStruct((length + 8, inner), F32),
        ],
        scratch_shapes=[
            pltpu.VMEM((length, width), BF16),
            pltpu.VMEM((length, width), BF16),
            pltpu.VMEM((width, inner), BF16),
            pltpu.VMEM((width, inner), BF16),
            pltpu.VMEM((width, inner), BF16),
            pltpu.SemaphoreType.DMA,
            pltpu.SemaphoreType.DMA((3 * (width // DEPTH),)),
        ],
        compiler_params=pltpu.CompilerParams(vmem_limit_bytes=STREAM_LIMIT),
        cost_estimate=pl.CostEstimate(
            flops=6 * length * width * inner, bytes_accessed=6 * width * inner, transcendentals=0
        ),
    )(limit, x, wq, wk, wv, gain[None], bias[None], aq.T, av.T, bq, bv)


def token_spec():
    return pl.BlockSpec(memory_space=pl.ANY)


def call(kernel, ins, outs, token, scalars=()):
    tokens = [] if token is None else [token]

    def body(*refs):
        count = len(scalars) + len(ins)
        kernel(*refs[:count], *refs[count + len(tokens) :])

    return pl.pallas_call(
        body,
        in_specs=[SMEM] * len(scalars) + [VMEM] * len(ins) + [token_spec()] * len(tokens),
        out_specs=[VMEM] * len(outs),
        out_shape=[jax.ShapeDtypeStruct(shape, kind) for shape, kind in outs],
        compiler_params=pltpu.CompilerParams(vmem_limit_bytes=LIMIT),
        cost_estimate=STEP_COST,
    )(*scalars, *ins, *tokens)


def rows_of(own_ref, got_ref, length):
    return jnp.concatenate(
        [own_ref[:length].astype(BF16), got_ref[:length].astype(BF16)], axis=1
    )


def put_tail(out_ref, own_ref, got_ref, length):
    out_ref[length:] = jnp.zeros((8, out_ref.shape[1]), F32)
    out_ref[length:, :HEAD_DIM] = own_ref[length:, :HEAD_DIM] + got_ref[length:, :HEAD_DIM]


def first_spread(index, length, own, got, own_w, other_w, token):
    inner, cols = own_w.shape
    height = length + (8 if index == 0 else 0)

    def kernel(own_ref, got_ref, own_w_ref, other_w_ref, out_ref, pair_ref):
        pair_ref[:inner] = own_w_ref[...]
        pair_ref[inner:] = other_w_ref[...].astype(BF16)
        out_ref[:length] = dot32(rows_of(own_ref, got_ref, length), pair_ref[...])
        if index == 0:
            put_tail(out_ref, own_ref, got_ref, length)

    outs = [((height, cols), F32), ((2 * inner, cols), BF16)]
    return call(kernel, [own, got, own_w, other_w], outs, token)


def spread(index, length, own, got, pair, token):
    height = length + (8 if index == 0 else 0)

    def kernel(own_ref, got_ref, pair_ref, out_ref):
        out_ref[:length] = dot32(rows_of(own_ref, got_ref, length), pair_ref[...])
        if index == 0:
            put_tail(out_ref, own_ref, got_ref, length)

    return call(kernel, [own, got, pair], [((height, pair.shape[1]), F32)], token)[0]


def add(first, second, token):
    def kernel(first_ref, second_ref, out_ref):
        out_ref[...] = first_ref[...] + second_ref[: first_ref.shape[0]]

    return call(kernel, [first, second], [(first.shape, F32)], token)[0]


def add_and_pick(first, second, ends, outer, token):
    def kernel(ends_ref, first_ref, second_ref, outer_ref, sum_ref, sent_ref):
        total = first_ref[...] + second_ref[...]
        sum_ref[...] = total
        rows = outer_ref.shape[0]
        sent_ref[:rows] = jnp.where(ends_ref[0] > 0, outer_ref[...], total[:rows])
        if total.shape[0] > rows:
            sent_ref[rows:] = total[rows:]

    outs = [(first.shape, F32)] * 2
    return call(kernel, [first, second, outer], outs, token, [ends])


def gather(index, length, ends, got, held, pair, sums, limit, gap, token):
    inner = pair.shape[0] // 2
    extra = [] if gap is None else [gap]

    def kernel(ends_ref, limit_ref, got_ref, held_ref, pair_ref, *refs):
        refs = list(refs)
        gap_ref = refs.pop(0) if gap is not None else None
        before = [refs.pop(0), refs.pop(0)] if index else None
        own_ref, other_ref = refs[:2]
        total = jnp.where(ends_ref[0] > 0, got_ref[...], held_ref[...])
        total = total[: length + (8 if index == 0 else 0)]
        if index == 0:
            refs[2][...] = total[length:, :128]
            total = total[:length]
        if gap_ref is not None:
            kept = rows_below(limit_ref[0], length, total.shape[1])
            total = jnp.where(kept, total + gap_ref[...], 0.0)
        rounded = total.astype(BF16)
        own = dot_nt(rounded, pair_ref[:inner])
        other = dot_nt(rounded, pair_ref[inner:])
        squares = jnp.full((8, inner), jnp.sum(total * total), F32)
        if index:
            own = own + before[0][...]
            other = other + before[1][:length]
            squares = squares + before[1][length:]
        own_ref[...] = own
        other_ref[:length] = other
        other_ref[length:] = squares

    outs = [((length, inner), F32), ((length + 8, inner), F32)]
    if index == 0:
        outs.append(((8, 128), F32))
    return call(kernel, [got, held, pair] + extra + sums, outs, token, [ends, limit])


def cotangent_kernel(
    share, limit_ref, own_ref, other_ref, got_ref, soft_ref, key_ref, value_ref, down_q_ref,
    down_v_ref, out_ref,
):
    length, inner = own_ref.shape
    rank = down_q_ref.shape[1]
    live = live_pairs(limit_ref[0], length)
    pulled = (own_ref[...] + got_ref[:length]).astype(BF16)
    out_ref[2 * rank :] = other_ref[length:] + got_ref[length:]
    queries, values = [], []
    for h in range(inner // HEAD_DIM):
        soft = soft_ref[h]
        rows = pulled[:, head(h)]
        d_probs = dot_nt(rows, value_ref[:, head(h)]).astype(BF16).astype(F32)
        values.append(dot_tn(soft.astype(BF16), rows).astype(BF16).astype(F32))
        d_scores = soft * (d_probs - jnp.sum(soft * d_probs, axis=-1, keepdims=True))
        d_scores = jnp.where(live, d_scores, 0.0) * SCALE
        d_query = dot32(d_scores.astype(BF16), key_ref[:, head(h)])
        queries.append(d_query.astype(BF16).astype(F32))
    out_ref[:rank] = share * lax.dot_general(
        down_q_ref[...], jnp.concatenate(queries, axis=1), (((0,), (0,)), ((), ())),
        precision=HIGH, preferred_element_type=F32,
    )
    out_ref[rank : 2 * rank] = share * lax.dot_general(
        down_v_ref[...], jnp.concatenate(values, axis=1), (((0,), (0,)), ((), ())),
        precision=HIGH, preferred_element_type=F32,
    )


def cotangent(share, limit, own, other, got, attention):
    inner = own.shape[1]
    rank = attention[3].shape[1]
    return pl.pallas_call(
        functools.partial(cotangent_kernel, share),
        in_specs=[SMEM] + [VMEM] * 8,
        out_specs=VMEM,
        out_shape=jax.ShapeDtypeStruct((2 * rank + 8, inner), F32),
        compiler_params=pltpu.CompilerParams(vmem_limit_bytes=LIMIT),
    )(limit, own, other, got, *attention)


def tangent_of(vector, limit, soft_ref, key_ref, value_ref, down_q_ref, down_v_ref, out_ref):
    length = key_ref.shape[0]
    rank = down_q_ref.shape[1]
    live = live_pairs(limit, length)
    kept = rows_below(limit, length, HEAD_DIM)
    d_query = (ADAPTER_SCALE * high(down_q_ref[...], vector[:rank])).astype(BF16)
    d_value = (ADAPTER_SCALE * high(down_v_ref[...], vector[rank:])).astype(BF16)
    for h in range(key_ref.shape[1] // HEAD_DIM):
        soft = soft_ref[h]
        d_scores = dot_nt(d_query[:, head(h)], key_ref[:, head(h)]) * SCALE
        d_scores = jnp.where(live, d_scores, 0.0)
        d_probs = soft * (d_scores - jnp.sum(soft * d_scores, axis=-1, keepdims=True))
        d_mixed = dot32(d_probs.astype(BF16), value_ref[:, head(h)]) + dot32(
            soft.astype(BF16), d_value[:, head(h)]
        )
        out_ref[:length, head(h)] = jnp.where(kept, d_mixed.astype(BF16).astype(F32), 0.0)


def total_of(terms):
    while len(terms) > 1:
        terms = [terms[i] + terms[i + 1] for i in range(0, len(terms), 2)]
    return terms[0]


def put_sums(out_ref, remain, image):
    lane = lax.broadcasted_iota(jnp.int32, (8, out_ref.shape[1]), 1)
    cross = 0.0 if image is None else jnp.sum(remain * image)
    out_ref[out_ref.shape[0] - 8 :] = jnp.where(lane == 0, jnp.sum(remain * remain), cross)


def first_kernel(n_dp, *refs):
    terms, refs = refs[:n_dp], refs[n_dp:]
    limit_ref, *attention, remain_ref, out_ref = refs
    grads = total_of([term[...] for term in terms])
    remain = -grads[: remain_ref.shape[0]]
    remain_ref[...] = remain
    put_sums(out_ref, remain, None)
    tangent_of(remain, limit_ref[0], *attention, out_ref)


def first_step(terms, limit, attention):
    inner = terms[0].shape[1]
    length = attention[1].shape[0]
    rank = attention[3].shape[1]
    return pl.pallas_call(
        functools.partial(first_kernel, len(terms)),
        in_specs=[VMEM] * len(terms) + [SMEM] + [VMEM] * 5,
        out_specs=[VMEM] * 2,
        out_shape=[
            jax.ShapeDtypeStruct((2 * rank, inner), F32),
            jax.ShapeDtypeStruct((length + 8, inner), F32),
        ],
        compiler_params=pltpu.CompilerParams(vmem_limit_bytes=LIMIT),
    )(*terms, limit, *attention)


def step_kernel(n_dp, token_count, index, last, *refs):
    terms, refs = refs[:n_dp], refs[n_dp:]
    sums_ref, remain_ref, *refs = refs
    if index:
        before_ref, newton_ref, direction_ref, image_ref, *refs = refs
    part = total_of([term[...] for term in terms])
    remain = remain_ref[...]
    rows = remain.shape[0]
    norm, cross = sums_ref[:1, 0:1], sums_ref[:1, 1:2]
    fresh = part[:rows] + DAMP * remain
    curv = part[rows : rows + 1, 0:1] / token_count + DAMP * norm
    if index:
        ratio = norm / before_ref[:1, 0:1]
        curv = curv + 2.0 * ratio * cross + ratio * ratio * before_ref[:1, 1:2]
        direction = remain + ratio * direction_ref[...]
        image = fresh + ratio * image_ref[...]
    else:
        direction, image = remain, fresh
    alpha = norm / curv
    newton = alpha * direction
    if index:
        newton = newton_ref[...] + newton
    remain = remain - alpha * image
    if last:
        step_q_ref, step_v_ref, remain_q_ref, remain_v_ref = refs
        rank = rows // 2
        step_q_ref[...] = newton[:rank]
        step_v_ref[...] = newton[rank:]
        remain_q_ref[...] = remain[:rank]
        remain_v_ref[...] = remain[rank:]
        return
    limit_ref, *refs = refs
    attention, refs = refs[:5], refs[5:]
    next_remain, next_before, next_newton, next_direction, next_image, out_ref = refs
    lane = lax.broadcasted_iota(jnp.int32, next_before.shape, 1)
    next_remain[...] = remain
    next_before[...] = jnp.where(lane == 0, norm, curv)
    next_newton[...] = newton
    next_direction[...] = direction
    next_image[...] = image
    put_sums(out_ref, remain, image)
    tangent_of(remain, limit_ref[0], *attention, out_ref)


def cg_step(index, token_count, terms, sums, remain, state, limit, attention):
    last = index == CG_STEPS - 1
    rows, inner = remain.shape
    matrix = jax.ShapeDtypeStruct((rows, inner), F32)
    scalars = jax.ShapeDtypeStruct((8, 128), F32)
    args = [*terms, sums, remain, *state]
    specs = [VMEM] * len(args)
    if last:
        shapes = [jax.ShapeDtypeStruct((rows // 2, inner), F32)] * 4
    else:
        args += [limit, *attention]
        specs += [SMEM] + [VMEM] * 5
        length = attention[1].shape[0]
        shapes = [matrix, scalars, matrix, matrix, matrix]
        shapes.append(jax.ShapeDtypeStruct((length + 8, inner), F32))
    return pl.pallas_call(
        functools.partial(step_kernel, len(terms), token_count, index, last),
        in_specs=specs,
        out_specs=[VMEM] * len(shapes),
        out_shape=shapes,
        compiler_params=pltpu.CompilerParams(vmem_limit_bytes=LIMIT),
    )(*args)


def on_device(
    inputs,
    targets,
    lengths,
    ln_gain,
    ln_bias,
    query_weight,
    w_key,
    value_weight,
    w_out,
    down_query,
    down_value,
    query_up_factor,
    value_up_factor,
):
    length, width = inputs.shape
    n_dp = lax.axis_size("dp")
    n_chip = lax.axis_size("chip")
    core = lax.axis_index("core")
    chip = lax.axis_index("chip")
    token_count = length * n_dp
    half = width // 2

    def swap(part):
        return lax.ppermute(part, "core", [(0, 1), (1, 0)])

    def data_terms(part):
        sent = [
            lax.ppermute(part, "dp", [(d, d ^ step) for d in range(n_dp)])
            for step in range(1, n_dp)
        ]
        return [part, *sent]

    where = core.astype(jnp.int32)[None]
    own_w, other_w = split(where, w_out)
    other_w = [swap(part) for part in other_w]
    cols = half // CHUNKS
    gap = lax.dynamic_slice_in_dim(inputs, core * half, half, 1).astype(F32)
    gap = gap - lax.dynamic_slice_in_dim(targets, core * half, half, 1).astype(F32)

    soft, key, value, down_q, down_v, mixed = project(
        lengths, inputs, ln_gain, ln_bias, query_weight, w_key, value_weight, down_query,
        down_value, query_up_factor, value_up_factor,
    )
    attention = (soft, key, value, down_q, down_v)

    ends = ((chip == 0) | (chip == n_chip - 1)).astype(jnp.int32)[None]

    def outer_swap(part):
        return lax.ppermute(part, "chip", [(0, 1), (1, 0), (2, 3), (3, 2)])

    def inner_swap(part):
        hops = [(2, 4), (4, 2), (3, 5), (5, 3), (0, 1), (1, 0), (6, 7), (7, 6)]
        return lax.ppermute(part, ("chip", "core"), hops)

    def product(rows, pairs):
        got_rows = swap(rows)
        first = not pairs
        pairs.extend([None] * (CHUNKS - len(pairs)))
        parts, scalars = [], None
        own_part, total, outer, inner = {}, {}, {}, {}
        token = None

        def begin(k):
            if first:
                own_part[k], pairs[k] = first_spread(
                    k, length, rows, got_rows, own_w[k], other_w[k], token
                )
            else:
                own_part[k] = spread(k, length, rows, got_rows, pairs[k], token)
            return own_part[k]

        def finish(k, got):
            gap_part = gap[:, k * cols : (k + 1) * cols] if first else None
            return gather(k, length, ends, got, total[k], pairs[k], parts, lengths, gap_part, token)

        if n_chip != 4:
            for k in range(CHUNKS):
                token = begin(k)
            for k in range(CHUNKS):
                total[k] = lax.psum(own_part[k], "chip")
                out = finish(k, total[k])
                parts, scalars = list(out[:2]), out[2] if k == 0 else scalars
        else:
            for k in [0, 1, 2] if first else [0, *range(2, CHUNKS), 1]:
                token = begin(k)
            for k in (0, 1):
                outer[k] = outer_swap(own_part[k])
            for tick in range(CHUNKS + 3):
                if tick < CHUNKS:
                    own_part[tick] = add(own_part[tick], outer[tick], token)
                    token = own_part[tick]
                    inner[tick] = inner_swap(token)
                later = tick + 2
                if tick == CHUNKS:
                    out = finish(tick - 3, outer[tick])
                    parts = list(out[:2])
                    token = parts[0]
                if 1 <= tick <= CHUNKS:
                    k = tick - 1
                    if later < CHUNKS:
                        total[k], sent = add_and_pick(
                            own_part[k], inner[k], ends, own_part[later], token
                        )
                    else:
                        total[k] = sent = add(own_part[k], inner[k], token)
                    token = sent
                    outer[later] = outer_swap(sent)
                elif tick == 0:
                    outer[later] = outer_swap(own_part[later])
                if tick + 3 < CHUNKS and first:
                    token = begin(tick + 3)
                if tick >= 3 and tick != CHUNKS:
                    out = finish(tick - 3, outer[tick])
                    parts, scalars = list(out[:2]), out[2] if tick == 3 else scalars
                    token = parts[0]
        own, other = parts
        share = ADAPTER_SCALE / token_count
        part = cotangent(share, lengths, own, other, swap(other), attention)
        return data_terms(part), scalars

    pairs = []
    terms, _ = product(mixed, pairs)
    remain, rows = first_step(terms, lengths, attention)
    state = ()
    for index in range(CG_STEPS):
        terms, sums = product(rows, pairs)
        out = cg_step(index, token_count, terms, sums, remain, state, lengths, attention)
        if index < CG_STEPS - 1:
            remain, *state, rows = out
    return tuple(out)


def solution(mesh):
    fine = Mesh(mesh.devices.reshape(mesh.shape["dp"], -1, 2), ("dp", "chip", "core"))
    tensor = ("chip", "core")
    in_specs = (
        P("dp", None),
        P("dp", None),
        P("dp"),
        P(),
        P(),
        P(None, tensor),
        P(None, tensor),
        P(None, tensor),
        P(tensor, None),
        P(),
        P(),
        P(None, tensor),
        P(None, tensor),
    )
    out_specs = (P(None, tensor),) * 4
    return jax.shard_map(
        on_device, mesh=fine, in_specs=in_specs, out_specs=out_specs, check_vma=False
    )
```

```python
import functools

import jax
import jax.numpy as jnp
from jax import lax
from jax.experimental import pallas as pl
from jax.experimental.pallas import tpu as pltpu
from jax.sharding import Mesh
from jax.sharding import PartitionSpec as P

HEAD_DIM = 128
CG_STEPS = 3
CHUNKS = 6
DEPTH = 1024

EPS = 1e-05
ADAPTER_SCALE = 2.0
DAMP = 0.05
NEG = -1e30
F32 = jnp.float32
BF16 = jnp.bfloat16
HIGH = lax.Precision.HIGHEST
SCALE = HEAD_DIM ** (-0.5)
VMEM = pl.BlockSpec(memory_space=pltpu.VMEM)
SMEM = pl.BlockSpec(memory_space=pltpu.SMEM)
LIMIT = 16 * 1024 * 1024
STEP_COST = pl.CostEstimate(flops=10**9, bytes_accessed=10**7, transcendentals=0)
STREAM_LIMIT = 50 * 1024 * 1024


def dot32(first, second):
    return jnp.dot(first, second, preferred_element_type=F32)


def dot_nt(first, second):
    return lax.dot_general(
        first, second, (((1,), (1,)), ((), ())), preferred_element_type=F32
    )


def dot_tn(first, second):
    return lax.dot_general(
        first, second, (((0,), (0,)), ((), ())), preferred_element_type=F32
    )


def high(first, second):
    return jnp.dot(first, second, precision=HIGH, preferred_element_type=F32)


def head(index):
    return slice(index * HEAD_DIM, (index + 1) * HEAD_DIM)


def rows_below(limit, length, width):
    return lax.broadcasted_iota(jnp.int32, (length, width), 0) < limit


def live_pairs(limit, length):
    row = lax.broadcasted_iota(jnp.int32, (length, length), 0)
    column = lax.broadcasted_iota(jnp.int32, (length, length), 1)
    return (column <= row) & (column < limit)


def split_kernel(core_ref, w_ref, *refs):
    own_refs, other_refs = refs[:CHUNKS], refs[CHUNKS : 2 * CHUNKS]
    landed, own_sem, other_sem = refs[2 * CHUNKS :]
    cols = own_refs[0].shape[1]
    half = CHUNKS * cols
    core = core_ref[0]

    def own_copy(k):
        start = pl.multiple_of(core * half + k * cols, HEAD_DIM)
        return pltpu.make_async_copy(
            w_ref.at[:, pl.ds(start, cols)], own_refs[k], own_sem.at[k]
        )

    def other_copy(k):
        start = pl.multiple_of((1 - core) * half + k * cols, HEAD_DIM)
        return pltpu.make_async_copy(
            w_ref.at[:, pl.ds(start, cols)], landed.at[k], other_sem.at[k]
        )

    for k in range(CHUNKS):
        other_copy(k).start()
    for k in range(CHUNKS):
        own_copy(k).start()
    for k in range(CHUNKS):
        other_copy(k).wait()
        other_refs[k][...] = landed[k].astype(F32)
    for k in range(CHUNKS):
        own_copy(k).wait()


def split(core, w_out):
    inner, width = w_out.shape
    cols = width // 2 // CHUNKS
    out = pl.pallas_call(
        split_kernel,
        in_specs=[SMEM, pl.BlockSpec(memory_space=pltpu.HBM)],
        out_specs=[VMEM] * (2 * CHUNKS),
        out_shape=[jax.ShapeDtypeStruct((inner, cols), BF16)] * CHUNKS
        + [jax.ShapeDtypeStruct((inner, cols), F32)] * CHUNKS,
        scratch_shapes=[
            pltpu.VMEM((CHUNKS, inner, cols), BF16),
            pltpu.SemaphoreType.DMA((CHUNKS,)),
            pltpu.SemaphoreType.DMA((CHUNKS,)),
        ],
        compiler_params=pltpu.CompilerParams(vmem_limit_bytes=LIMIT),
    )(core, w_out)
    return out[:CHUNKS], out[CHUNKS:]


def project_kernel(
    limit_ref, x_ref, wq_ref, wk_ref, wv_ref, gain_ref, bias_ref, aq_ref, av_ref, bq_ref, bv_ref,
    soft_ref, key_ref, value_ref, down_q_ref, down_v_ref, mixed_ref,
    rows_in, normed, wq_in, wk_in, wv_in, rows_sem, weight_sem,
):
    length, width = normed.shape
    inner = key_ref.shape[1]
    blocks = [slice(i, i + DEPTH) for i in range(0, width, DEPTH)]
    rows_copy = pltpu.make_async_copy(x_ref, rows_in, rows_sem)
    rows_copy.start()
    copies = []
    for i, block in enumerate(blocks):
        for j, (source, target) in enumerate(
            [(wq_ref, wq_in), (wk_ref, wk_in), (wv_ref, wv_in)]
        ):
            copies.append(
                pltpu.make_async_copy(
                    source.at[block], target.at[block], weight_sem.at[3 * i + j]
                )
            )
            copies[-1].start()
    rows_copy.wait()
    total = jnp.zeros((length, 1), F32)
    for block in blocks:
        total = total + jnp.sum(rows_in[:, block].astype(F32), axis=-1, keepdims=True)
    mean = total / width
    total = jnp.zeros((length, 1), F32)
    for block in blocks:
        centred = rows_in[:, block].astype(F32) - mean
        total = total + jnp.sum(centred * centred, axis=-1, keepdims=True)
    spread = lax.rsqrt(total / width + EPS)
    for block in blocks:
        centred = rows_in[:, block].astype(F32) - mean
        full = centred * spread * gain_ref[:, block] + bias_ref[:, block]
        normed[:, block] = full.astype(BF16)
    down_q = dot_nt(normed[...], aq_ref[...])
    down_v = dot_nt(normed[...], av_ref[...])
    query = jnp.zeros((length, inner), F32)
    key = jnp.zeros((length, inner), F32)
    value = jnp.zeros((length, inner), F32)
    for i, block in enumerate(blocks):
        part = normed[:, block]
        for j in range(3):
            copies[3 * i + j].wait()
        query = query + dot32(part, wq_in[block])
        key = key + dot32(part, wk_in[block])
        value = value + dot32(part, wv_in[block])
    down_q_ref[...] = down_q
    down_v_ref[...] = down_v
    limit = limit_ref[0]
    live = live_pairs(limit, length)
    kept = rows_below(limit, length, HEAD_DIM)
    query = (query + ADAPTER_SCALE * high(down_q, bq_ref[...])).astype(BF16)
    value = (value + ADAPTER_SCALE * high(down_v, bv_ref[...])).astype(BF16)
    key = key.astype(BF16)
    key_ref[...] = key
    value_ref[...] = value
    for h in range(inner // HEAD_DIM):
        scores = dot_nt(query[:, head(h)], key[:, head(h)]) * SCALE
        scores = jnp.where(live, scores, NEG)
        weights = jnp.exp(scores - jnp.max(scores, axis=-1, keepdims=True))
        soft = weights / jnp.sum(weights, axis=-1, keepdims=True)
        soft_ref[h] = soft
        mixed = dot32(soft.astype(BF16), value[:, head(h)]).astype(BF16)
        mixed_ref[:length, head(h)] = jnp.where(kept, mixed.astype(F32), 0.0)
    mixed_ref[length:] = jnp.zeros((8, inner), F32)


def project(limit, x, gain, bias, wq, wk, wv, aq, av, bq, bv):
    length, width = x.shape
    inner = wq.shape[1]
    rank = aq.shape[1]
    heads = inner // HEAD_DIM
    hbm = pl.BlockSpec(memory_space=pltpu.HBM)
    return pl.pallas_call(
        project_kernel,
        in_specs=[SMEM] + [hbm] * 4 + [VMEM] * 6,
        out_specs=[VMEM] * 6,
        out_shape=[
            jax.ShapeDtypeStruct((heads, length, length), F32),
            jax.ShapeDtypeStruct((length, inner), BF16),
            jax.ShapeDtypeStruct((length, inner), BF16),
            jax.ShapeDtypeStruct((length, rank), F32),
            jax.ShapeDtypeStruct((length, rank), F32),
            jax.ShapeDtypeStruct((length + 8, inner), F32),
        ],
        scratch_shapes=[
            pltpu.VMEM((length, width), BF16),
            pltpu.VMEM((length, width), BF16),
            pltpu.VMEM((width, inner), BF16),
            pltpu.VMEM((width, inner), BF16),
            pltpu.VMEM((width, inner), BF16),
            pltpu.SemaphoreType.DMA,
            pltpu.SemaphoreType.DMA((3 * (width // DEPTH),)),
        ],
        compiler_params=pltpu.CompilerParams(vmem_limit_bytes=STREAM_LIMIT),
        cost_estimate=pl.CostEstimate(
            flops=6 * length * width * inner, bytes_accessed=6 * width * inner, transcendentals=0
        ),
    )(limit, x, wq, wk, wv, gain[None], bias[None], aq.T, av.T, bq, bv)


def token_spec():
    return pl.BlockSpec(memory_space=pl.ANY)


def call(kernel, ins, outs, token, scalars=()):
    tokens = [] if token is None else [token]

    def body(*refs):
        count = len(scalars) + len(ins)
        kernel(*refs[:count], *refs[count + len(tokens) :])

    return pl.pallas_call(
        body,
        in_specs=[SMEM] * len(scalars) + [VMEM] * len(ins) + [token_spec()] * len(tokens),
        out_specs=[VMEM] * len(outs),
        out_shape=[jax.ShapeDtypeStruct(shape, kind) for shape, kind in outs],
        compiler_params=pltpu.CompilerParams(vmem_limit_bytes=LIMIT),
        cost_estimate=STEP_COST,
    )(*scalars, *ins, *tokens)


def rows_of(own_ref, got_ref, length):
    return jnp.concatenate(
        [own_ref[:length].astype(BF16), got_ref[:length].astype(BF16)], axis=1
    )


def put_tail(out_ref, own_ref, got_ref, length):
    out_ref[length:] = jnp.zeros((8, out_ref.shape[1]), F32)
    out_ref[length:, :HEAD_DIM] = own_ref[length:, :HEAD_DIM] + got_ref[length:, :HEAD_DIM]


def first_spread(index, length, own, got, own_w, other_w, token):
    inner, cols = own_w.shape
    height = length + (8 if index == 0 else 0)

    def kernel(own_ref, got_ref, own_w_ref, other_w_ref, out_ref, pair_ref):
        pair_ref[:inner] = own_w_ref[...]
        pair_ref[inner:] = other_w_ref[...].astype(BF16)
        out_ref[:length] = dot32(rows_of(own_ref, got_ref, length), pair_ref[...])
        if index == 0:
            put_tail(out_ref, own_ref, got_ref, length)

    outs = [((height, cols), F32), ((2 * inner, cols), BF16)]
    return call(kernel, [own, got, own_w, other_w], outs, token)


def spread(index, length, own, got, pair, token):
    height = length + (8 if index == 0 else 0)

    def kernel(own_ref, got_ref, pair_ref, out_ref):
        out_ref[:length] = dot32(rows_of(own_ref, got_ref, length), pair_ref[...])
        if index == 0:
            put_tail(out_ref, own_ref, got_ref, length)

    return call(kernel, [own, got, pair], [((height, pair.shape[1]), F32)], token)[0]


def add(first, second, token):
    def kernel(first_ref, second_ref, out_ref):
        out_ref[...] = first_ref[...] + second_ref[: first_ref.shape[0]]

    return call(kernel, [first, second], [(first.shape, F32)], token)[0]


def add_and_pick(first, second, ends, outer, token):
    def kernel(ends_ref, first_ref, second_ref, outer_ref, sum_ref, sent_ref):
        total = first_ref[...] + second_ref[...]
        sum_ref[...] = total
        rows = outer_ref.shape[0]
        sent_ref[:rows] = jnp.where(ends_ref[0] > 0, outer_ref[...], total[:rows])
        if total.shape[0] > rows:
            sent_ref[rows:] = total[rows:]

    outs = [(first.shape, F32)] * 2
    return call(kernel, [first, second, outer], outs, token, [ends])


def gather(index, length, ends, got, held, pair, sums, limit, gap, token):
    inner = pair.shape[0] // 2
    extra = [] if gap is None else [gap]

    def kernel(ends_ref, limit_ref, got_ref, held_ref, pair_ref, *refs):
        refs = list(refs)
        gap_ref = refs.pop(0) if gap is not None else None
        before = [refs.pop(0), refs.pop(0)] if index else None
        own_ref, other_ref = refs[:2]
        total = jnp.where(ends_ref[0] > 0, got_ref[...], held_ref[...])
        total = total[: length + (8 if index == 0 else 0)]
        if index == 0:
            refs[2][...] = total[length:, :128]
            total = total[:length]
        if gap_ref is not None:
            kept = rows_below(limit_ref[0], length, total.shape[1])
            total = jnp.where(kept, total + gap_ref[...], 0.0)
        rounded = total.astype(BF16)
        own = dot_nt(rounded, pair_ref[:inner])
        other = dot_nt(rounded, pair_ref[inner:])
        squares = jnp.full((8, inner), jnp.sum(total * total), F32)
        if index:
            own = own + before[0][...]
            other = other + before[1][:length]
            squares = squares + before[1][length:]
        own_ref[...] = own
        other_ref[:length] = other
        other_ref[length:] = squares

    outs = [((length, inner), F32), ((length + 8, inner), F32)]
    if index == 0:
        outs.append(((8, 128), F32))
    return call(kernel, [got, held, pair] + extra + sums, outs, token, [ends, limit])


def cotangent_kernel(
    share, limit_ref, own_ref, other_ref, got_ref, soft_ref, key_ref, value_ref, down_q_ref,
    down_v_ref, out_ref,
):
    length, inner = own_ref.shape
    rank = down_q_ref.shape[1]
    live = live_pairs(limit_ref[0], length)
    pulled = (own_ref[...] + got_ref[:length]).astype(BF16)
    out_ref[2 * rank :] = other_ref[length:] + got_ref[length:]
    queries, values = [], []
    for h in range(inner // HEAD_DIM):
        soft = soft_ref[h]
        rows = pulled[:, head(h)]
        d_probs = dot_nt(rows, value_ref[:, head(h)]).astype(BF16).astype(F32)
        values.append(dot_tn(soft.astype(BF16), rows).astype(BF16).astype(F32))
        d_scores = soft * (d_probs - jnp.sum(soft * d_probs, axis=-1, keepdims=True))
        d_scores = jnp.where(live, d_scores, 0.0) * SCALE
        d_query = dot32(d_scores.astype(BF16), key_ref[:, head(h)])
        queries.append(d_query.astype(BF16).astype(F32))
    out_ref[:rank] = share * lax.dot_general(
        down_q_ref[...], jnp.concatenate(queries, axis=1), (((0,), (0,)), ((), ())),
        precision=HIGH, preferred_element_type=F32,
    )
    out_ref[rank : 2 * rank] = share * lax.dot_general(
        down_v_ref[...], jnp.concatenate(values, axis=1), (((0,), (0,)), ((), ())),
        precision=HIGH, preferred_element_type=F32,
    )


def cotangent(share, limit, own, other, got, attention):
    inner = own.shape[1]
    rank = attention[3].shape[1]
    return pl.pallas_call(
        functools.partial(cotangent_kernel, share),
        in_specs=[SMEM] + [VMEM] * 8,
        out_specs=VMEM,
        out_shape=jax.ShapeDtypeStruct((2 * rank + 8, inner), F32),
        compiler_params=pltpu.CompilerParams(vmem_limit_bytes=LIMIT),
    )(limit, own, other, got, *attention)


def tangent_of(vector, limit, soft_ref, key_ref, value_ref, down_q_ref, down_v_ref, out_ref):
    length = key_ref.shape[0]
    rank = down_q_ref.shape[1]
    live = live_pairs(limit, length)
    kept = rows_below(limit, length, HEAD_DIM)
    d_query = (ADAPTER_SCALE * high(down_q_ref[...], vector[:rank])).astype(BF16)
    d_value = (ADAPTER_SCALE * high(down_v_ref[...], vector[rank:])).astype(BF16)
    for h in range(key_ref.shape[1] // HEAD_DIM):
        soft = soft_ref[h]
        d_scores = dot_nt(d_query[:, head(h)], key_ref[:, head(h)]) * SCALE
        d_scores = jnp.where(live, d_scores, 0.0)
        d_probs = soft * (d_scores - jnp.sum(soft * d_scores, axis=-1, keepdims=True))
        d_mixed = dot32(d_probs.astype(BF16), value_ref[:, head(h)]) + dot32(
            soft.astype(BF16), d_value[:, head(h)]
        )
        out_ref[:length, head(h)] = jnp.where(kept, d_mixed.astype(BF16).astype(F32), 0.0)


def total_of(terms):
    while len(terms) > 1:
        terms = [terms[i] + terms[i + 1] for i in range(0, len(terms), 2)]
    return terms[0]


def put_sums(out_ref, remain, image):
    lane = lax.broadcasted_iota(jnp.int32, (8, out_ref.shape[1]), 1)
    cross = 0.0 if image is None else jnp.sum(remain * image)
    out_ref[out_ref.shape[0] - 8 :] = jnp.where(lane == 0, jnp.sum(remain * remain), cross)


def first_kernel(n_dp, *refs):
    terms, refs = refs[:n_dp], refs[n_dp:]
    limit_ref, *attention, remain_ref, out_ref = refs
    grads = total_of([term[...] for term in terms])
    remain = -grads[: remain_ref.shape[0]]
    remain_ref[...] = remain
    put_sums(out_ref, remain, None)
    tangent_of(remain, limit_ref[0], *attention, out_ref)


def first_step(terms, limit, attention):
    inner = terms[0].shape[1]
    length = attention[1].shape[0]
    rank = attention[3].shape[1]
    return pl.pallas_call(
        functools.partial(first_kernel, len(terms)),
        in_specs=[VMEM] * len(terms) + [SMEM] + [VMEM] * 5,
        out_specs=[VMEM] * 2,
        out_shape=[
            jax.ShapeDtypeStruct((2 * rank, inner), F32),
            jax.ShapeDtypeStruct((length + 8, inner), F32),
        ],
        compiler_params=pltpu.CompilerParams(vmem_limit_bytes=LIMIT),
    )(*terms, limit, *attention)


def step_kernel(n_dp, token_count, index, last, *refs):
    terms, refs = refs[:n_dp], refs[n_dp:]
    sums_ref, remain_ref, *refs = refs
    if index:
        before_ref, newton_ref, direction_ref, image_ref, *refs = refs
    part = total_of([term[...] for term in terms])
    remain = remain_ref[...]
    rows = remain.shape[0]
    norm, cross = sums_ref[:1, 0:1], sums_ref[:1, 1:2]
    fresh = part[:rows] + DAMP * remain
    curv = part[rows : rows + 1, 0:1] / token_count + DAMP * norm
    if index:
        ratio = norm / before_ref[:1, 0:1]
        curv = curv + 2.0 * ratio * cross + ratio * ratio * before_ref[:1, 1:2]
        direction = remain + ratio * direction_ref[...]
        image = fresh + ratio * image_ref[...]
    else:
        direction, image = remain, fresh
    alpha = norm / curv
    newton = alpha * direction
    if index:
        newton = newton_ref[...] + newton
    remain = remain - alpha * image
    if last:
        step_q_ref, step_v_ref, remain_q_ref, remain_v_ref = refs
        rank = rows // 2
        step_q_ref[...] = newton[:rank]
        step_v_ref[...] = newton[rank:]
        remain_q_ref[...] = remain[:rank]
        remain_v_ref[...] = remain[rank:]
        return
    limit_ref, *refs = refs
    attention, refs = refs[:5], refs[5:]
    next_remain, next_before, next_newton, next_direction, next_image, out_ref = refs
    lane = lax.broadcasted_iota(jnp.int32, next_before.shape, 1)
    next_remain[...] = remain
    next_before[...] = jnp.where(lane == 0, norm, curv)
    next_newton[...] = newton
    next_direction[...] = direction
    next_image[...] = image
    put_sums(out_ref, remain, image)
    tangent_of(remain, limit_ref[0], *attention, out_ref)


def cg_step(index, token_count, terms, sums, remain, state, limit, attention):
    last = index == CG_STEPS - 1
    rows, inner = remain.shape
    matrix = jax.ShapeDtypeStruct((rows, inner), F32)
    scalars = jax.ShapeDtypeStruct((8, 128), F32)
    args = [*terms, sums, remain, *state]
    specs = [VMEM] * len(args)
    if last:
        shapes = [jax.ShapeDtypeStruct((rows // 2, inner), F32)] * 4
    else:
        args += [limit, *attention]
        specs += [SMEM] + [VMEM] * 5
        length = attention[1].shape[0]
        shapes = [matrix, scalars, matrix, matrix, matrix]
        shapes.append(jax.ShapeDtypeStruct((length + 8, inner), F32))
    return pl.pallas_call(
        functools.partial(step_kernel, len(terms), token_count, index, last),
        in_specs=specs,
        out_specs=[VMEM] * len(shapes),
        out_shape=shapes,
        compiler_params=pltpu.CompilerParams(vmem_limit_bytes=LIMIT),
    )(*args)


def on_device(
    inputs,
    targets,
    lengths,
    ln_gain,
    ln_bias,
    query_weight,
    w_key,
    value_weight,
    w_out,
    down_query,
    down_value,
    query_up_factor,
    value_up_factor,
):
    length, width = inputs.shape
    n_dp = lax.axis_size("dp")
    n_chip = lax.axis_size("chip")
    core = lax.axis_index("core")
    chip = lax.axis_index("chip")
    token_count = length * n_dp
    half = width // 2

    def swap(part):
        return lax.ppermute(part, "core", [(0, 1), (1, 0)])

    def data_terms(part):
        sent = [
            lax.ppermute(part, "dp", [(d, d ^ step) for d in range(n_dp)])
            for step in range(1, n_dp)
        ]
        return [part, *sent]

    where = core.astype(jnp.int32)[None]
    own_w, other_w = split(where, w_out)
    other_w = [swap(part) for part in other_w]
    cols = half // CHUNKS
    gap = lax.dynamic_slice_in_dim(inputs, core * half, half, 1).astype(F32)
    gap = gap - lax.dynamic_slice_in_dim(targets, core * half, half, 1).astype(F32)

    soft, key, value, down_q, down_v, mixed = project(
        lengths, inputs, ln_gain, ln_bias, query_weight, w_key, value_weight, down_query,
        down_value, query_up_factor, value_up_factor,
    )
    attention = (soft, key, value, down_q, down_v)

    ends = ((chip == 0) | (chip == n_chip - 1)).astype(jnp.int32)[None]

    def outer_swap(part):
        return lax.ppermute(part, "chip", [(0, 1), (1, 0), (2, 3), (3, 2)])

    def send_in(part):
        return lax.ppermute(part, "chip", [(0, 1), (3, 2)])

    def send_back(part):
        return lax.ppermute(part, "chip", [(1, 0), (2, 3)])

    def inner_swap(part):
        hops = [(2, 4), (4, 2), (3, 5), (5, 3), (0, 1), (1, 0), (6, 7), (7, 6)]
        return lax.ppermute(part, ("chip", "core"), hops)

    def product(rows, pairs):
        got_rows = swap(rows)
        first = not pairs
        pairs.extend([None] * (CHUNKS - len(pairs)))
        parts, scalars = [], None
        own_part, total, outer, inner = {}, {}, {}, {}
        token = None

        def begin(k):
            if first:
                own_part[k], pairs[k] = first_spread(
                    k, length, rows, got_rows, own_w[k], other_w[k], token
                )
            else:
                own_part[k] = spread(k, length, rows, got_rows, pairs[k], token)
            return own_part[k]

        def finish(k, got):
            gap_part = gap[:, k * cols : (k + 1) * cols] if first else None
            return gather(k, length, ends, got, total[k], pairs[k], parts, lengths, gap_part, token)

        if n_chip != 4:
            for k in range(CHUNKS):
                token = begin(k)
            for k in range(CHUNKS):
                total[k] = lax.psum(own_part[k], "chip")
                out = finish(k, total[k])
                parts, scalars = list(out[:2]), out[2] if k == 0 else scalars
        else:
            for k in [0, 1, 2] if first else [0, *range(2, CHUNKS), 1]:
                token = begin(k)
            for k in (0, 1):
                outer[k] = outer_swap(own_part[k])
            for tick in range(CHUNKS + 3):
                if tick < CHUNKS:
                    own_part[tick] = add(own_part[tick], outer[tick], token)
                    token = own_part[tick]
                    inner[tick] = inner_swap(token)
                later = tick + 2
                if tick == CHUNKS:
                    out = finish(tick - 3, outer[tick])
                    parts = list(out[:2])
                    token = parts[0]
                if 1 <= tick <= CHUNKS:
                    k = tick - 1
                    if later < CHUNKS:
                        total[k], sent = add_and_pick(
                            own_part[k], inner[k], ends, own_part[later], token
                        )
                    else:
                        total[k] = sent = add(own_part[k], inner[k], token)
                    token = sent
                    outer[later] = send_back(sent) if later == CHUNKS else outer_swap(sent)
                elif tick == 0:
                    outer[later] = send_in(own_part[later])
                if tick + 3 < CHUNKS and first:
                    token = begin(tick + 3)
                if tick >= 3 and tick != CHUNKS:
                    out = finish(tick - 3, outer[tick])
                    parts, scalars = list(out[:2]), out[2] if tick == 3 else scalars
                    token = parts[0]
        own, other = parts
        share = ADAPTER_SCALE / token_count
        part = cotangent(share, lengths, own, other, swap(other), attention)
        return data_terms(part), scalars

    pairs = []
    terms, _ = product(mixed, pairs)
    remain, rows = first_step(terms, lengths, attention)
    state = ()
    for index in range(CG_STEPS):
        terms, sums = product(rows, pairs)
        out = cg_step(index, token_count, terms, sums, remain, state, lengths, attention)
        if index < CG_STEPS - 1:
            remain, *state, rows = out
    return tuple(out)


def solution(mesh):
    fine = Mesh(mesh.devices.reshape(mesh.shape["dp"], -1, 2), ("dp", "chip", "core"))
    tensor = ("chip", "core")
    in_specs = (
        P("dp", None),
        P("dp", None),
        P("dp"),
        P(),
        P(),
        P(None, tensor),
        P(None, tensor),
        P(None, tensor),
        P(tensor, None),
        P(),
        P(),
        P(None, tensor),
        P(None, tensor),
    )
    out_specs = (P(None, tensor),) * 4
    return jax.shard_map(
        on_device, mesh=fine, in_specs=in_specs, out_specs=out_specs, check_vma=False
    )
```

```python
import functools

import jax
import jax.numpy as jnp
from jax import lax
from jax.experimental import pallas as pl
from jax.experimental.pallas import tpu as pltpu
from jax.sharding import Mesh
from jax.sharding import PartitionSpec as P

HEAD_DIM = 128
CG_STEPS = 3
CHUNKS = 6
DEPTH = 1024

EPS = 1e-05
ADAPTER_SCALE = 2.0
DAMP = 0.05
NEG = -1e30
F32 = jnp.float32
BF16 = jnp.bfloat16
HIGH = lax.Precision.HIGHEST
SCALE = HEAD_DIM ** (-0.5)
VMEM = pl.BlockSpec(memory_space=pltpu.VMEM)
SMEM = pl.BlockSpec(memory_space=pltpu.SMEM)
LIMIT = 16 * 1024 * 1024
STEP_COST = pl.CostEstimate(flops=10**9, bytes_accessed=10**7, transcendentals=0)
STREAM_LIMIT = 48 * 1024 * 1024


def dot32(first, second):
    return jnp.dot(first, second, preferred_element_type=F32)


def dot_nt(first, second):
    return lax.dot_general(
        first, second, (((1,), (1,)), ((), ())), preferred_element_type=F32
    )


def dot_tn(first, second):
    return lax.dot_general(
        first, second, (((0,), (0,)), ((), ())), preferred_element_type=F32
    )


def high(first, second):
    return jnp.dot(first, second, precision=HIGH, preferred_element_type=F32)


def head(index):
    return slice(index * HEAD_DIM, (index + 1) * HEAD_DIM)


def rows_below(limit, length, width):
    return lax.broadcasted_iota(jnp.int32, (length, width), 0) < limit


def live_pairs(limit, length):
    row = lax.broadcasted_iota(jnp.int32, (length, length), 0)
    column = lax.broadcasted_iota(jnp.int32, (length, length), 1)
    return (column <= row) & (column < limit)


def split_kernel(core_ref, w_ref, *refs):
    own_refs, other_refs = refs[:CHUNKS], refs[CHUNKS : 2 * CHUNKS]
    landed, own_sem, other_sem = refs[2 * CHUNKS :]
    cols = own_refs[0].shape[1]
    half = CHUNKS * cols
    core = core_ref[0]

    def own_copy(k):
        start = pl.multiple_of(core * half + k * cols, HEAD_DIM)
        return pltpu.make_async_copy(
            w_ref.at[:, pl.ds(start, cols)], own_refs[k], own_sem.at[k]
        )

    def other_copy(k):
        start = pl.multiple_of((1 - core) * half + k * cols, HEAD_DIM)
        return pltpu.make_async_copy(
            w_ref.at[:, pl.ds(start, cols)], landed.at[k], other_sem.at[k]
        )

    for k in range(CHUNKS):
        other_copy(k).start()
    for k in range(CHUNKS):
        own_copy(k).start()
    for k in range(CHUNKS):
        other_copy(k).wait()
        other_refs[k][...] = landed[k].astype(F32)
    for k in range(CHUNKS):
        own_copy(k).wait()


def split(core, w_out):
    inner, width = w_out.shape
    cols = width // 2 // CHUNKS
    out = pl.pallas_call(
        split_kernel,
        in_specs=[SMEM, pl.BlockSpec(memory_space=pltpu.HBM)],
        out_specs=[VMEM] * (2 * CHUNKS),
        out_shape=[jax.ShapeDtypeStruct((inner, cols), BF16)] * CHUNKS
        + [jax.ShapeDtypeStruct((inner, cols), F32)] * CHUNKS,
        scratch_shapes=[
            pltpu.VMEM((CHUNKS, inner, cols), BF16),
            pltpu.SemaphoreType.DMA((CHUNKS,)),
            pltpu.SemaphoreType.DMA((CHUNKS,)),
        ],
        compiler_params=pltpu.CompilerParams(vmem_limit_bytes=LIMIT),
    )(core, w_out)
    return out[:CHUNKS], out[CHUNKS:]


def project_kernel(
    limit_ref, x_ref, wq_ref, wk_ref, wv_ref, gain_ref, bias_ref, aq_ref, av_ref, bq_ref, bv_ref,
    soft_ref, key_ref, value_ref, down_q_ref, down_v_ref, mixed_ref,
    rows_in, normed, wq_in, wk_in, wv_in, rows_sem, weight_sem,
):
    length, width = normed.shape
    inner = key_ref.shape[1]
    blocks = [slice(i, i + DEPTH) for i in range(0, width, DEPTH)]
    rows_copy = pltpu.make_async_copy(x_ref, rows_in, rows_sem)
    rows_copy.start()
    copies = []
    for i, block in enumerate(blocks):
        for j, (source, target) in enumerate(
            [(wq_ref, wq_in), (wk_ref, wk_in), (wv_ref, wv_in)]
        ):
            copies.append(
                pltpu.make_async_copy(
                    source.at[block], target.at[block], weight_sem.at[3 * i + j]
                )
            )
            copies[-1].start()
    rows_copy.wait()
    total = jnp.zeros((length, 1), F32)
    for block in blocks:
        total = total + jnp.sum(rows_in[:, block].astype(F32), axis=-1, keepdims=True)
    mean = total / width
    total = jnp.zeros((length, 1), F32)
    for block in blocks:
        centred = rows_in[:, block].astype(F32) - mean
        total = total + jnp.sum(centred * centred, axis=-1, keepdims=True)
    spread = lax.rsqrt(total / width + EPS)
    for block in blocks:
        centred = rows_in[:, block].astype(F32) - mean
        full = centred * spread * gain_ref[:, block] + bias_ref[:, block]
        normed[:, block] = full.astype(BF16)
    down_q = dot_nt(normed[...], aq_ref[...])
    down_v = dot_nt(normed[...], av_ref[...])
    query = jnp.zeros((length, inner), F32)
    key = jnp.zeros((length, inner), F32)
    value = jnp.zeros((length, inner), F32)
    for i, block in enumerate(blocks):
        part = normed[:, block]
        for j in range(3):
            copies[3 * i + j].wait()
        query = query + dot32(part, wq_in[block])
        key = key + dot32(part, wk_in[block])
        value = value + dot32(part, wv_in[block])
    down_q_ref[...] = down_q
    down_v_ref[...] = down_v
    limit = limit_ref[0]
    live = live_pairs(limit, length)
    kept = rows_below(limit, length, HEAD_DIM)
    query = (query + ADAPTER_SCALE * high(down_q, bq_ref[...])).astype(BF16)
    value = (value + ADAPTER_SCALE * high(down_v, bv_ref[...])).astype(BF16)
    key = key.astype(BF16)
    key_ref[...] = key
    value_ref[...] = value
    for h in range(inner // HEAD_DIM):
        scores = dot_nt(query[:, head(h)], key[:, head(h)]) * SCALE
        scores = jnp.where(live, scores, NEG)
        weights = jnp.exp(scores - jnp.max(scores, axis=-1, keepdims=True))
        soft = weights / jnp.sum(weights, axis=-1, keepdims=True)
        soft_ref[h] = soft
        mixed = dot32(soft.astype(BF16), value[:, head(h)]).astype(BF16)
        mixed_ref[:length, head(h)] = jnp.where(kept, mixed.astype(F32), 0.0)
    mixed_ref[length:] = jnp.zeros((8, inner), F32)


def project(limit, x, gain, bias, wq, wk, wv, aq, av, bq, bv):
    length, width = x.shape
    inner = wq.shape[1]
    rank = aq.shape[1]
    heads = inner // HEAD_DIM
    hbm = pl.BlockSpec(memory_space=pltpu.HBM)
    return pl.pallas_call(
        project_kernel,
        in_specs=[SMEM] + [hbm] * 4 + [VMEM] * 6,
        out_specs=[VMEM] * 6,
        out_shape=[
            jax.ShapeDtypeStruct((heads, length, length), F32),
            jax.ShapeDtypeStruct((length, inner), BF16),
            jax.ShapeDtypeStruct((length, inner), BF16),
            jax.ShapeDtypeStruct((length, rank), F32),
            jax.ShapeDtypeStruct((length, rank), F32),
            jax.ShapeDtypeStruct((length + 8, inner), F32),
        ],
        scratch_shapes=[
            pltpu.VMEM((length, width), BF16),
            pltpu.VMEM((length, width), BF16),
            pltpu.VMEM((width, inner), BF16),
            pltpu.VMEM((width, inner), BF16),
            pltpu.VMEM((width, inner), BF16),
            pltpu.SemaphoreType.DMA,
            pltpu.SemaphoreType.DMA((3 * (width // DEPTH),)),
        ],
        compiler_params=pltpu.CompilerParams(vmem_limit_bytes=STREAM_LIMIT),
        cost_estimate=pl.CostEstimate(
            flops=6 * length * width * inner, bytes_accessed=6 * width * inner, transcendentals=0
        ),
    )(limit, x, wq, wk, wv, gain[None], bias[None], aq.T, av.T, bq, bv)


def token_spec():
    return pl.BlockSpec(memory_space=pl.ANY)


def call(kernel, ins, outs, token, scalars=()):
    tokens = [] if token is None else [token]

    def body(*refs):
        count = len(scalars) + len(ins)
        kernel(*refs[:count], *refs[count + len(tokens) :])

    return pl.pallas_call(
        body,
        in_specs=[SMEM] * len(scalars) + [VMEM] * len(ins) + [token_spec()] * len(tokens),
        out_specs=[VMEM] * len(outs),
        out_shape=[jax.ShapeDtypeStruct(shape, kind) for shape, kind in outs],
        compiler_params=pltpu.CompilerParams(vmem_limit_bytes=LIMIT),
        cost_estimate=STEP_COST,
    )(*scalars, *ins, *tokens)


def rows_of(own_ref, got_ref, length):
    return jnp.concatenate(
        [own_ref[:length].astype(BF16), got_ref[:length].astype(BF16)], axis=1
    )


def put_tail(out_ref, own_ref, got_ref, length):
    out_ref[length:] = jnp.zeros((8, out_ref.shape[1]), F32)
    out_ref[length:, :HEAD_DIM] = own_ref[length:, :HEAD_DIM] + got_ref[length:, :HEAD_DIM]


def first_spread(index, length, own, got, own_w, other_w, token):
    inner, cols = own_w.shape
    height = length + (8 if index == 0 else 0)

    def kernel(own_ref, got_ref, own_w_ref, other_w_ref, out_ref, pair_ref):
        pair_ref[:inner] = own_w_ref[...]
        pair_ref[inner:] = other_w_ref[...].astype(BF16)
        out_ref[:length] = dot32(rows_of(own_ref, got_ref, length), pair_ref[...])
        if index == 0:
            put_tail(out_ref, own_ref, got_ref, length)

    outs = [((height, cols), F32), ((2 * inner, cols), BF16)]
    return call(kernel, [own, got, own_w, other_w], outs, token)


def spread(index, length, own, got, pair, token):
    height = length + (8 if index == 0 else 0)

    def kernel(own_ref, got_ref, pair_ref, out_ref):
        out_ref[:length] = dot32(rows_of(own_ref, got_ref, length), pair_ref[...])
        if index == 0:
            put_tail(out_ref, own_ref, got_ref, length)

    return call(kernel, [own, got, pair], [((height, pair.shape[1]), F32)], token)[0]


def add(first, second, token):
    def kernel(first_ref, second_ref, out_ref):
        out_ref[...] = first_ref[...] + second_ref[: first_ref.shape[0]]

    return call(kernel, [first, second], [(first.shape, F32)], token)[0]


def add_and_pick(first, second, ends, outer, token):
    def kernel(ends_ref, first_ref, second_ref, outer_ref, sum_ref, sent_ref):
        total = first_ref[...] + second_ref[...]
        sum_ref[...] = total
        rows = outer_ref.shape[0]
        sent_ref[:rows] = jnp.where(ends_ref[0] > 0, outer_ref[...], total[:rows])
        if total.shape[0] > rows:
            sent_ref[rows:] = total[rows:]

    outs = [(first.shape, F32)] * 2
    return call(kernel, [first, second, outer], outs, token, [ends])


def gather(index, length, ends, got, held, pair, sums, limit, gap, token):
    inner = pair.shape[0] // 2
    extra = [] if gap is None else [gap]

    def kernel(ends_ref, limit_ref, got_ref, held_ref, pair_ref, *refs):
        refs = list(refs)
        gap_ref = refs.pop(0) if gap is not None else None
        before = [refs.pop(0), refs.pop(0)] if index else None
        own_ref, other_ref = refs[:2]
        total = jnp.where(ends_ref[0] > 0, got_ref[...], held_ref[...])
        total = total[: length + (8 if index == 0 else 0)]
        if index == 0:
            refs[2][...] = total[length:, :128]
            total = total[:length]
        if gap_ref is not None:
            kept = rows_below(limit_ref[0], length, total.shape[1])
            total = jnp.where(kept, total + gap_ref[...], 0.0)
        rounded = total.astype(BF16)
        own = dot_nt(rounded, pair_ref[:inner])
        other = dot_nt(rounded, pair_ref[inner:])
        squares = jnp.full((8, inner), jnp.sum(total * total), F32)
        if index:
            own = own + before[0][...]
            other = other + before[1][:length]
            squares = squares + before[1][length:]
        own_ref[...] = own
        other_ref[:length] = other
        other_ref[length:] = squares

    outs = [((length, inner), F32), ((length + 8, inner), F32)]
    if index == 0:
        outs.append(((8, 128), F32))
    return call(kernel, [got, held, pair] + extra + sums, outs, token, [ends, limit])


def cotangent_kernel(
    share, limit_ref, own_ref, other_ref, got_ref, soft_ref, key_ref, value_ref, down_q_ref,
    down_v_ref, out_ref,
):
    length, inner = own_ref.shape
    rank = down_q_ref.shape[1]
    live = live_pairs(limit_ref[0], length)
    pulled = (own_ref[...] + got_ref[:length]).astype(BF16)
    out_ref[2 * rank :] = other_ref[length:] + got_ref[length:]
    queries, values = [], []
    for h in range(inner // HEAD_DIM):
        soft = soft_ref[h]
        rows = pulled[:, head(h)]
        d_probs = dot_nt(rows, value_ref[:, head(h)]).astype(BF16).astype(F32)
        values.append(dot_tn(soft.astype(BF16), rows).astype(BF16).astype(F32))
        d_scores = soft * (d_probs - jnp.sum(soft * d_probs, axis=-1, keepdims=True))
        d_scores = jnp.where(live, d_scores, 0.0) * SCALE
        d_query = dot32(d_scores.astype(BF16), key_ref[:, head(h)])
        queries.append(d_query.astype(BF16).astype(F32))
    out_ref[:rank] = share * lax.dot_general(
        down_q_ref[...], jnp.concatenate(queries, axis=1), (((0,), (0,)), ((), ())),
        precision=HIGH, preferred_element_type=F32,
    )
    out_ref[rank : 2 * rank] = share * lax.dot_general(
        down_v_ref[...], jnp.concatenate(values, axis=1), (((0,), (0,)), ((), ())),
        precision=HIGH, preferred_element_type=F32,
    )


def cotangent(share, limit, own, other, got, attention):
    inner = own.shape[1]
    rank = attention[3].shape[1]
    return pl.pallas_call(
        functools.partial(cotangent_kernel, share),
        in_specs=[SMEM] + [VMEM] * 8,
        out_specs=VMEM,
        out_shape=jax.ShapeDtypeStruct((2 * rank + 8, inner), F32),
        compiler_params=pltpu.CompilerParams(vmem_limit_bytes=LIMIT),
    )(limit, own, other, got, *attention)


def tangent_of(vector, limit, soft_ref, key_ref, value_ref, down_q_ref, down_v_ref, out_ref):
    length = key_ref.shape[0]
    rank = down_q_ref.shape[1]
    live = live_pairs(limit, length)
    kept = rows_below(limit, length, HEAD_DIM)
    d_query = (ADAPTER_SCALE * high(down_q_ref[...], vector[:rank])).astype(BF16)
    d_value = (ADAPTER_SCALE * high(down_v_ref[...], vector[rank:])).astype(BF16)
    for h in range(key_ref.shape[1] // HEAD_DIM):
        soft = soft_ref[h]
        d_scores = dot_nt(d_query[:, head(h)], key_ref[:, head(h)]) * SCALE
        d_scores = jnp.where(live, d_scores, 0.0)
        d_probs = soft * (d_scores - jnp.sum(soft * d_scores, axis=-1, keepdims=True))
        d_mixed = dot32(d_probs.astype(BF16), value_ref[:, head(h)]) + dot32(
            soft.astype(BF16), d_value[:, head(h)]
        )
        out_ref[:length, head(h)] = jnp.where(kept, d_mixed.astype(BF16).astype(F32), 0.0)


def total_of(terms):
    while len(terms) > 1:
        terms = [terms[i] + terms[i + 1] for i in range(0, len(terms), 2)]
    return terms[0]


def put_sums(out_ref, remain, image):
    lane = lax.broadcasted_iota(jnp.int32, (8, out_ref.shape[1]), 1)
    cross = 0.0 if image is None else jnp.sum(remain * image)
    out_ref[out_ref.shape[0] - 8 :] = jnp.where(lane == 0, jnp.sum(remain * remain), cross)


def first_kernel(n_dp, *refs):
    terms, refs = refs[:n_dp], refs[n_dp:]
    limit_ref, *attention, remain_ref, out_ref = refs
    grads = total_of([term[...] for term in terms])
    remain = -grads[: remain_ref.shape[0]]
    remain_ref[...] = remain
    put_sums(out_ref, remain, None)
    tangent_of(remain, limit_ref[0], *attention, out_ref)


def first_step(terms, limit, attention):
    inner = terms[0].shape[1]
    length = attention[1].shape[0]
    rank = attention[3].shape[1]
    return pl.pallas_call(
        functools.partial(first_kernel, len(terms)),
        in_specs=[VMEM] * len(terms) + [SMEM] + [VMEM] * 5,
        out_specs=[VMEM] * 2,
        out_shape=[
            jax.ShapeDtypeStruct((2 * rank, inner), F32),
            jax.ShapeDtypeStruct((length + 8, inner), F32),
        ],
        compiler_params=pltpu.CompilerParams(vmem_limit_bytes=LIMIT),
    )(*terms, limit, *attention)


def step_kernel(n_dp, token_count, index, last, *refs):
    terms, refs = refs[:n_dp], refs[n_dp:]
    sums_ref, remain_ref, *refs = refs
    if index:
        before_ref, newton_ref, direction_ref, image_ref, *refs = refs
    part = total_of([term[...] for term in terms])
    remain = remain_ref[...]
    rows = remain.shape[0]
    norm, cross = sums_ref[:1, 0:1], sums_ref[:1, 1:2]
    fresh = part[:rows] + DAMP * remain
    curv = part[rows : rows + 1, 0:1] / token_count + DAMP * norm
    if index:
        ratio = norm / before_ref[:1, 0:1]
        curv = curv + 2.0 * ratio * cross + ratio * ratio * before_ref[:1, 1:2]
        direction = remain + ratio * direction_ref[...]
        image = fresh + ratio * image_ref[...]
    else:
        direction, image = remain, fresh
    alpha = norm / curv
    newton = alpha * direction
    if index:
        newton = newton_ref[...] + newton
    remain = remain - alpha * image
    if last:
        step_q_ref, step_v_ref, remain_q_ref, remain_v_ref = refs
        rank = rows // 2
        step_q_ref[...] = newton[:rank]
        step_v_ref[...] = newton[rank:]
        remain_q_ref[...] = remain[:rank]
        remain_v_ref[...] = remain[rank:]
        return
    limit_ref, *refs = refs
    attention, refs = refs[:5], refs[5:]
    next_remain, next_before, next_newton, next_direction, next_image, out_ref = refs
    lane = lax.broadcasted_iota(jnp.int32, next_before.shape, 1)
    next_remain[...] = remain
    next_before[...] = jnp.where(lane == 0, norm, curv)
    next_newton[...] = newton
    next_direction[...] = direction
    next_image[...] = image
    put_sums(out_ref, remain, image)
    tangent_of(remain, limit_ref[0], *attention, out_ref)


def cg_step(index, token_count, terms, sums, remain, state, limit, attention):
    last = index == CG_STEPS - 1
    rows, inner = remain.shape
    matrix = jax.ShapeDtypeStruct((rows, inner), F32)
    scalars = jax.ShapeDtypeStruct((8, 128), F32)
    args = [*terms, sums, remain, *state]
    specs = [VMEM] * len(args)
    if last:
        shapes = [jax.ShapeDtypeStruct((rows // 2, inner), F32)] * 4
    else:
        args += [limit, *attention]
        specs += [SMEM] + [VMEM] * 5
        length = attention[1].shape[0]
        shapes = [matrix, scalars, matrix, matrix, matrix]
        shapes.append(jax.ShapeDtypeStruct((length + 8, inner), F32))
    return pl.pallas_call(
        functools.partial(step_kernel, len(terms), token_count, index, last),
        in_specs=specs,
        out_specs=[VMEM] * len(shapes),
        out_shape=shapes,
        compiler_params=pltpu.CompilerParams(vmem_limit_bytes=LIMIT),
    )(*args)


def on_device(
    inputs,
    targets,
    lengths,
    ln_gain,
    ln_bias,
    query_weight,
    w_key,
    value_weight,
    w_out,
    down_query,
    down_value,
    query_up_factor,
    value_up_factor,
):
    length, width = inputs.shape
    n_dp = lax.axis_size("dp")
    n_chip = lax.axis_size("chip")
    core = lax.axis_index("core")
    chip = lax.axis_index("chip")
    token_count = length * n_dp
    half = width // 2

    def swap(part):
        return lax.ppermute(part, "core", [(0, 1), (1, 0)])

    def data_terms(part):
        sent = [
            lax.ppermute(part, "dp", [(d, d ^ step) for d in range(n_dp)])
            for step in range(1, n_dp)
        ]
        return [part, *sent]

    where = core.astype(jnp.int32)[None]
    own_w, other_w = split(where, w_out)
    other_w = [swap(part) for part in other_w]
    cols = half // CHUNKS
    gap = lax.dynamic_slice_in_dim(inputs, core * half, half, 1).astype(F32)
    gap = gap - lax.dynamic_slice_in_dim(targets, core * half, half, 1).astype(F32)

    soft, key, value, down_q, down_v, mixed = project(
        lengths, inputs, ln_gain, ln_bias, query_weight, w_key, value_weight, down_query,
        down_value, query_up_factor, value_up_factor,
    )
    attention = (soft, key, value, down_q, down_v)

    ends = ((chip == 0) | (chip == n_chip - 1)).astype(jnp.int32)[None]

    def outer_swap(part):
        return lax.ppermute(part, "chip", [(0, 1), (1, 0), (2, 3), (3, 2)])

    def send_in(part):
        return lax.ppermute(part, "chip", [(0, 1), (3, 2)])

    def send_back(part):
        return lax.ppermute(part, "chip", [(1, 0), (2, 3)])

    def inner_swap(part):
        hops = [(2, 4), (4, 2), (3, 5), (5, 3), (0, 1), (1, 0), (6, 7), (7, 6)]
        return lax.ppermute(part, ("chip", "core"), hops)

    def product(rows, pairs):
        got_rows = swap(rows)
        first = not pairs
        pairs.extend([None] * (CHUNKS - len(pairs)))
        parts, scalars = [], None
        own_part, total, outer, inner = {}, {}, {}, {}
        token = None

        def begin(k):
            if first:
                own_part[k], pairs[k] = first_spread(
                    k, length, rows, got_rows, own_w[k], other_w[k], token
                )
            else:
                own_part[k] = spread(k, length, rows, got_rows, pairs[k], token)
            return own_part[k]

        def finish(k, got):
            gap_part = gap[:, k * cols : (k + 1) * cols] if first else None
            return gather(k, length, ends, got, total[k], pairs[k], parts, lengths, gap_part, token)

        if n_chip != 4:
            for k in range(CHUNKS):
                token = begin(k)
            for k in range(CHUNKS):
                total[k] = lax.psum(own_part[k], "chip")
                out = finish(k, total[k])
                parts, scalars = list(out[:2]), out[2] if k == 0 else scalars
        else:
            for k in [0, 1, 2] if first else [0, *range(2, CHUNKS), 1]:
                token = begin(k)
            for k in (0, 1):
                outer[k] = outer_swap(own_part[k])
            for tick in range(CHUNKS + 3):
                if tick < CHUNKS:
                    own_part[tick] = add(own_part[tick], outer[tick], token)
                    token = own_part[tick]
                    inner[tick] = inner_swap(token)
                later = tick + 2
                if tick == CHUNKS:
                    out = finish(tick - 3, outer[tick])
                    parts = list(out[:2])
                    token = parts[0]
                if 1 <= tick <= CHUNKS:
                    k = tick - 1
                    if later < CHUNKS:
                        total[k], sent = add_and_pick(
                            own_part[k], inner[k], ends, own_part[later], token
                        )
                    else:
                        total[k] = sent = add(own_part[k], inner[k], token)
                    token = sent
                    outer[later] = send_back(sent) if later == CHUNKS else outer_swap(sent)
                elif tick == 0:
                    outer[later] = send_in(own_part[later])
                if tick + 3 < CHUNKS and first:
                    token = begin(tick + 3)
                if tick >= 3 and tick != CHUNKS:
                    out = finish(tick - 3, outer[tick])
                    parts, scalars = list(out[:2]), out[2] if tick == 3 else scalars
                    token = parts[0]
        own, other = parts
        share = ADAPTER_SCALE / token_count
        part = cotangent(share, lengths, own, other, swap(other), attention)
        return data_terms(part), scalars

    pairs = []
    terms, _ = product(mixed, pairs)
    remain, rows = first_step(terms, lengths, attention)
    state = ()
    for index in range(CG_STEPS):
        terms, sums = product(rows, pairs)
        out = cg_step(index, token_count, terms, sums, remain, state, lengths, attention)
        if index < CG_STEPS - 1:
            remain, *state, rows = out
    return tuple(out)


def solution(mesh):
    fine = Mesh(mesh.devices.reshape(mesh.shape["dp"], -1, 2), ("dp", "chip", "core"))
    tensor = ("chip", "core")
    in_specs = (
        P("dp", None),
        P("dp", None),
        P("dp"),
        P(),
        P(),
        P(None, tensor),
        P(None, tensor),
        P(None, tensor),
        P(tensor, None),
        P(),
        P(),
        P(None, tensor),
        P(None, tensor),
    )
    out_specs = (P(None, tensor),) * 4
    return jax.shard_map(
        on_device, mesh=fine, in_specs=in_specs, out_specs=out_specs, check_vma=False
    )
```

```python
import functools

import jax
import jax.numpy as jnp
from jax import lax
from jax.experimental import pallas as pl
from jax.experimental.pallas import tpu as pltpu
from jax.sharding import Mesh
from jax.sharding import PartitionSpec as P

HEAD_DIM = 128
CG_STEPS = 3
CHUNKS = 6
DEPTH = 1024

EPS = 1e-05
ADAPTER_SCALE = 2.0
DAMP = 0.05
NEG = -1e30
F32 = jnp.float32
BF16 = jnp.bfloat16
HIGH = lax.Precision.HIGHEST
SCALE = HEAD_DIM ** (-0.5)
VMEM = pl.BlockSpec(memory_space=pltpu.VMEM)
SMEM = pl.BlockSpec(memory_space=pltpu.SMEM)
LIMIT = 16 * 1024 * 1024
STEP_COST = pl.CostEstimate(flops=10**9, bytes_accessed=10**7, transcendentals=0)
STREAM_LIMIT = 48 * 1024 * 1024


def dot32(first, second):
    return jnp.dot(first, second, preferred_element_type=F32)


def dot_nt(first, second):
    return lax.dot_general(
        first, second, (((1,), (1,)), ((), ())), preferred_element_type=F32
    )


def dot_tn(first, second):
    return lax.dot_general(
        first, second, (((0,), (0,)), ((), ())), preferred_element_type=F32
    )


def high(first, second):
    return jnp.dot(first, second, precision=HIGH, preferred_element_type=F32)


def head(index):
    return slice(index * HEAD_DIM, (index + 1) * HEAD_DIM)


def rows_below(limit, length, width):
    return lax.broadcasted_iota(jnp.int32, (length, width), 0) < limit


def live_pairs(limit, length):
    row = lax.broadcasted_iota(jnp.int32, (length, length), 0)
    column = lax.broadcasted_iota(jnp.int32, (length, length), 1)
    return (column <= row) & (column < limit)


def split_kernel(core_ref, w_ref, *refs):
    own_refs, other_refs = refs[:CHUNKS], refs[CHUNKS : 2 * CHUNKS]
    landed, own_sem, other_sem = refs[2 * CHUNKS :]
    cols = own_refs[0].shape[1]
    half = CHUNKS * cols
    core = core_ref[0]

    def own_copy(k):
        start = pl.multiple_of(core * half + k * cols, HEAD_DIM)
        return pltpu.make_async_copy(
            w_ref.at[:, pl.ds(start, cols)], own_refs[k], own_sem.at[k]
        )

    def other_copy(k):
        start = pl.multiple_of((1 - core) * half + k * cols, HEAD_DIM)
        return pltpu.make_async_copy(
            w_ref.at[:, pl.ds(start, cols)], landed.at[k], other_sem.at[k]
        )

    for k in range(CHUNKS):
        other_copy(k).start()
    for k in range(CHUNKS):
        own_copy(k).start()
    for k in range(CHUNKS):
        other_copy(k).wait()
        other_refs[k][...] = landed[k].astype(F32)
    for k in range(CHUNKS):
        own_copy(k).wait()


def split(core, w_out):
    inner, width = w_out.shape
    cols = width // 2 // CHUNKS
    out = pl.pallas_call(
        split_kernel,
        in_specs=[SMEM, pl.BlockSpec(memory_space=pltpu.HBM)],
        out_specs=[VMEM] * (2 * CHUNKS),
        out_shape=[jax.ShapeDtypeStruct((inner, cols), BF16)] * CHUNKS
        + [jax.ShapeDtypeStruct((inner, cols), F32)] * CHUNKS,
        scratch_shapes=[
            pltpu.VMEM((CHUNKS, inner, cols), BF16),
            pltpu.SemaphoreType.DMA((CHUNKS,)),
            pltpu.SemaphoreType.DMA((CHUNKS,)),
        ],
        compiler_params=pltpu.CompilerParams(vmem_limit_bytes=LIMIT),
    )(core, w_out)
    return out[:CHUNKS], out[CHUNKS:]


def project_kernel(
    limit_ref, x_ref, wq_ref, wk_ref, wv_ref, gain_ref, bias_ref, aq_ref, av_ref, bq_ref, bv_ref,
    soft_ref, key_ref, value_ref, down_q_ref, down_v_ref, mixed_ref,
    rows_in, normed, wq_in, wk_in, wv_in, rows_sem, weight_sem,
):
    length, width = normed.shape
    inner = key_ref.shape[1]
    blocks = [slice(i, i + DEPTH) for i in range(0, width, DEPTH)]
    rows_copy = pltpu.make_async_copy(x_ref, rows_in, rows_sem)
    rows_copy.start()
    copies = []
    for i, block in enumerate(blocks):
        for j, (source, target) in enumerate(
            [(wq_ref, wq_in), (wk_ref, wk_in), (wv_ref, wv_in)]
        ):
            copies.append(
                pltpu.make_async_copy(
                    source.at[block], target.at[block], weight_sem.at[3 * i + j]
                )
            )
            copies[-1].start()
    rows_copy.wait()
    total = jnp.zeros((length, 1), F32)
    for block in blocks:
        total = total + jnp.sum(rows_in[:, block].astype(F32), axis=-1, keepdims=True)
    mean = total / width
    total = jnp.zeros((length, 1), F32)
    for block in blocks:
        centred = rows_in[:, block].astype(F32) - mean
        total = total + jnp.sum(centred * centred, axis=-1, keepdims=True)
    spread = lax.rsqrt(total / width + EPS)
    for block in blocks:
        centred = rows_in[:, block].astype(F32) - mean
        full = centred * spread * gain_ref[:, block] + bias_ref[:, block]
        normed[:, block] = full.astype(BF16)
    down_q = dot_nt(normed[...], aq_ref[...])
    down_v = dot_nt(normed[...], av_ref[...])
    query = jnp.zeros((length, inner), F32)
    key = jnp.zeros((length, inner), F32)
    value = jnp.zeros((length, inner), F32)
    for i, block in enumerate(blocks):
        part = normed[:, block]
        for j in range(3):
            copies[3 * i + j].wait()
        query = query + dot32(part, wq_in[block])
        key = key + dot32(part, wk_in[block])
        value = value + dot32(part, wv_in[block])
    down_q_ref[...] = down_q
    down_v_ref[...] = down_v
    limit = limit_ref[0]
    live = live_pairs(limit, length)
    kept = rows_below(limit, length, HEAD_DIM)
    query = (query + ADAPTER_SCALE * high(down_q, bq_ref[...])).astype(BF16)
    value = (value + ADAPTER_SCALE * high(down_v, bv_ref[...])).astype(BF16)
    key = key.astype(BF16)
    key_ref[...] = key
    value_ref[...] = value
    for h in range(inner // HEAD_DIM):
        scores = dot_nt(query[:, head(h)], key[:, head(h)]) * SCALE
        scores = jnp.where(live, scores, NEG)
        weights = jnp.exp(scores - jnp.max(scores, axis=-1, keepdims=True))
        soft = weights / jnp.sum(weights, axis=-1, keepdims=True)
        soft_ref[h] = soft
        mixed = dot32(soft.astype(BF16), value[:, head(h)]).astype(BF16)
        mixed_ref[:length, head(h)] = jnp.where(kept, mixed.astype(F32), 0.0)
    mixed_ref[length:] = jnp.zeros((8, inner), F32)


def project(limit, x, gain, bias, wq, wk, wv, aq, av, bq, bv):
    length, width = x.shape
    inner = wq.shape[1]
    rank = aq.shape[1]
    heads = inner // HEAD_DIM
    hbm = pl.BlockSpec(memory_space=pltpu.HBM)
    return pl.pallas_call(
        project_kernel,
        in_specs=[SMEM] + [hbm] * 4 + [VMEM] * 6,
        out_specs=[VMEM] * 6,
        out_shape=[
            jax.ShapeDtypeStruct((heads, length, length), F32),
            jax.ShapeDtypeStruct((length, inner), BF16),
            jax.ShapeDtypeStruct((length, inner), BF16),
            jax.ShapeDtypeStruct((length, rank), F32),
            jax.ShapeDtypeStruct((length, rank), F32),
            jax.ShapeDtypeStruct((length + 8, inner), F32),
        ],
        scratch_shapes=[
            pltpu.VMEM((length, width), BF16),
            pltpu.VMEM((length, width), BF16),
            pltpu.VMEM((width, inner), BF16),
            pltpu.VMEM((width, inner), BF16),
            pltpu.VMEM((width, inner), BF16),
            pltpu.SemaphoreType.DMA,
            pltpu.SemaphoreType.DMA((3 * (width // DEPTH),)),
        ],
        compiler_params=pltpu.CompilerParams(vmem_limit_bytes=STREAM_LIMIT),
        cost_estimate=pl.CostEstimate(
            flops=6 * length * width * inner, bytes_accessed=6 * width * inner, transcendentals=0
        ),
    )(limit, x, wq, wk, wv, gain[None], bias[None], aq.T, av.T, bq, bv)


def token_spec():
    return pl.BlockSpec(memory_space=pl.ANY)


def call(kernel, ins, outs, token, scalars=()):
    tokens = [] if token is None else [token]

    def body(*refs):
        count = len(scalars) + len(ins)
        kernel(*refs[:count], *refs[count + len(tokens) :])

    return pl.pallas_call(
        body,
        in_specs=[SMEM] * len(scalars) + [VMEM] * len(ins) + [token_spec()] * len(tokens),
        out_specs=[VMEM] * len(outs),
        out_shape=[jax.ShapeDtypeStruct(shape, kind) for shape, kind in outs],
        compiler_params=pltpu.CompilerParams(vmem_limit_bytes=LIMIT),
        cost_estimate=STEP_COST,
    )(*scalars, *ins, *tokens)


def rows_of(own_ref, got_ref, length):
    return jnp.concatenate(
        [own_ref[:length].astype(BF16), got_ref[:length].astype(BF16)], axis=1
    )


def put_tail(out_ref, own_ref, got_ref, length):
    out_ref[length:] = jnp.zeros((8, out_ref.shape[1]), F32)
    out_ref[length:, :HEAD_DIM] = own_ref[length:, :HEAD_DIM] + got_ref[length:, :HEAD_DIM]


def first_spread(index, length, own, got, own_w, other_w, token):
    inner, cols = own_w.shape
    height = length + (8 if index == 0 else 0)

    def kernel(own_ref, got_ref, own_w_ref, other_w_ref, out_ref, pair_ref):
        pair_ref[:inner] = own_w_ref[...]
        pair_ref[inner:] = other_w_ref[...].astype(BF16)
        out_ref[:length] = dot32(rows_of(own_ref, got_ref, length), pair_ref[...])
        if index == 0:
            put_tail(out_ref, own_ref, got_ref, length)

    outs = [((height, cols), F32), ((2 * inner, cols), BF16)]
    return call(kernel, [own, got, own_w, other_w], outs, token)


def spread(index, length, own, got, pair, token):
    height = length + (8 if index == 0 else 0)
    last = index == CHUNKS - 1

    def kernel(own_ref, got_ref, pair_ref, out_ref, *meet_ref):
        out_ref[:length] = dot32(rows_of(own_ref, got_ref, length), pair_ref[...])
        if index == 0:
            put_tail(out_ref, own_ref, got_ref, length)
        if last:
            meet_ref[0][...] = own_ref[length:, :HEAD_DIM]

    outs = [((height, pair.shape[1]), F32)]
    if last:
        outs.append(((8, HEAD_DIM), F32))
    return call(kernel, [own, got, pair], outs, token)


def add(first, second, token):
    def kernel(first_ref, second_ref, out_ref):
        out_ref[...] = first_ref[...] + second_ref[: first_ref.shape[0]]

    return call(kernel, [first, second], [(first.shape, F32)], token)[0]


def add_and_pick(first, second, ends, outer, token):
    def kernel(ends_ref, first_ref, second_ref, outer_ref, sum_ref, sent_ref):
        total = first_ref[...] + second_ref[...]
        sum_ref[...] = total
        rows = outer_ref.shape[0]
        sent_ref[:rows] = jnp.where(ends_ref[0] > 0, outer_ref[...], total[:rows])
        if total.shape[0] > rows:
            sent_ref[rows:] = total[rows:]

    outs = [(first.shape, F32)] * 2
    return call(kernel, [first, second, outer], outs, token, [ends])


def gather(index, length, ends, got, held, pair, sums, limit, gap, token):
    inner = pair.shape[0] // 2
    extra = [] if gap is None else [gap]

    def kernel(ends_ref, limit_ref, got_ref, held_ref, pair_ref, *refs):
        refs = list(refs)
        gap_ref = refs.pop(0) if gap is not None else None
        before = [refs.pop(0), refs.pop(0)] if index else None
        own_ref, other_ref = refs[:2]
        total = jnp.where(ends_ref[0] > 0, got_ref[...], held_ref[...])
        total = total[: length + (8 if index == 0 else 0)]
        if index == 0:
            refs[2][...] = total[length:, :128]
            total = total[:length]
        if gap_ref is not None:
            kept = rows_below(limit_ref[0], length, total.shape[1])
            total = jnp.where(kept, total + gap_ref[...], 0.0)
        rounded = total.astype(BF16)
        own = dot_nt(rounded, pair_ref[:inner])
        other = dot_nt(rounded, pair_ref[inner:])
        squares = jnp.full((8, inner), jnp.sum(total * total), F32)
        if index:
            own = own + before[0][...]
            other = other + before[1][:length]
            squares = squares + before[1][length:]
        own_ref[...] = own
        other_ref[:length] = other
        other_ref[length:] = squares

    outs = [((length, inner), F32), ((length + 8, inner), F32)]
    if index == 0:
        outs.append(((8, 128), F32))
    return call(kernel, [got, held, pair] + extra + sums, outs, token, [ends, limit])


def cotangent_kernel(
    share, limit_ref, own_ref, other_ref, got_ref, soft_ref, key_ref, value_ref, down_q_ref,
    down_v_ref, out_ref,
):
    length, inner = own_ref.shape
    rank = down_q_ref.shape[1]
    live = live_pairs(limit_ref[0], length)
    pulled = (own_ref[...] + got_ref[:length]).astype(BF16)
    out_ref[2 * rank :] = other_ref[length:] + got_ref[length:]
    queries, values = [], []
    for h in range(inner // HEAD_DIM):
        soft = soft_ref[h]
        rows = pulled[:, head(h)]
        d_probs = dot_nt(rows, value_ref[:, head(h)]).astype(BF16).astype(F32)
        values.append(dot_tn(soft.astype(BF16), rows).astype(BF16).astype(F32))
        d_scores = soft * (d_probs - jnp.sum(soft * d_probs, axis=-1, keepdims=True))
        d_scores = jnp.where(live, d_scores, 0.0) * SCALE
        d_query = dot32(d_scores.astype(BF16), key_ref[:, head(h)])
        queries.append(d_query.astype(BF16).astype(F32))
    out_ref[:rank] = share * lax.dot_general(
        down_q_ref[...], jnp.concatenate(queries, axis=1), (((0,), (0,)), ((), ())),
        precision=HIGH, preferred_element_type=F32,
    )
    out_ref[rank : 2 * rank] = share * lax.dot_general(
        down_v_ref[...], jnp.concatenate(values, axis=1), (((0,), (0,)), ((), ())),
        precision=HIGH, preferred_element_type=F32,
    )


def cotangent(share, limit, own, other, got, attention):
    inner = own.shape[1]
    rank = attention[3].shape[1]
    return pl.pallas_call(
        functools.partial(cotangent_kernel, share),
        in_specs=[SMEM] + [VMEM] * 8,
        out_specs=VMEM,
        out_shape=jax.ShapeDtypeStruct((2 * rank + 8, inner), F32),
        compiler_params=pltpu.CompilerParams(vmem_limit_bytes=LIMIT),
    )(limit, own, other, got, *attention)


def tangent_of(vector, limit, soft_ref, key_ref, value_ref, down_q_ref, down_v_ref, out_ref):
    length = key_ref.shape[0]
    rank = down_q_ref.shape[1]
    live = live_pairs(limit, length)
    kept = rows_below(limit, length, HEAD_DIM)
    d_query = (ADAPTER_SCALE * high(down_q_ref[...], vector[:rank])).astype(BF16)
    d_value = (ADAPTER_SCALE * high(down_v_ref[...], vector[rank:])).astype(BF16)
    for h in range(key_ref.shape[1] // HEAD_DIM):
        soft = soft_ref[h]
        d_scores = dot_nt(d_query[:, head(h)], key_ref[:, head(h)]) * SCALE
        d_scores = jnp.where(live, d_scores, 0.0)
        d_probs = soft * (d_scores - jnp.sum(soft * d_scores, axis=-1, keepdims=True))
        d_mixed = dot32(d_probs.astype(BF16), value_ref[:, head(h)]) + dot32(
            soft.astype(BF16), d_value[:, head(h)]
        )
        out_ref[:length, head(h)] = jnp.where(kept, d_mixed.astype(BF16).astype(F32), 0.0)


def total_of(terms):
    while len(terms) > 1:
        terms = [terms[i] + terms[i + 1] for i in range(0, len(terms), 2)]
    return terms[0]


def put_sums(out_ref, remain, image):
    lane = lax.broadcasted_iota(jnp.int32, (8, out_ref.shape[1]), 1)
    cross = 0.0 if image is None else jnp.sum(remain * image)
    out_ref[out_ref.shape[0] - 8 :] = jnp.where(lane == 0, jnp.sum(remain * remain), cross)


def first_kernel(n_dp, *refs):
    terms, refs = refs[:n_dp], refs[n_dp:]
    limit_ref, *attention, remain_ref, out_ref = refs
    grads = total_of([term[...] for term in terms])
    remain = -grads[: remain_ref.shape[0]]
    remain_ref[...] = remain
    put_sums(out_ref, remain, None)
    tangent_of(remain, limit_ref[0], *attention, out_ref)


def first_step(terms, limit, attention):
    inner = terms[0].shape[1]
    length = attention[1].shape[0]
    rank = attention[3].shape[1]
    return pl.pallas_call(
        functools.partial(first_kernel, len(terms)),
        in_specs=[VMEM] * len(terms) + [SMEM] + [VMEM] * 5,
        out_specs=[VMEM] * 2,
        out_shape=[
            jax.ShapeDtypeStruct((2 * rank, inner), F32),
            jax.ShapeDtypeStruct((length + 8, inner), F32),
        ],
        compiler_params=pltpu.CompilerParams(vmem_limit_bytes=LIMIT),
    )(*terms, limit, *attention)


def step_kernel(n_dp, token_count, index, last, *refs):
    terms, refs = refs[:n_dp], refs[n_dp:]
    sums_ref, remain_ref, *refs = refs
    if index:
        before_ref, newton_ref, direction_ref, image_ref, *refs = refs
    part = total_of([term[...] for term in terms])
    remain = remain_ref[...]
    rows = remain.shape[0]
    norm, cross = sums_ref[:1, 0:1], sums_ref[:1, 1:2]
    fresh = part[:rows] + DAMP * remain
    curv = part[rows : rows + 1, 0:1] / token_count + DAMP * norm
    if index:
        ratio = norm / before_ref[:1, 0:1]
        curv = curv + 2.0 * ratio * cross + ratio * ratio * before_ref[:1, 1:2]
        direction = remain + ratio * direction_ref[...]
        image = fresh + ratio * image_ref[...]
    else:
        direction, image = remain, fresh
    alpha = norm / curv
    newton = alpha * direction
    if index:
        newton = newton_ref[...] + newton
    remain = remain - alpha * image
    if last:
        step_q_ref, step_v_ref, remain_q_ref, remain_v_ref = refs
        rank = rows // 2
        step_q_ref[...] = newton[:rank]
        step_v_ref[...] = newton[rank:]
        remain_q_ref[...] = remain[:rank]
        remain_v_ref[...] = remain[rank:]
        return
    limit_ref, *refs = refs
    attention, refs = refs[:5], refs[5:]
    next_remain, next_before, next_newton, next_direction, next_image, out_ref = refs
    lane = lax.broadcasted_iota(jnp.int32, next_before.shape, 1)
    next_remain[...] = remain
    next_before[...] = jnp.where(lane == 0, norm, curv)
    next_newton[...] = newton
    next_direction[...] = direction
    next_image[...] = image
    put_sums(out_ref, remain, image)
    tangent_of(remain, limit_ref[0], *attention, out_ref)


def cg_step(index, token_count, terms, sums, remain, state, limit, attention):
    last = index == CG_STEPS - 1
    rows, inner = remain.shape
    matrix = jax.ShapeDtypeStruct((rows, inner), F32)
    scalars = jax.ShapeDtypeStruct((8, 128), F32)
    args = [*terms, sums, remain, *state]
    specs = [VMEM] * len(args)
    if last:
        shapes = [jax.ShapeDtypeStruct((rows // 2, inner), F32)] * 4
    else:
        args += [limit, *attention]
        specs += [SMEM] + [VMEM] * 5
        length = attention[1].shape[0]
        shapes = [matrix, scalars, matrix, matrix, matrix]
        shapes.append(jax.ShapeDtypeStruct((length + 8, inner), F32))
    return pl.pallas_call(
        functools.partial(step_kernel, len(terms), token_count, index, last),
        in_specs=specs,
        out_specs=[VMEM] * len(shapes),
        out_shape=shapes,
        compiler_params=pltpu.CompilerParams(vmem_limit_bytes=LIMIT),
    )(*args)


def on_device(
    inputs,
    targets,
    lengths,
    ln_gain,
    ln_bias,
    query_weight,
    w_key,
    value_weight,
    w_out,
    down_query,
    down_value,
    query_up_factor,
    value_up_factor,
):
    length, width = inputs.shape
    n_dp = lax.axis_size("dp")
    n_chip = lax.axis_size("chip")
    core = lax.axis_index("core")
    chip = lax.axis_index("chip")
    token_count = length * n_dp
    half = width // 2

    def swap(part):
        return lax.ppermute(part, "core", [(0, 1), (1, 0)])

    def data_terms(part):
        sent = [
            lax.ppermute(part, "dp", [(d, d ^ step) for d in range(n_dp)])
            for step in range(1, n_dp)
        ]
        return [part, *sent]

    where = core.astype(jnp.int32)[None]
    own_w, other_w = split(where, w_out)
    other_w = [swap(part) for part in other_w]
    cols = half // CHUNKS
    gap = lax.dynamic_slice_in_dim(inputs, core * half, half, 1).astype(F32)
    gap = gap - lax.dynamic_slice_in_dim(targets, core * half, half, 1).astype(F32)

    soft, key, value, down_q, down_v, mixed = project(
        lengths, inputs, ln_gain, ln_bias, query_weight, w_key, value_weight, down_query,
        down_value, query_up_factor, value_up_factor,
    )
    attention = (soft, key, value, down_q, down_v)

    ends = ((chip == 0) | (chip == n_chip - 1)).astype(jnp.int32)[None]

    def outer_swap(part):
        return lax.ppermute(part, "chip", [(0, 1), (1, 0), (2, 3), (3, 2)])

    def send_in(part):
        return lax.ppermute(part, "chip", [(0, 1), (3, 2)])

    def send_back(part):
        return lax.ppermute(part, "chip", [(1, 0), (2, 3)])

    def inner_swap(part):
        hops = [(2, 4), (4, 2), (3, 5), (5, 3), (0, 1), (1, 0), (6, 7), (7, 6)]
        return lax.ppermute(part, ("chip", "core"), hops)

    def product(rows, pairs):
        got_rows = swap(rows)
        first = not pairs
        pairs.extend([None] * (CHUNKS - len(pairs)))
        parts, scalars = [], None
        own_part, total, outer, inner = {}, {}, {}, {}
        token = None

        def begin(k):
            if first:
                own_part[k], pairs[k] = first_spread(
                    k, length, rows, got_rows, own_w[k], other_w[k], token
                )
            else:
                own_part[k], *meet = spread(k, length, rows, got_rows, pairs[k], token)
                if meet:
                    return swap(meet[0])
            return own_part[k]

        def finish(k, got):
            gap_part = gap[:, k * cols : (k + 1) * cols] if first else None
            return gather(k, length, ends, got, total[k], pairs[k], parts, lengths, gap_part, token)

        if n_chip != 4:
            for k in range(CHUNKS):
                token = begin(k)
            for k in range(CHUNKS):
                total[k] = lax.psum(own_part[k], "chip")
                out = finish(k, total[k])
                parts, scalars = list(out[:2]), out[2] if k == 0 else scalars
        else:
            for k in [0, 1, 2] if first else [0, *range(2, CHUNKS), 1]:
                token = begin(k)
            for k in (0, 1):
                outer[k] = outer_swap(own_part[k])
            for tick in range(CHUNKS + 3):
                if tick < CHUNKS:
                    own_part[tick] = add(own_part[tick], outer[tick], token)
                    token = own_part[tick]
                    inner[tick] = inner_swap(token)
                later = tick + 2
                if tick == CHUNKS:
                    out = finish(tick - 3, outer[tick])
                    parts = list(out[:2])
                    token = parts[0]
                if 1 <= tick <= CHUNKS:
                    k = tick - 1
                    if later < CHUNKS:
                        total[k], sent = add_and_pick(
                            own_part[k], inner[k], ends, own_part[later], token
                        )
                    else:
                        total[k] = sent = add(own_part[k], inner[k], token)
                    token = sent
                    outer[later] = send_back(sent) if later == CHUNKS else outer_swap(sent)
                elif tick == 0:
                    outer[later] = send_in(own_part[later])
                if tick + 3 < CHUNKS and first:
                    token = begin(tick + 3)
                if tick >= 3 and tick != CHUNKS:
                    out = finish(tick - 3, outer[tick])
                    parts, scalars = list(out[:2]), out[2] if tick == 3 else scalars
                    token = parts[0]
        own, other = parts
        share = ADAPTER_SCALE / token_count
        part = cotangent(share, lengths, own, other, swap(other), attention)
        return data_terms(part), scalars

    pairs = []
    terms, _ = product(mixed, pairs)
    remain, rows = first_step(terms, lengths, attention)
    state = ()
    for index in range(CG_STEPS):
        terms, sums = product(rows, pairs)
        out = cg_step(index, token_count, terms, sums, remain, state, lengths, attention)
        if index < CG_STEPS - 1:
            remain, *state, rows = out
    return tuple(out)


def solution(mesh):
    fine = Mesh(mesh.devices.reshape(mesh.shape["dp"], -1, 2), ("dp", "chip", "core"))
    tensor = ("chip", "core")
    in_specs = (
        P("dp", None),
        P("dp", None),
        P("dp"),
        P(),
        P(),
        P(None, tensor),
        P(None, tensor),
        P(None, tensor),
        P(tensor, None),
        P(),
        P(),
        P(None, tensor),
        P(None, tensor),
    )
    out_specs = (P(None, tensor),) * 4
    return jax.shard_map(
        on_device, mesh=fine, in_specs=in_specs, out_specs=out_specs, check_vma=False
    )
```
